32 devices in a mesh: ctx: 32 (over z, y, x, core).
Axes of the slice: x: 2, y: 2, z: 4, core: 2. Of those that a mesh axis runs over, the one named last changes fastest.
Arguments:
- tiles: bfloat16 [8192, 768], P('ctx'), may hold values from -6 to 6
- w_qkv: bfloat16 [768, 2304], replicated, may hold values from -1 to 1
- w_out: bfloat16 [768, 768], replicated, may hold values from -0.21875 to 0.21875
- cotangent: bfloat16 [8192, 768], P('ctx'), may hold values from -6 to 6
- offsets: int32 [2, 12], replicated, may hold values from 0 to 31, as said below
- pad_count: int32 [1], replicated, may hold values from 0 to 127
Outputs:
- out_rows: bfloat16 [8192, 768], P('ctx')
- grad_tiles: bfloat16 [8192, 768], P('ctx')
- grad_wqkv: float32 [768, 2304], P('ctx')
- grad_wout: float32 [768, 768], P('ctx')
The draws below stay inside these ranges and needn't reach their ends.
Inputs may be any that keep to these rules, and one draw needn't show every extreme that they name: offsets[0, h] is below 8; offsets[1, h] is below 32.
All inputs are finite; a program needn't handle non-finite values.
Results may differ from the reference program's by a relative error of at most 0.033.
Values may be sent and summed in bfloat16 or wider, within the bound.
No kernel may reach another device: no remote copies, remote signals or barrier semaphores. Data moves between devices by JAX's collectives and lax.ppermute only.
A program may use at most 128 MiB of HBM per device.

```python
import jax
import jax.numpy as jnp
from jax import lax

D = 768
HEADS = 12
HEAD_DIM = 64
TOK_DEV = 256
GROUP = 8
TOKENS = 8192
N_CTX = 32


def offset_table(key):
    middle = jax.random.randint(jax.random.fold_in(key, 11), (HEADS,), 0, GROUP, dtype=jnp.int32)
    top = jax.random.randint(jax.random.fold_in(key, 12), (HEADS,), 0, TOKENS // TOK_DEV, dtype=jnp.int32)
    head_index = jnp.arange(HEADS, dtype=jnp.int32)
    low_head = jax.random.randint(jax.random.fold_in(key, 13), (), 0, HEADS, dtype=jnp.int32)
    high_head = jax.random.randint(jax.random.fold_in(key, 14), (), 0, HEADS, dtype=jnp.int32)
    middle = jnp.where(head_index == low_head, jnp.int32(0), middle)
    top = jnp.where(head_index == high_head, jnp.int32(TOKENS // TOK_DEV - 1), top)
    return jnp.stack([middle, top])


def draw_offsets(key, part):
    return offset_table(key)


def weight_table(key):
    drawn_weight = jax.random.truncated_normal(jax.random.fold_in(key, 21), -4.0, 4.0, (D, 3 * D), jnp.float32)
    drawn_weight = drawn_weight / jnp.sqrt(jnp.float32(D))
    return drawn_weight


def draw_w_qkv(key, part):
    drawn_weight = weight_table(key)
    return drawn_weight.astype(jnp.bfloat16)


def draw_tiles(key, part):
    return jax.random.truncated_normal(jax.random.fold_in(key, 30), -6.0, 6.0, (TOKENS, D), jnp.float32).astype(jnp.bfloat16)


def block_levels(rng, extent, cuts, smallest, high):
    level = 1.0
    for dim, blocks in cuts:
        draws = jax.random.uniform(jax.random.fold_in(jax.random.fold_in(rng, 6), dim), (blocks,), jnp.float32, smallest / len(cuts), high / len(cuts))
        level = level * jnp.repeat(jnp.exp(draws), extent[dim] // blocks).reshape((-1,) + (1,) * (len(extent) - 1 - dim))
    return level


def centred(own_key, extent, scale, reach, cuts=(), held_as=jnp.bfloat16):
    loudness = block_levels(own_key, extent, cuts, -0.22, 0.18) if cuts else 1.0
    entries = jax.random.normal(own_key, extent, jnp.float32) * scale * loudness
    return jnp.minimum(jnp.maximum(entries, -reach), reach).astype(held_as)


def setup_inputs(seed: int = 0) -> dict:
    arg_keys = jax.random.split(jax.random.key(seed), 7)
    return {
        "tiles": draw_tiles(jax.random.fold_in(arg_keys[6], 71), 0),
        "w_qkv": draw_w_qkv(jax.random.fold_in(arg_keys[6], 71), 0),
        "w_out": centred(arg_keys[2], (D, D), D ** -0.5, 0.21875),
        "cotangent": centred(arg_keys[3], (TOKENS, D), 1.0, 6.0, ((0, 32),)),
        "offsets": draw_offsets(jax.random.fold_in(arg_keys[6], 71), 0),
        "pad_count": jax.random.randint(arg_keys[5], (1,), 0, TOK_DEV // 2).astype(jnp.int32),
    }


scale_factor = 0.125


def rounded(array_in):
    return lax.optimization_barrier(array_in.astype(jnp.bfloat16)).astype(jnp.float32)


def pick_rows(array_in, stride, offsets_row):
    row_count = array_in.shape[0]
    blocked = array_in.reshape((row_count // stride, stride) + array_in.shape[1:])
    chosen = jnp.arange(stride, dtype=jnp.int32)[:, None] == offsets_row[None, :].astype(jnp.int32)
    chosen = chosen.reshape((1, stride, offsets_row.shape[0]) + (1,) * (array_in.ndim - 2))
    return jnp.sum(jnp.where(chosen, blocked, jnp.zeros((), array_in.dtype)), axis=1).astype(array_in.dtype)


def spread_rows(array_in, stride, offsets_row, fill):
    chosen = jnp.arange(stride, dtype=jnp.int32)[:, None] == offsets_row[None, :].astype(jnp.int32)
    chosen = chosen.reshape((1, stride, offsets_row.shape[0]) + (1,) * (array_in.ndim - 2))
    widened = jnp.where(chosen, array_in[:, None], jnp.asarray(fill, array_in.dtype))
    return widened.reshape((array_in.shape[0] * stride,) + array_in.shape[1:])


def masked_scores(queries, key_rows, key_valid):
    scores = jnp.einsum("nhe,mhe->hnm", queries.astype(jnp.float32), key_rows.astype(jnp.float32),
                        precision=lax.Precision.HIGHEST) * scale_factor
    return jnp.where(key_valid[:, None, :], scores, -jnp.inf)


def level_forward(queries, key_rows, value_rows, key_valid):
    scores = masked_scores(queries, key_rows, key_valid)
    peak = jnp.max(scores, axis=-1, keepdims=True)
    log_total = peak[..., 0] + jnp.log(jnp.sum(jnp.exp(scores - peak), axis=-1))
    weights = rounded(jnp.exp(scores - log_total[..., None]))
    mixed = jnp.einsum("hnm,mhe->nhe", weights, value_rows.astype(jnp.float32), precision=lax.Precision.HIGHEST)
    return mixed, log_total.T


def level_grads(queries, key_rows, value_rows, key_valid, log_total, grad_out, delta_rows):
    scores = masked_scores(queries, key_rows, key_valid)
    probs = jnp.exp(scores - log_total.T[:, :, None])
    grad_probs = jnp.einsum("nhe,mhe->hnm", grad_out.astype(jnp.float32), value_rows.astype(jnp.float32),
                            precision=lax.Precision.HIGHEST)
    grad_scores = rounded(probs * (grad_probs - delta_rows.T[:, :, None]))
    grad_query = scale_factor * jnp.einsum("hnm,mhe->nhe", grad_scores, key_rows.astype(jnp.float32),
                                           precision=lax.Precision.HIGHEST)
    grad_key = scale_factor * jnp.einsum("hnm,nhe->mhe", grad_scores, queries.astype(jnp.float32),
                                         precision=lax.Precision.HIGHEST)
    grad_value = jnp.einsum("hnm,nhe->mhe", rounded(probs), grad_out.astype(jnp.float32),
                            precision=lax.Precision.HIGHEST)
    return grad_query, grad_key, grad_value


def reference(tiles, w_qkv, w_out, cotangent, offsets, pad_count):
    token_count = tiles.shape[0]
    shaped = (token_count, HEADS, HEAD_DIM)
    packed = jnp.dot(tiles, w_qkv, preferred_element_type=jnp.float32).astype(jnp.bfloat16)
    queries = packed[:, :D].reshape(shaped)
    key_all = packed[:, D:2 * D].reshape(shaped)
    value_all = packed[:, 2 * D:].reshape(shaped)
    limit = token_count - pad_count[0]
    levels = ((1, jnp.zeros((HEADS,), jnp.int32)), (GROUP, offsets[0]), (N_CTX, offsets[1]))

    def segments_of(array_in, stride, offs):
        picked = pick_rows(array_in, stride, offs)
        return picked.reshape((picked.shape[0] // TOK_DEV, TOK_DEV) + picked.shape[1:])

    def valid_of(stride, offs):
        selected = token_count // stride
        key_pos = jnp.arange(selected, dtype=jnp.int32)[:, None] * stride + offs[None, :].astype(jnp.int32)
        return (key_pos < limit).reshape(selected // TOK_DEV, TOK_DEV, HEADS).transpose(0, 2, 1)

    mixed_levels = []
    lse_levels = []
    for stride, offs in levels:
        parts = (segments_of(queries, stride, offs), segments_of(key_all, stride, offs),
                 segments_of(value_all, stride, offs), valid_of(stride, offs))
        mixed, lse_part = lax.map(lambda block: level_forward(*block), parts)
        mixed_levels.append(spread_rows(mixed.reshape(-1, HEADS, HEAD_DIM), stride, offs, 0.0))
        lse_levels.append(spread_rows(lse_part.reshape(-1, HEADS), stride, offs, -jnp.inf))
    log_total = jnp.logaddexp(jnp.logaddexp(lse_levels[0], lse_levels[1]), lse_levels[2])
    combined = jnp.exp(lse_levels[0] - log_total)[..., None] * mixed_levels[0]
    combined = combined + jnp.exp(lse_levels[1] - log_total)[..., None] * mixed_levels[1]
    combined = combined + jnp.exp(lse_levels[2] - log_total)[..., None] * mixed_levels[2]
    attn = combined.astype(jnp.bfloat16).reshape(token_count, D)
    out_rows = (tiles.astype(jnp.float32) + jnp.dot(attn, w_out, preferred_element_type=jnp.float32)).astype(jnp.bfloat16)
    grad_attn = jnp.dot(cotangent, w_out.T, preferred_element_type=jnp.float32).astype(jnp.bfloat16)
    grad_wout = jnp.dot(attn.T, cotangent, preferred_element_type=jnp.float32)
    grad_heads = grad_attn.reshape(shaped)
    delta_rows = jnp.sum(grad_heads.astype(jnp.float32) * attn.reshape(shaped).astype(jnp.float32), axis=-1)
    grad_sums = None
    for stride, offs in levels:
        parts = (segments_of(queries, stride, offs), segments_of(key_all, stride, offs),
                 segments_of(value_all, stride, offs), valid_of(stride, offs),
                 segments_of(log_total, stride, offs), segments_of(grad_heads, stride, offs),
                 segments_of(delta_rows, stride, offs))
        results = lax.map(lambda block: level_grads(*block), parts)
        spread = [spread_rows(item.reshape(-1, HEADS, HEAD_DIM), stride, offs, 0.0) for item in results]
        grad_sums = spread if grad_sums is None else [grad_sums[i] + spread[i] for i in range(3)]
    grad_packed = jnp.concatenate([item.reshape(token_count, D) for item in grad_sums], axis=1).astype(jnp.bfloat16)
    grad_tiles = jnp.dot(grad_packed, w_qkv.T, preferred_element_type=jnp.float32).astype(jnp.bfloat16)
    grad_wqkv = jnp.dot(tiles.T, grad_packed, preferred_element_type=jnp.float32)
    return out_rows, grad_tiles, grad_wqkv, grad_wout
```

```python
import functools

import jax
import jax.numpy as jnp
import numpy as np
from jax import lax
from jax.experimental import pallas as pl
from jax.experimental.pallas import tpu as pltpu
from jax.sharding import PartitionSpec as P

HEAD_DIM = 64
GROUP = 8
PAIR = 2 * HEAD_DIM
LANES = 128
SECOND = 16
SCALE = 0.125
BF = jnp.bfloat16
F32 = jnp.float32
NT = (((1,), (1,)), ((), ()))
NN = (((1,), (0,)), ((), ()))
TN = (((0,), (0,)), ((), ()))
VMEM_BYTES = 40 * 1024 * 1024


def dot(a, b, dims=NN):
    return lax.dot_general(a, b, dims, preferred_element_type=F32)


def dot_exact(a, b):
    return lax.dot_general(a, b, NN, preferred_element_type=F32, precision=lax.Precision.HIGHEST)


def iota(shape, dim):
    return lax.broadcasted_iota(jnp.int32, shape, dim)


def low_half(shape):
    return iota(shape, len(shape) - 1) % PAIR < HEAD_DIM


def halves(x):
    low = low_half(x.shape)
    zero = jnp.zeros((), x.dtype)
    return jnp.where(low, x, zero), jnp.where(low, zero, x)


def by_head(first, second, rows):
    return jnp.where(low_half((rows, PAIR)), first, second)


class Sizes:
    def __init__(self, rows, width, dev_count):
        self.rows = rows
        self.width = width
        self.devs = dev_count
        self.heads = width // HEAD_DIM
        self.pairs = self.heads // 2
        self.mid = rows // GROUP
        self.far = rows // dev_count
        self.sel = 2 * self.mid
        self.upper = dev_count // GROUP
        self.strip = width // dev_count
        self.half = width // 2


def chosen_row(z, index, off_mid, off_far):
    row = jnp.where(index < z.mid, index * GROUP + off_mid, (index - z.mid) * z.devs + off_far)
    return jnp.where(index < z.mid + z.far, row, -1)


def spread(z, offs_ref, pair, picked):
    lane = iota((1, 4 * z.sel), 1)
    second = (lane // z.sel) % 2 == 1
    off_mid = jnp.where(second, offs_ref[0, 2 * pair + 1], offs_ref[0, 2 * pair])
    off_far = jnp.where(second, offs_ref[1, 2 * pair + 1], offs_ref[1, 2 * pair])
    target = chosen_row(z, lane % z.sel, off_mid, off_far)
    place = (iota((z.rows, 4 * z.sel), 0) == target).astype(F32).astype(BF)
    high = picked.astype(BF)
    rest = (picked - high.astype(F32)).astype(BF)
    first_high, second_high = halves(high)
    first_rest, second_rest = halves(rest)
    stacked = jnp.concatenate([first_high, second_high, first_rest, second_rest], axis=0)
    return dot(place, stacked)


def lane_offsets(z, offs_ref):
    lane = iota((1, LANES), 1)
    off_mid = jnp.full((1, LANES), -1, jnp.int32)
    off_far = jnp.full((1, LANES), -1, jnp.int32)
    for head in range(z.heads):
        here = (lane == head) | (lane == SECOND + head)
        off_mid = jnp.where(here, offs_ref[0, head], off_mid)
        off_far = jnp.where(here, offs_ref[1, head], off_far)
    return off_mid, off_far


def stat_masks(z, offs_ref):
    off_mid, off_far = lane_offsets(z, offs_ref)
    row = iota((z.rows, LANES), 0)
    return row % GROUP == off_mid, row % z.devs == off_far


def pick_stats(z, masks, stats):
    entry = iota((z.sel, z.rows), 0)
    row = iota((z.sel, z.rows), 1)
    take_mid = ((entry < z.mid) & (row // GROUP == entry)).astype(F32)
    take_far = (row // z.devs == entry - z.mid).astype(F32)
    return dot_exact(take_mid, jnp.where(masks[0], stats, 0.0)) + dot_exact(
        take_far, jnp.where(masks[1], stats, 0.0)
    )


def spread_stats(z, masks, picked):
    row = iota((z.rows, z.sel), 0)
    entry = iota((z.rows, z.sel), 1)
    give_mid = ((entry < z.mid) & (row // GROUP == entry)).astype(F32)
    give_far = (row // z.devs == entry - z.mid).astype(F32)
    return (
        jnp.where(masks[0], dot_exact(give_mid, picked), -jnp.inf),
        jnp.where(masks[1], dot_exact(give_far, picked), -jnp.inf),
    )


def gathered_place(z, own):
    index = iota((1, 2 * z.rows), 1)
    core = index // z.rows
    plane = (index % z.rows) // z.sel
    inner = index % z.sel
    is_mid = inner < z.mid
    upper = jnp.where(is_mid, 0, (inner - z.mid) // z.far)
    step = jnp.where(is_mid, inner * GROUP, ((inner - z.mid) % z.far) * z.devs)
    dev = own ^ (core + 2 * plane + GROUP * upper)
    return dev * z.rows + step, is_mid


def project_kernel(z, offs_ref, tiles, w_qkv, cot, w_out, q, k, v, g, sel, far):
    width = z.width
    own = tiles[...]
    k[...] = dot(own, w_qkv[:, width : 2 * width]).astype(BF)
    v[...] = dot(own, w_qkv[:, 2 * width :]).astype(BF)
    q[...] = dot(own, w_qkv[:, :width]).astype(BF) * jnp.asarray(SCALE, BF)
    g[...] = dot(cot[...], w_out[...], NT).astype(BF)
    entry = iota((2 * z.sel, z.rows), 0)
    column = iota((2 * z.sel, z.rows), 1)
    second = entry >= z.sel
    for pair in range(z.pairs):
        lanes = slice(pair * PAIR, (pair + 1) * PAIR)
        off_mid = jnp.where(second, offs_ref[0, 2 * pair + 1], offs_ref[0, 2 * pair])
        off_far = jnp.where(second, offs_ref[1, 2 * pair + 1], offs_ref[1, 2 * pair])
        target = chosen_row(z, entry % z.sel, off_mid, off_far)
        take = (column == target).astype(F32).astype(BF)
        every = jnp.concatenate([k[:, lanes], v[:, lanes], q[:, lanes], g[:, lanes]], axis=1)
        both = dot(take, every)
        picked = jnp.where(low_half((z.sel, 4 * PAIR)), both[: z.sel], both[z.sel :]).astype(BF)
        far_part = jnp.where(
            low_half((z.far, 4 * PAIR)),
            both[z.mid : z.mid + z.far],
            both[z.sel + z.mid : z.sel + z.mid + z.far],
        ).astype(BF)
        for part in range(4):
            to = slice(part * width + pair * PAIR, part * width + (pair + 1) * PAIR)
            sel[:, to] = picked[:, part * PAIR : (part + 1) * PAIR]
            far[:, to] = far_part[:, part * PAIR : (part + 1) * PAIR]


def near_kernel(z, pad_ref, q, k, v, tiles, order, mixed, lse, turned, turned_out):
    own = lax.axis_index("ctx")
    limit = z.rows * z.devs - pad_ref[0] - own * z.rows
    valid = iota((1, z.rows), 1) < limit
    lane = iota((z.rows, LANES), 1)
    lse_all = jnp.zeros((z.rows, LANES), F32)
    for pair in range(z.pairs):
        lanes = slice(pair * PAIR, (pair + 1) * PAIR)
        query = q[:, lanes]
        keys = halves(k[:, lanes])
        values = halves(v[:, lanes])
        total = None
        for side in range(2):
            scores = jnp.where(valid, dot(query, keys[side], NT), -jnp.inf)
            peak = jnp.max(scores, axis=1, keepdims=True)
            powers = jnp.exp(scores - peak)
            summed = jnp.sum(powers, axis=1, keepdims=True)
            part = dot(powers.astype(BF), values[side]) * (1.0 / summed)
            total = part if total is None else total + part
            lse_all = jnp.where(lane == 2 * pair + side, peak + jnp.log(summed), lse_all)
        mixed[:, lanes] = total
    lse[...] = lse_all
    count = 2 * z.width
    for start in range(0, count, 256):
        rows = slice(start, start + 256)
        place = (iota((256, z.width), 1) == order[rows, :]).astype(F32).astype(BF)
        result = dot(place, tiles[...], NT).astype(BF)
        if start < z.width:
            turned[rows, :] = result
        else:
            turned_out[start - z.width : start - z.width + 256, :] = result


def join_kernel(z, offs_ref, pad_ref, sel, first, second, mixed, lse, g, attn, stats, picked, held):
    own = lax.axis_index("ctx")
    limit = z.rows * z.devs - pad_ref[0]
    place, is_mid = gathered_place(z, own)
    lane = iota((z.sel, LANES), 1)
    same = (iota((z.sel, 1), 0) < z.mid) == is_mid
    lse_sel = jnp.zeros((z.sel, LANES), F32)
    width = z.width
    for pair in range(z.pairs):
        lanes = slice(pair * PAIR, (pair + 1) * PAIR)
        value_lanes = slice(width + pair * PAIR, width + (pair + 1) * PAIR)
        query = sel[:, 2 * width + pair * PAIR : 2 * width + (pair + 1) * PAIR]
        keys = halves(jnp.concatenate([first[:, lanes], second[:, lanes]], axis=0))
        values = halves(jnp.concatenate([first[:, value_lanes], second[:, value_lanes]], axis=0))
        total = None
        for side in range(2):
            head = 2 * pair + side
            valid = place + jnp.where(is_mid, offs_ref[0, head], offs_ref[1, head]) < limit
            scores = jnp.where(same & valid, dot(query, keys[side], NT), -jnp.inf)
            peak = jnp.max(scores, axis=1, keepdims=True)
            powers = jnp.exp(scores - peak)
            summed = jnp.sum(powers, axis=1, keepdims=True)
            part = dot(powers.astype(BF), values[side]) * (1.0 / summed)
            total = part if total is None else total + part
            lse_sel = jnp.where(lane == head, peak + jnp.log(summed), lse_sel)
        held[:, lanes] = total
    masks = stat_masks(z, offs_ref)
    lse_near = lse[...]
    lse_mid, lse_far = spread_stats(z, masks, lse_sel)
    top = jnp.maximum(lse_near, jnp.maximum(lse_mid, lse_far))
    total_lse = top + jnp.log(
        jnp.exp(lse_near - top) + jnp.exp(lse_mid - top) + jnp.exp(lse_far - top)
    )
    near_share = jnp.exp(lse_near - total_lse)
    sel_share = jnp.exp(lse_sel - pick_stats(z, masks, total_lse))
    lane = iota((z.rows, LANES), 1)
    both = total_lse
    for pair in range(z.pairs):
        lanes = slice(pair * PAIR, (pair + 1) * PAIR)
        share = by_head(
            sel_share[:, 2 * pair : 2 * pair + 1], sel_share[:, 2 * pair + 1 : 2 * pair + 2], z.sel
        )
        near = by_head(
            near_share[:, 2 * pair : 2 * pair + 1],
            near_share[:, 2 * pair + 1 : 2 * pair + 2],
            z.rows,
        )
        combined = near * mixed[:, lanes] + spread(z, offs_ref, pair, share * held[:, lanes])
        rounded = combined.astype(BF)
        attn[:, lanes] = rounded
        product = g[:, lanes].astype(F32) * rounded.astype(F32)
        parts = halves(product)
        for side in range(2):
            delta = jnp.sum(parts[side], axis=1, keepdims=True)
            both = jnp.where(lane == SECOND + 2 * pair + side, delta, both)
    stats[...] = both
    picked[...] = pick_stats(z, masks, both)


def output_kernel(z, attn, tiles, w_out, order, rows_out, turned, turned_out):
    rows_out[...] = (tiles[...].astype(F32) + dot(attn[...], w_out[...])).astype(BF)
    for start in range(0, z.width, z.half):
        source = order[2 * start : 2 * start + z.half, :]
        place = (iota((z.half, z.width), 1) == source).astype(F32).astype(BF)
        result = dot(place, attn[...], NT).astype(BF)
        if start == 0:
            turned[...] = result
        else:
            turned_out[...] = result


def near_grads_kernel(
    z, offs_ref, pad_ref, q, k, v, g, stats, sel, first, second, picked, dq, dk, dv
):
    own = lax.axis_index("ctx")
    limit = z.rows * z.devs - pad_ref[0]
    place, is_mid = gathered_place(z, own)
    same = (iota((z.sel, 1), 0) < z.mid) == is_mid
    valid_near = iota((z.rows, 1), 0) < limit - own * z.rows
    across = jnp.transpose(stats[...])
    width = z.width
    for pair in range(z.pairs):
        lanes = slice(pair * PAIR, (pair + 1) * PAIR)
        value_lanes = slice(width + pair * PAIR, width + (pair + 1) * PAIR)
        query, grad = q[:, lanes], g[:, lanes]
        queries, grads = halves(query), halves(grad)
        keys, values = halves(k[:, lanes]), halves(v[:, lanes])
        query_sel = sel[:, 2 * width + pair * PAIR : 2 * width + (pair + 1) * PAIR]
        grad_sel = sel[:, 3 * width + pair * PAIR : 3 * width + (pair + 1) * PAIR]
        keys_all = halves(jnp.concatenate([first[:, lanes], second[:, lanes]], axis=0))
        values_all = halves(
            jnp.concatenate([first[:, value_lanes], second[:, value_lanes]], axis=0)
        )
        sum_q = sum_k = sum_v = sum_sel = None
        for side in range(2):
            head = 2 * pair + side
            scores = jnp.where(valid_near, dot(keys[side], query, NT), -jnp.inf)
            probs = jnp.exp(scores - across[head : head + 1, :])
            grad_probs = dot(values[side], grad, NT)
            grad_scores = probs * (grad_probs - across[SECOND + head : SECOND + head + 1, :])
            grad_scores = grad_scores.astype(BF)
            part_k = dot(grad_scores, queries[side])
            part_v = dot(probs.astype(BF), grads[side])
            part_q = dot(grad_scores, keys[side], TN)
            valid = place + jnp.where(is_mid, offs_ref[0, head], offs_ref[1, head]) < limit
            scores = jnp.where(same & valid, dot(query_sel, keys_all[side], NT), -jnp.inf)
            probs = jnp.exp(scores - picked[:, head : head + 1])
            grad_probs = dot(grad_sel, values_all[side], NT)
            grad_scores = probs * (grad_probs - picked[:, SECOND + head : SECOND + head + 1])
            part_sel = dot(grad_scores.astype(BF), keys_all[side])
            if side == 0:
                sum_q, sum_k, sum_v, sum_sel = part_q, part_k, part_v, part_sel
            else:
                sum_q, sum_k, sum_v = sum_q + part_q, sum_k + part_k, sum_v + part_v
                sum_sel = sum_sel + part_sel
        dk[:, lanes] = sum_k
        dv[:, lanes] = sum_v
        dq[:, lanes] = (SCALE * (sum_q + spread(z, offs_ref, pair, sum_sel))).astype(BF)


def key_grads_kernel(
    z, offs_ref, pad_ref, sel, first, second, first_stats, second_stats, dk_near, dv_near, dk, dv
):
    own = lax.axis_index("ctx")
    limit = z.rows * z.devs - pad_ref[0] - own * z.rows
    _, is_mid = gathered_place(z, own)
    entry = iota((z.sel, 1), 0)
    same = (entry < z.mid) == is_mid
    across = jnp.transpose(jnp.concatenate([first_stats[...], second_stats[...]], axis=0))
    width = z.width
    for pair in range(z.pairs):
        lanes = slice(pair * PAIR, (pair + 1) * PAIR)
        value_lanes = slice(width + pair * PAIR, width + (pair + 1) * PAIR)
        keys, values = sel[:, lanes], sel[:, value_lanes]
        queries = halves(jnp.concatenate([first[:, lanes], second[:, lanes]], axis=0))
        grads = halves(jnp.concatenate([first[:, value_lanes], second[:, value_lanes]], axis=0))
        sum_k = sum_v = None
        for side in range(2):
            head = 2 * pair + side
            at = chosen_row(z, entry, offs_ref[0, head], offs_ref[1, head])
            valid = (at >= 0) & (at < limit)
            scores = jnp.where(same & valid, dot(keys, queries[side], NT), -jnp.inf)
            probs = jnp.exp(scores - across[head : head + 1, :])
            grad_probs = dot(values, grads[side], NT)
            grad_scores = probs * (grad_probs - across[SECOND + head : SECOND + head + 1, :])
            part_k = dot(grad_scores.astype(BF), queries[side])
            part_v = dot(probs.astype(BF), grads[side])
            sum_k = part_k if side == 0 else sum_k + part_k
            sum_v = part_v if side == 0 else sum_v + part_v
        dk[:, lanes] = (dk_near[:, lanes] + spread(z, offs_ref, pair, sum_k)).astype(BF)
        dv[:, lanes] = (dv_near[:, lanes] + spread(z, offs_ref, pair, sum_v)).astype(BF)


def weight_kernel(count, *refs):
    left_own, left_other = refs[0], refs[1]
    out = refs[-1]
    width = refs[2].shape[1]
    for i in range(count):
        out[:, i * width : (i + 1) * width] = (
            dot(left_own[...], refs[2 + i][...]) + dot(left_other[...], refs[2 + count + i][...])
        ).astype(BF)


def tiles_kernel(z, dq, dk, dv, w_qkv, out):
    width = z.width
    out[...] = (
        dot(dq[...], w_qkv[:, :width], NT)
        + dot(dk[...], w_qkv[:, width : 2 * width], NT)
        + dot(dv[...], w_qkv[:, 2 * width :], NT)
    ).astype(BF)


def call(kernel, outs, flops, scratch=(), smem=0):
    def run(*args):
        moved = sum(int(np.prod(a.shape)) * a.dtype.itemsize for a in args)
        moved += sum(int(np.prod(s)) * jnp.dtype(t).itemsize for s, t in outs)
        specs = [
            pl.BlockSpec(memory_space=pltpu.SMEM if i < smem else pltpu.VMEM)
            for i in range(len(args))
        ]
        return pl.pallas_call(
            kernel,
            out_shape=tuple(jax.ShapeDtypeStruct(s, t) for s, t in outs),
            in_specs=specs,
            out_specs=tuple(pl.BlockSpec(memory_space=pltpu.VMEM) for _ in outs),
            scratch_shapes=list(scratch),
            compiler_params=pltpu.CompilerParams(vmem_limit_bytes=VMEM_BYTES),
            cost_estimate=pl.CostEstimate(
                flops=int(flops), bytes_accessed=int(moved), transcendentals=0
            ),
        )(*args)

    return run


def swap(value, mask, dev_count):
    return lax.ppermute(value, "ctx", [(d, d ^ mask) for d in range(dev_count)])


def upper_steps(dev_count):
    steps, base = [], GROUP
    while base < dev_count:
        count = 4 if base * 4 <= dev_count else 2
        steps.append((base, count))
        base *= count
    return steps


PLANE = (2, 4)


def collect(value, step, dev_count):
    base, count = step
    return jnp.concatenate(
        [value] + [swap(value, base * i, dev_count) for i in range(1, count)], axis=0
    )


def reduce_step(value, step, dev_count, dtype):
    base, count = step
    size = value.shape[0] // count
    total = value[:size].astype(F32)
    for i in range(1, count):
        total = total + swap(value[i * size : (i + 1) * size], base * i, dev_count).astype(F32)
    return total.astype(dtype)


def reduce_all(value, steps, dev_count):
    for i, step in enumerate(steps):
        value = reduce_step(value, step, dev_count, F32 if i == len(steps) - 1 else BF)
    return value


def strip_order(z, own):
    entries = []
    for core in range(2):
        for first_plane in (True, False):
            outer, inner = (4, z.upper) if first_plane else (z.upper, 4)
            a, b, r = np.meshgrid(
                np.arange(outer), np.arange(inner), np.arange(z.strip), indexing="ij"
            )
            plane, upper = (a, b) if first_plane else (b, a)
            entries.append(
                np.stack([(core + 2 * plane + GROUP * upper).ravel(), r.ravel()], axis=1)
            )
    table = np.concatenate(entries, axis=0).astype(np.int32)
    return (own ^ table[:, :1]) * z.strip + table[:, 1:]


def per_device(tiles, w_qkv, w_out, cotangent, offsets, pad_count):
    n = lax.axis_size("ctx")
    z = Sizes(tiles.shape[0], tiles.shape[1], n)
    own = lax.axis_index("ctx")
    rows, width = z.rows, z.width
    ups = upper_steps(n)
    order = strip_order(z, own)
    base_flops = 2 * rows * rows * width

    q, k, v, g, sel, far = call(
        functools.partial(project_kernel, z),
        [((rows, width), BF)] * 4 + [((z.sel, 4 * width), BF), ((z.far, 4 * width), BF)],
        2 * rows * width * 4 * width,
        smem=1,
    )(offsets, tiles, w_qkv, cotangent, w_out)

    far_up = far
    for step in ups:
        far_up = collect(far_up, step, n)
    mixed, lse, turned, turned_out = call(
        functools.partial(near_kernel, z),
        [
            ((rows, width), F32),
            ((rows, LANES), F32),
            ((width, rows), BF),
            ((width, rows), BF),
        ],
        8 * base_flops,
        smem=1,
    )(pad_count, q, k, v, tiles, order)
    kv_first = collect(
        jnp.concatenate([sel[: z.mid, : 2 * width], far_up[:, : 2 * width]], axis=0), PLANE, n
    )
    kv_second = swap(kv_first, 1, n)
    qg_first = collect(
        jnp.concatenate([sel[: z.mid, 2 * width :], far_up[:, 2 * width :]], axis=0), PLANE, n
    )
    qg_second = swap(qg_first, 1, n)
    turned_other = swap(turned_out, 1, n)
    cot_other = swap(cotangent, 1, n)

    attn, stats, picked = call(
        functools.partial(join_kernel, z),
        [((rows, width), BF), ((rows, LANES), F32), ((z.sel, LANES), F32)],
        3 * base_flops,
        scratch=[pltpu.VMEM((z.sel, width), F32)],
        smem=2,
    )(offsets, pad_count, sel, kv_first, kv_second, mixed, lse, g)

    stats_up = picked[z.mid : z.mid + z.far]
    for step in ups:
        stats_up = collect(stats_up, step, n)
    stats_first = collect(jnp.concatenate([picked[: z.mid], stats_up], axis=0), PLANE, n)
    stats_second = swap(stats_first, 1, n)

    out_rows, attn_turned, attn_turned_out = call(
        functools.partial(output_kernel, z),
        [((rows, width), BF), ((z.half, rows), BF), ((z.half, rows), BF)],
        4 * rows * width * width,
    )(attn, tiles, w_out, order)
    attn_other = swap(attn_turned_out, 1, n)

    dq, dk_near, dv_near = call(
        functools.partial(near_grads_kernel, z),
        [((rows, width), BF), ((rows, width), F32), ((rows, width), F32)],
        8 * base_flops,
        smem=2,
    )(offsets, pad_count, q, k, v, g, stats, sel, kv_first, kv_second, picked)
    dq_other = swap(dq, 1, n)

    (wout_half,) = call(
        functools.partial(weight_kernel, 1), [((z.half, width), BF)], 2 * rows * width * width
    )(attn_turned, attn_other, cotangent, cot_other)
    grad_wout = reduce_all(wout_half, [PLANE] + ups[::-1], n)

    (wq_half,) = call(
        functools.partial(weight_kernel, 1), [((z.half, width), BF)], 2 * rows * width * width
    )(turned[z.half :], turned_other[z.half :], dq, dq_other)
    grad_wq = reduce_all(wq_half, ups[::-1] + [PLANE], n)

    dk, dv = call(
        functools.partial(key_grads_kernel, z),
        [((rows, width), BF), ((rows, width), BF)],
        3 * base_flops,
        smem=2,
    )(offsets, pad_count, sel, qg_first, qg_second, stats_first, stats_second, dk_near, dv_near)
    dk_other = swap(dk, 1, n)
    dv_other = swap(dv, 1, n)
    (wkv_half,) = call(
        functools.partial(weight_kernel, 2), [((z.half, 2 * width), BF)], 4 * rows * width * width
    )(turned[: z.half], turned_other[: z.half], dk, dv, dk_other, dv_other)
    grad_wkv = reduce_all(wkv_half, [PLANE] + ups[::-1], n)

    (grad_tiles,) = call(
        functools.partial(tiles_kernel, z), [((rows, width), BF)], 6 * rows * width * width
    )(dq, dk, dv, w_qkv)
    grad_wqkv = jnp.concatenate([grad_wq, grad_wkv], axis=1)
    return out_rows, grad_tiles, grad_wqkv, grad_wout


def solution(mesh):
    return jax.shard_map(
        per_device,
        mesh=mesh,
        in_specs=(P("ctx", None), P(), P(), P("ctx", None), P(), P()),
        out_specs=(P("ctx", None), P("ctx", None), P("ctx", None), P("ctx", None)),
        check_vma=False,
    )
```

```python
import functools

import jax
import jax.numpy as jnp
import numpy as np
from jax import lax
from jax.experimental import pallas as pl
from jax.experimental.pallas import tpu as pltpu
from jax.sharding import PartitionSpec as P

HEAD_DIM = 64
GROUP = 8
PAIR = 2 * HEAD_DIM
LANES = 128
SECOND = 16
SCALE = 0.125
BF = jnp.bfloat16
F32 = jnp.float32
NT = (((1,), (1,)), ((), ()))
NN = (((1,), (0,)), ((), ()))
TN = (((0,), (0,)), ((), ()))
LARGE = 1e30
VMEM_BYTES = 40 * 1024 * 1024


def dot(a, b, dims=NN):
    return lax.dot_general(a, b, dims, preferred_element_type=F32)


def dot_exact(a, b):
    return lax.dot_general(a, b, NN, preferred_element_type=F32, precision=lax.Precision.HIGHEST)


def iota(shape, dim):
    return lax.broadcasted_iota(jnp.int32, shape, dim)


def low_half(shape):
    return iota(shape, len(shape) - 1) % PAIR < HEAD_DIM


def halves(x):
    low = low_half(x.shape)
    zero = jnp.zeros((), x.dtype)
    return jnp.where(low, x, zero), jnp.where(low, zero, x)


def by_head(first, second, rows):
    return jnp.where(low_half((rows, PAIR)), first, second)


class Sizes:
    def __init__(self, rows, width, dev_count):
        self.rows = rows
        self.width = width
        self.devs = dev_count
        self.heads = width // HEAD_DIM
        self.pairs = self.heads // 2
        self.mid = rows // GROUP
        self.far = rows // dev_count
        self.sel = 2 * self.mid
        self.far_held = -(-self.far // 16) * 16
        self.upper = dev_count // GROUP
        self.strip = width // dev_count
        self.half = width // 2


def chosen_row(z, index, off_mid, off_far):
    row = jnp.where(index < z.mid, index * GROUP + off_mid, (index - z.mid) * z.devs + off_far)
    return jnp.where(index < z.mid + z.far, row, -1)


def spread(z, offs_ref, pair, picked):
    lane = iota((1, 4 * z.sel), 1)
    second = (lane // z.sel) % 2 == 1
    off_mid = jnp.where(second, offs_ref[0, 2 * pair + 1], offs_ref[0, 2 * pair])
    off_far = jnp.where(second, offs_ref[1, 2 * pair + 1], offs_ref[1, 2 * pair])
    target = chosen_row(z, lane % z.sel, off_mid, off_far)
    place = (iota((z.rows, 4 * z.sel), 0) == target).astype(F32).astype(BF)
    high = picked.astype(BF)
    rest = (picked - high.astype(F32)).astype(BF)
    first_high, second_high = halves(high)
    first_rest, second_rest = halves(rest)
    stacked = jnp.concatenate([first_high, second_high, first_rest, second_rest], axis=0)
    return dot(place, stacked)


def lane_offsets(z, offs_ref):
    lane = iota((1, LANES), 1)
    off_mid = jnp.full((1, LANES), -1, jnp.int32)
    off_far = jnp.full((1, LANES), -1, jnp.int32)
    for head in range(z.heads):
        here = (lane == head) | (lane == SECOND + head)
        off_mid = jnp.where(here, offs_ref[0, head], off_mid)
        off_far = jnp.where(here, offs_ref[1, head], off_far)
    return off_mid, off_far


def stat_masks(z, offs_ref):
    off_mid, off_far = lane_offsets(z, offs_ref)
    row = iota((z.rows, LANES), 0)
    return row % GROUP == off_mid, row % z.devs == off_far


def pick_stats(z, masks, stats):
    entry = iota((z.sel, z.rows), 0)
    row = iota((z.sel, z.rows), 1)
    take_mid = ((entry < z.mid) & (row // GROUP == entry)).astype(F32)
    take_far = (row // z.devs == entry - z.mid).astype(F32)
    return dot_exact(take_mid, jnp.where(masks[0], stats, 0.0)) + dot_exact(
        take_far, jnp.where(masks[1], stats, 0.0)
    )


def spread_stats(z, masks, picked):
    row = iota((z.rows, z.sel), 0)
    entry = iota((z.rows, z.sel), 1)
    give_mid = ((entry < z.mid) & (row // GROUP == entry)).astype(F32)
    give_far = (row // z.devs == entry - z.mid).astype(F32)
    fill = jnp.where(iota((z.rows, LANES), 1) < SECOND, -jnp.inf, 0.0)
    return (
        jnp.where(masks[0], dot_exact(give_mid, picked), fill),
        jnp.where(masks[1], dot_exact(give_far, picked), fill),
    )


def gathered_place(z, own, level):
    index = iota((1, z.rows), 1)
    core = index // (4 * z.mid)
    plane = (index // z.mid) % 4
    inner = index % z.mid
    if level == 0:
        return (own ^ (core + 2 * plane)) * z.rows + inner * GROUP
    dev = own ^ (core + 2 * plane + GROUP * (inner // z.far))
    return dev * z.rows + (inner % z.far) * z.devs


def level_parts(z):
    return ((0, z.mid), (z.mid, z.mid + z.far_held))


def project_kernel(z, offs_ref, tiles, w_qkv, cot, w_out, q, k, v, g, sel, far):
    width = z.width
    own = tiles[...]
    k[...] = dot(own, w_qkv[:, width : 2 * width]).astype(BF)
    v[...] = dot(own, w_qkv[:, 2 * width :]).astype(BF)
    q[...] = dot(own, w_qkv[:, :width]).astype(BF) * jnp.asarray(SCALE, BF)
    g[...] = dot(cot[...], w_out[...], NT).astype(BF)
    entry = iota((2 * z.sel, z.rows), 0)
    column = iota((2 * z.sel, z.rows), 1)
    second = entry >= z.sel
    for pair in range(z.pairs):
        lanes = slice(pair * PAIR, (pair + 1) * PAIR)
        off_mid = jnp.where(second, offs_ref[0, 2 * pair + 1], offs_ref[0, 2 * pair])
        off_far = jnp.where(second, offs_ref[1, 2 * pair + 1], offs_ref[1, 2 * pair])
        target = chosen_row(z, entry % z.sel, off_mid, off_far)
        take = (column == target).astype(F32).astype(BF)
        every = jnp.concatenate([k[:, lanes], v[:, lanes], q[:, lanes], g[:, lanes]], axis=1)
        both = dot(take, every)
        picked = jnp.where(low_half((z.sel, 4 * PAIR)), both[: z.sel], both[z.sel :]).astype(BF)
        far_part = jnp.where(
            low_half((z.far, 4 * PAIR)),
            both[z.mid : z.mid + z.far],
            both[z.sel + z.mid : z.sel + z.mid + z.far],
        ).astype(BF)
        for part in range(4):
            to = slice(part * width + pair * PAIR, part * width + (pair + 1) * PAIR)
            sel[:, to] = picked[:, part * PAIR : (part + 1) * PAIR]
            far[:, to] = far_part[:, part * PAIR : (part + 1) * PAIR]


def near_kernel(z, pad_ref, q, k, v, g, tiles, order, mixed, stats, turned, turned_out):
    own = lax.axis_index("ctx")
    limit = z.rows * z.devs - pad_ref[0] - own * z.rows
    valid = iota((1, z.rows), 1) < limit
    lane = iota((z.rows, LANES), 1)
    both = jnp.zeros((z.rows, LANES), F32)
    for pair in range(z.pairs):
        lanes = slice(pair * PAIR, (pair + 1) * PAIR)
        query = q[:, lanes]
        grad = g[:, lanes].astype(F32)
        keys = halves(k[:, lanes])
        values = halves(v[:, lanes])
        total = None
        for side in range(2):
            head = 2 * pair + side
            scores = jnp.where(valid, dot(query, keys[side], NT), -jnp.inf)
            peak = jnp.max(scores, axis=1, keepdims=True)
            powers = jnp.exp(scores - peak)
            summed = jnp.sum(powers, axis=1, keepdims=True)
            part = dot(powers.astype(BF), values[side]) * (1.0 / summed)
            total = part if total is None else total + part
            both = jnp.where(lane == head, peak + jnp.log(summed), both)
            meets = jnp.sum(grad * part, axis=1, keepdims=True)
            both = jnp.where(lane == SECOND + head, meets, both)
        mixed[:, lanes] = total
    stats[...] = both
    count = 2 * z.width
    for start in range(0, count, 256):
        rows = slice(start, start + 256)
        place = (iota((256, z.width), 1) == order[rows, :]).astype(F32).astype(BF)
        result = dot(place, tiles[...], NT).astype(BF)
        if start < z.width:
            turned[rows, :] = result
        else:
            turned_out[start - z.width : start - z.width + 256, :] = result


def gathered(pieces, lanes):
    return jnp.concatenate([piece[:, lanes] for piece in pieces], axis=0)


def join_kernel(
    z, offs_ref, pad_ref, sel, mid_0, mid_1, far_0, far_1, near_stats, stats, picked, held
):
    own = lax.axis_index("ctx")
    limit = z.rows * z.devs - pad_ref[0]
    places = [gathered_place(z, own, level) for level in range(2)]
    width = z.width
    pieces = ((mid_0, mid_1), (far_0, far_1))
    parts = level_parts(z)
    sel_stats = [jnp.zeros((stop - start, LANES), F32) for start, stop in parts]
    held_tail = z.sel - parts[1][1]
    for pair in range(z.pairs):
        lanes = slice(pair * PAIR, (pair + 1) * PAIR)
        value_lanes = slice(width + pair * PAIR, width + (pair + 1) * PAIR)
        query_lanes = slice(2 * width + pair * PAIR, 2 * width + (pair + 1) * PAIR)
        grad_lanes = slice(3 * width + pair * PAIR, 3 * width + (pair + 1) * PAIR)
        totals = []
        for level, (start, stop) in enumerate(parts):
            lane = iota((stop - start, LANES), 1)
            query = sel[start:stop, query_lanes]
            grad = sel[start:stop, grad_lanes].astype(F32)
            keys = halves(gathered(pieces[level], lanes))
            values = halves(gathered(pieces[level], value_lanes))
            total = None
            for side in range(2):
                head = 2 * pair + side
                valid = places[level] + offs_ref[level, head] < limit
                scores = jnp.where(valid, dot(query, keys[side], NT), -jnp.inf)
                peak = jnp.max(scores, axis=1, keepdims=True)
                powers = jnp.exp(scores - peak)
                summed = jnp.sum(powers, axis=1, keepdims=True)
                part = dot(powers.astype(BF), values[side]) * (1.0 / summed)
                total = part if total is None else total + part
                meets = jnp.sum(grad * part, axis=1, keepdims=True)
                here = jnp.where(lane == head, peak + jnp.log(summed), sel_stats[level])
                sel_stats[level] = jnp.where(lane == SECOND + head, meets, here)
            totals.append(total)
        totals.append(jnp.zeros((held_tail, PAIR), F32))
        held[:, lanes] = jnp.concatenate(totals, axis=0)
    sel_both = jnp.concatenate(sel_stats + [jnp.zeros((held_tail, LANES), F32)], axis=0)
    masks = stat_masks(z, offs_ref)
    near = near_stats[...]
    mid, far = spread_stats(z, masks, sel_both)
    top = jnp.maximum(near, jnp.maximum(mid, far))
    total_lse = top + jnp.log(jnp.exp(near - top) + jnp.exp(mid - top) + jnp.exp(far - top))
    delta = sum(
        pltpu.roll(jnp.exp(value - total_lse), SECOND, 1) * value
        for value in (
            near,
            jnp.where(masks[0], mid, -LARGE),
            jnp.where(masks[1], far, -LARGE),
        )
    )
    both = jnp.where(iota((z.rows, LANES), 1) < SECOND, total_lse, delta)
    stats[...] = both
    both_sel = pick_stats(z, masks, both)
    picked[...] = both_sel
    share = jnp.exp(sel_both - both_sel)
    for pair in range(z.pairs):
        lanes = slice(pair * PAIR, (pair + 1) * PAIR)
        held[:, lanes] = held[:, lanes] * by_head(
            share[:, 2 * pair : 2 * pair + 1], share[:, 2 * pair + 1 : 2 * pair + 2], z.sel
        )


def output_kernel(
    z, offs_ref, near_stats, stats, mixed, held, tiles, w_out, order, rows_out, turned, turned_out, attn
):
    near_share = jnp.exp(near_stats[...] - stats[...])
    for pair in range(z.pairs):
        lanes = slice(pair * PAIR, (pair + 1) * PAIR)
        near = by_head(
            near_share[:, 2 * pair : 2 * pair + 1],
            near_share[:, 2 * pair + 1 : 2 * pair + 2],
            z.rows,
        )
        combined = near * mixed[:, lanes] + spread(z, offs_ref, pair, held[:, lanes])
        attn[:, lanes] = combined.astype(BF)
    rows_out[...] = (tiles[...].astype(F32) + dot(attn[...], w_out[...])).astype(BF)
    for start in range(0, z.width, z.half):
        source = order[2 * start : 2 * start + z.half, :]
        place = (iota((z.half, z.width), 1) == source).astype(F32).astype(BF)
        result = dot(place, attn[...], NT).astype(BF)
        if start == 0:
            turned[...] = result
        else:
            turned_out[...] = result


def near_grads_kernel(
    z, offs_ref, pad_ref, q, k, v, g, stats, sel, mid_0, mid_1, far_0, far_1, picked, dq, dk, dv
):
    own = lax.axis_index("ctx")
    limit = z.rows * z.devs - pad_ref[0]
    places = [gathered_place(z, own, level) for level in range(2)]
    pieces = ((mid_0, mid_1), (far_0, far_1))
    parts = level_parts(z)
    held_tail = z.sel - parts[1][1]
    valid_near = iota((z.rows, 1), 0) < limit - own * z.rows
    across = jnp.transpose(stats[...])
    width = z.width
    for pair in range(z.pairs):
        lanes = slice(pair * PAIR, (pair + 1) * PAIR)
        value_lanes = slice(width + pair * PAIR, width + (pair + 1) * PAIR)
        query_lanes = slice(2 * width + pair * PAIR, 2 * width + (pair + 1) * PAIR)
        grad_lanes = slice(3 * width + pair * PAIR, 3 * width + (pair + 1) * PAIR)
        query, grad = q[:, lanes], g[:, lanes]
        queries, grads = halves(query), halves(grad)
        keys, values = halves(k[:, lanes]), halves(v[:, lanes])
        sum_q = sum_k = sum_v = None
        for side in range(2):
            head = 2 * pair + side
            scores = jnp.where(valid_near, dot(keys[side], query, NT), -jnp.inf)
            probs = jnp.exp(scores - across[head : head + 1, :])
            grad_probs = dot(values[side], grad, NT)
            grad_scores = probs * (grad_probs - across[SECOND + head : SECOND + head + 1, :])
            grad_scores = grad_scores.astype(BF)
            part_k = dot(grad_scores, queries[side])
            part_v = dot(probs.astype(BF), grads[side])
            part_q = dot(grad_scores, keys[side], TN)
            if side == 0:
                sum_q, sum_k, sum_v = part_q, part_k, part_v
            else:
                sum_q, sum_k, sum_v = sum_q + part_q, sum_k + part_k, sum_v + part_v
        sums = []
        for level, (start, stop) in enumerate(parts):
            rows = slice(start, stop)
            keys = halves(gathered(pieces[level], lanes))
            values = halves(gathered(pieces[level], value_lanes))
            total = None
            for side in range(2):
                head = 2 * pair + side
                valid = places[level] + offs_ref[level, head] < limit
                scores = dot(sel[rows, query_lanes], keys[side], NT)
                scores = jnp.where(valid, scores, -jnp.inf)
                probs = jnp.exp(scores - picked[rows, head : head + 1])
                grad_probs = dot(sel[rows, grad_lanes], values[side], NT)
                grad_probs = grad_probs - picked[rows, SECOND + head : SECOND + head + 1]
                part = dot((probs * grad_probs).astype(BF), keys[side])
                total = part if total is None else total + part
            sums.append(total)
        sums.append(jnp.zeros((held_tail, PAIR), F32))
        dk[:, lanes] = sum_k
        dv[:, lanes] = sum_v
        sum_sel = jnp.concatenate(sums, axis=0)
        dq[:, lanes] = (SCALE * (sum_q + spread(z, offs_ref, pair, sum_sel))).astype(BF)


def key_grads_kernel(
    z, offs_ref, pad_ref, sel, first, second, first_stats, second_stats, dk_near, dv_near, dk, dv
):
    own = lax.axis_index("ctx")
    limit = z.rows * z.devs - pad_ref[0] - own * z.rows
    width = z.width
    parts = level_parts(z)
    held_tail = z.sel - parts[1][1]

    def of_level(level, refs, lanes):
        return jnp.concatenate(
            [
                ref[p * z.sel + level * z.mid : p * z.sel + (level + 1) * z.mid, lanes]
                for ref in refs
                for p in range(4)
            ],
            axis=0,
        )

    across = [
        jnp.transpose(of_level(level, (first_stats, second_stats), slice(0, LANES)))
        for level in range(2)
    ]
    for pair in range(z.pairs):
        lanes = slice(pair * PAIR, (pair + 1) * PAIR)
        value_lanes = slice(width + pair * PAIR, width + (pair + 1) * PAIR)
        sums_k, sums_v = [], []
        for level, (start, stop) in enumerate(parts):
            entry = iota((stop - start, 1), 0) + start
            keys, values = sel[start:stop, lanes], sel[start:stop, value_lanes]
            queries = halves(of_level(level, (first, second), lanes))
            grads = halves(of_level(level, (first, second), value_lanes))
            sum_k = sum_v = None
            for side in range(2):
                head = 2 * pair + side
                at = chosen_row(z, entry, offs_ref[0, head], offs_ref[1, head])
                valid = (at >= 0) & (at < limit)
                scores = jnp.where(valid, dot(keys, queries[side], NT), -jnp.inf)
                probs = jnp.exp(scores - across[level][head : head + 1, :])
                grad_probs = dot(values, grads[side], NT)
                grad_probs = grad_probs - across[level][SECOND + head : SECOND + head + 1, :]
                part_k = dot((probs * grad_probs).astype(BF), queries[side])
                part_v = dot(probs.astype(BF), grads[side])
                sum_k = part_k if side == 0 else sum_k + part_k
                sum_v = part_v if side == 0 else sum_v + part_v
            sums_k.append(sum_k)
            sums_v.append(sum_v)
        tail = [jnp.zeros((held_tail, PAIR), F32)]
        sum_k = jnp.concatenate(sums_k + tail, axis=0)
        sum_v = jnp.concatenate(sums_v + tail, axis=0)
        dk[:, lanes] = (dk_near[:, lanes] + spread(z, offs_ref, pair, sum_k)).astype(BF)
        dv[:, lanes] = (dv_near[:, lanes] + spread(z, offs_ref, pair, sum_v)).astype(BF)


def early_weights_kernel(z, turned, turned_other, attn, attn_other, dq, dq_other, cot, cot_other, out):
    width = z.width
    out[:, :width] = (dot(attn[...], cot[...]) + dot(attn_other[...], cot_other[...])).astype(BF)
    out[:, width:] = (
        dot(turned[: z.half, :], dq[...]) + dot(turned_other[: z.half, :], dq_other[...])
    ).astype(BF)


def late_weights_kernel(z, turned, turned_other, dk, dv, dk_other, dv_other, out_a, out_b):
    width = z.width
    cut = out_a.shape[1] - width
    left, left_other = turned[: z.half, :], turned_other[: z.half, :]
    out_b[...] = (
        dot(turned[z.half :, :], dv[:, cut:]) + dot(turned_other[z.half :, :], dv_other[:, cut:])
    ).astype(BF)
    out_a[:, :width] = (dot(left, dk[...]) + dot(left_other, dk_other[...])).astype(BF)
    out_a[:, width:] = (dot(left, dv[:, :cut]) + dot(left_other, dv_other[:, :cut])).astype(BF)


def tiles_kernel(z, dq, dk, dv, w_qkv, out):
    width = z.width
    out[...] = (
        dot(dq[...], w_qkv[:, :width], NT)
        + dot(dk[...], w_qkv[:, width : 2 * width], NT)
        + dot(dv[...], w_qkv[:, 2 * width :], NT)
    ).astype(BF)


def call(kernel, outs, flops, scratch=(), smem=0):
    def run(*args):
        moved = sum(int(np.prod(a.shape)) * a.dtype.itemsize for a in args)
        moved += sum(int(np.prod(s)) * jnp.dtype(t).itemsize for s, t in outs)
        specs = [
            pl.BlockSpec(memory_space=pltpu.SMEM if i < smem else pltpu.VMEM)
            for i in range(len(args))
        ]
        return pl.pallas_call(
            kernel,
            out_shape=tuple(jax.ShapeDtypeStruct(s, t) for s, t in outs),
            in_specs=specs,
            out_specs=tuple(pl.BlockSpec(memory_space=pltpu.VMEM) for _ in outs),
            scratch_shapes=list(scratch),
            compiler_params=pltpu.CompilerParams(vmem_limit_bytes=VMEM_BYTES),
            cost_estimate=pl.CostEstimate(
                flops=int(flops), bytes_accessed=int(moved), transcendentals=0
            ),
        )(*args)

    return run


def swap(value, mask, dev_count):
    return lax.ppermute(value, "ctx", [(d, d ^ mask) for d in range(dev_count)])


def upper_steps(dev_count):
    steps, base = [], GROUP
    while base < dev_count:
        count = 4 if base * 4 <= dev_count else 2
        steps.append((base, count))
        base *= count
    return steps


PLANE = (2, 4)


def collect(value, step, dev_count, first=()):
    base, count = step
    parts = [value] + [swap(value, base * i, dev_count) for i in range(1, count)]
    if first:
        parts = lax.optimization_barrier((*parts, *first))[:count]
    return jnp.concatenate(parts, axis=0)


def reduce_step(value, step, dev_count, dtype):
    base, count = step
    size = value.shape[0] // count
    total = value[:size].astype(F32)
    for i in range(1, count):
        total = total + swap(value[i * size : (i + 1) * size], base * i, dev_count).astype(F32)
    return total.astype(dtype)


def reduce_all(value, steps, dev_count):
    for i, step in enumerate(steps):
        value = reduce_step(value, step, dev_count, F32 if i == len(steps) - 1 else BF)
    return value


def strip_order(z, own):
    entries = []
    for core in range(2):
        for first_plane in (True, False):
            outer, inner = (4, z.upper) if first_plane else (z.upper, 4)
            a, b, r = np.meshgrid(
                np.arange(outer), np.arange(inner), np.arange(z.strip), indexing="ij"
            )
            plane, upper = (a, b) if first_plane else (b, a)
            entries.append(
                np.stack([(core + 2 * plane + GROUP * upper).ravel(), r.ravel()], axis=1)
            )
    table = np.concatenate(entries, axis=0).astype(np.int32)
    return (own ^ table[:, :1]) * z.strip + table[:, 1:]


def after(value, *others):
    return lax.optimization_barrier((value, *others))[0]


def per_device(tiles, w_qkv, w_out, cotangent, offsets, pad_count):
    n = lax.axis_size("ctx")
    z = Sizes(tiles.shape[0], tiles.shape[1], n)
    own = lax.axis_index("ctx")
    rows, width = z.rows, z.width
    ups = upper_steps(n)
    order = strip_order(z, own)
    base_flops = 2 * rows * rows * width

    q, k, v, g, sel, far = call(
        functools.partial(project_kernel, z),
        [((rows, width), BF)] * 4 + [((z.sel, 4 * width), BF), ((z.far, 4 * width), BF)],
        2 * rows * width * 4 * width,
        smem=1,
    )(offsets, tiles, w_qkv, cotangent, w_out)

    mixed, near_stats, turned, turned_out = call(
        functools.partial(near_kernel, z),
        [
            ((rows, width), F32),
            ((rows, LANES), F32),
            ((width, rows), BF),
            ((width, rows), BF),
        ],
        8 * base_flops,
        smem=1,
    )(pad_count, q, k, v, g, tiles, order)

    far_up = far
    for i, step in enumerate(ups):
        far_up = collect(far_up, step, n, (near_stats,) if i == 0 else ())
    mid_0 = collect(sel[: z.mid, : 2 * width], PLANE, n)
    mid_1 = swap(mid_0, 1, n)
    far_0 = collect(far_up[:, : 2 * width], PLANE, n)
    far_1 = swap(far_0, 1, n)
    qg = jnp.concatenate([sel[: z.mid, 2 * width :], far_up[:, 2 * width :]], axis=0)
    qg_first = collect(after(qg, far_0), PLANE, n)
    qg_second = swap(qg_first, 1, n)
    turned_other = swap(turned_out, 1, n)
    cot_other = swap(cotangent, 1, n)

    stats, picked, held = call(
        functools.partial(join_kernel, z),
        [((rows, LANES), F32), ((z.sel, LANES), F32), ((z.sel, width), F32)],
        3 * base_flops,
        smem=2,
    )(offsets, pad_count, sel, mid_0, mid_1, far_0, far_1, near_stats)

    out_rows, attn_turned, attn_turned_out = call(
        functools.partial(output_kernel, z),
        [((rows, width), BF), ((z.half, rows), BF), ((z.half, rows), BF)],
        6 * rows * width * width,
        scratch=[pltpu.VMEM((rows, width), BF)],
        smem=1,
    )(offsets, near_stats, stats, mixed, held, tiles, w_out, order)
    attn_other = swap(attn_turned_out, 1, n)

    dq, dk_near, dv_near = call(
        functools.partial(near_grads_kernel, z),
        [((rows, width), BF), ((rows, width), F32), ((rows, width), F32)],
        8 * base_flops,
        smem=2,
    )(offsets, pad_count, q, k, v, g, stats, sel, mid_0, mid_1, far_0, far_1, picked)
    dq_other = swap(dq, 1, n)

    stats_up = picked[z.mid : z.mid + z.far]
    for i, step in enumerate(ups):
        stats_up = collect(stats_up, step, n, (out_rows,) if i == 0 else ())
    stats_first = collect(
        jnp.concatenate([picked[: z.mid], stats_up], axis=0), PLANE, n, (dk_near,)
    )
    stats_second = swap(stats_first, 1, n)

    (early_half,) = call(
        functools.partial(early_weights_kernel, z),
        [((z.half, 2 * width), BF)],
        4 * rows * width * width,
    )(turned, turned_other, attn_turned, attn_other, dq, dq_other, cotangent, cot_other)
    early = reduce_all(early_half, [PLANE] + ups[::-1], n)

    dk, dv = call(
        functools.partial(key_grads_kernel, z),
        [((rows, width), BF), ((rows, width), BF)],
        3 * base_flops,
        smem=2,
    )(offsets, pad_count, sel, qg_first, qg_second, stats_first, stats_second, dk_near, dv_near)
    dk_other = swap(dk, 1, n)
    dv_other = swap(dv, 1, n)
    cut = width // 3
    late_a, late_b = call(
        functools.partial(late_weights_kernel, z),
        [((z.half, width + cut), BF), ((z.half, width - cut), BF)],
        4 * rows * width * width,
    )(turned, turned_other, dk, dv, dk_other, dv_other)
    grad_a = reduce_all(late_a, [PLANE] + ups[::-1], n)
    grad_b = reduce_all(late_b, ups[::-1] + [PLANE], n)

    (grad_tiles,) = call(
        functools.partial(tiles_kernel, z), [((rows, width), BF)], 6 * rows * width * width
    )(dq, dk, dv, w_qkv)
    grad_wqkv = jnp.concatenate([early[:, width:], grad_a, grad_b], axis=1)
    return out_rows, grad_tiles, grad_wqkv, early[:, :width]


def solution(mesh):
    return jax.shard_map(
        per_device,
        mesh=mesh,
        in_specs=(P("ctx", None), P(), P(), P("ctx", None), P(), P()),
        out_specs=(P("ctx", None), P("ctx", None), P("ctx", None), P("ctx", None)),
        check_vma=False,
    )
```

```python
import functools

import jax
import jax.numpy as jnp
import numpy as np
from jax import lax
from jax.experimental import pallas as pl
from jax.experimental.pallas import tpu as pltpu
from jax.sharding import PartitionSpec as P

HEAD_DIM = 64
GROUP = 8
PAIR = 2 * HEAD_DIM
LANES = 128
SECOND = 16
SCALE = 0.125
BF = jnp.bfloat16
F32 = jnp.float32
NT = (((1,), (1,)), ((), ()))
NN = (((1,), (0,)), ((), ()))
TN = (((0,), (0,)), ((), ()))
LARGE = 1e30
LOAD_CUTS = 4
VMEM_BYTES = 40 * 1024 * 1024


def dot(a, b, dims=NN):
    return lax.dot_general(a, b, dims, preferred_element_type=F32)


def dot_exact(a, b):
    return lax.dot_general(a, b, NN, preferred_element_type=F32, precision=lax.Precision.HIGHEST)


def iota(shape, dim):
    return lax.broadcasted_iota(jnp.int32, shape, dim)


def low_half(shape):
    return iota(shape, len(shape) - 1) % PAIR < HEAD_DIM


def halves(x):
    low = low_half(x.shape)
    zero = jnp.zeros((), x.dtype)
    return jnp.where(low, x, zero), jnp.where(low, zero, x)


def by_head(first, second, rows):
    return jnp.where(low_half((rows, PAIR)), first, second)


class Sizes:
    def __init__(self, rows, width, dev_count):
        self.rows = rows
        self.width = width
        self.devs = dev_count
        self.heads = width // HEAD_DIM
        self.pairs = self.heads // 2
        self.mid = rows // GROUP
        self.far = rows // dev_count
        self.sel = 2 * self.mid
        self.far_held = -(-self.far // 16) * 16
        self.upper = dev_count // GROUP
        self.strip = width // dev_count
        self.half = width // 2


def chosen_row(z, index, off_mid, off_far):
    row = jnp.where(index < z.mid, index * GROUP + off_mid, (index - z.mid) * z.devs + off_far)
    return jnp.where(index < z.mid + z.far, row, -1)


def spread(z, offs_ref, pair, picked):
    lane = iota((1, 4 * z.sel), 1)
    second = (lane // z.sel) % 2 == 1
    off_mid = jnp.where(second, offs_ref[0, 2 * pair + 1], offs_ref[0, 2 * pair])
    off_far = jnp.where(second, offs_ref[1, 2 * pair + 1], offs_ref[1, 2 * pair])
    target = chosen_row(z, lane % z.sel, off_mid, off_far)
    place = (iota((z.rows, 4 * z.sel), 0) == target).astype(F32).astype(BF)
    high = picked.astype(BF)
    rest = (picked - high.astype(F32)).astype(BF)
    first_high, second_high = halves(high)
    first_rest, second_rest = halves(rest)
    stacked = jnp.concatenate([first_high, second_high, first_rest, second_rest], axis=0)
    return dot(place, stacked)


def lane_offsets(z, offs_ref):
    lane = iota((1, LANES), 1)
    off_mid = jnp.full((1, LANES), -1, jnp.int32)
    off_far = jnp.full((1, LANES), -1, jnp.int32)
    for head in range(z.heads):
        here = (lane == head) | (lane == SECOND + head)
        off_mid = jnp.where(here, offs_ref[0, head], off_mid)
        off_far = jnp.where(here, offs_ref[1, head], off_far)
    return off_mid, off_far


def stat_masks(z, offs_ref):
    off_mid, off_far = lane_offsets(z, offs_ref)
    row = iota((z.rows, LANES), 0)
    return row % GROUP == off_mid, row % z.devs == off_far


def pick_stats(z, masks, stats):
    entry = iota((z.sel, z.rows), 0)
    row = iota((z.sel, z.rows), 1)
    take_mid = ((entry < z.mid) & (row // GROUP == entry)).astype(F32)
    take_far = (row // z.devs == entry - z.mid).astype(F32)
    return dot_exact(take_mid, jnp.where(masks[0], stats, 0.0)) + dot_exact(
        take_far, jnp.where(masks[1], stats, 0.0)
    )


def spread_stats(z, masks, picked):
    row = iota((z.rows, z.sel), 0)
    entry = iota((z.rows, z.sel), 1)
    give_mid = ((entry < z.mid) & (row // GROUP == entry)).astype(F32)
    give_far = (row // z.devs == entry - z.mid).astype(F32)
    fill = jnp.where(iota((z.rows, LANES), 1) < SECOND, -jnp.inf, 0.0)
    return (
        jnp.where(masks[0], dot_exact(give_mid, picked), fill),
        jnp.where(masks[1], dot_exact(give_far, picked), fill),
    )


def gathered_place(z, own, level):
    index = iota((1, z.rows), 1)
    core = index // (4 * z.mid)
    plane = (index // z.mid) % 4
    inner = index % z.mid
    if level == 0:
        return (own ^ (core + 2 * plane)) * z.rows + inner * GROUP
    dev = own ^ (core + 2 * plane + GROUP * (inner // z.far))
    return dev * z.rows + (inner % z.far) * z.devs


def level_parts(z):
    return ((0, z.mid), (z.mid, z.mid + z.far_held))


def project_kernel(
    z, offs_hbm, tiles_hbm, w_qkv_hbm, cot_hbm, w_out_hbm, q, k, v, g, sel, far,
    offs_ref, tiles, w_qkv, cot, w_out, sems,
):
    width = z.width
    step = width // LOAD_CUTS

    def column_block(block):
        return [
            (
                w_qkv_hbm.at[pl.ds(i * step, step), pl.ds(block * width, width)],
                w_qkv.at[pl.ds(i * step, step), pl.ds(block * width, width)],
            )
            for i in range(LOAD_CUTS)
        ]

    groups = [
        [(tiles_hbm, tiles)] + column_block(1),
        column_block(2),
        column_block(0),
        [(cot_hbm, cot)]
        + [
            (w_out_hbm.at[pl.ds(i * step, step), :], w_out.at[pl.ds(i * step, step), :])
            for i in range(LOAD_CUTS)
        ],
        [(offs_hbm, offs_ref)],
    ]
    copies, index = [], 0
    for group in groups:
        made = []
        for source, target in group:
            copy = pltpu.make_async_copy(source, target, sems.at[index])
            copy.start()
            made.append(copy)
            index += 1
        copies.append(made)

    def arrived(group):
        for copy in copies[group]:
            copy.wait()

    arrived(0)
    own = tiles[...]
    k[...] = dot(own, w_qkv[:, width : 2 * width]).astype(BF)
    arrived(1)
    v[...] = dot(own, w_qkv[:, 2 * width :]).astype(BF)
    arrived(2)
    q[...] = dot(own, w_qkv[:, :width]).astype(BF) * jnp.asarray(SCALE, BF)
    arrived(3)
    g[...] = dot(cot[...], w_out[...], NT).astype(BF)
    arrived(4)
    entry = iota((2 * z.sel, z.rows), 0)
    column = iota((2 * z.sel, z.rows), 1)
    second = entry >= z.sel
    for pair in range(z.pairs):
        lanes = slice(pair * PAIR, (pair + 1) * PAIR)
        off_mid = jnp.where(second, offs_ref[0, 2 * pair + 1], offs_ref[0, 2 * pair])
        off_far = jnp.where(second, offs_ref[1, 2 * pair + 1], offs_ref[1, 2 * pair])
        target = chosen_row(z, entry % z.sel, off_mid, off_far)
        take = (column == target).astype(F32).astype(BF)
        every = jnp.concatenate([k[:, lanes], v[:, lanes], q[:, lanes], g[:, lanes]], axis=1)
        both = dot(take, every)
        picked = jnp.where(low_half((z.sel, 4 * PAIR)), both[: z.sel], both[z.sel :]).astype(BF)
        far_part = jnp.where(
            low_half((z.far, 4 * PAIR)),
            both[z.mid : z.mid + z.far],
            both[z.sel + z.mid : z.sel + z.mid + z.far],
        ).astype(BF)
        for part in range(4):
            to = slice(part * width + pair * PAIR, part * width + (pair + 1) * PAIR)
            sel[:, to] = picked[:, part * PAIR : (part + 1) * PAIR]
            far[:, to] = far_part[:, part * PAIR : (part + 1) * PAIR]


def near_kernel(z, pad_ref, q, k, v, g, tiles, order, mixed, stats, turned, turned_out):
    own = lax.axis_index("ctx")
    limit = z.rows * z.devs - pad_ref[0] - own * z.rows
    valid = iota((1, z.rows), 1) < limit
    lane = iota((z.rows, LANES), 1)
    both = jnp.zeros((z.rows, LANES), F32)
    for pair in range(z.pairs):
        lanes = slice(pair * PAIR, (pair + 1) * PAIR)
        query = q[:, lanes]
        grad = g[:, lanes].astype(F32)
        keys = halves(k[:, lanes])
        values = halves(v[:, lanes])
        total = None
        for side in range(2):
            head = 2 * pair + side
            scores = jnp.where(valid, dot(query, keys[side], NT), -jnp.inf)
            peak = jnp.max(scores, axis=1, keepdims=True)
            powers = jnp.exp(scores - peak)
            summed = jnp.sum(powers, axis=1, keepdims=True)
            part = dot(powers.astype(BF), values[side]) * (1.0 / summed)
            total = part if total is None else total + part
            both = jnp.where(lane == head, peak + jnp.log(summed), both)
            meets = jnp.sum(grad * part, axis=1, keepdims=True)
            both = jnp.where(lane == SECOND + head, meets, both)
        mixed[:, lanes] = total
    stats[...] = both
    for part, target in enumerate((turned, turned_out)):
        source = order[part * z.half : (part + 1) * z.half, :]
        place = (iota((z.half, z.width), 1) == source).astype(F32).astype(BF)
        target[...] = dot(place, tiles[...], NT).astype(BF)


def of_level(level, refs, lanes):
    return jnp.concatenate([ref[:, lanes] for ref in refs[level]], axis=0)


def part_lanes(z, part, pair):
    return slice(part * z.width + pair * PAIR, part * z.width + (pair + 1) * PAIR)


def own_scores(z, limit, offs_ref, sel, refs):
    own = lax.axis_index("ctx")
    scores, places = [], []
    for level, (start, stop) in enumerate(level_parts(z)):
        place = gathered_place(z, own, level)
        for pair in range(z.pairs):
            query = sel[start:stop, part_lanes(z, 2, pair)]
            keys = halves(of_level(level, refs, part_lanes(z, 0, pair)))
            for side in range(2):
                valid = place + offs_ref[level, 2 * pair + side] < limit
                scores.append(jnp.where(valid, dot(query, keys[side], NT), -jnp.inf))
                places.append((level, 2 * pair + side, start, stop))
    spots, at = [], 0
    for level, head, start, stop in places:
        spots.append((level, head, at, at + stop - start))
        at += stop - start
    return jnp.concatenate(scores, axis=0), spots


def to_lanes(z, spots, columns):
    parts = []
    for level, (start, stop) in enumerate(level_parts(z)):
        lane = iota((stop - start, LANES), 1)
        part = jnp.zeros((stop - start, LANES), F32)
        for found, head, first, last in spots:
            if found == level:
                for shift, column in columns:
                    part = jnp.where(lane == shift + head, column[first:last], part)
        parts.append(part)
    parts.append(jnp.zeros((z.sel - level_parts(z)[1][1], LANES), F32))
    return jnp.concatenate(parts, axis=0)


def from_lanes(spots, array, shift):
    return lambda z: jnp.concatenate(
        [
            array[level_parts(z)[level][0] : level_parts(z)[level][1], shift + head : shift + head + 1]
            for level, head, _, _ in spots
        ],
        axis=0,
    )


def spot_of(spots, level, head):
    return next((first, last) for found, at, first, last in spots if (found, at) == (level, head))


def join_kernel(
    z, offs_ref, pad_ref, sel, mid_0, mid_1, far_0, far_1, near_stats, stats, picked, raw, held
):
    refs = ((mid_0, mid_1), (far_0, far_1))
    scores, spots = own_scores(z, z.rows * z.devs - pad_ref[0], offs_ref, sel, refs)
    peak = jnp.max(scores, axis=1, keepdims=True)
    powers = jnp.exp(scores - peak)
    summed = jnp.sum(powers, axis=1, keepdims=True)
    lse = peak + jnp.log(summed)
    scale = 1.0 / summed
    powers = powers.astype(BF)
    products = []
    tail = jnp.zeros((z.sel - level_parts(z)[1][1], PAIR), F32)
    for pair in range(z.pairs):
        totals = []
        for level, (start, stop) in enumerate(level_parts(z)):
            values = halves(of_level(level, refs, part_lanes(z, 1, pair)))
            parts = []
            for side in range(2):
                at, to = spot_of(spots, level, 2 * pair + side)
                parts.append(dot(powers[at:to], values[side]) * scale[at:to])
            totals.append(parts[0] + parts[1])
            grad = sel[start:stop, part_lanes(z, 3, pair)].astype(F32)
            products.append((level, pair, [grad * part for part in parts]))
        held[:, pair * PAIR : (pair + 1) * PAIR] = jnp.concatenate(totals + [tail], axis=0)
    products.sort(key=lambda entry: entry[:2])
    stacked = jnp.concatenate([part for _, _, both in products for part in both], axis=0)
    meets = jnp.sum(stacked, axis=1, keepdims=True)
    sel_both = to_lanes(z, spots, ((0, lse), (SECOND, meets)))
    raw[...] = sel_both
    masks = stat_masks(z, offs_ref)
    near = near_stats[...]
    mid, far = spread_stats(z, masks, sel_both)
    top = jnp.maximum(near, jnp.maximum(mid, far))
    total_lse = top + jnp.log(jnp.exp(near - top) + jnp.exp(mid - top) + jnp.exp(far - top))
    delta = sum(
        pltpu.roll(jnp.exp(value - total_lse), SECOND, 1) * value
        for value in (
            near,
            jnp.where(masks[0], mid, -LARGE),
            jnp.where(masks[1], far, -LARGE),
        )
    )
    both = jnp.where(iota((z.rows, LANES), 1) < SECOND, total_lse, delta)
    stats[...] = both
    picked[...] = pick_stats(z, masks, both)


def output_kernel(
    z, offs_ref, near_stats, stats, picked, raw, mixed, held, tiles, w_out, order,
    rows_out, turned, turned_out, attn,
):
    near_share = jnp.exp(near_stats[...] - stats[...])
    share = jnp.exp(raw[...] - picked[...])
    for pair in range(z.pairs):
        lanes = slice(pair * PAIR, (pair + 1) * PAIR)
        near = by_head(
            near_share[:, 2 * pair : 2 * pair + 1],
            near_share[:, 2 * pair + 1 : 2 * pair + 2],
            z.rows,
        )
        own = by_head(share[:, 2 * pair : 2 * pair + 1], share[:, 2 * pair + 1 : 2 * pair + 2], z.sel)
        combined = near * mixed[:, lanes] + spread(z, offs_ref, pair, own * held[:, lanes])
        attn[:, lanes] = combined.astype(BF)
    rows_out[...] = (tiles[...].astype(F32) + dot(attn[...], w_out[...])).astype(BF)
    for part, target in enumerate((turned, turned_out)):
        source = order[part * z.half : (part + 1) * z.half, :]
        place = (iota((z.half, z.width), 1) == source).astype(F32).astype(BF)
        target[...] = dot(place, attn[...], NT).astype(BF)


def near_grads_kernel(
    z, offs_ref, pad_ref, q, k, v, g, stats, sel, mid_0, mid_1, far_0, far_1, picked,
    dq, dk, dv, dq_sel,
):
    own = lax.axis_index("ctx")
    limit = z.rows * z.devs - pad_ref[0]
    refs = ((mid_0, mid_1), (far_0, far_1))
    scores, spots = own_scores(z, limit, offs_ref, sel, refs)
    probs = jnp.exp(scores - from_lanes(spots, picked, 0)(z))
    grad_probs = []
    for level, (start, stop) in enumerate(level_parts(z)):
        for pair in range(z.pairs):
            grad = sel[start:stop, part_lanes(z, 3, pair)]
            values = halves(of_level(level, refs, part_lanes(z, 1, pair)))
            grad_probs += [dot(grad, values[side], NT) for side in range(2)]
    grad_probs = jnp.concatenate(grad_probs, axis=0) - from_lanes(spots, picked, SECOND)(z)
    grad_scores = (probs * grad_probs).astype(BF)
    tail = jnp.zeros((z.sel - level_parts(z)[1][1], PAIR), F32)
    for pair in range(z.pairs):
        sums = []
        for level in range(2):
            keys = halves(of_level(level, refs, part_lanes(z, 0, pair)))
            at, to = spot_of(spots, level, 2 * pair)
            low = dot(grad_scores[at:to], keys[0])
            at, to = spot_of(spots, level, 2 * pair + 1)
            sums.append(low + dot(grad_scores[at:to], keys[1]))
        dq_sel[:, pair * PAIR : (pair + 1) * PAIR] = jnp.concatenate(sums + [tail], axis=0)
    valid_near = iota((z.rows, 1), 0) < limit - own * z.rows
    across = jnp.transpose(stats[...])
    for pair in range(z.pairs):
        lanes = slice(pair * PAIR, (pair + 1) * PAIR)
        query, grad = q[:, lanes], g[:, lanes]
        queries, grads = halves(query), halves(grad)
        keys, values = halves(k[:, lanes]), halves(v[:, lanes])
        sum_q = sum_k = sum_v = None
        for side in range(2):
            head = 2 * pair + side
            scores = jnp.where(valid_near, dot(keys[side], query, NT), -jnp.inf)
            probs = jnp.exp(scores - across[head : head + 1, :])
            grad_probs = dot(values[side], grad, NT)
            grad_scores = probs * (grad_probs - across[SECOND + head : SECOND + head + 1, :])
            grad_scores = grad_scores.astype(BF)
            part_k = dot(grad_scores, queries[side])
            part_v = dot(probs.astype(BF), grads[side])
            part_q = dot(grad_scores, keys[side], TN)
            if side == 0:
                sum_q, sum_k, sum_v = part_q, part_k, part_v
            else:
                sum_q, sum_k, sum_v = sum_q + part_q, sum_k + part_k, sum_v + part_v
        dk[:, lanes] = sum_k
        dv[:, lanes] = sum_v
        dq[:, lanes] = (SCALE * (sum_q + spread(z, offs_ref, pair, dq_sel[:, lanes]))).astype(BF)


def key_grads_kernel(
    z, offs_ref, pad_ref, sel, mid_0, mid_1, far_0, far_1, stats_0, stats_1, dk_near, dv_near, dk, dv
):
    own = lax.axis_index("ctx")
    limit = z.rows * z.devs - pad_ref[0] - own * z.rows
    parts = level_parts(z)
    refs = ((mid_0, mid_1), (far_0, far_1))
    stat_refs = (stats_0, stats_1)
    first_part = (2, 0)
    tail = jnp.zeros((z.sel - parts[1][1], PAIR), F32)
    probs, grad_scores = {}, {}
    for level, (start, stop) in enumerate(parts):
        across = jnp.transpose(jnp.concatenate([ref[level * 4 * z.mid : (level + 1) * 4 * z.mid, :] for ref in stat_refs], axis=0))
        entry = iota((stop - start, 1), 0) + start
        for pair in range(z.pairs):
            keys = sel[start:stop, part_lanes(z, 0, pair)]
            values = sel[start:stop, part_lanes(z, 1, pair)]
            queries = halves(of_level(level, refs, part_lanes(z, first_part[level], pair)))
            grads = halves(of_level(level, refs, part_lanes(z, first_part[level] + 1, pair)))
            for side in range(2):
                head = 2 * pair + side
                at = chosen_row(z, entry, offs_ref[0, head], offs_ref[1, head])
                valid = (at >= 0) & (at < limit)
                scores = jnp.where(valid, dot(keys, queries[side], NT), -jnp.inf)
                exps = jnp.exp(scores - across[head : head + 1, :])
                grad_probs = dot(values, grads[side], NT)
                grad_probs = grad_probs - across[SECOND + head : SECOND + head + 1, :]
                probs[level, head] = exps.astype(BF)
                grad_scores[level, head] = (exps * grad_probs).astype(BF)
    sums_k, sums_v = {}, {}
    for pair in range(z.pairs):
        both_k, both_v = [], []
        for level in range(2):
            queries = halves(of_level(level, refs, part_lanes(z, first_part[level], pair)))
            grads = halves(of_level(level, refs, part_lanes(z, first_part[level] + 1, pair)))
            low, high = 2 * pair, 2 * pair + 1
            both_k.append(
                dot(grad_scores[level, low], queries[0]) + dot(grad_scores[level, high], queries[1])
            )
            both_v.append(dot(probs[level, low], grads[0]) + dot(probs[level, high], grads[1]))
        sums_k[pair] = jnp.concatenate(both_k + [tail], axis=0)
        sums_v[pair] = jnp.concatenate(both_v + [tail], axis=0)
    for pair in range(z.pairs):
        lanes = slice(pair * PAIR, (pair + 1) * PAIR)
        both = jnp.concatenate([sums_k[pair], sums_v[pair]], axis=1)
        moved = spread(z, offs_ref, pair, both)
        dk[:, lanes] = (dk_near[:, lanes] + moved[:, :PAIR]).astype(BF)
        dv[:, lanes] = (dv_near[:, lanes] + moved[:, PAIR:]).astype(BF)


def early_weights_kernel(
    z, turned, turned_other, attn, attn_other, dq, dq_other, cot, cot_other, out
):
    width = z.width
    out[:, :width] = (dot(attn[...], cot[...]) + dot(attn_other[...], cot_other[...])).astype(BF)
    out[:, width:] = (dot(turned[...], dq[...]) + dot(turned_other[...], dq_other[...])).astype(BF)


def late_weights_kernel(z, turned, turned_other, dk, dv, dk_other, dv_other, out):
    width = z.width
    out[:, :width] = (dot(turned[...], dk[...]) + dot(turned_other[...], dk_other[...])).astype(BF)
    out[:, width:] = (dot(turned[...], dv[...]) + dot(turned_other[...], dv_other[...])).astype(BF)


def tiles_kernel(z, dq, dk, dv, w_qkv, out):
    width = z.width
    out[...] = (
        dot(dq[...], w_qkv[:, :width], NT)
        + dot(dk[...], w_qkv[:, width : 2 * width], NT)
        + dot(dv[...], w_qkv[:, 2 * width :], NT)
    ).astype(BF)


def call(kernel, outs, flops, scratch=(), smem=0, spaces=None, vmem=VMEM_BYTES):
    def run(*args):
        moved = sum(int(np.prod(a.shape)) * a.dtype.itemsize for a in args)
        moved += sum(int(np.prod(s)) * jnp.dtype(t).itemsize for s, t in outs)
        specs = [
            pl.BlockSpec(memory_space=spaces or (pltpu.SMEM if i < smem else pltpu.VMEM))
            for i in range(len(args))
        ]
        return pl.pallas_call(
            kernel,
            out_shape=tuple(jax.ShapeDtypeStruct(s, t) for s, t in outs),
            in_specs=specs,
            out_specs=tuple(pl.BlockSpec(memory_space=pltpu.VMEM) for _ in outs),
            scratch_shapes=list(scratch),
            compiler_params=pltpu.CompilerParams(vmem_limit_bytes=vmem),
            cost_estimate=pl.CostEstimate(
                flops=int(flops), bytes_accessed=int(moved), transcendentals=0
            ),
        )(*args)

    return run


def swap(value, mask, dev_count):
    return lax.ppermute(value, "ctx", [(d, d ^ mask) for d in range(dev_count)])


def upper_steps(dev_count):
    steps, base = [], GROUP
    while base < dev_count:
        count = 4 if base * 4 <= dev_count else 2
        steps.append((base, count))
        base *= count
    return steps


PLANE = (2, 4)


def tied(parts, first):
    return list(lax.optimization_barrier((*parts, *first))[: len(parts)]) if first else list(parts)


def plane_parts(value, dev_count, first=()):
    base, count = PLANE
    return tied(
        [value] + [swap(value, base * i, dev_count) for i in range(1, count)], first
    )


def doubled(value, masks, dev_count, first=()):
    for i, mask in enumerate(masks):
        parts = tied([value, swap(value, mask, dev_count)], first if i == 0 else ())
        value = jnp.concatenate(parts, axis=0)
    return value


def halved(value, masks, dev_count):
    for i, mask in enumerate(masks):
        size = value.shape[0] // 2
        total = value[:size].astype(F32) + swap(value[size:], mask, dev_count).astype(F32)
        value = total if i == len(masks) - 1 else total.astype(BF)
    return value


def reduce_step(value, step, dev_count, dtype, first=()):
    base, count = step
    size = value.shape[0] // count
    parts = [value[:size]] + [
        swap(value[i * size : (i + 1) * size], base * i, dev_count) for i in range(1, count)
    ]
    return sum(part.astype(F32) for part in tied(parts, first)).astype(dtype)


def reduce_all(value, steps, dev_count):
    for i, step in enumerate(steps):
        value = reduce_step(value, step, dev_count, F32 if i == len(steps) - 1 else BF)
    return value


def strip_order(z, own):
    core, plane, upper, row = np.meshgrid(
        np.arange(2), np.arange(4), np.arange(z.upper), np.arange(z.strip), indexing="ij"
    )
    mask = (core + 2 * plane + GROUP * upper).reshape(-1, 1).astype(np.int32)
    return (own ^ mask) * z.strip + row.reshape(-1, 1).astype(np.int32)


def after(value, *others):
    return lax.optimization_barrier((value, *others))[0]


def per_device(tiles, w_qkv, w_out, cotangent, offsets, pad_count):
    n = lax.axis_size("ctx")
    z = Sizes(tiles.shape[0], tiles.shape[1], n)
    own = lax.axis_index("ctx")
    rows, width = z.rows, z.width
    order = strip_order(z, own)
    base_flops = 2 * rows * rows * width

    q, k, v, g, sel, far = call(
        functools.partial(project_kernel, z),
        [((rows, width), BF)] * 4 + [((z.sel, 4 * width), BF), ((z.far, 4 * width), BF)],
        2 * rows * width * 4 * width,
        scratch=[
            pltpu.SMEM(offsets.shape, jnp.int32),
            pltpu.VMEM(tiles.shape, BF),
            pltpu.VMEM(w_qkv.shape, BF),
            pltpu.VMEM(cotangent.shape, BF),
            pltpu.VMEM(w_out.shape, BF),
            pltpu.SemaphoreType.DMA((4 * LOAD_CUTS + 3,)),
        ],
        spaces=pltpu.HBM,
        vmem=61 * 1024 * 1024,
    )(offsets, tiles, w_qkv, cotangent, w_out)

    masks = [mask for mask in (2**i for i in range(30)) if GROUP <= mask < n]
    far_up = doubled(far, masks, n)
    mid_parts = plane_parts(sel[: z.mid], n)
    mixed, near_stats, turned, turned_out = call(
        functools.partial(near_kernel, z),
        [
            ((rows, width), F32),
            ((rows, LANES), F32),
            ((z.half, rows), BF),
            ((z.half, rows), BF),
        ],
        8 * base_flops,
        smem=1,
    )(pad_count, after(q, far_up), k, v, g, tiles, order)
    mid_0 = jnp.concatenate(mid_parts, axis=0)
    mid_1 = swap(mid_0, 1, n)
    far_parts = plane_parts(far_up, n, (near_stats,))
    far_0 = jnp.concatenate([part[:, : 2 * width] for part in far_parts], axis=0)
    far_1 = swap(far_0, 1, n)
    far_qg_0 = jnp.concatenate([part[:, 2 * width :] for part in far_parts], axis=0)
    far_qg_1 = swap(far_qg_0, 1, n)

    stats, picked, raw, held = call(
        functools.partial(join_kernel, z),
        [((rows, LANES), F32), ((z.sel, LANES), F32), ((z.sel, LANES), F32), ((z.sel, width), F32)],
        3 * base_flops,
        smem=2,
    )(offsets, pad_count, sel, mid_0, mid_1, far_0, far_1, near_stats)

    out_rows, attn_turned, attn_turned_out = call(
        functools.partial(output_kernel, z),
        [((rows, width), BF), ((z.half, rows), BF), ((z.half, rows), BF)],
        6 * rows * width * width,
        scratch=[pltpu.VMEM((rows, width), BF)],
        smem=1,
    )(offsets, near_stats, stats, picked, raw, mixed, held, tiles, w_out, order)
    attn_other = swap(attn_turned_out, 1, n)
    turned_other = swap(after(turned_out, picked), 1, n)
    cot_other = swap(after(cotangent, picked), 1, n)

    dq, dk_near, dv_near = call(
        functools.partial(near_grads_kernel, z),
        [((rows, width), BF), ((rows, width), F32), ((rows, width), F32)],
        8 * base_flops,
        scratch=[pltpu.VMEM((z.sel, width), F32)],
        smem=2,
    )(offsets, pad_count, q, k, v, g, stats, sel, mid_0, mid_1, far_0, far_1, picked)
    dq_other = swap(dq, 1, n)

    stats_up = doubled(picked[z.mid : z.mid + z.far], masks, n, (out_rows,))
    stats_plane = [doubled(part, (2, 4), n) for part in (jnp.concatenate([picked[: z.mid], stats_up], axis=1),)]
    stats_0 = jnp.concatenate([stats_plane[0][:, :LANES], stats_plane[0][:, LANES:]], axis=0)
    stats_1 = swap(stats_0, 1, n)

    (early_half,) = call(
        functools.partial(early_weights_kernel, z),
        [((z.half, 2 * width), BF)],
        4 * rows * width * width,
    )(turned, turned_other, attn_turned, attn_other, dq, dq_other, cotangent, cot_other)

    dk, dv = call(
        functools.partial(key_grads_kernel, z),
        [((rows, width), BF), ((rows, width), BF)],
        3 * base_flops,
        smem=2,
    )(
        offsets, pad_count, sel, mid_0, mid_1, far_qg_0, far_qg_1, stats_0, stats_1,
        after(dk_near, early_half), dv_near,
    )
    dk_other = swap(dk, 1, n)
    dv_other = swap(dv, 1, n)
    (late_half,) = call(
        functools.partial(late_weights_kernel, z),
        [((z.half, 2 * width), BF)],
        4 * rows * width * width,
    )(turned, turned_other, dk, dv, dk_other, dv_other)
    (grad_tiles,) = call(
        functools.partial(tiles_kernel, z), [((rows, width), BF)], 6 * rows * width * width
    )(after(dq, late_half), dk, dv, w_qkv)
    late = reduce_step(late_half, PLANE, n, BF)
    early = reduce_step(early_half, PLANE, n, BF, (late_half,))
    early = halved(early, masks[::-1], n)
    late = reduce_all(late, upper_steps(n)[::-1], n)
    grad_wqkv = jnp.concatenate([early[:, width:], late], axis=1)
    return out_rows, grad_tiles, grad_wqkv, early[:, :width]


def solution(mesh):
    return jax.shard_map(
        per_device,
        mesh=mesh,
        in_specs=(P("ctx", None), P(), P(), P("ctx", None), P(), P()),
        out_specs=(P("ctx", None), P("ctx", None), P("ctx", None), P("ctx", None)),
        check_vma=False,
    )
```

```python
import functools

import jax
import jax.numpy as jnp
import numpy as np
from jax import lax
from jax.experimental import pallas as pl
from jax.experimental.pallas import tpu as pltpu
from jax.sharding import PartitionSpec as P

HEAD_DIM = 64
GROUP = 8
PAIR = 2 * HEAD_DIM
LANES = 128
SECOND = 16
SCALE = 0.125
BF = jnp.bfloat16
F32 = jnp.float32
NT = (((1,), (1,)), ((), ()))
NN = (((1,), (0,)), ((), ()))
TN = (((0,), (0,)), ((), ()))
LARGE = 1e30
LOAD_CUTS = 4
VMEM_BYTES = 40 * 1024 * 1024
PROJECT_VMEM_BYTES = 57 * 1024 * 1024


def dot(a, b, dims=NN):
    return lax.dot_general(a, b, dims, preferred_element_type=F32)


def dot_exact(a, b):
    return lax.dot_general(a, b, NN, preferred_element_type=F32, precision=lax.Precision.HIGHEST)


def iota(shape, dim):
    return lax.broadcasted_iota(jnp.int32, shape, dim)


def low_half(shape):
    return iota(shape, len(shape) - 1) % PAIR < HEAD_DIM


def halves(x):
    low = low_half(x.shape)
    zero = jnp.zeros((), x.dtype)
    return jnp.where(low, x, zero), jnp.where(low, zero, x)


def by_head(first, second, rows):
    return jnp.where(low_half((rows, PAIR)), first, second)


class Sizes:
    def __init__(self, rows, width, dev_count):
        self.rows = rows
        self.width = width
        self.devs = dev_count
        self.heads = width // HEAD_DIM
        self.pairs = self.heads // 2
        self.mid = rows // GROUP
        self.far = rows // dev_count
        self.sel = 2 * self.mid
        self.far_held = -(-self.far // 16) * 16
        self.upper = dev_count // GROUP
        self.strip = width // dev_count
        self.half = width // 2


def chosen_row(z, index, off_mid, off_far):
    row = jnp.where(index < z.mid, index * GROUP + off_mid, (index - z.mid) * z.devs + off_far)
    return jnp.where(index < z.mid + z.far, row, -1)


def spread(z, offs_ref, pair, picked):
    lane = iota((1, 4 * z.sel), 1)
    second = (lane // z.sel) % 2 == 1
    off_mid = jnp.where(second, offs_ref[0, 2 * pair + 1], offs_ref[0, 2 * pair])
    off_far = jnp.where(second, offs_ref[1, 2 * pair + 1], offs_ref[1, 2 * pair])
    target = chosen_row(z, lane % z.sel, off_mid, off_far)
    place = (iota((z.rows, 4 * z.sel), 0) == target).astype(F32).astype(BF)
    high = picked.astype(BF)
    rest = (picked - high.astype(F32)).astype(BF)
    first_high, second_high = halves(high)
    first_rest, second_rest = halves(rest)
    stacked = jnp.concatenate([first_high, second_high, first_rest, second_rest], axis=0)
    return dot(place, stacked)


def lane_offsets(z, offs_ref):
    lane = iota((1, LANES), 1)
    off_mid = jnp.full((1, LANES), -1, jnp.int32)
    off_far = jnp.full((1, LANES), -1, jnp.int32)
    for head in range(z.heads):
        here = (lane == head) | (lane == SECOND + head)
        off_mid = jnp.where(here, offs_ref[0, head], off_mid)
        off_far = jnp.where(here, offs_ref[1, head], off_far)
    return off_mid, off_far


def stat_masks(z, offs_ref):
    off_mid, off_far = lane_offsets(z, offs_ref)
    row = iota((z.rows, LANES), 0)
    return row % GROUP == off_mid, row % z.devs == off_far


def pick_stats(z, masks, stats):
    entry = iota((z.sel, z.rows), 0)
    row = iota((z.sel, z.rows), 1)
    take_mid = ((entry < z.mid) & (row // GROUP == entry)).astype(F32)
    take_far = (row // z.devs == entry - z.mid).astype(F32)
    return dot_exact(take_mid, jnp.where(masks[0], stats, 0.0)) + dot_exact(
        take_far, jnp.where(masks[1], stats, 0.0)
    )


def spread_stats(z, masks, picked):
    row = iota((z.rows, z.sel), 0)
    entry = iota((z.rows, z.sel), 1)
    give_mid = ((entry < z.mid) & (row // GROUP == entry)).astype(F32)
    give_far = (row // z.devs == entry - z.mid).astype(F32)
    fill = jnp.where(iota((z.rows, LANES), 1) < SECOND, -jnp.inf, 0.0)
    return (
        jnp.where(masks[0], dot_exact(give_mid, picked), fill),
        jnp.where(masks[1], dot_exact(give_far, picked), fill),
    )


def gathered_place(z, own, level):
    index = iota((1, z.rows), 1)
    core = index // (4 * z.mid)
    plane = (index // z.mid) % 4
    inner = index % z.mid
    if level == 0:
        return (own ^ (core + 2 * plane)) * z.rows + inner * GROUP
    dev = own ^ (core + 2 * plane + GROUP * (inner // z.far))
    return dev * z.rows + (inner % z.far) * z.devs


def level_parts(z):
    return ((0, z.mid), (z.mid, z.mid + z.far_held))


def project_kernel(
    z, offs_hbm, tiles_hbm, w_qkv_hbm, cot_hbm, w_out_hbm, q, k, v, g, sel, mid, far,
    offs_ref, tiles, w_qkv, cot, w_out, sems,
):
    width = z.width
    step = width // LOAD_CUTS

    def column_block(block):
        return [
            (
                w_qkv_hbm.at[pl.ds(i * step, step), pl.ds(block * width, width)],
                w_qkv.at[pl.ds(i * step, step), pl.ds(block * width, width)],
            )
            for i in range(LOAD_CUTS)
        ]

    groups = [
        [(tiles_hbm, tiles)] + column_block(1),
        column_block(2),
        column_block(0),
        [(cot_hbm, cot)]
        + [
            (w_out_hbm.at[pl.ds(i * step, step), :], w_out.at[pl.ds(i * step, step), :])
            for i in range(LOAD_CUTS)
        ],
        [(offs_hbm, offs_ref)],
    ]
    copies, index = [], 0
    for group in groups:
        made = []
        for source, target in group:
            copy = pltpu.make_async_copy(source, target, sems.at[index])
            copy.start()
            made.append(copy)
            index += 1
        copies.append(made)

    def arrived(group):
        for copy in copies[group]:
            copy.wait()

    arrived(0)
    own = tiles[...]
    k[...] = dot(own, w_qkv[:, width : 2 * width]).astype(BF)
    arrived(1)
    v[...] = dot(own, w_qkv[:, 2 * width :]).astype(BF)
    arrived(2)
    q[...] = dot(own, w_qkv[:, :width]).astype(BF) * jnp.asarray(SCALE, BF)
    arrived(3)
    g[...] = dot(cot[...], w_out[...], NT).astype(BF)
    arrived(4)
    entry = iota((2 * z.sel, z.rows), 0)
    column = iota((2 * z.sel, z.rows), 1)
    second = entry >= z.sel
    for pair in range(z.pairs):
        lanes = slice(pair * PAIR, (pair + 1) * PAIR)
        off_mid = jnp.where(second, offs_ref[0, 2 * pair + 1], offs_ref[0, 2 * pair])
        off_far = jnp.where(second, offs_ref[1, 2 * pair + 1], offs_ref[1, 2 * pair])
        target = chosen_row(z, entry % z.sel, off_mid, off_far)
        take = (column == target).astype(F32).astype(BF)
        every = jnp.concatenate([k[:, lanes], v[:, lanes], q[:, lanes], g[:, lanes]], axis=1)
        both = dot(take, every)
        picked = jnp.where(low_half((z.sel, 4 * PAIR)), both[: z.sel], both[z.sel :]).astype(BF)
        far_part = jnp.where(
            low_half((z.far, 4 * PAIR)),
            both[z.mid : z.mid + z.far],
            both[z.sel + z.mid : z.sel + z.mid + z.far],
        ).astype(BF)
        for part in range(4):
            to = slice(part * width + pair * PAIR, part * width + (pair + 1) * PAIR)
            sel[:, to] = picked[:, part * PAIR : (part + 1) * PAIR]
            mid[:, to] = picked[: z.mid, part * PAIR : (part + 1) * PAIR]
            far[:, to] = far_part[:, part * PAIR : (part + 1) * PAIR]


def near_kernel(
    z, pad_ref, q, k, v, g, tiles, order, order_q, mixed, stats, turned, turned_out
):
    own = lax.axis_index("ctx")
    limit = z.rows * z.devs - pad_ref[0] - own * z.rows
    valid = iota((1, z.rows), 1) < limit
    lane = iota((z.rows, LANES), 1)
    both = jnp.zeros((z.rows, LANES), F32)
    for pair in range(z.pairs):
        lanes = slice(pair * PAIR, (pair + 1) * PAIR)
        query = q[:, lanes]
        grad = g[:, lanes].astype(F32)
        keys = halves(k[:, lanes])
        values = halves(v[:, lanes])
        total = None
        for side in range(2):
            head = 2 * pair + side
            scores = jnp.where(valid, dot(query, keys[side], NT), -jnp.inf)
            peak = jnp.max(scores, axis=1, keepdims=True)
            powers = jnp.exp(scores - peak)
            summed = jnp.sum(powers, axis=1, keepdims=True)
            part = dot(powers.astype(BF), values[side]) * (1.0 / summed)
            total = part if total is None else total + part
            both = jnp.where(lane == head, peak + jnp.log(summed), both)
            meets = jnp.sum(grad * part, axis=1, keepdims=True)
            both = jnp.where(lane == SECOND + head, meets, both)
        mixed[:, lanes] = total
    stats[...] = both
    for which, source_rows in enumerate((order, order_q)):
        for part, target in enumerate((turned, turned_out)):
            source = source_rows[part * z.half : (part + 1) * z.half, :]
            place = (iota((z.half, z.width), 1) == source).astype(F32).astype(BF)
            result = dot(place, tiles[...], NT).astype(BF)
            target[which * z.half : (which + 1) * z.half, :] = result


def of_level(level, refs, lanes):
    return jnp.concatenate([ref[:, lanes] for ref in refs[level]], axis=0)


def part_lanes(z, part, pair):
    return slice(part * z.width + pair * PAIR, part * z.width + (pair + 1) * PAIR)


def own_scores(z, limit, offs_ref, sel, refs):
    own = lax.axis_index("ctx")
    scores, places = [], []
    for level, (start, stop) in enumerate(level_parts(z)):
        place = gathered_place(z, own, level)
        for pair in range(z.pairs):
            query = sel[start:stop, part_lanes(z, 2, pair)]
            keys = halves(of_level(level, refs, part_lanes(z, 0, pair)))
            for side in range(2):
                valid = place + offs_ref[level, 2 * pair + side] < limit
                scores.append(jnp.where(valid, dot(query, keys[side], NT), -jnp.inf))
                places.append((level, 2 * pair + side, start, stop))
    spots, at = [], 0
    for level, head, start, stop in places:
        spots.append((level, head, at, at + stop - start))
        at += stop - start
    return jnp.concatenate(scores, axis=0), spots


def to_lanes(z, spots, columns):
    parts = []
    for level, (start, stop) in enumerate(level_parts(z)):
        lane = iota((stop - start, LANES), 1)
        part = jnp.zeros((stop - start, LANES), F32)
        for found, head, first, last in spots:
            if found == level:
                for shift, column in columns:
                    part = jnp.where(lane == shift + head, column[first:last], part)
        parts.append(part)
    parts.append(jnp.zeros((z.sel - level_parts(z)[1][1], LANES), F32))
    return jnp.concatenate(parts, axis=0)


def from_lanes(spots, array, shift):
    return lambda z: jnp.concatenate(
        [
            array[level_parts(z)[level][0] : level_parts(z)[level][1], shift + head : shift + head + 1]
            for level, head, _, _ in spots
        ],
        axis=0,
    )


def spot_of(spots, level, head):
    return next((first, last) for found, at, first, last in spots if (found, at) == (level, head))


def join_kernel(
    z, offs_ref, pad_ref, sel, mid_0, mid_1, far_0, far_1, near_stats, stats, picked, raw, held
):
    refs = ((mid_0, mid_1), (far_0, far_1))
    scores, spots = own_scores(z, z.rows * z.devs - pad_ref[0], offs_ref, sel, refs)
    peak = jnp.max(scores, axis=1, keepdims=True)
    powers = jnp.exp(scores - peak)
    summed = jnp.sum(powers, axis=1, keepdims=True)
    lse = peak + jnp.log(summed)
    scale = 1.0 / summed
    powers = powers.astype(BF)
    products = []
    tail = jnp.zeros((z.sel - level_parts(z)[1][1], PAIR), F32)
    for pair in range(z.pairs):
        totals = []
        for level, (start, stop) in enumerate(level_parts(z)):
            values = halves(of_level(level, refs, part_lanes(z, 1, pair)))
            parts = []
            for side in range(2):
                at, to = spot_of(spots, level, 2 * pair + side)
                parts.append(dot(powers[at:to], values[side]) * scale[at:to])
            totals.append(parts[0] + parts[1])
            grad = sel[start:stop, part_lanes(z, 3, pair)].astype(F32)
            products.append((level, pair, [grad * part for part in parts]))
        held[:, pair * PAIR : (pair + 1) * PAIR] = jnp.concatenate(totals + [tail], axis=0)
    products.sort(key=lambda entry: entry[:2])
    stacked = jnp.concatenate([part for _, _, both in products for part in both], axis=0)
    meets = jnp.sum(stacked, axis=1, keepdims=True)
    sel_both = to_lanes(z, spots, ((0, lse), (SECOND, meets)))
    raw[...] = sel_both
    masks = stat_masks(z, offs_ref)
    near = near_stats[...]
    mid, far = spread_stats(z, masks, sel_both)
    top = jnp.maximum(near, jnp.maximum(mid, far))
    total_lse = top + jnp.log(jnp.exp(near - top) + jnp.exp(mid - top) + jnp.exp(far - top))
    delta = sum(
        pltpu.roll(jnp.exp(value - total_lse), SECOND, 1) * value
        for value in (
            near,
            jnp.where(masks[0], mid, -LARGE),
            jnp.where(masks[1], far, -LARGE),
        )
    )
    both = jnp.where(iota((z.rows, LANES), 1) < SECOND, total_lse, delta)
    stats[...] = both
    picked[...] = pick_stats(z, masks, both)


def output_kernel(
    z, offs_ref, near_stats, stats, picked, raw, mixed, held, tiles, w_out, order,
    rows_out, turned, turned_out, attn,
):
    near_share = jnp.exp(near_stats[...] - stats[...])
    share = jnp.exp(raw[...] - picked[...])
    for pair in range(z.pairs):
        lanes = slice(pair * PAIR, (pair + 1) * PAIR)
        near = by_head(
            near_share[:, 2 * pair : 2 * pair + 1],
            near_share[:, 2 * pair + 1 : 2 * pair + 2],
            z.rows,
        )
        own = by_head(share[:, 2 * pair : 2 * pair + 1], share[:, 2 * pair + 1 : 2 * pair + 2], z.sel)
        combined = near * mixed[:, lanes] + spread(z, offs_ref, pair, own * held[:, lanes])
        attn[:, lanes] = combined.astype(BF)
    rows_out[...] = (tiles[...].astype(F32) + dot(attn[...], w_out[...])).astype(BF)
    for part, target in enumerate((turned, turned_out)):
        source = order[part * z.half : (part + 1) * z.half, :]
        place = (iota((z.half, z.width), 1) == source).astype(F32).astype(BF)
        target[...] = dot(place, attn[...], NT).astype(BF)


def near_grads_kernel(
    z, offs_ref, pad_ref, q, k, v, g, stats, sel, mid_0, mid_1, far_0, far_1, picked,
    dq, dk, dv, dq_sel,
):
    own = lax.axis_index("ctx")
    limit = z.rows * z.devs - pad_ref[0]
    refs = ((mid_0, mid_1), (far_0, far_1))
    scores, spots = own_scores(z, limit, offs_ref, sel, refs)
    probs = jnp.exp(scores - from_lanes(spots, picked, 0)(z))
    grad_probs = []
    for level, (start, stop) in enumerate(level_parts(z)):
        for pair in range(z.pairs):
            grad = sel[start:stop, part_lanes(z, 3, pair)]
            values = halves(of_level(level, refs, part_lanes(z, 1, pair)))
            grad_probs += [dot(grad, values[side], NT) for side in range(2)]
    grad_probs = jnp.concatenate(grad_probs, axis=0) - from_lanes(spots, picked, SECOND)(z)
    grad_scores = (probs * grad_probs).astype(BF)
    tail = jnp.zeros((z.sel - level_parts(z)[1][1], PAIR), F32)
    for pair in range(z.pairs):
        sums = []
        for level in range(2):
            keys = halves(of_level(level, refs, part_lanes(z, 0, pair)))
            at, to = spot_of(spots, level, 2 * pair)
            low = dot(grad_scores[at:to], keys[0])
            at, to = spot_of(spots, level, 2 * pair + 1)
            sums.append(low + dot(grad_scores[at:to], keys[1]))
        dq_sel[:, pair * PAIR : (pair + 1) * PAIR] = jnp.concatenate(sums + [tail], axis=0)
    valid_near = iota((z.rows, 1), 0) < limit - own * z.rows
    across = jnp.transpose(stats[...])
    for pair in range(z.pairs):
        lanes = slice(pair * PAIR, (pair + 1) * PAIR)
        query, grad = q[:, lanes], g[:, lanes]
        queries, grads = halves(query), halves(grad)
        keys, values = halves(k[:, lanes]), halves(v[:, lanes])
        sum_q = sum_k = sum_v = None
        for side in range(2):
            head = 2 * pair + side
            scores = jnp.where(valid_near, dot(keys[side], query, NT), -jnp.inf)
            probs = jnp.exp(scores - across[head : head + 1, :])
            grad_probs = dot(values[side], grad, NT)
            grad_scores = probs * (grad_probs - across[SECOND + head : SECOND + head + 1, :])
            grad_scores = grad_scores.astype(BF)
            part_k = dot(grad_scores, queries[side])
            part_v = dot(probs.astype(BF), grads[side])
            part_q = dot(grad_scores, keys[side], TN)
            if side == 0:
                sum_q, sum_k, sum_v = part_q, part_k, part_v
            else:
                sum_q, sum_k, sum_v = sum_q + part_q, sum_k + part_k, sum_v + part_v
        dk[:, lanes] = sum_k
        dv[:, lanes] = sum_v
        dq[:, lanes] = (SCALE * (sum_q + spread(z, offs_ref, pair, dq_sel[:, lanes]))).astype(BF)


def key_grads_kernel(
    z, offs_ref, pad_ref, sel, mid_0, mid_1, far_0, far_1, stats_0, stats_1, dk_near, dv_near, dk, dv
):
    own = lax.axis_index("ctx")
    limit = z.rows * z.devs - pad_ref[0] - own * z.rows
    parts = level_parts(z)
    refs = ((mid_0, mid_1), (far_0, far_1))
    stat_refs = (stats_0, stats_1)
    first_part = (2, 0)
    tail = jnp.zeros((z.sel - parts[1][1], PAIR), F32)
    probs, grad_scores = {}, {}
    for level, (start, stop) in enumerate(parts):
        across = jnp.transpose(jnp.concatenate([ref[level * 4 * z.mid : (level + 1) * 4 * z.mid, :] for ref in stat_refs], axis=0))
        entry = iota((stop - start, 1), 0) + start
        for pair in range(z.pairs):
            keys = sel[start:stop, part_lanes(z, 0, pair)]
            values = sel[start:stop, part_lanes(z, 1, pair)]
            queries = halves(of_level(level, refs, part_lanes(z, first_part[level], pair)))
            grads = halves(of_level(level, refs, part_lanes(z, first_part[level] + 1, pair)))
            for side in range(2):
                head = 2 * pair + side
                at = chosen_row(z, entry, offs_ref[0, head], offs_ref[1, head])
                valid = (at >= 0) & (at < limit)
                scores = jnp.where(valid, dot(keys, queries[side], NT), -jnp.inf)
                exps = jnp.exp(scores - across[head : head + 1, :])
                grad_probs = dot(values, grads[side], NT)
                grad_probs = grad_probs - across[SECOND + head : SECOND + head + 1, :]
                probs[level, head] = exps.astype(BF)
                grad_scores[level, head] = (exps * grad_probs).astype(BF)
    sums_k, sums_v = {}, {}
    for pair in range(z.pairs):
        both_k, both_v = [], []
        for level in range(2):
            queries = halves(of_level(level, refs, part_lanes(z, first_part[level], pair)))
            grads = halves(of_level(level, refs, part_lanes(z, first_part[level] + 1, pair)))
            low, high = 2 * pair, 2 * pair + 1
            both_k.append(
                dot(grad_scores[level, low], queries[0]) + dot(grad_scores[level, high], queries[1])
            )
            both_v.append(dot(probs[level, low], grads[0]) + dot(probs[level, high], grads[1]))
        sums_k[pair] = jnp.concatenate(both_k + [tail], axis=0)
        sums_v[pair] = jnp.concatenate(both_v + [tail], axis=0)
    for pair in range(z.pairs):
        lanes = slice(pair * PAIR, (pair + 1) * PAIR)
        both = jnp.concatenate([sums_k[pair], sums_v[pair]], axis=1)
        moved = spread(z, offs_ref, pair, both)
        dk[:, lanes] = (dk_near[:, lanes] + moved[:, :PAIR]).astype(BF)
        dv[:, lanes] = (dv_near[:, lanes] + moved[:, PAIR:]).astype(BF)


def weights_kernel(start, left, left_other, right, right_other, out):
    rows = slice(start, start + out.shape[0])
    out[...] = (dot(left[rows, :], right[...]) + dot(left_other[rows, :], right_other[...])).astype(BF)


def late_weights_kernel(z, turned, turned_other, dk, dv, dk_other, dv_other, out):
    width = z.width
    left, other = turned[: z.half, :], turned_other[: z.half, :]
    out[:, :width] = (dot(left, dk[...]) + dot(other, dk_other[...])).astype(BF)
    out[:, width:] = (dot(left, dv[...]) + dot(other, dv_other[...])).astype(BF)


def tiles_kernel(z, dq, dk, dv, w_qkv, out):
    width = z.width
    out[...] = (
        dot(dq[...], w_qkv[:, :width], NT)
        + dot(dk[...], w_qkv[:, width : 2 * width], NT)
        + dot(dv[...], w_qkv[:, 2 * width :], NT)
    ).astype(BF)


def call(kernel, outs, flops, scratch=(), smem=0, spaces=None, vmem=VMEM_BYTES):
    def run(*args):
        moved = sum(int(np.prod(a.shape)) * a.dtype.itemsize for a in args)
        moved += sum(int(np.prod(s)) * jnp.dtype(t).itemsize for s, t in outs)
        specs = [
            pl.BlockSpec(memory_space=spaces or (pltpu.SMEM if i < smem else pltpu.VMEM))
            for i in range(len(args))
        ]
        return pl.pallas_call(
            kernel,
            out_shape=tuple(jax.ShapeDtypeStruct(s, t) for s, t in outs),
            in_specs=specs,
            out_specs=tuple(pl.BlockSpec(memory_space=pltpu.VMEM) for _ in outs),
            scratch_shapes=list(scratch),
            compiler_params=pltpu.CompilerParams(vmem_limit_bytes=vmem),
            cost_estimate=pl.CostEstimate(
                flops=int(flops), bytes_accessed=int(moved), transcendentals=0
            ),
        )(*args)

    return run


def swap(value, mask, dev_count):
    return lax.ppermute(value, "ctx", [(d, d ^ mask) for d in range(dev_count)])


def upper_steps(dev_count):
    steps, base = [], GROUP
    while base < dev_count:
        count = 4 if base * 4 <= dev_count else 2
        steps.append((base, count))
        base *= count
    return steps


PLANE = (2, 4)


def tied(parts, first):
    return list(lax.optimization_barrier((*parts, *first))[: len(parts)]) if first else list(parts)


def step_parts(value, step, dev_count, first=()):
    base, count = step
    return tied(
        [value] + [swap(value, base * i, dev_count) for i in range(1, count)], first
    )


def doubled(value, masks, dev_count, first=()):
    for i, mask in enumerate(masks):
        parts = tied([value, swap(value, mask, dev_count)], first if i == len(masks) - 1 else ())
        value = jnp.concatenate(parts, axis=0)
    return value


def halved(value, masks, dev_count, firsts=()):
    for i, mask in enumerate(masks):
        size = value.shape[0] // 2
        first = firsts[i] if i < len(firsts) else ()
        parts = tied([value[:size], swap(value[size:], mask, dev_count)], first)
        value = parts[0].astype(F32) + parts[1].astype(F32)
        value = value if i == len(masks) - 1 else value.astype(BF)
    return value


def reduce_step(value, step, dev_count, dtype, first=()):
    base, count = step
    size = value.shape[0] // count
    parts = [value[:size]] + [
        swap(value[i * size : (i + 1) * size], base * i, dev_count) for i in range(1, count)
    ]
    return sum(part.astype(F32) for part in tied(parts, first)).astype(dtype)


def reduce_all(value, steps, dev_count):
    for i, step in enumerate(steps):
        value = reduce_step(value, step, dev_count, F32 if i == len(steps) - 1 else BF)
    return value


def strip_order(z, own, masks):
    digits = np.meshgrid(*[np.arange(2) for _ in masks], np.arange(z.strip), indexing="ij")
    moved = sum(digit * mask for digit, mask in zip(digits, masks)).reshape(-1, 1)
    return (own ^ moved.astype(np.int32)) * z.strip + digits[-1].reshape(-1, 1).astype(np.int32)


def after(value, *others):
    return lax.optimization_barrier((value, *others))[0]


def per_device(tiles, w_qkv, w_out, cotangent, offsets, pad_count):
    n = lax.axis_size("ctx")
    z = Sizes(tiles.shape[0], tiles.shape[1], n)
    own = lax.axis_index("ctx")
    rows, width = z.rows, z.width
    masks = [mask for mask in (2**i for i in range(30)) if GROUP <= mask < n]
    order = strip_order(z, own, [1, 4, 2] + masks[::-1])
    order_q = strip_order(z, own, [1] + masks + [2, 4])
    order_out = strip_order(z, own, [1, 2, 4] + masks)
    base_flops = 2 * rows * rows * width

    q, k, v, g, sel, mid, far = call(
        functools.partial(project_kernel, z),
        [((rows, width), BF)] * 4 + [((count, 4 * width), BF) for count in (z.sel, z.mid, z.far)],
        2 * rows * width * 4 * width,
        scratch=[
            pltpu.SMEM(offsets.shape, jnp.int32),
            pltpu.VMEM(tiles.shape, BF),
            pltpu.VMEM(w_qkv.shape, BF),
            pltpu.VMEM(cotangent.shape, BF),
            pltpu.VMEM(w_out.shape, BF),
            pltpu.SemaphoreType.DMA((4 * LOAD_CUTS + 3,)),
        ],
        spaces=pltpu.HBM,
        vmem=PROJECT_VMEM_BYTES,
    )(offsets, tiles, w_qkv, cotangent, w_out)

    far_up = far
    for step in upper_steps(n):
        far_up = jnp.concatenate(step_parts(far_up, step, n), axis=0)
    mid_parts = step_parts(mid, PLANE, n)
    mixed, near_stats, turned, turned_out = call(
        functools.partial(near_kernel, z),
        [
            ((rows, width), F32),
            ((rows, LANES), F32),
            ((width, rows), BF),
            ((width, rows), BF),
        ],
        8 * base_flops,
        smem=1,
    )(pad_count, after(q, far_up), k, v, g, tiles, order, order_q)
    mid_0 = jnp.concatenate(mid_parts, axis=0)
    mid_1 = swap(mid_0, 1, n)
    far_parts = step_parts(far_up, PLANE, n, (near_stats,))
    far_0 = jnp.concatenate([part[:, : 2 * width] for part in far_parts], axis=0)
    far_1 = swap(far_0, 1, n)
    far_qg_0 = jnp.concatenate([part[:, 2 * width :] for part in far_parts], axis=0)
    far_qg_1 = swap(far_qg_0, 1, n)

    stats, picked, raw, held = call(
        functools.partial(join_kernel, z),
        [((rows, LANES), F32), ((z.sel, LANES), F32), ((z.sel, LANES), F32), ((z.sel, width), F32)],
        3 * base_flops,
        smem=2,
    )(offsets, pad_count, sel, mid_0, mid_1, far_0, far_1, near_stats)

    out_rows, attn_turned, attn_turned_out = call(
        functools.partial(output_kernel, z),
        [((rows, width), BF), ((z.half, rows), BF), ((z.half, rows), BF)],
        6 * rows * width * width,
        scratch=[pltpu.VMEM((rows, width), BF)],
        smem=1,
    )(offsets, near_stats, stats, picked, raw, mixed, held, tiles, w_out, order_out)
    attn_other = swap(attn_turned_out, 1, n)
    turned_other = swap(after(turned_out, picked), 1, n)
    cot_other = swap(after(cotangent, picked), 1, n)

    stats_up = picked[z.mid : z.mid + z.far]
    for i, step in enumerate(upper_steps(n)):
        parts = step_parts(stats_up, step, n, (out_rows,) if i == 0 else ())
        stats_up = jnp.concatenate(parts, axis=0)
    def weights(start, *args):
        kernel = functools.partial(weights_kernel, start)
        return call(kernel, [((z.half, width), BF)], 4 * rows * width * width)(*args)[0]

    wout_half = weights(0, attn_turned, attn_other, cotangent, after(cot_other, stats_up))

    dq, dk_near, dv_near = call(
        functools.partial(near_grads_kernel, z),
        [((rows, width), BF), ((rows, width), F32), ((rows, width), F32)],
        8 * base_flops,
        scratch=[pltpu.VMEM((z.sel, width), F32)],
        smem=2,
    )(
        offsets, pad_count, after(q, wout_half), k, v, g, stats, sel, mid_0, mid_1, far_0, far_1, picked
    )
    dq_other = swap(dq, 1, n)
    stats_plane = doubled(jnp.concatenate([picked[: z.mid], stats_up], axis=1), (2, 4), n, (dk_near,))
    stats_0 = jnp.concatenate([stats_plane[:, :LANES], stats_plane[:, LANES:]], axis=0)
    stats_1 = swap(stats_0, 1, n)
    early_half = weights(z.half, turned, turned_other, dq, dq_other)

    dk, dv = call(
        functools.partial(key_grads_kernel, z),
        [((rows, width), BF), ((rows, width), BF)],
        3 * base_flops,
        smem=2,
    )(
        offsets, pad_count, sel, mid_0, mid_1, far_qg_0, far_qg_1, stats_0, stats_1,
        after(dk_near, early_half), dv_near,
    )
    dk_other = swap(dk, 1, n)
    dv_other = swap(dv, 1, n)
    (late_half,) = call(
        functools.partial(late_weights_kernel, z),
        [((z.half, 2 * width), BF)],
        4 * rows * width * width,
    )(turned, turned_other, dk, dv, dk_other, dv_other)
    (grad_tiles,) = call(
        functools.partial(tiles_kernel, z), [((rows, width), BF)], 6 * rows * width * width
    )(after(dq, late_half), dk, dv, w_qkv)
    late = reduce_step(late_half, PLANE, n, BF)
    early = halved(early_half, masks + [2, 4], n, ((grad_tiles,),))
    grad_wout = halved(wout_half, [2, 4] + masks, n, ((dq,), (dk,), (grad_tiles,)))
    late = reduce_all(late, upper_steps(n)[::-1], n)
    grad_wqkv = jnp.concatenate([early, late], axis=1)
    return out_rows, grad_tiles, grad_wqkv, grad_wout


def solution(mesh):
    return jax.shard_map(
        per_device,
        mesh=mesh,
        in_specs=(P("ctx", None), P(), P(), P("ctx", None), P(), P()),
        out_specs=(P("ctx", None), P("ctx", None), P("ctx", None), P("ctx", None)),
        check_vma=False,
    )
```

```python
import functools

import jax
import jax.numpy as jnp
import numpy as np
from jax import lax
from jax.experimental import pallas as pl
from jax.experimental.pallas import tpu as pltpu
from jax.sharding import PartitionSpec as P

HEAD_DIM = 64
GROUP = 8
PAIR = 2 * HEAD_DIM
LANES = 128
SECOND = 16
SCALE = 0.125
BF = jnp.bfloat16
F32 = jnp.float32
NT = (((1,), (1,)), ((), ()))
NN = (((1,), (0,)), ((), ()))
TN = (((0,), (0,)), ((), ()))
LARGE = 1e30
LOAD_CUTS = 4
VMEM_BYTES = 40 * 1024 * 1024
PROJECT_VMEM_BYTES = 57 * 1024 * 1024


def dot(a, b, dims=NN):
    return lax.dot_general(a, b, dims, preferred_element_type=F32)


def dot_exact(a, b):
    return lax.dot_general(a, b, NN, preferred_element_type=F32, precision=lax.Precision.HIGHEST)


def iota(shape, dim):
    return lax.broadcasted_iota(jnp.int32, shape, dim)


def low_half(shape):
    return iota(shape, len(shape) - 1) % PAIR < HEAD_DIM


def halves(x):
    low = low_half(x.shape)
    zero = jnp.zeros((), x.dtype)
    return jnp.where(low, x, zero), jnp.where(low, zero, x)


def by_head(first, second, rows):
    return jnp.where(low_half((rows, PAIR)), first, second)


class Sizes:
    def __init__(self, rows, width, dev_count):
        self.rows = rows
        self.width = width
        self.devs = dev_count
        self.heads = width // HEAD_DIM
        self.pairs = self.heads // 2
        self.mid = rows // GROUP
        self.far = rows // dev_count
        self.sel = 2 * self.mid
        self.far_held = -(-self.far // 16) * 16
        self.upper = dev_count // GROUP
        self.strip = width // dev_count
        self.half = width // 2


def chosen_row(z, index, off_mid, off_far):
    row = jnp.where(index < z.mid, index * GROUP + off_mid, (index - z.mid) * z.devs + off_far)
    return jnp.where(index < z.mid + z.far, row, -1)


def spread(z, offs_ref, pair, picked):
    lane = iota((1, 4 * z.sel), 1)
    second = (lane // z.sel) % 2 == 1
    off_mid = jnp.where(second, offs_ref[0, 2 * pair + 1], offs_ref[0, 2 * pair])
    off_far = jnp.where(second, offs_ref[1, 2 * pair + 1], offs_ref[1, 2 * pair])
    target = chosen_row(z, lane % z.sel, off_mid, off_far)
    place = (iota((z.rows, 4 * z.sel), 0) == target).astype(F32).astype(BF)
    high = picked.astype(BF)
    rest = (picked - high.astype(F32)).astype(BF)
    first_high, second_high = halves(high)
    first_rest, second_rest = halves(rest)
    stacked = jnp.concatenate([first_high, second_high, first_rest, second_rest], axis=0)
    return dot(place, stacked)


def lane_offsets(z, offs_ref):
    lane = iota((1, LANES), 1)
    off_mid = jnp.full((1, LANES), -1, jnp.int32)
    off_far = jnp.full((1, LANES), -1, jnp.int32)
    for head in range(z.heads):
        here = (lane == head) | (lane == SECOND + head)
        off_mid = jnp.where(here, offs_ref[0, head], off_mid)
        off_far = jnp.where(here, offs_ref[1, head], off_far)
    return off_mid, off_far


def stat_masks(z, offs_ref):
    off_mid, off_far = lane_offsets(z, offs_ref)
    row = iota((z.rows, LANES), 0)
    return row % GROUP == off_mid, row % z.devs == off_far


def pick_stats(z, masks, stats):
    entry = iota((z.sel, z.rows), 0)
    row = iota((z.sel, z.rows), 1)
    take_mid = ((entry < z.mid) & (row // GROUP == entry)).astype(F32)
    take_far = (row // z.devs == entry - z.mid).astype(F32)
    return dot_exact(take_mid, jnp.where(masks[0], stats, 0.0)) + dot_exact(
        take_far, jnp.where(masks[1], stats, 0.0)
    )


def spread_stats(z, masks, picked):
    row = iota((z.rows, z.sel), 0)
    entry = iota((z.rows, z.sel), 1)
    give_mid = ((entry < z.mid) & (row // GROUP == entry)).astype(F32)
    give_far = (row // z.devs == entry - z.mid).astype(F32)
    fill = jnp.where(iota((z.rows, LANES), 1) < SECOND, -jnp.inf, 0.0)
    return (
        jnp.where(masks[0], dot_exact(give_mid, picked), fill),
        jnp.where(masks[1], dot_exact(give_far, picked), fill),
    )


def gathered_place(z, own, level):
    index = iota((1, z.rows), 1)
    core = index // (4 * z.mid)
    plane = (index // z.mid) % 4
    inner = index % z.mid
    if level == 0:
        return (own ^ (core + 2 * plane)) * z.rows + inner * GROUP
    dev = own ^ (core + 2 * plane + GROUP * (inner // z.far))
    return dev * z.rows + (inner % z.far) * z.devs


def level_parts(z):
    return ((0, z.mid), (z.mid, z.mid + z.far_held))


def project_kernel(
    z, offs_hbm, tiles_hbm, w_qkv_hbm, cot_hbm, w_out_hbm,
    q_hbm, k_hbm, v_hbm, g_hbm, sel, mid_kv, mid_qg, far,
    offs_ref, tiles, w_qkv, cot, w_out, q, k, v, g, sems, out_sems,
):
    width = z.width
    step = width // LOAD_CUTS

    def column_block(block):
        return [
            (
                w_qkv_hbm.at[pl.ds(i * step, step), pl.ds(block * width, width)],
                w_qkv.at[pl.ds(i * step, step), pl.ds(block * width, width)],
            )
            for i in range(LOAD_CUTS)
        ]

    groups = [
        [(tiles_hbm, tiles)] + column_block(1),
        column_block(2),
        column_block(0),
        [(cot_hbm, cot)]
        + [
            (w_out_hbm.at[pl.ds(i * step, step), :], w_out.at[pl.ds(i * step, step), :])
            for i in range(LOAD_CUTS)
        ],
        [(offs_hbm, offs_ref)],
    ]
    copies, index = [], 0
    for group in groups:
        made = []
        for source, target in group:
            copy = pltpu.make_async_copy(source, target, sems.at[index])
            copy.start()
            made.append(copy)
            index += 1
        copies.append(made)

    def arrived(group):
        for copy in copies[group]:
            copy.wait()

    leaving = []

    def leave(source, target):
        copy = pltpu.make_async_copy(source, target, out_sems.at[len(leaving)])
        copy.start()
        leaving.append(copy)

    arrived(0)
    own = tiles[...]
    k[...] = dot(own, w_qkv[:, width : 2 * width]).astype(BF)
    leave(k, k_hbm)
    arrived(1)
    v[...] = dot(own, w_qkv[:, 2 * width :]).astype(BF)
    leave(v, v_hbm)
    arrived(2)
    q[...] = dot(own, w_qkv[:, :width]).astype(BF) * jnp.asarray(SCALE, BF)
    leave(q, q_hbm)
    arrived(3)
    g[...] = dot(cot[...], w_out[...], NT).astype(BF)
    leave(g, g_hbm)
    arrived(4)
    entry = iota((2 * z.sel, z.rows), 0)
    column = iota((2 * z.sel, z.rows), 1)
    second = entry >= z.sel
    for pair in range(z.pairs):
        lanes = slice(pair * PAIR, (pair + 1) * PAIR)
        off_mid = jnp.where(second, offs_ref[0, 2 * pair + 1], offs_ref[0, 2 * pair])
        off_far = jnp.where(second, offs_ref[1, 2 * pair + 1], offs_ref[1, 2 * pair])
        target = chosen_row(z, entry % z.sel, off_mid, off_far)
        take = (column == target).astype(F32).astype(BF)
        every = jnp.concatenate([k[:, lanes], v[:, lanes], q[:, lanes], g[:, lanes]], axis=1)
        both = dot(take, every)
        picked = jnp.where(low_half((z.sel, 4 * PAIR)), both[: z.sel], both[z.sel :]).astype(BF)
        far_part = jnp.where(
            low_half((z.far, 4 * PAIR)),
            both[z.mid : z.mid + z.far],
            both[z.sel + z.mid : z.sel + z.mid + z.far],
        ).astype(BF)
        for part in range(4):
            to = slice(part * width + pair * PAIR, part * width + (pair + 1) * PAIR)
            sel[:, to] = picked[:, part * PAIR : (part + 1) * PAIR]
            near_to = slice(to.start % (2 * width), to.start % (2 * width) + PAIR)
            mid = mid_kv if part < 2 else mid_qg
            mid[:, near_to] = picked[: z.mid, part * PAIR : (part + 1) * PAIR]
            far[:, to] = far_part[:, part * PAIR : (part + 1) * PAIR]
    for copy in leaving:
        copy.wait()


def near_kernel(
    z, pad_ref, q, k, v, g, tiles, order, order_q, mixed, stats, turned, turned_out
):
    own = lax.axis_index("ctx")
    limit = z.rows * z.devs - pad_ref[0] - own * z.rows
    valid = iota((1, z.rows), 1) < limit
    lane = iota((z.rows, LANES), 1)
    both = jnp.zeros((z.rows, LANES), F32)
    for pair in range(z.pairs):
        lanes = slice(pair * PAIR, (pair + 1) * PAIR)
        query = q[:, lanes]
        grad = g[:, lanes].astype(F32)
        keys = halves(k[:, lanes])
        values = halves(v[:, lanes])
        total = None
        for side in range(2):
            head = 2 * pair + side
            scores = jnp.where(valid, dot(query, keys[side], NT), -jnp.inf)
            peak = jnp.max(scores, axis=1, keepdims=True)
            powers = jnp.exp(scores - peak)
            summed = jnp.sum(powers, axis=1, keepdims=True)
            part = dot(powers.astype(BF), values[side]) * (1.0 / summed)
            total = part if total is None else total + part
            both = jnp.where(lane == head, peak + jnp.log(summed), both)
            meets = jnp.sum(grad * part, axis=1, keepdims=True)
            both = jnp.where(lane == SECOND + head, meets, both)
        mixed[:, lanes] = total
    stats[...] = both
    for which, source_rows in enumerate((order, order_q)):
        for part, target in enumerate((turned, turned_out)):
            source = source_rows[part * z.half : (part + 1) * z.half, :]
            place = (iota((z.half, z.width), 1) == source).astype(F32).astype(BF)
            result = dot(place, tiles[...], NT).astype(BF)
            target[which * z.half : (which + 1) * z.half, :] = result


def of_level(level, refs, lanes):
    return jnp.concatenate([ref[:, lanes] for ref in refs[level]], axis=0)


def part_lanes(z, part, pair):
    return slice(part * z.width + pair * PAIR, part * z.width + (pair + 1) * PAIR)


def own_scores(z, limit, offs_ref, sel, refs):
    own = lax.axis_index("ctx")
    scores, places = [], []
    for level, (start, stop) in enumerate(level_parts(z)):
        place = gathered_place(z, own, level)
        for pair in range(z.pairs):
            query = sel[start:stop, part_lanes(z, 2, pair)]
            keys = halves(of_level(level, refs, part_lanes(z, 0, pair)))
            for side in range(2):
                valid = place + offs_ref[level, 2 * pair + side] < limit
                scores.append(jnp.where(valid, dot(query, keys[side], NT), -jnp.inf))
                places.append((level, 2 * pair + side, start, stop))
    spots, at = [], 0
    for level, head, start, stop in places:
        spots.append((level, head, at, at + stop - start))
        at += stop - start
    return jnp.concatenate(scores, axis=0), spots


def to_lanes(z, spots, columns):
    parts = []
    for level, (start, stop) in enumerate(level_parts(z)):
        lane = iota((stop - start, LANES), 1)
        part = jnp.zeros((stop - start, LANES), F32)
        for found, head, first, last in spots:
            if found == level:
                for shift, column in columns:
                    part = jnp.where(lane == shift + head, column[first:last], part)
        parts.append(part)
    parts.append(jnp.zeros((z.sel - level_parts(z)[1][1], LANES), F32))
    return jnp.concatenate(parts, axis=0)


def from_lanes(spots, array, shift):
    return lambda z: jnp.concatenate(
        [
            array[level_parts(z)[level][0] : level_parts(z)[level][1], shift + head : shift + head + 1]
            for level, head, _, _ in spots
        ],
        axis=0,
    )


def spot_of(spots, level, head):
    return next((first, last) for found, at, first, last in spots if (found, at) == (level, head))


def join_kernel(
    z, offs_ref, pad_ref, sel, mid_0, mid_1, far_0, far_1, near_stats, stats, picked, raw, held
):
    refs = ((mid_0, mid_1), (far_0, far_1))
    scores, spots = own_scores(z, z.rows * z.devs - pad_ref[0], offs_ref, sel, refs)
    peak = jnp.max(scores, axis=1, keepdims=True)
    powers = jnp.exp(scores - peak)
    summed = jnp.sum(powers, axis=1, keepdims=True)
    lse = peak + jnp.log(summed)
    scale = 1.0 / summed
    powers = powers.astype(BF)
    products = []
    tail = jnp.zeros((z.sel - level_parts(z)[1][1], PAIR), F32)
    for pair in range(z.pairs):
        totals = []
        for level, (start, stop) in enumerate(level_parts(z)):
            values = halves(of_level(level, refs, part_lanes(z, 1, pair)))
            parts = []
            for side in range(2):
                at, to = spot_of(spots, level, 2 * pair + side)
                parts.append(dot(powers[at:to], values[side]) * scale[at:to])
            totals.append(parts[0] + parts[1])
            grad = sel[start:stop, part_lanes(z, 3, pair)].astype(F32)
            products.append((level, pair, [grad * part for part in parts]))
        held[:, pair * PAIR : (pair + 1) * PAIR] = jnp.concatenate(totals + [tail], axis=0)
    products.sort(key=lambda entry: entry[:2])
    stacked = jnp.concatenate([part for _, _, both in products for part in both], axis=0)
    meets = jnp.sum(stacked, axis=1, keepdims=True)
    sel_both = to_lanes(z, spots, ((0, lse), (SECOND, meets)))
    raw[...] = sel_both
    masks = stat_masks(z, offs_ref)
    near = near_stats[...]
    mid, far = spread_stats(z, masks, sel_both)
    top = jnp.maximum(near, jnp.maximum(mid, far))
    total_lse = top + jnp.log(jnp.exp(near - top) + jnp.exp(mid - top) + jnp.exp(far - top))
    delta = sum(
        pltpu.roll(jnp.exp(value - total_lse), SECOND, 1) * value
        for value in (
            near,
            jnp.where(masks[0], mid, -LARGE),
            jnp.where(masks[1], far, -LARGE),
        )
    )
    both = jnp.where(iota((z.rows, LANES), 1) < SECOND, total_lse, delta)
    stats[...] = both
    picked[...] = pick_stats(z, masks, both)


def output_kernel(
    z, offs_ref, near_stats, stats, picked, raw, mixed, held, tiles, w_out, order,
    rows_out, turned, turned_out, attn,
):
    near_share = jnp.exp(near_stats[...] - stats[...])
    share = jnp.exp(raw[...] - picked[...])
    for pair in range(z.pairs):
        lanes = slice(pair * PAIR, (pair + 1) * PAIR)
        near = by_head(
            near_share[:, 2 * pair : 2 * pair + 1],
            near_share[:, 2 * pair + 1 : 2 * pair + 2],
            z.rows,
        )
        own = by_head(share[:, 2 * pair : 2 * pair + 1], share[:, 2 * pair + 1 : 2 * pair + 2], z.sel)
        combined = near * mixed[:, lanes] + spread(z, offs_ref, pair, own * held[:, lanes])
        attn[:, lanes] = combined.astype(BF)
    rows_out[...] = (tiles[...].astype(F32) + dot(attn[...], w_out[...])).astype(BF)
    for part, target in enumerate((turned, turned_out)):
        source = order[part * z.half : (part + 1) * z.half, :]
        place = (iota((z.half, z.width), 1) == source).astype(F32).astype(BF)
        target[...] = dot(place, attn[...], NT).astype(BF)


def own_grads_kernel(z, offs_ref, pad_ref, sel, mid_0, mid_1, far_0, far_1, picked, dq_sel):
    limit = z.rows * z.devs - pad_ref[0]
    refs = ((mid_0, mid_1), (far_0, far_1))
    scores, spots = own_scores(z, limit, offs_ref, sel, refs)
    probs = jnp.exp(scores - from_lanes(spots, picked, 0)(z))
    grad_probs = []
    for level, (start, stop) in enumerate(level_parts(z)):
        for pair in range(z.pairs):
            grad = sel[start:stop, part_lanes(z, 3, pair)]
            values = halves(of_level(level, refs, part_lanes(z, 1, pair)))
            grad_probs += [dot(grad, values[side], NT) for side in range(2)]
    grad_probs = jnp.concatenate(grad_probs, axis=0) - from_lanes(spots, picked, SECOND)(z)
    grad_scores = (probs * grad_probs).astype(BF)
    tail = jnp.zeros((z.sel - level_parts(z)[1][1], PAIR), F32)
    for pair in range(z.pairs):
        sums = []
        for level in range(2):
            keys = halves(of_level(level, refs, part_lanes(z, 0, pair)))
            at, to = spot_of(spots, level, 2 * pair)
            low = dot(grad_scores[at:to], keys[0])
            at, to = spot_of(spots, level, 2 * pair + 1)
            sums.append(low + dot(grad_scores[at:to], keys[1]))
        dq_sel[:, pair * PAIR : (pair + 1) * PAIR] = jnp.concatenate(sums + [tail], axis=0)


def near_grads_kernel(z, offs_ref, pad_ref, q, k, v, g, stats, dq_sel, dq, dk, dv):
    own = lax.axis_index("ctx")
    limit = z.rows * z.devs - pad_ref[0]
    valid_near = iota((z.rows, 1), 0) < limit - own * z.rows
    across = jnp.transpose(stats[...])
    for pair in range(z.pairs):
        lanes = slice(pair * PAIR, (pair + 1) * PAIR)
        query, grad = q[:, lanes], g[:, lanes]
        queries, grads = halves(query), halves(grad)
        keys, values = halves(k[:, lanes]), halves(v[:, lanes])
        sum_q = sum_k = sum_v = None
        for side in range(2):
            head = 2 * pair + side
            scores = jnp.where(valid_near, dot(keys[side], query, NT), -jnp.inf)
            probs = jnp.exp(scores - across[head : head + 1, :])
            grad_probs = dot(values[side], grad, NT)
            grad_scores = probs * (grad_probs - across[SECOND + head : SECOND + head + 1, :])
            grad_scores = grad_scores.astype(BF)
            part_k = dot(grad_scores, queries[side])
            part_v = dot(probs.astype(BF), grads[side])
            part_q = dot(grad_scores, keys[side], TN)
            if side == 0:
                sum_q, sum_k, sum_v = part_q, part_k, part_v
            else:
                sum_q, sum_k, sum_v = sum_q + part_q, sum_k + part_k, sum_v + part_v
        dk[:, lanes] = sum_k
        dv[:, lanes] = sum_v
        dq[:, lanes] = (SCALE * (sum_q + spread(z, offs_ref, pair, dq_sel[:, lanes]))).astype(BF)


def key_grads_kernel(
    z, offs_ref, pad_ref, sel, qg_0, qg_1, stats_0, stats_1, dk_near, dv_near, dk, dv
):
    own = lax.axis_index("ctx")
    limit = z.rows * z.devs - pad_ref[0] - own * z.rows
    parts = level_parts(z)
    stat_refs = (stats_0, stats_1)

    def rows_of(level, lanes):
        cuts = [slice(p * z.sel + level * z.mid, p * z.sel + (level + 1) * z.mid) for p in range(4)]
        return jnp.concatenate([ref[cut, lanes] for ref in (qg_0, qg_1) for cut in cuts], axis=0)

    tail = jnp.zeros((z.sel - parts[1][1], PAIR), F32)
    probs, grad_scores = {}, {}
    for level, (start, stop) in enumerate(parts):
        across = jnp.transpose(jnp.concatenate([ref[level * 4 * z.mid : (level + 1) * 4 * z.mid, :] for ref in stat_refs], axis=0))
        entry = iota((stop - start, 1), 0) + start
        for pair in range(z.pairs):
            keys = sel[start:stop, part_lanes(z, 0, pair)]
            values = sel[start:stop, part_lanes(z, 1, pair)]
            queries = halves(rows_of(level, part_lanes(z, 0, pair)))
            grads = halves(rows_of(level, part_lanes(z, 1, pair)))
            for side in range(2):
                head = 2 * pair + side
                at = chosen_row(z, entry, offs_ref[0, head], offs_ref[1, head])
                valid = (at >= 0) & (at < limit)
                scores = jnp.where(valid, dot(keys, queries[side], NT), -jnp.inf)
                exps = jnp.exp(scores - across[head : head + 1, :])
                grad_probs = dot(values, grads[side], NT)
                grad_probs = grad_probs - across[SECOND + head : SECOND + head + 1, :]
                probs[level, head] = exps.astype(BF)
                grad_scores[level, head] = (exps * grad_probs).astype(BF)
    sums_k, sums_v = {}, {}
    for pair in range(z.pairs):
        both_k, both_v = [], []
        for level in range(2):
            queries = halves(rows_of(level, part_lanes(z, 0, pair)))
            grads = halves(rows_of(level, part_lanes(z, 1, pair)))
            low, high = 2 * pair, 2 * pair + 1
            both_k.append(
                dot(grad_scores[level, low], queries[0]) + dot(grad_scores[level, high], queries[1])
            )
            both_v.append(dot(probs[level, low], grads[0]) + dot(probs[level, high], grads[1]))
        sums_k[pair] = jnp.concatenate(both_k + [tail], axis=0)
        sums_v[pair] = jnp.concatenate(both_v + [tail], axis=0)
    for pair in range(z.pairs):
        lanes = slice(pair * PAIR, (pair + 1) * PAIR)
        both = jnp.concatenate([sums_k[pair], sums_v[pair]], axis=1)
        moved = spread(z, offs_ref, pair, both)
        dk[:, lanes] = (dk_near[:, lanes] + moved[:, :PAIR]).astype(BF)
        dv[:, lanes] = (dv_near[:, lanes] + moved[:, PAIR:]).astype(BF)


def weights_kernel(start, left, left_other, right, right_other, out):
    rows = slice(start, start + out.shape[0])
    out[...] = (dot(left[rows, :], right[...]) + dot(left_other[rows, :], right_other[...])).astype(BF)


def late_weights_kernel(z, turned, turned_other, dk, dv, dk_other, dv_other, out):
    width = z.width
    left, other = turned[: z.half, :], turned_other[: z.half, :]
    out[:, :width] = (dot(left, dk[...]) + dot(other, dk_other[...])).astype(BF)
    out[:, width:] = (dot(left, dv[...]) + dot(other, dv_other[...])).astype(BF)


def tiles_kernel(z, dq, dk, dv, w_qkv, out):
    width = z.width
    out[...] = (
        dot(dq[...], w_qkv[:, :width], NT)
        + dot(dk[...], w_qkv[:, width : 2 * width], NT)
        + dot(dv[...], w_qkv[:, 2 * width :], NT)
    ).astype(BF)


def call(kernel, outs, flops, scratch=(), smem=0, spaces=None, vmem=VMEM_BYTES, hbm_outs=0):
    def run(*args):
        moved = sum(int(np.prod(a.shape)) * a.dtype.itemsize for a in args)
        moved += sum(int(np.prod(s)) * jnp.dtype(t).itemsize for s, t in outs)
        specs = [
            pl.BlockSpec(memory_space=spaces or (pltpu.SMEM if i < smem else pltpu.VMEM))
            for i in range(len(args))
        ]
        return pl.pallas_call(
            kernel,
            out_shape=tuple(jax.ShapeDtypeStruct(s, t) for s, t in outs),
            in_specs=specs,
            out_specs=tuple(
                pl.BlockSpec(memory_space=pltpu.HBM if i < hbm_outs else pltpu.VMEM)
                for i in range(len(outs))
            ),
            scratch_shapes=list(scratch),
            compiler_params=pltpu.CompilerParams(vmem_limit_bytes=vmem),
            cost_estimate=pl.CostEstimate(
                flops=int(flops), bytes_accessed=int(moved), transcendentals=0
            ),
        )(*args)

    return run


def swap(value, mask, dev_count):
    return lax.ppermute(value, "ctx", [(d, d ^ mask) for d in range(dev_count)])


def upper_steps(dev_count):
    steps, base = [], GROUP
    while base < dev_count:
        count = 4 if base * 4 <= dev_count else 2
        steps.append((base, count))
        base *= count
    return steps


PLANE = (2, 4)


def tied(parts, first):
    return list(lax.optimization_barrier((*parts, *first))[: len(parts)]) if first else list(parts)


def step_parts(value, step, dev_count, first=()):
    base, count = step
    return tied([value] + [swap(value, base * i, dev_count) for i in range(1, count)], first)


def block_parts(value, step, dev_count):
    base, count = step
    size = value.shape[0] // count
    return [value[:size]] + [
        swap(value[i * size : (i + 1) * size], base * i, dev_count) for i in range(1, count)
    ]


def sum_parts(parts, dtype):
    return sum(part.astype(F32) for part in parts).astype(dtype)


def doubled(value, masks, dev_count, firsts=()):
    for i, mask in enumerate(masks):
        parts = tied([value, swap(value, mask, dev_count)], firsts[i] if i < len(firsts) else ())
        value = jnp.concatenate(parts, axis=0)
    return value


def halved(value, masks, dev_count, firsts=()):
    for i, mask in enumerate(masks):
        size = value.shape[0] // 2
        first = firsts[i] if i < len(firsts) else ()
        parts = tied([value[:size], swap(value[size:], mask, dev_count)], first)
        value = parts[0].astype(F32) + parts[1].astype(F32)
        value = value if i == len(masks) - 1 else value.astype(BF)
    return value


def reduce_all(value, steps, dev_count):
    for i, step in enumerate(steps):
        value = sum_parts(block_parts(value, step, dev_count), F32 if i == len(steps) - 1 else BF)
    return value


def strip_order(z, own, masks):
    digits = np.meshgrid(*[np.arange(2) for _ in masks], np.arange(z.strip), indexing="ij")
    moved = sum(digit * mask for digit, mask in zip(digits, masks)).reshape(-1, 1)
    return (own ^ moved.astype(np.int32)) * z.strip + digits[-1].reshape(-1, 1).astype(np.int32)


def after(value, *others):
    return lax.optimization_barrier((value, *others))[0]


def per_device(tiles, w_qkv, w_out, cotangent, offsets, pad_count):
    n = lax.axis_size("ctx")
    z = Sizes(tiles.shape[0], tiles.shape[1], n)
    own = lax.axis_index("ctx")
    rows, width = z.rows, z.width
    masks = [mask for mask in (2**i for i in range(30)) if GROUP <= mask < n]
    order = strip_order(z, own, [1, 4, 2] + masks[::-1])
    order_q = strip_order(z, own, [1] + masks + [2, 4])
    order_out = strip_order(z, own, [1, 2, 4] + masks)
    base_flops = 2 * rows * rows * width

    q, k, v, g, sel, mid_kv, mid_qg, far = call(
        functools.partial(project_kernel, z),
        [((rows, width), BF)] * 4
        + [((z.sel, 4 * width), BF)]
        + [((z.mid, 2 * width), BF)] * 2
        + [((z.far, 4 * width), BF)],
        2 * rows * width * 4 * width,
        scratch=[
            pltpu.SMEM(offsets.shape, jnp.int32),
            pltpu.VMEM(tiles.shape, BF),
            pltpu.VMEM(w_qkv.shape, BF),
            pltpu.VMEM(cotangent.shape, BF),
            pltpu.VMEM(w_out.shape, BF),
        ]
        + [pltpu.VMEM((rows, width), BF)] * 4
        + [pltpu.SemaphoreType.DMA((4 * LOAD_CUTS + 3,)), pltpu.SemaphoreType.DMA((4,))],
        hbm_outs=4,
        spaces=pltpu.HBM,
        vmem=PROJECT_VMEM_BYTES,
    )(offsets, tiles, w_qkv, cotangent, w_out)

    far_up = far
    for step in upper_steps(n):
        far_up = jnp.concatenate(step_parts(far_up, step, n), axis=0)
    mid_parts = step_parts(mid_kv, PLANE, n)
    mixed, near_stats, turned, turned_out = call(
        functools.partial(near_kernel, z),
        [
            ((rows, width), F32),
            ((rows, LANES), F32),
            ((width, rows), BF),
            ((width, rows), BF),
        ],
        8 * base_flops,
        smem=1,
    )(pad_count, after(q, far_up), k, v, g, tiles, order, order_q)
    mid_0 = jnp.concatenate(mid_parts, axis=0)
    mid_1 = swap(mid_0, 1, n)
    far_0 = jnp.concatenate(
        step_parts(far_up[:, : 2 * width], PLANE, n, (near_stats,)), axis=0
    )
    far_1 = swap(far_0, 1, n)
    qg = jnp.concatenate([mid_qg, far_up[:, 2 * width :]], axis=0)
    qg_parts = step_parts(after(qg, far_0), PLANE, n)

    stats, picked, raw, held = call(
        functools.partial(join_kernel, z),
        [((rows, LANES), F32), ((z.sel, LANES), F32), ((z.sel, LANES), F32), ((z.sel, width), F32)],
        3 * base_flops,
        smem=2,
    )(offsets, pad_count, sel, mid_0, mid_1, far_0, far_1, near_stats)

    out_rows, attn_turned, attn_turned_out = call(
        functools.partial(output_kernel, z),
        [((rows, width), BF), ((z.half, rows), BF), ((z.half, rows), BF)],
        6 * rows * width * width,
        scratch=[pltpu.VMEM((rows, width), BF)],
        smem=1,
    )(offsets, near_stats, stats, picked, raw, mixed, held, tiles, w_out, order_out)
    attn_other = swap(attn_turned_out, 1, n)
    (dq_sel,) = call(
        functools.partial(own_grads_kernel, z),
        [((z.sel, width), F32)],
        2 * base_flops,
        smem=2,
    )(offsets, pad_count, sel, mid_0, mid_1, far_0, far_1, after(picked, attn_turned))
    turned_other = swap(after(turned_out, picked), 1, n)
    cot_other = swap(after(cotangent, picked), 1, n)

    qg_0 = jnp.concatenate(tied(qg_parts, (out_rows,)), axis=0)
    qg_1 = swap(qg_0, 1, n)
    stats_up = picked[z.mid : z.mid + z.far]
    for i, step in enumerate(upper_steps(n)):
        parts = step_parts(stats_up, step, n, (out_rows,) if i == 0 else ())
        stats_up = jnp.concatenate(parts, axis=0)
    def weights(start, *args):
        kernel = functools.partial(weights_kernel, start)
        return call(kernel, [((z.half, width), BF)], 4 * rows * width * width)(*args)[0]

    wout_half = weights(0, attn_turned, attn_other, cotangent, after(cot_other, stats_up))

    dq, dk_near, dv_near = call(
        functools.partial(near_grads_kernel, z),
        [((rows, width), BF), ((rows, width), F32), ((rows, width), F32)],
        8 * base_flops,
        smem=2,
    )(offsets, pad_count, after(q, wout_half), k, v, g, stats, dq_sel)
    dq_other = swap(dq, 1, n)
    stats_plane = doubled(jnp.concatenate([picked[: z.mid], stats_up], axis=1), (2, 4), n, ((dq_sel,), (dk_near,)))
    stats_0 = jnp.concatenate([stats_plane[:, :LANES], stats_plane[:, LANES:]], axis=0)
    stats_1 = swap(stats_0, 1, n)
    early_half = weights(z.half, turned, turned_other, dq, dq_other)

    dk, dv = call(
        functools.partial(key_grads_kernel, z),
        [((rows, width), BF), ((rows, width), BF)],
        3 * base_flops,
        smem=2,
    )(
        offsets, pad_count, sel, qg_0, qg_1, stats_0, stats_1,
        after(dk_near, early_half), dv_near,
    )
    dk_other = swap(dk, 1, n)
    dv_other = swap(dv, 1, n)
    (late_half,) = call(
        functools.partial(late_weights_kernel, z),
        [((z.half, 2 * width), BF)],
        4 * rows * width * width,
    )(turned, turned_other, dk, dv, dk_other, dv_other)
    (grad_tiles,) = call(
        functools.partial(tiles_kernel, z), [((rows, width), BF)], 6 * rows * width * width
    )(after(dq, late_half), dk, dv, w_qkv)
    late_parts = block_parts(late_half, PLANE, n)
    early = halved(early_half, masks + [2, 4], n, ((late_parts[1],),))
    grad_wout = halved(wout_half, [2, 4] + masks, n, ((dq,), (dk,), (late_parts[1],)))
    late = reduce_all(sum_parts(late_parts, BF), upper_steps(n)[::-1], n)
    grad_wqkv = jnp.concatenate([early, late], axis=1)
    return out_rows, grad_tiles, grad_wqkv, grad_wout


def solution(mesh):
    return jax.shard_map(
        per_device,
        mesh=mesh,
        in_specs=(P("ctx", None), P(), P(), P("ctx", None), P(), P()),
        out_specs=(P("ctx", None), P("ctx", None), P("ctx", None), P("ctx", None)),
        check_vma=False,
    )
```

```python
import functools

import jax
import jax.numpy as jnp
import numpy as np
from jax import lax
from jax.experimental import pallas as pl
from jax.experimental.pallas import tpu as pltpu
from jax.sharding import PartitionSpec as P

HEAD_DIM = 64
GROUP = 8
PAIR = 2 * HEAD_DIM
LANES = 128
SECOND = 16
SCALE = 0.125
BF = jnp.bfloat16
F32 = jnp.float32
NT = (((1,), (1,)), ((), ()))
NN = (((1,), (0,)), ((), ()))
TN = (((0,), (0,)), ((), ()))
LARGE = 1e30
COST = 0.05
LOAD_CUTS = 4
VMEM_BYTES = 40 * 1024 * 1024
PROJECT_VMEM_BYTES = 57 * 1024 * 1024


def dot(a, b, dims=NN):
    return lax.dot_general(a, b, dims, preferred_element_type=F32)


def dot_exact(a, b):
    return lax.dot_general(a, b, NN, preferred_element_type=F32, precision=lax.Precision.HIGHEST)


def iota(shape, dim):
    return lax.broadcasted_iota(jnp.int32, shape, dim)


def low_half(shape):
    return iota(shape, len(shape) - 1) % PAIR < HEAD_DIM


def halves(x):
    low = low_half(x.shape)
    zero = jnp.zeros((), x.dtype)
    return jnp.where(low, x, zero), jnp.where(low, zero, x)


def by_head(first, second, rows):
    return jnp.where(low_half((rows, PAIR)), first, second)


class Sizes:
    def __init__(self, rows, width, dev_count):
        self.rows = rows
        self.width = width
        self.devs = dev_count
        self.heads = width // HEAD_DIM
        self.pairs = self.heads // 2
        self.mid = rows // GROUP
        self.far = rows // dev_count
        self.sel = 2 * self.mid
        self.far_held = -(-self.far // 16) * 16
        self.upper = dev_count // GROUP
        self.strip = width // dev_count
        self.half = width // 2


def chosen_row(z, index, off_mid, off_far):
    row = jnp.where(index < z.mid, index * GROUP + off_mid, (index - z.mid) * z.devs + off_far)
    return jnp.where(index < z.mid + z.far, row, -1)


def spread(z, offs_ref, pair, picked):
    lane = iota((1, 4 * z.sel), 1)
    second = (lane // z.sel) % 2 == 1
    off_mid = jnp.where(second, offs_ref[0, 2 * pair + 1], offs_ref[0, 2 * pair])
    off_far = jnp.where(second, offs_ref[1, 2 * pair + 1], offs_ref[1, 2 * pair])
    target = chosen_row(z, lane % z.sel, off_mid, off_far)
    place = (iota((z.rows, 4 * z.sel), 0) == target).astype(F32).astype(BF)
    high = picked.astype(BF)
    rest = (picked - high.astype(F32)).astype(BF)
    first_high, second_high = halves(high)
    first_rest, second_rest = halves(rest)
    stacked = jnp.concatenate([first_high, second_high, first_rest, second_rest], axis=0)
    return dot(place, stacked)


def lane_offsets(z, offs_ref):
    lane = iota((1, LANES), 1)
    off_mid = jnp.full((1, LANES), -1, jnp.int32)
    off_far = jnp.full((1, LANES), -1, jnp.int32)
    for head in range(z.heads):
        here = (lane == head) | (lane == SECOND + head)
        off_mid = jnp.where(here, offs_ref[0, head], off_mid)
        off_far = jnp.where(here, offs_ref[1, head], off_far)
    return off_mid, off_far


def stat_masks(z, offs_ref):
    off_mid, off_far = lane_offsets(z, offs_ref)
    row = iota((z.rows, LANES), 0)
    return row % GROUP == off_mid, row % z.devs == off_far


def pick_stats(z, masks, stats):
    entry = iota((z.sel, z.rows), 0)
    row = iota((z.sel, z.rows), 1)
    take_mid = ((entry < z.mid) & (row // GROUP == entry)).astype(F32)
    take_far = (row // z.devs == entry - z.mid).astype(F32)
    return dot_exact(take_mid, jnp.where(masks[0], stats, 0.0)) + dot_exact(
        take_far, jnp.where(masks[1], stats, 0.0)
    )


def spread_stats(z, masks, picked):
    row = iota((z.rows, z.sel), 0)
    entry = iota((z.rows, z.sel), 1)
    give_mid = ((entry < z.mid) & (row // GROUP == entry)).astype(F32)
    give_far = (row // z.devs == entry - z.mid).astype(F32)
    fill = jnp.where(iota((z.rows, LANES), 1) < SECOND, -jnp.inf, 0.0)
    return (
        jnp.where(masks[0], dot_exact(give_mid, picked), fill),
        jnp.where(masks[1], dot_exact(give_far, picked), fill),
    )


def gathered_place(z, own, level):
    index = iota((1, z.rows), 1)
    core = index // (4 * z.mid)
    plane = (index // z.mid) % 4
    inner = index % z.mid
    if level == 0:
        return (own ^ (core + 2 * plane)) * z.rows + inner * GROUP
    dev = own ^ (core + 2 * plane + GROUP * (inner // z.far))
    return dev * z.rows + (inner % z.far) * z.devs


def level_parts(z):
    return ((0, z.mid), (z.mid, z.mid + z.far_held))


def project_kernel(
    z, offs_hbm, tiles_hbm, w_qkv_hbm, cot_hbm, w_out_hbm,
    q_hbm, k_hbm, v_hbm, g_hbm, sel, mid_kv, mid_qg, far,
    offs_ref, tiles, w_qkv, cot, w_out, q, k, v, g, sems, out_sems,
):
    width = z.width
    step = width // LOAD_CUTS

    def column_block(block):
        return [
            (
                w_qkv_hbm.at[pl.ds(i * step, step), pl.ds(block * width, width)],
                w_qkv.at[pl.ds(i * step, step), pl.ds(block * width, width)],
            )
            for i in range(LOAD_CUTS)
        ]

    groups = [
        [(tiles_hbm, tiles)] + column_block(1),
        column_block(2),
        column_block(0),
        [(cot_hbm, cot)]
        + [
            (w_out_hbm.at[pl.ds(i * step, step), :], w_out.at[pl.ds(i * step, step), :])
            for i in range(LOAD_CUTS)
        ],
        [(offs_hbm, offs_ref)],
    ]
    copies, index = [], 0
    for group in groups:
        made = []
        for source, target in group:
            copy = pltpu.make_async_copy(source, target, sems.at[index])
            copy.start()
            made.append(copy)
            index += 1
        copies.append(made)

    def arrived(group):
        for copy in copies[group]:
            copy.wait()

    leaving = []

    def leave(source, target):
        copy = pltpu.make_async_copy(source, target, out_sems.at[len(leaving)])
        copy.start()
        leaving.append(copy)

    arrived(0)
    own = tiles[...]
    k[...] = dot(own, w_qkv[:, width : 2 * width]).astype(BF)
    leave(k, k_hbm)
    arrived(1)
    v[...] = dot(own, w_qkv[:, 2 * width :]).astype(BF)
    leave(v, v_hbm)
    arrived(2)
    q[...] = dot(own, w_qkv[:, :width]).astype(BF) * jnp.asarray(SCALE, BF)
    leave(q, q_hbm)
    arrived(3)
    g[...] = dot(cot[...], w_out[...], NT).astype(BF)
    leave(g, g_hbm)
    arrived(4)
    entry = iota((2 * z.sel, z.rows), 0)
    column = iota((2 * z.sel, z.rows), 1)
    second = entry >= z.sel
    for pair in range(z.pairs):
        lanes = slice(pair * PAIR, (pair + 1) * PAIR)
        off_mid = jnp.where(second, offs_ref[0, 2 * pair + 1], offs_ref[0, 2 * pair])
        off_far = jnp.where(second, offs_ref[1, 2 * pair + 1], offs_ref[1, 2 * pair])
        target = chosen_row(z, entry % z.sel, off_mid, off_far)
        take = (column == target).astype(F32).astype(BF)
        every = jnp.concatenate([k[:, lanes], v[:, lanes], q[:, lanes], g[:, lanes]], axis=1)
        both = dot(take, every)
        picked = jnp.where(low_half((z.sel, 4 * PAIR)), both[: z.sel], both[z.sel :]).astype(BF)
        far_part = jnp.where(
            low_half((z.far, 4 * PAIR)),
            both[z.mid : z.mid + z.far],
            both[z.sel + z.mid : z.sel + z.mid + z.far],
        ).astype(BF)
        for part in range(4):
            to = slice(part * width + pair * PAIR, part * width + (pair + 1) * PAIR)
            sel[:, to] = picked[:, part * PAIR : (part + 1) * PAIR]
            near_to = slice(to.start % (2 * width), to.start % (2 * width) + PAIR)
            mid = mid_kv if part < 2 else mid_qg
            mid[:, near_to] = picked[: z.mid, part * PAIR : (part + 1) * PAIR]
            far[:, to] = far_part[:, part * PAIR : (part + 1) * PAIR]
    for copy in leaving:
        copy.wait()


def near_kernel(
    z, pad_ref, q, k, v, g, tiles, order, order_q, mixed, stats, turned, turned_out
):
    own = lax.axis_index("ctx")
    limit = z.rows * z.devs - pad_ref[0] - own * z.rows
    valid = iota((1, z.rows), 1) < limit
    lane = iota((z.rows, LANES), 1)
    both = jnp.zeros((z.rows, LANES), F32)
    for pair in range(z.pairs):
        lanes = slice(pair * PAIR, (pair + 1) * PAIR)
        query = q[:, lanes]
        grad = g[:, lanes].astype(F32)
        keys = halves(k[:, lanes])
        values = halves(v[:, lanes])
        total = None
        for side in range(2):
            head = 2 * pair + side
            scores = jnp.where(valid, dot(query, keys[side], NT), -jnp.inf)
            peak = jnp.max(scores, axis=1, keepdims=True)
            powers = jnp.exp(scores - peak)
            summed = jnp.sum(powers, axis=1, keepdims=True)
            part = dot(powers.astype(BF), values[side]) * (1.0 / summed)
            total = part if total is None else total + part
            both = jnp.where(lane == head, peak + jnp.log(summed), both)
            meets = jnp.sum(grad * part, axis=1, keepdims=True)
            both = jnp.where(lane == SECOND + head, meets, both)
        mixed[:, lanes] = total
    stats[...] = both
    for which, source_rows in enumerate((order, order_q)):
        for part, target in enumerate((turned, turned_out)):
            source = source_rows[part * z.half : (part + 1) * z.half, :]
            place = (iota((z.half, z.width), 1) == source).astype(F32).astype(BF)
            result = dot(place, tiles[...], NT).astype(BF)
            target[which * z.half : (which + 1) * z.half, :] = result


def of_level(level, refs, lanes):
    return jnp.concatenate([ref[:, lanes] for ref in refs[level]], axis=0)


def part_lanes(z, part, pair):
    return slice(part * z.width + pair * PAIR, part * z.width + (pair + 1) * PAIR)


def own_scores(z, limit, offs_ref, sel, refs):
    own = lax.axis_index("ctx")
    scores, places = [], []
    for level, (start, stop) in enumerate(level_parts(z)):
        place = gathered_place(z, own, level)
        for pair in range(z.pairs):
            query = sel[start:stop, part_lanes(z, 2, pair)]
            keys = halves(of_level(level, refs, part_lanes(z, 0, pair)))
            for side in range(2):
                valid = place + offs_ref[level, 2 * pair + side] < limit
                scores.append(jnp.where(valid, dot(query, keys[side], NT), -jnp.inf))
                places.append((level, 2 * pair + side, start, stop))
    spots, at = [], 0
    for level, head, start, stop in places:
        spots.append((level, head, at, at + stop - start))
        at += stop - start
    return jnp.concatenate(scores, axis=0), spots


def to_lanes(z, spots, columns):
    parts = []
    for level, (start, stop) in enumerate(level_parts(z)):
        lane = iota((stop - start, LANES), 1)
        part = jnp.zeros((stop - start, LANES), F32)
        for found, head, first, last in spots:
            if found == level:
                for shift, column in columns:
                    part = jnp.where(lane == shift + head, column[first:last], part)
        parts.append(part)
    parts.append(jnp.zeros((z.sel - level_parts(z)[1][1], LANES), F32))
    return jnp.concatenate(parts, axis=0)


def from_lanes(spots, array, shift):
    return lambda z: jnp.concatenate(
        [
            array[level_parts(z)[level][0] : level_parts(z)[level][1], shift + head : shift + head + 1]
            for level, head, _, _ in spots
        ],
        axis=0,
    )


def spot_of(spots, level, head):
    return next((first, last) for found, at, first, last in spots if (found, at) == (level, head))


def join_kernel(
    z, offs_ref, pad_ref, sel, mid_0, mid_1, far_0, far_1, near_stats, stats, picked, raw, held
):
    refs = ((mid_0, mid_1), (far_0, far_1))
    scores, spots = own_scores(z, z.rows * z.devs - pad_ref[0], offs_ref, sel, refs)
    peak = jnp.max(scores, axis=1, keepdims=True)
    powers = jnp.exp(scores - peak)
    summed = jnp.sum(powers, axis=1, keepdims=True)
    lse = peak + jnp.log(summed)
    scale = 1.0 / summed
    powers = powers.astype(BF)
    products = []
    tail = jnp.zeros((z.sel - level_parts(z)[1][1], PAIR), F32)
    for pair in range(z.pairs):
        totals = []
        for level, (start, stop) in enumerate(level_parts(z)):
            values = halves(of_level(level, refs, part_lanes(z, 1, pair)))
            parts = []
            for side in range(2):
                at, to = spot_of(spots, level, 2 * pair + side)
                parts.append(dot(powers[at:to], values[side]) * scale[at:to])
            totals.append(parts[0] + parts[1])
            grad = sel[start:stop, part_lanes(z, 3, pair)].astype(F32)
            products.append((level, pair, [grad * part for part in parts]))
        held[:, pair * PAIR : (pair + 1) * PAIR] = jnp.concatenate(totals + [tail], axis=0)
    products.sort(key=lambda entry: entry[:2])
    stacked = jnp.concatenate([part for _, _, both in products for part in both], axis=0)
    meets = jnp.sum(stacked, axis=1, keepdims=True)
    sel_both = to_lanes(z, spots, ((0, lse), (SECOND, meets)))
    raw[...] = sel_both
    masks = stat_masks(z, offs_ref)
    near = near_stats[...]
    mid, far = spread_stats(z, masks, sel_both)
    top = jnp.maximum(near, jnp.maximum(mid, far))
    total_lse = top + jnp.log(jnp.exp(near - top) + jnp.exp(mid - top) + jnp.exp(far - top))
    delta = sum(
        pltpu.roll(jnp.exp(value - total_lse), SECOND, 1) * value
        for value in (
            near,
            jnp.where(masks[0], mid, -LARGE),
            jnp.where(masks[1], far, -LARGE),
        )
    )
    both = jnp.where(iota((z.rows, LANES), 1) < SECOND, total_lse, delta)
    stats[...] = both
    picked[...] = pick_stats(z, masks, both)


def output_kernel(
    z, offs_ref, near_stats, stats, picked, raw, mixed, held, tiles, w_out, order,
    rows_out, turned, turned_out, attn,
):
    near_share = jnp.exp(near_stats[...] - stats[...])
    share = jnp.exp(raw[...] - picked[...])
    for pair in range(z.pairs):
        lanes = slice(pair * PAIR, (pair + 1) * PAIR)
        near = by_head(
            near_share[:, 2 * pair : 2 * pair + 1],
            near_share[:, 2 * pair + 1 : 2 * pair + 2],
            z.rows,
        )
        own = by_head(share[:, 2 * pair : 2 * pair + 1], share[:, 2 * pair + 1 : 2 * pair + 2], z.sel)
        combined = near * mixed[:, lanes] + spread(z, offs_ref, pair, own * held[:, lanes])
        attn[:, lanes] = combined.astype(BF)
    rows_out[...] = (tiles[...].astype(F32) + dot(attn[...], w_out[...])).astype(BF)
    for part, target in enumerate((turned, turned_out)):
        source = order[part * z.half : (part + 1) * z.half, :]
        place = (iota((z.half, z.width), 1) == source).astype(F32).astype(BF)
        target[...] = dot(place, attn[...], NT).astype(BF)


def own_grads_kernel(z, offs_ref, pad_ref, sel, mid_0, mid_1, far_0, far_1, picked, dq_sel):
    limit = z.rows * z.devs - pad_ref[0]
    refs = ((mid_0, mid_1), (far_0, far_1))
    scores, spots = own_scores(z, limit, offs_ref, sel, refs)
    probs = jnp.exp(scores - from_lanes(spots, picked, 0)(z))
    grad_probs = []
    for level, (start, stop) in enumerate(level_parts(z)):
        for pair in range(z.pairs):
            grad = sel[start:stop, part_lanes(z, 3, pair)]
            values = halves(of_level(level, refs, part_lanes(z, 1, pair)))
            grad_probs += [dot(grad, values[side], NT) for side in range(2)]
    grad_probs = jnp.concatenate(grad_probs, axis=0) - from_lanes(spots, picked, SECOND)(z)
    grad_scores = (probs * grad_probs).astype(BF)
    tail = jnp.zeros((z.sel - level_parts(z)[1][1], PAIR), F32)
    for pair in range(z.pairs):
        sums = []
        for level in range(2):
            keys = halves(of_level(level, refs, part_lanes(z, 0, pair)))
            at, to = spot_of(spots, level, 2 * pair)
            low = dot(grad_scores[at:to], keys[0])
            at, to = spot_of(spots, level, 2 * pair + 1)
            sums.append(low + dot(grad_scores[at:to], keys[1]))
        dq_sel[:, pair * PAIR : (pair + 1) * PAIR] = jnp.concatenate(sums + [tail], axis=0)


def near_grads_kernel(z, offs_ref, pad_ref, q, k, v, g, stats, dq_sel, dq, dk, dv):
    own = lax.axis_index("ctx")
    limit = z.rows * z.devs - pad_ref[0]
    valid_near = iota((z.rows, 1), 0) < limit - own * z.rows
    across = jnp.transpose(stats[...])
    for pair in range(z.pairs):
        lanes = slice(pair * PAIR, (pair + 1) * PAIR)
        query, grad = q[:, lanes], g[:, lanes]
        queries, grads = halves(query), halves(grad)
        keys, values = halves(k[:, lanes]), halves(v[:, lanes])
        sum_q = sum_k = sum_v = None
        for side in range(2):
            head = 2 * pair + side
            scores = jnp.where(valid_near, dot(keys[side], query, NT), -jnp.inf)
            probs = jnp.exp(scores - across[head : head + 1, :])
            grad_probs = dot(values[side], grad, NT)
            grad_scores = probs * (grad_probs - across[SECOND + head : SECOND + head + 1, :])
            grad_scores = grad_scores.astype(BF)
            part_k = dot(grad_scores, queries[side])
            part_v = dot(probs.astype(BF), grads[side])
            part_q = dot(grad_scores, keys[side], TN)
            if side == 0:
                sum_q, sum_k, sum_v = part_q, part_k, part_v
            else:
                sum_q, sum_k, sum_v = sum_q + part_q, sum_k + part_k, sum_v + part_v
        dk[:, lanes] = sum_k
        dv[:, lanes] = sum_v
        dq[:, lanes] = (SCALE * (sum_q + spread(z, offs_ref, pair, dq_sel[:, lanes]))).astype(BF)


def key_grads_kernel(
    z, offs_ref, pad_ref, sel, qg_0, qg_1, stats_0, stats_1, dk_near, dv_near, dk, dv
):
    own = lax.axis_index("ctx")
    limit = z.rows * z.devs - pad_ref[0] - own * z.rows
    parts = level_parts(z)
    stat_refs = (stats_0, stats_1)

    def rows_of(level, lanes):
        cuts = [slice(p * z.sel + level * z.mid, p * z.sel + (level + 1) * z.mid) for p in range(4)]
        return jnp.concatenate([ref[cut, lanes] for ref in (qg_0, qg_1) for cut in cuts], axis=0)

    tail = jnp.zeros((z.sel - parts[1][1], PAIR), F32)
    probs, grad_scores = {}, {}
    for level, (start, stop) in enumerate(parts):
        across = jnp.transpose(jnp.concatenate([ref[level * 4 * z.mid : (level + 1) * 4 * z.mid, :] for ref in stat_refs], axis=0))
        entry = iota((stop - start, 1), 0) + start
        for pair in range(z.pairs):
            keys = sel[start:stop, part_lanes(z, 0, pair)]
            values = sel[start:stop, part_lanes(z, 1, pair)]
            queries = halves(rows_of(level, part_lanes(z, 0, pair)))
            grads = halves(rows_of(level, part_lanes(z, 1, pair)))
            for side in range(2):
                head = 2 * pair + side
                at = chosen_row(z, entry, offs_ref[0, head], offs_ref[1, head])
                valid = (at >= 0) & (at < limit)
                scores = jnp.where(valid, dot(keys, queries[side], NT), -jnp.inf)
                exps = jnp.exp(scores - across[head : head + 1, :])
                grad_probs = dot(values, grads[side], NT)
                grad_probs = grad_probs - across[SECOND + head : SECOND + head + 1, :]
                probs[level, head] = exps.astype(BF)
                grad_scores[level, head] = (exps * grad_probs).astype(BF)
    sums_k, sums_v = {}, {}
    for pair in range(z.pairs):
        both_k, both_v = [], []
        for level in range(2):
            queries = halves(rows_of(level, part_lanes(z, 0, pair)))
            grads = halves(rows_of(level, part_lanes(z, 1, pair)))
            low, high = 2 * pair, 2 * pair + 1
            both_k.append(
                dot(grad_scores[level, low], queries[0]) + dot(grad_scores[level, high], queries[1])
            )
            both_v.append(dot(probs[level, low], grads[0]) + dot(probs[level, high], grads[1]))
        sums_k[pair] = jnp.concatenate(both_k + [tail], axis=0)
        sums_v[pair] = jnp.concatenate(both_v + [tail], axis=0)
    for pair in range(z.pairs):
        lanes = slice(pair * PAIR, (pair + 1) * PAIR)
        both = jnp.concatenate([sums_k[pair], sums_v[pair]], axis=1)
        moved = spread(z, offs_ref, pair, both)
        dk[:, lanes] = (dk_near[:, lanes] + moved[:, :PAIR]).astype(BF)
        dv[:, lanes] = (dv_near[:, lanes] + moved[:, PAIR:]).astype(BF)


def weights_kernel(start, left, left_other, right, right_other, out):
    rows = slice(start, start + out.shape[0])
    out[...] = (dot(left[rows, :], right[...]) + dot(left_other[rows, :], right_other[...])).astype(BF)


def late_weights_kernel(z, turned, turned_other, dk, dv, dk_other, dv_other, *blocks):
    left, other = turned[: z.half, :], turned_other[: z.half, :]
    size = z.half // len(blocks)
    for part, (own, far) in enumerate(((dk, dk_other), (dv, dv_other))):
        result = (dot(left, own[...]) + dot(other, far[...])).astype(BF)
        for i, block in enumerate(blocks):
            block[part * size : (part + 1) * size, :] = result[i * size : (i + 1) * size]


def tiles_kernel(z, dq, dk, dv, w_qkv, out):
    width = z.width
    out[...] = (
        dot(dq[...], w_qkv[:, :width], NT)
        + dot(dk[...], w_qkv[:, width : 2 * width], NT)
        + dot(dv[...], w_qkv[:, 2 * width :], NT)
    ).astype(BF)


def call(kernel, outs, flops, scratch=(), smem=0, spaces=None, vmem=VMEM_BYTES, hbm_outs=0):
    def run(*args):
        moved = sum(int(np.prod(a.shape)) * a.dtype.itemsize for a in args)
        moved += sum(int(np.prod(s)) * jnp.dtype(t).itemsize for s, t in outs)
        specs = [
            pl.BlockSpec(memory_space=spaces or (pltpu.SMEM if i < smem else pltpu.VMEM))
            for i in range(len(args))
        ]
        return pl.pallas_call(
            kernel,
            out_shape=tuple(jax.ShapeDtypeStruct(s, t) for s, t in outs),
            in_specs=specs,
            out_specs=tuple(
                pl.BlockSpec(memory_space=pltpu.HBM if i < hbm_outs else pltpu.VMEM)
                for i in range(len(outs))
            ),
            scratch_shapes=list(scratch),
            compiler_params=pltpu.CompilerParams(vmem_limit_bytes=vmem),
            cost_estimate=pl.CostEstimate(
                flops=int(flops * COST), bytes_accessed=int(moved * COST), transcendentals=0
            ),
        )(*args)

    return run


def swap(value, mask, dev_count):
    return lax.ppermute(value, "ctx", [(d, d ^ mask) for d in range(dev_count)])


def upper_steps(dev_count):
    steps, base = [], GROUP
    while base < dev_count:
        count = 4 if base * 4 <= dev_count else 2
        steps.append((base, count))
        base *= count
    return steps


PLANE = (2, 4)


def tied(parts, first):
    return list(lax.optimization_barrier((*parts, *first))[: len(parts)]) if first else list(parts)


def step_parts(value, step, dev_count, first=()):
    base, count = step
    return tied([value] + [swap(value, base * i, dev_count) for i in range(1, count)], first)


def sum_parts(parts, dtype):
    return sum(part.astype(F32) for part in parts).astype(dtype)


def doubled(value, masks, dev_count, firsts=()):
    for i, mask in enumerate(masks):
        parts = tied([value, swap(value, mask, dev_count)], firsts[i] if i < len(firsts) else ())
        value = jnp.concatenate(parts, axis=0)
    return value


def halved(value, masks, dev_count, firsts, dtype):
    for mask, first in zip(masks, firsts):
        size = value.shape[0] // 2
        parts = tied([value[:size], swap(value[size:], mask, dev_count)], first)
        value = sum_parts(parts, dtype)
    return value


def strip_order(z, own, masks):
    digits = np.meshgrid(*[np.arange(2) for _ in masks], np.arange(z.strip), indexing="ij")
    moved = sum(digit * mask for digit, mask in zip(digits, masks)).reshape(-1, 1)
    return (own ^ moved.astype(np.int32)) * z.strip + digits[-1].reshape(-1, 1).astype(np.int32)


def after(value, *others):
    return lax.optimization_barrier((value, *others))[0]


def per_device(tiles, w_qkv, w_out, cotangent, offsets, pad_count):
    n = lax.axis_size("ctx")
    z = Sizes(tiles.shape[0], tiles.shape[1], n)
    own = lax.axis_index("ctx")
    rows, width = z.rows, z.width
    masks = [mask for mask in (2**i for i in range(30)) if GROUP <= mask < n]
    order = strip_order(z, own, [1, 4, 2] + masks[::-1])
    order_q = strip_order(z, own, [1] + masks[:-1] + [4, 2] + masks[-1:])
    order_out = strip_order(z, own, [1, 2, 4] + masks[::-1])
    base_flops = 2 * rows * rows * width

    def weights(start, *args):
        kernel = functools.partial(weights_kernel, start)
        return call(kernel, [((z.half, width), BF)], 4 * rows * width * width)(*args)[0]

    q, k, v, g, sel, mid_kv, mid_qg, far = call(
        functools.partial(project_kernel, z),
        [((rows, width), BF)] * 4
        + [((z.sel, 4 * width), BF)]
        + [((z.mid, 2 * width), BF)] * 2
        + [((z.far, 4 * width), BF)],
        2 * rows * width * 4 * width,
        scratch=[
            pltpu.SMEM(offsets.shape, jnp.int32),
            pltpu.VMEM(tiles.shape, BF),
            pltpu.VMEM(w_qkv.shape, BF),
            pltpu.VMEM(cotangent.shape, BF),
            pltpu.VMEM(w_out.shape, BF),
        ]
        + [pltpu.VMEM((rows, width), BF)] * 4
        + [pltpu.SemaphoreType.DMA((4 * LOAD_CUTS + 3,)), pltpu.SemaphoreType.DMA((4,))],
        hbm_outs=4,
        spaces=pltpu.HBM,
        vmem=PROJECT_VMEM_BYTES,
    )(offsets, tiles, w_qkv, cotangent, w_out)

    far_up = far
    for step in upper_steps(n):
        far_up = jnp.concatenate(step_parts(far_up, step, n), axis=0)
    mid_parts = step_parts(mid_kv, PLANE, n)
    mixed, near_stats, turned, turned_out = call(
        functools.partial(near_kernel, z),
        [
            ((rows, width), F32),
            ((rows, LANES), F32),
            ((width, rows), BF),
            ((width, rows), BF),
        ],
        8 * base_flops,
        smem=1,
    )(pad_count, after(q, far_up, *mid_parts[1:3]), k, v, g, tiles, order, order_q)
    mid_0 = jnp.concatenate(mid_parts, axis=0)
    mid_1 = swap(mid_0, 1, n)
    far_0 = jnp.concatenate(
        step_parts(after(far_up[:, : 2 * width], *mid_parts[1:3]), PLANE, n, (near_stats,)), axis=0
    )
    far_1 = swap(far_0, 1, n)
    qg = jnp.concatenate([mid_qg, far_up[:, 2 * width :]], axis=0)
    qg_parts = step_parts(after(qg, far_0), PLANE, n)

    stats, picked, raw, held = call(
        functools.partial(join_kernel, z),
        [((rows, LANES), F32), ((z.sel, LANES), F32), ((z.sel, LANES), F32), ((z.sel, width), F32)],
        3 * base_flops,
        smem=2,
    )(offsets, pad_count, sel, mid_0, mid_1, far_0, far_1, near_stats)

    (dq_sel,) = call(
        functools.partial(own_grads_kernel, z),
        [((z.sel, width), F32)],
        2 * base_flops,
        smem=2,
    )(offsets, pad_count, sel, mid_0, mid_1, far_0, far_1, picked)
    stats_up = doubled(picked[z.mid : z.mid + z.far], masks[:1], n, ((dq_sel,),))
    dq, dk_near, dv_near = call(
        functools.partial(near_grads_kernel, z),
        [((rows, width), BF), ((rows, width), F32), ((rows, width), F32)],
        8 * base_flops,
        smem=2,
    )(offsets, pad_count, after(q, stats_up), k, v, g, stats, dq_sel)
    turned_other = swap(after(turned_out, dk_near), 1, n)
    cot_other = swap(after(cotangent, dk_near), 1, n)
    dq_other = swap(dq, 1, n)

    qg_0 = jnp.concatenate(tied(qg_parts, (dk_near,)), axis=0)
    qg_1 = swap(qg_0, 1, n)
    stats_up = doubled(stats_up, masks[1:], n, ((dk_near,),))
    out_rows, attn_turned, attn_turned_out = call(
        functools.partial(output_kernel, z),
        [((rows, width), BF), ((z.half, rows), BF), ((z.half, rows), BF)],
        6 * rows * width * width,
        scratch=[pltpu.VMEM((rows, width), BF)],
        smem=1,
    )(offsets, near_stats, stats, after(picked, stats_up), raw, mixed, held, tiles, w_out, order_out)
    attn_other = swap(attn_turned_out, 1, n)
    wout_half = weights(0, attn_turned, attn_other, cotangent, cot_other)

    early_half = weights(z.half, turned, turned_other, dq, dq_other)
    stats_plane = doubled(
        jnp.concatenate([picked[: z.mid], stats_up], axis=1),
        (2, 4),
        n,
        ((out_rows,), (wout_half, early_half)),
    )
    stats_0 = jnp.concatenate([stats_plane[:, :LANES], stats_plane[:, LANES:]], axis=0)
    stats_1 = swap(stats_0, 1, n)

    dk, dv = call(
        functools.partial(key_grads_kernel, z),
        [((rows, width), BF), ((rows, width), BF)],
        3 * base_flops,
        smem=2,
    )(
        offsets, pad_count, sel, qg_0, qg_1, stats_0, stats_1,
        after(dk_near, early_half), dv_near,
    )
    dk_other = swap(dk, 1, n)
    dv_other = swap(dv, 1, n)
    count = PLANE[1]
    block = z.half // count
    late = call(
        functools.partial(late_weights_kernel, z),
        [((2 * block, width), BF)] * count,
        4 * rows * width * width,
    )(turned, turned_other, dk, dv, dk_other, dv_other)
    (grad_tiles,) = call(
        functools.partial(tiles_kernel, z), [((rows, width), BF)], 6 * rows * width * width
    )(after(dq, late[0]), dk, dv, w_qkv)

    wout = halved(wout_half, [2], n, ((dk,),), BF)
    wq = halved(early_half, masks[:-1], n, ((dk,),) * len(masks[:-1]), BF)
    sums = [[late[0][:block]], [late[0][block:]], [wout[:block]], [wq[: wq.shape[0] // count]]]
    for i in range(1, count):
        parts = [late[i], wq[i * wq.shape[0] // count : (i + 1) * wq.shape[0] // count]]
        if PLANE[0] * i == 4:
            parts.append(wout[block:])
        got = swap(jnp.concatenate(parts, axis=0), PLANE[0] * i, n)
        sums[0].append(got[:block])
        sums[1].append(got[block : 2 * block])
        rest = 2 * block + parts[1].shape[0]
        sums[3].append(got[2 * block : rest])
        if PLANE[0] * i == 4:
            sums[2].append(got[rest:])
    steps = upper_steps(n)[::-1]
    for at, (base, count) in enumerate(steps):
        held = [sum_parts(parts, BF) for parts in sums]
        size = held[0].shape[0] // count
        last = at == len(steps) - 1
        sums = [[array[:size]] for array in held[:3]] + [held[3:]]
        meets_top = held[3].shape[0] > z.strip
        if meets_top:
            sums[3] = [held[3][: z.strip]]
        for i in range(1, count):
            parts = [array[i * size : (i + 1) * size] for array in held[:3]]
            if meets_top and base * i == masks[-1]:
                parts.append(held[3][z.strip :])
            got = swap(jnp.concatenate(parts, axis=0), base * i, n)
            for k in range(3):
                sums[k].append(got[k * size : (k + 1) * size])
            if len(parts) == 4:
                sums[3].append(got[3 * size :])
    grad_k, grad_v, grad_wout, grad_q = [sum_parts(parts, F32) for parts in sums]
    grad_wqkv = jnp.concatenate([grad_q, grad_k, grad_v], axis=1)
    return out_rows, grad_tiles, grad_wqkv, grad_wout


def solution(mesh):
    return jax.shard_map(
        per_device,
        mesh=mesh,
        in_specs=(P("ctx", None), P(), P(), P("ctx", None), P(), P()),
        out_specs=(P("ctx", None), P("ctx", None), P("ctx", None), P("ctx", None)),
        check_vma=False,
    )
```

```python
import functools

import jax
import jax.numpy as jnp
import numpy as np
from jax import lax
from jax.experimental import pallas as pl
from jax.experimental.pallas import tpu as pltpu
from jax.sharding import PartitionSpec as P

HEAD_DIM = 64
GROUP = 8
PAIR = 2 * HEAD_DIM
LANES = 128
SECOND = 16
SCALE = 0.125
BF = jnp.bfloat16
F32 = jnp.float32
NT = (((1,), (1,)), ((), ()))
NN = (((1,), (0,)), ((), ()))
TN = (((0,), (0,)), ((), ()))
LARGE = 1e30
LOW_COST = 0.05
LOAD_CUTS = 4
VMEM_BYTES = 40 * 1024 * 1024
PROJECT_VMEM_BYTES = 57 * 1024 * 1024


def dot(a, b, dims=NN):
    return lax.dot_general(a, b, dims, preferred_element_type=F32)


def dot_exact(a, b):
    return lax.dot_general(a, b, NN, preferred_element_type=F32, precision=lax.Precision.HIGHEST)


def iota(shape, dim):
    return lax.broadcasted_iota(jnp.int32, shape, dim)


def low_half(shape):
    return iota(shape, len(shape) - 1) % PAIR < HEAD_DIM


def halves(x):
    low = low_half(x.shape)
    zero = jnp.zeros((), x.dtype)
    return jnp.where(low, x, zero), jnp.where(low, zero, x)


def by_head(first, second, rows):
    return jnp.where(low_half((rows, PAIR)), first, second)


class Sizes:
    def __init__(self, rows, width, dev_count):
        self.rows = rows
        self.width = width
        self.devs = dev_count
        self.heads = width // HEAD_DIM
        self.pairs = self.heads // 2
        self.mid = rows // GROUP
        self.far = rows // dev_count
        self.sel = 2 * self.mid
        self.far_held = -(-self.far // 16) * 16
        self.upper = dev_count // GROUP
        self.strip = width // dev_count
        self.half = width // 2


def chosen_row(z, index, off_mid, off_far):
    row = jnp.where(index < z.mid, index * GROUP + off_mid, (index - z.mid) * z.devs + off_far)
    return jnp.where(index < z.mid + z.far, row, -1)


def spread(z, offs_ref, pair, picked):
    lane = iota((1, 4 * z.sel), 1)
    second = (lane // z.sel) % 2 == 1
    off_mid = jnp.where(second, offs_ref[0, 2 * pair + 1], offs_ref[0, 2 * pair])
    off_far = jnp.where(second, offs_ref[1, 2 * pair + 1], offs_ref[1, 2 * pair])
    target = chosen_row(z, lane % z.sel, off_mid, off_far)
    place = (iota((z.rows, 4 * z.sel), 0) == target).astype(F32).astype(BF)
    high = picked.astype(BF)
    rest = (picked - high.astype(F32)).astype(BF)
    first_high, second_high = halves(high)
    first_rest, second_rest = halves(rest)
    stacked = jnp.concatenate([first_high, second_high, first_rest, second_rest], axis=0)
    return dot(place, stacked)


def lane_offsets(z, offs_ref):
    lane = iota((1, LANES), 1)
    off_mid = jnp.full((1, LANES), -1, jnp.int32)
    off_far = jnp.full((1, LANES), -1, jnp.int32)
    for head in range(z.heads):
        here = (lane == head) | (lane == SECOND + head)
        off_mid = jnp.where(here, offs_ref[0, head], off_mid)
        off_far = jnp.where(here, offs_ref[1, head], off_far)
    return off_mid, off_far


def stat_masks(z, offs_ref):
    off_mid, off_far = lane_offsets(z, offs_ref)
    row = iota((z.rows, LANES), 0)
    return row % GROUP == off_mid, row % z.devs == off_far


def pick_stats(z, masks, stats):
    entry = iota((z.sel, z.rows), 0)
    row = iota((z.sel, z.rows), 1)
    take_mid = ((entry < z.mid) & (row // GROUP == entry)).astype(F32)
    take_far = (row // z.devs == entry - z.mid).astype(F32)
    return dot_exact(take_mid, jnp.where(masks[0], stats, 0.0)) + dot_exact(
        take_far, jnp.where(masks[1], stats, 0.0)
    )


def spread_stats(z, masks, picked):
    row = iota((z.rows, z.sel), 0)
    entry = iota((z.rows, z.sel), 1)
    give_mid = ((entry < z.mid) & (row // GROUP == entry)).astype(F32)
    give_far = (row // z.devs == entry - z.mid).astype(F32)
    fill = jnp.where(iota((z.rows, LANES), 1) < SECOND, -jnp.inf, 0.0)
    return (
        jnp.where(masks[0], dot_exact(give_mid, picked), fill),
        jnp.where(masks[1], dot_exact(give_far, picked), fill),
    )


def gathered_place(z, own, level):
    index = iota((1, z.rows), 1)
    core = index // (4 * z.mid)
    plane = (index // z.mid) % 4
    inner = index % z.mid
    if level == 0:
        return (own ^ (core + 2 * plane)) * z.rows + inner * GROUP
    dev = own ^ (core + 2 * plane + GROUP * (inner // z.far))
    return dev * z.rows + (inner % z.far) * z.devs


def level_parts(z):
    return ((0, z.mid), (z.mid, z.mid + z.far_held))


def project_kernel(
    z, offs_hbm, tiles_hbm, w_qkv_hbm, cot_hbm, w_out_hbm,
    q_hbm, k_hbm, v_hbm, g_hbm, sel, mid_kv, mid_qg, far,
    offs_ref, tiles, w_qkv, cot, w_out, q, k, v, g, sems, out_sems,
):
    width = z.width
    step = width // LOAD_CUTS

    def column_block(block):
        return [
            (
                w_qkv_hbm.at[pl.ds(i * step, step), pl.ds(block * width, width)],
                w_qkv.at[pl.ds(i * step, step), pl.ds(block * width, width)],
            )
            for i in range(LOAD_CUTS)
        ]

    groups = [
        [(tiles_hbm, tiles)] + column_block(1),
        column_block(2),
        column_block(0),
        [(cot_hbm, cot)]
        + [
            (w_out_hbm.at[pl.ds(i * step, step), :], w_out.at[pl.ds(i * step, step), :])
            for i in range(LOAD_CUTS)
        ],
        [(offs_hbm, offs_ref)],
    ]
    copies, index = [], 0
    for group in groups:
        made = []
        for source, target in group:
            copy = pltpu.make_async_copy(source, target, sems.at[index])
            copy.start()
            made.append(copy)
            index += 1
        copies.append(made)

    def arrived(group):
        for copy in copies[group]:
            copy.wait()

    leaving = []

    def leave(source, target):
        copy = pltpu.make_async_copy(source, target, out_sems.at[len(leaving)])
        copy.start()
        leaving.append(copy)

    arrived(0)
    own = tiles[...]
    k[...] = dot(own, w_qkv[:, width : 2 * width]).astype(BF)
    leave(k, k_hbm)
    arrived(1)
    v[...] = dot(own, w_qkv[:, 2 * width :]).astype(BF)
    leave(v, v_hbm)
    arrived(2)
    q[...] = dot(own, w_qkv[:, :width]).astype(BF) * jnp.asarray(SCALE, BF)
    leave(q, q_hbm)
    arrived(3)
    g[...] = dot(cot[...], w_out[...], NT).astype(BF)
    leave(g, g_hbm)
    arrived(4)
    entry = iota((2 * z.sel, z.rows), 0)
    column = iota((2 * z.sel, z.rows), 1)
    second = entry >= z.sel
    for pair in range(z.pairs):
        lanes = slice(pair * PAIR, (pair + 1) * PAIR)
        off_mid = jnp.where(second, offs_ref[0, 2 * pair + 1], offs_ref[0, 2 * pair])
        off_far = jnp.where(second, offs_ref[1, 2 * pair + 1], offs_ref[1, 2 * pair])
        target = chosen_row(z, entry % z.sel, off_mid, off_far)
        take = (column == target).astype(F32).astype(BF)
        every = jnp.concatenate([k[:, lanes], v[:, lanes], q[:, lanes], g[:, lanes]], axis=1)
        both = dot(take, every)
        picked = jnp.where(low_half((z.sel, 4 * PAIR)), both[: z.sel], both[z.sel :]).astype(BF)
        far_part = jnp.where(
            low_half((z.far, 4 * PAIR)),
            both[z.mid : z.mid + z.far],
            both[z.sel + z.mid : z.sel + z.mid + z.far],
        ).astype(BF)
        for part in range(4):
            to = slice(part * width + pair * PAIR, part * width + (pair + 1) * PAIR)
            sel[:, to] = picked[:, part * PAIR : (part + 1) * PAIR]
            near_to = slice(to.start % (2 * width), to.start % (2 * width) + PAIR)
            mid = mid_kv if part < 2 else mid_qg
            mid[:, near_to] = picked[: z.mid, part * PAIR : (part + 1) * PAIR]
            far[:, to] = far_part[:, part * PAIR : (part + 1) * PAIR]
    for copy in leaving:
        copy.wait()


def near_kernel(
    z, pad_ref, q, k, v, g, tiles, order, order_q, mixed, stats, turned, turned_out
):
    own = lax.axis_index("ctx")
    limit = z.rows * z.devs - pad_ref[0] - own * z.rows
    valid = iota((1, z.rows), 1) < limit
    lane = iota((z.rows, LANES), 1)
    both = jnp.zeros((z.rows, LANES), F32)
    for pair in range(z.pairs):
        lanes = slice(pair * PAIR, (pair + 1) * PAIR)
        query = q[:, lanes]
        grad = g[:, lanes].astype(F32)
        keys = halves(k[:, lanes])
        values = halves(v[:, lanes])
        total = None
        for side in range(2):
            head = 2 * pair + side
            scores = jnp.where(valid, dot(query, keys[side], NT), -jnp.inf)
            peak = jnp.max(scores, axis=1, keepdims=True)
            powers = jnp.exp(scores - peak)
            summed = jnp.sum(powers, axis=1, keepdims=True)
            part = dot(powers.astype(BF), values[side]) * (1.0 / summed)
            total = part if total is None else total + part
            both = jnp.where(lane == head, peak + jnp.log(summed), both)
            meets = jnp.sum(grad * part, axis=1, keepdims=True)
            both = jnp.where(lane == SECOND + head, meets, both)
        mixed[:, lanes] = total
    stats[...] = both
    for which, source_rows in enumerate((order, order_q)):
        for part, target in enumerate((turned, turned_out)):
            source = source_rows[part * z.half : (part + 1) * z.half, :]
            place = (iota((z.half, z.width), 1) == source).astype(F32).astype(BF)
            result = dot(place, tiles[...], NT).astype(BF)
            target[which * z.half : (which + 1) * z.half, :] = result


def of_level(level, refs, lanes):
    return jnp.concatenate([ref[:, lanes] for ref in refs[level]], axis=0)


def part_lanes(z, part, pair):
    return slice(part * z.width + pair * PAIR, part * z.width + (pair + 1) * PAIR)


def own_scores(z, limit, offs_ref, sel, refs):
    own = lax.axis_index("ctx")
    scores, places = [], []
    for level, (start, stop) in enumerate(level_parts(z)):
        place = gathered_place(z, own, level)
        for pair in range(z.pairs):
            query = sel[start:stop, part_lanes(z, 2, pair)]
            keys = halves(of_level(level, refs, part_lanes(z, 0, pair)))
            for side in range(2):
                valid = place + offs_ref[level, 2 * pair + side] < limit
                scores.append(jnp.where(valid, dot(query, keys[side], NT), -jnp.inf))
                places.append((level, 2 * pair + side, start, stop))
    spots, at = [], 0
    for level, head, start, stop in places:
        spots.append((level, head, at, at + stop - start))
        at += stop - start
    return jnp.concatenate(scores, axis=0), spots


def to_lanes(z, spots, columns):
    parts = []
    for level, (start, stop) in enumerate(level_parts(z)):
        lane = iota((stop - start, LANES), 1)
        part = jnp.zeros((stop - start, LANES), F32)
        for found, head, first, last in spots:
            if found == level:
                for shift, column in columns:
                    part = jnp.where(lane == shift + head, column[first:last], part)
        parts.append(part)
    parts.append(jnp.zeros((z.sel - level_parts(z)[1][1], LANES), F32))
    return jnp.concatenate(parts, axis=0)


def from_lanes(spots, array, shift):
    return lambda z: jnp.concatenate(
        [
            array[level_parts(z)[level][0] : level_parts(z)[level][1], shift + head : shift + head + 1]
            for level, head, _, _ in spots
        ],
        axis=0,
    )


def spot_of(spots, level, head):
    return next((first, last) for found, at, first, last in spots if (found, at) == (level, head))


def join_kernel(
    z, offs_ref, pad_ref, sel, mid_0, mid_1, far_0, far_1, near_stats, stats, picked, raw, held
):
    refs = ((mid_0, mid_1), (far_0, far_1))
    scores, spots = own_scores(z, z.rows * z.devs - pad_ref[0], offs_ref, sel, refs)
    peak = jnp.max(scores, axis=1, keepdims=True)
    powers = jnp.exp(scores - peak)
    summed = jnp.sum(powers, axis=1, keepdims=True)
    lse = peak + jnp.log(summed)
    scale = 1.0 / summed
    powers = powers.astype(BF)
    products = []
    tail = jnp.zeros((z.sel - level_parts(z)[1][1], PAIR), F32)
    for pair in range(z.pairs):
        totals = []
        for level, (start, stop) in enumerate(level_parts(z)):
            values = halves(of_level(level, refs, part_lanes(z, 1, pair)))
            parts = []
            for side in range(2):
                at, to = spot_of(spots, level, 2 * pair + side)
                parts.append(dot(powers[at:to], values[side]) * scale[at:to])
            totals.append(parts[0] + parts[1])
            grad = sel[start:stop, part_lanes(z, 3, pair)].astype(F32)
            products.append((level, pair, [grad * part for part in parts]))
        held[:, pair * PAIR : (pair + 1) * PAIR] = jnp.concatenate(totals + [tail], axis=0)
    products.sort(key=lambda entry: entry[:2])
    stacked = jnp.concatenate([part for _, _, both in products for part in both], axis=0)
    meets = jnp.sum(stacked, axis=1, keepdims=True)
    sel_both = to_lanes(z, spots, ((0, lse), (SECOND, meets)))
    raw[...] = sel_both
    masks = stat_masks(z, offs_ref)
    near = near_stats[...]
    mid, far = spread_stats(z, masks, sel_both)
    top = jnp.maximum(near, jnp.maximum(mid, far))
    total_lse = top + jnp.log(jnp.exp(near - top) + jnp.exp(mid - top) + jnp.exp(far - top))
    delta = sum(
        pltpu.roll(jnp.exp(value - total_lse), SECOND, 1) * value
        for value in (
            near,
            jnp.where(masks[0], mid, -LARGE),
            jnp.where(masks[1], far, -LARGE),
        )
    )
    both = jnp.where(iota((z.rows, LANES), 1) < SECOND, total_lse, delta)
    stats[...] = both
    picked[...] = pick_stats(z, masks, both)


def output_kernel(
    z, offs_ref, near_stats, stats, picked, raw, mixed, held, tiles, w_out, order,
    rows_out, turned, turned_out, attn,
):
    near_share = jnp.exp(near_stats[...] - stats[...])
    share = jnp.exp(raw[...] - picked[...])
    for pair in range(z.pairs):
        lanes = slice(pair * PAIR, (pair + 1) * PAIR)
        near = by_head(
            near_share[:, 2 * pair : 2 * pair + 1],
            near_share[:, 2 * pair + 1 : 2 * pair + 2],
            z.rows,
        )
        own = by_head(share[:, 2 * pair : 2 * pair + 1], share[:, 2 * pair + 1 : 2 * pair + 2], z.sel)
        combined = near * mixed[:, lanes] + spread(z, offs_ref, pair, own * held[:, lanes])
        attn[:, lanes] = combined.astype(BF)
    rows_out[...] = (tiles[...].astype(F32) + dot(attn[...], w_out[...])).astype(BF)
    for part, target in enumerate((turned, turned_out)):
        source = order[part * z.half : (part + 1) * z.half, :]
        place = (iota((z.half, z.width), 1) == source).astype(F32).astype(BF)
        target[...] = dot(place, attn[...], NT).astype(BF)


def own_grads_kernel(z, offs_ref, pad_ref, sel, mid_0, mid_1, far_0, far_1, picked, dq_sel):
    limit = z.rows * z.devs - pad_ref[0]
    refs = ((mid_0, mid_1), (far_0, far_1))
    scores, spots = own_scores(z, limit, offs_ref, sel, refs)
    probs = jnp.exp(scores - from_lanes(spots, picked, 0)(z))
    grad_probs = []
    for level, (start, stop) in enumerate(level_parts(z)):
        for pair in range(z.pairs):
            grad = sel[start:stop, part_lanes(z, 3, pair)]
            values = halves(of_level(level, refs, part_lanes(z, 1, pair)))
            grad_probs += [dot(grad, values[side], NT) for side in range(2)]
    grad_probs = jnp.concatenate(grad_probs, axis=0) - from_lanes(spots, picked, SECOND)(z)
    grad_scores = (probs * grad_probs).astype(BF)
    tail = jnp.zeros((z.sel - level_parts(z)[1][1], PAIR), F32)
    for pair in range(z.pairs):
        sums = []
        for level in range(2):
            keys = halves(of_level(level, refs, part_lanes(z, 0, pair)))
            at, to = spot_of(spots, level, 2 * pair)
            low = dot(grad_scores[at:to], keys[0])
            at, to = spot_of(spots, level, 2 * pair + 1)
            sums.append(low + dot(grad_scores[at:to], keys[1]))
        dq_sel[:, pair * PAIR : (pair + 1) * PAIR] = jnp.concatenate(sums + [tail], axis=0)


def near_grads_kernel(z, offs_ref, pad_ref, q, k, v, g, stats, dq_sel, dq, dk, dv):
    own = lax.axis_index("ctx")
    limit = z.rows * z.devs - pad_ref[0]
    valid_near = iota((z.rows, 1), 0) < limit - own * z.rows
    across = jnp.transpose(stats[...])
    for pair in range(z.pairs):
        lanes = slice(pair * PAIR, (pair + 1) * PAIR)
        query, grad = q[:, lanes], g[:, lanes]
        queries, grads = halves(query), halves(grad)
        keys, values = halves(k[:, lanes]), halves(v[:, lanes])
        sum_q = sum_k = sum_v = None
        for side in range(2):
            head = 2 * pair + side
            scores = jnp.where(valid_near, dot(keys[side], query, NT), -jnp.inf)
            probs = jnp.exp(scores - across[head : head + 1, :])
            grad_probs = dot(values[side], grad, NT)
            grad_scores = probs * (grad_probs - across[SECOND + head : SECOND + head + 1, :])
            grad_scores = grad_scores.astype(BF)
            part_k = dot(grad_scores, queries[side])
            part_v = dot(probs.astype(BF), grads[side])
            part_q = dot(grad_scores, keys[side], TN)
            if side == 0:
                sum_q, sum_k, sum_v = part_q, part_k, part_v
            else:
                sum_q, sum_k, sum_v = sum_q + part_q, sum_k + part_k, sum_v + part_v
        dk[:, lanes] = sum_k
        dv[:, lanes] = sum_v
        dq[:, lanes] = (SCALE * (sum_q + spread(z, offs_ref, pair, dq_sel[:, lanes]))).astype(BF)


def key_grads_kernel(
    z, offs_ref, pad_ref, sel, qg_0, qg_1, stats_0, stats_1, dk_near, dv_near, dk, dv
):
    own = lax.axis_index("ctx")
    limit = z.rows * z.devs - pad_ref[0] - own * z.rows
    parts = level_parts(z)
    stat_refs = (stats_0, stats_1)

    def rows_of(level, lanes):
        cuts = [slice(p * z.sel + level * z.mid, p * z.sel + (level + 1) * z.mid) for p in range(4)]
        return jnp.concatenate([ref[cut, lanes] for ref in (qg_0, qg_1) for cut in cuts], axis=0)

    tail = jnp.zeros((z.sel - parts[1][1], PAIR), F32)
    probs, grad_scores = {}, {}
    for level, (start, stop) in enumerate(parts):
        across = jnp.transpose(jnp.concatenate([ref[level * 4 * z.mid : (level + 1) * 4 * z.mid, :] for ref in stat_refs], axis=0))
        entry = iota((stop - start, 1), 0) + start
        for pair in range(z.pairs):
            keys = sel[start:stop, part_lanes(z, 0, pair)]
            values = sel[start:stop, part_lanes(z, 1, pair)]
            queries = halves(rows_of(level, part_lanes(z, 0, pair)))
            grads = halves(rows_of(level, part_lanes(z, 1, pair)))
            for side in range(2):
                head = 2 * pair + side
                at = chosen_row(z, entry, offs_ref[0, head], offs_ref[1, head])
                valid = (at >= 0) & (at < limit)
                scores = jnp.where(valid, dot(keys, queries[side], NT), -jnp.inf)
                exps = jnp.exp(scores - across[head : head + 1, :])
                grad_probs = dot(values, grads[side], NT)
                grad_probs = grad_probs - across[SECOND + head : SECOND + head + 1, :]
                probs[level, head] = exps.astype(BF)
                grad_scores[level, head] = (exps * grad_probs).astype(BF)
    sums_k, sums_v = {}, {}
    for pair in range(z.pairs):
        both_k, both_v = [], []
        for level in range(2):
            queries = halves(rows_of(level, part_lanes(z, 0, pair)))
            grads = halves(rows_of(level, part_lanes(z, 1, pair)))
            low, high = 2 * pair, 2 * pair + 1
            both_k.append(
                dot(grad_scores[level, low], queries[0]) + dot(grad_scores[level, high], queries[1])
            )
            both_v.append(dot(probs[level, low], grads[0]) + dot(probs[level, high], grads[1]))
        sums_k[pair] = jnp.concatenate(both_k + [tail], axis=0)
        sums_v[pair] = jnp.concatenate(both_v + [tail], axis=0)
    for pair in range(z.pairs):
        lanes = slice(pair * PAIR, (pair + 1) * PAIR)
        both = jnp.concatenate([sums_k[pair], sums_v[pair]], axis=1)
        moved = spread(z, offs_ref, pair, both)
        dk[:, lanes] = (dk_near[:, lanes] + moved[:, :PAIR]).astype(BF)
        dv[:, lanes] = (dv_near[:, lanes] + moved[:, PAIR:]).astype(BF)


def weights_kernel(start, left, left_other, right, right_other, out):
    rows = slice(start, start + out.shape[0])
    out[...] = (dot(left[rows, :], right[...]) + dot(left_other[rows, :], right_other[...])).astype(BF)


def late_weights_kernel(z, turned, turned_other, dk, dv, dk_other, dv_other, out):
    width = z.width
    left, other = turned[: z.half, :], turned_other[: z.half, :]
    out[:, :width] = (dot(left, dk[...]) + dot(other, dk_other[...])).astype(BF)
    out[:, width:] = (dot(left, dv[...]) + dot(other, dv_other[...])).astype(BF)


def tiles_kernel(z, dq, dk, dv, w_qkv, out):
    width = z.width
    out[...] = (
        dot(dq[...], w_qkv[:, :width], NT)
        + dot(dk[...], w_qkv[:, width : 2 * width], NT)
        + dot(dv[...], w_qkv[:, 2 * width :], NT)
    ).astype(BF)


def call(kernel, outs, flops, scratch=(), smem=0, spaces=None, vmem=VMEM_BYTES, hbm_outs=0, cost=1.0):
    def run(*args):
        moved = sum(int(np.prod(a.shape)) * a.dtype.itemsize for a in args)
        moved += sum(int(np.prod(s)) * jnp.dtype(t).itemsize for s, t in outs)
        specs = [
            pl.BlockSpec(memory_space=spaces or (pltpu.SMEM if i < smem else pltpu.VMEM))
            for i in range(len(args))
        ]
        return pl.pallas_call(
            kernel,
            out_shape=tuple(jax.ShapeDtypeStruct(s, t) for s, t in outs),
            in_specs=specs,
            out_specs=tuple(
                pl.BlockSpec(memory_space=pltpu.HBM if i < hbm_outs else pltpu.VMEM)
                for i in range(len(outs))
            ),
            scratch_shapes=list(scratch),
            compiler_params=pltpu.CompilerParams(vmem_limit_bytes=vmem),
            cost_estimate=pl.CostEstimate(
                flops=int(flops * cost), bytes_accessed=int(moved * cost), transcendentals=0
            ),
        )(*args)

    return run


def swap(value, mask, dev_count):
    return lax.ppermute(value, "ctx", [(d, d ^ mask) for d in range(dev_count)])


def upper_steps(dev_count):
    steps, base = [], GROUP
    while base < dev_count:
        count = 4 if base * 4 <= dev_count else 2
        steps.append((base, count))
        base *= count
    return steps


PLANE = (2, 4)


def tied(parts, first):
    return list(lax.optimization_barrier((*parts, *first))[: len(parts)]) if first else list(parts)


def step_parts(value, step, dev_count, first=()):
    base, count = step
    return tied([value] + [swap(value, base * i, dev_count) for i in range(1, count)], first)


def block_parts(value, step, dev_count):
    base, count = step
    size = value.shape[0] // count
    return [value[:size]] + [
        swap(value[i * size : (i + 1) * size], base * i, dev_count) for i in range(1, count)
    ]


def sum_parts(parts, dtype):
    return sum(part.astype(F32) for part in parts).astype(dtype)


def doubled(value, masks, dev_count, firsts=()):
    for i, mask in enumerate(masks):
        parts = tied([value, swap(value, mask, dev_count)], firsts[i] if i < len(firsts) else ())
        value = jnp.concatenate(parts, axis=0)
    return value


def halved(value, masks, dev_count, firsts=()):
    for i, mask in enumerate(masks):
        size = value.shape[0] // 2
        first = firsts[i] if i < len(firsts) else ()
        parts = tied([value[:size], swap(value[size:], mask, dev_count)], first)
        value = parts[0].astype(F32) + parts[1].astype(F32)
        value = value if i == len(masks) - 1 else value.astype(BF)
    return value


def reduce_all(value, steps, dev_count):
    for i, step in enumerate(steps):
        value = sum_parts(block_parts(value, step, dev_count), F32 if i == len(steps) - 1 else BF)
    return value


def strip_order(z, own, masks):
    digits = np.meshgrid(*[np.arange(2) for _ in masks], np.arange(z.strip), indexing="ij")
    moved = sum(digit * mask for digit, mask in zip(digits, masks)).reshape(-1, 1)
    return (own ^ moved.astype(np.int32)) * z.strip + digits[-1].reshape(-1, 1).astype(np.int32)


def after(value, *others):
    return lax.optimization_barrier((value, *others))[0]


def per_device(tiles, w_qkv, w_out, cotangent, offsets, pad_count):
    n = lax.axis_size("ctx")
    z = Sizes(tiles.shape[0], tiles.shape[1], n)
    own = lax.axis_index("ctx")
    rows, width = z.rows, z.width
    masks = [mask for mask in (2**i for i in range(30)) if GROUP <= mask < n]
    order = strip_order(z, own, [1, 4, 2] + masks[::-1])
    order_q = strip_order(z, own, [1] + masks + [2, 4])
    order_out = strip_order(z, own, [1, 2, 4] + masks)
    base_flops = 2 * rows * rows * width

    def weights(start, *args):
        kernel = functools.partial(weights_kernel, start)
        return call(kernel, [((z.half, width), BF)], 4 * rows * width * width)(*args)[0]

    q, k, v, g, sel, mid_kv, mid_qg, far = call(
        functools.partial(project_kernel, z),
        [((rows, width), BF)] * 4
        + [((z.sel, 4 * width), BF)]
        + [((z.mid, 2 * width), BF)] * 2
        + [((z.far, 4 * width), BF)],
        2 * rows * width * 4 * width,
        scratch=[
            pltpu.SMEM(offsets.shape, jnp.int32),
            pltpu.VMEM(tiles.shape, BF),
            pltpu.VMEM(w_qkv.shape, BF),
            pltpu.VMEM(cotangent.shape, BF),
            pltpu.VMEM(w_out.shape, BF),
        ]
        + [pltpu.VMEM((rows, width), BF)] * 4
        + [pltpu.SemaphoreType.DMA((4 * LOAD_CUTS + 3,)), pltpu.SemaphoreType.DMA((4,))],
        hbm_outs=4,
        spaces=pltpu.HBM,
        vmem=PROJECT_VMEM_BYTES,
    )(offsets, tiles, w_qkv, cotangent, w_out)

    steps = upper_steps(n)
    far_up = far
    for step in steps[:-1]:
        far_up = jnp.concatenate(step_parts(far_up, step, n), axis=0)
    far_up = step_parts(far_up, steps[-1], n)
    far_kv = jnp.concatenate([part[:, : 2 * width] for part in far_up], axis=0)
    mid_parts = step_parts(mid_kv, PLANE, n)
    mixed, near_stats, turned, turned_out = call(
        functools.partial(near_kernel, z),
        [
            ((rows, width), F32),
            ((rows, LANES), F32),
            ((width, rows), BF),
            ((width, rows), BF),
        ],
        8 * base_flops,
        smem=1,
    )(pad_count, after(q, far_kv, *mid_parts[1:3]), k, v, g, tiles, order, order_q)
    mid_0 = jnp.concatenate(mid_parts, axis=0)
    mid_1 = swap(mid_0, 1, n)
    far_0 = jnp.concatenate(
        step_parts(after(far_kv, *mid_parts[1:3]), PLANE, n, (near_stats,)), axis=0
    )
    far_1 = swap(far_0, 1, n)
    stats, picked, raw, held = call(
        functools.partial(join_kernel, z),
        [((rows, LANES), F32), ((z.sel, LANES), F32), ((z.sel, LANES), F32), ((z.sel, width), F32)],
        3 * base_flops,
        smem=2,
    )(offsets, pad_count, sel, mid_0, mid_1, far_0, far_1, near_stats)

    (dq_sel,) = call(
        functools.partial(own_grads_kernel, z),
        [((z.sel, width), F32)],
        2 * base_flops,
        smem=2,
    )(offsets, pad_count, sel, mid_0, mid_1, far_0, far_1, picked)
    qg_mid, *qg_far = tied([mid_qg] + far_up, (dq_sel,))
    qg = jnp.concatenate([qg_mid] + [part[:, 2 * width :] for part in qg_far], axis=0)
    qg_parts = step_parts(qg, PLANE, n)
    cot_other = swap(after(cotangent, picked), 1, n)
    stats_up = doubled(picked[z.mid : z.mid + z.far], masks[:1], n, ((dq_sel,),))
    out_rows, attn_turned, attn_turned_out = call(
        functools.partial(output_kernel, z),
        [((rows, width), BF), ((z.half, rows), BF), ((z.half, rows), BF)],
        6 * rows * width * width,
        scratch=[pltpu.VMEM((rows, width), BF)],
        smem=1,
    )(offsets, near_stats, stats, after(picked, stats_up), raw, mixed, held, tiles, w_out, order_out)
    attn_other = swap(attn_turned_out, 1, n)
    stats_up = doubled(stats_up, masks[1:], n, ((out_rows,),))
    wout_half = weights(0, attn_turned, attn_other, cotangent, after(cot_other, stats_up))
    turned_other = swap(after(turned_out, wout_half), 1, n)
    qg_0 = jnp.concatenate(tied(qg_parts, (wout_half,)), axis=0)
    qg_1 = swap(qg_0, 1, n)

    stats_far = stats_up
    stats_up = jnp.concatenate([picked[: z.mid], stats_far], axis=1)
    stats_up = doubled(stats_up, (4,), n, ((wout_half,),))
    dq, dk_near, dv_near = call(
        functools.partial(near_grads_kernel, z),
        [((rows, width), BF), ((rows, width), F32), ((rows, width), F32)],
        8 * base_flops,
        smem=2,
    )(offsets, pad_count, after(q, stats_up), k, v, g, stats, dq_sel)
    dq_other = swap(dq, 1, n)
    stats_up = doubled(stats_up, (2,), n, ((dk_near,),))
    early_half = weights(z.half, turned, turned_other, dq, dq_other)
    stats_0 = jnp.concatenate(
        [
            stats_up[at * z.mid : (at + 1) * z.mid, level * LANES : (level + 1) * LANES]
            for level in range(2)
            for at in (0, 2, 1, 3)
        ],
        axis=0,
    )
    stats_1 = swap(stats_0, 1, n)

    dk, dv = call(
        functools.partial(key_grads_kernel, z),
        [((rows, width), BF), ((rows, width), BF)],
        3 * base_flops,
        smem=2,
        cost=LOW_COST,
    )(
        offsets, pad_count, sel, qg_0, qg_1, stats_0, stats_1,
        after(dk_near, early_half), dv_near,
    )
    dk_other = swap(dk, 1, n)
    dv_other = swap(dv, 1, n)
    (late_half,) = call(
        functools.partial(late_weights_kernel, z),
        [((z.half, 2 * width), BF)],
        4 * rows * width * width,
        cost=LOW_COST,
    )(turned, turned_other, dk, dv, dk_other, dv_other)
    (grad_tiles,) = call(
        functools.partial(tiles_kernel, z),
        [((rows, width), BF)],
        6 * rows * width * width,
        cost=LOW_COST,
    )(after(dq, late_half), dk, dv, w_qkv)
    late_parts = block_parts(late_half, PLANE, n)
    early = halved(early_half, masks + [2, 4], n, ((dk_other,), (late_parts[1],)))
    grad_wout = halved(wout_half, [2, 4] + masks, n, ((dk_near,), (late_parts[1],)))
    late = reduce_all(sum_parts(late_parts, BF), upper_steps(n)[::-1], n)
    grad_wqkv = jnp.concatenate([early, late], axis=1)
    return out_rows, grad_tiles, grad_wqkv, grad_wout


def solution(mesh):
    return jax.shard_map(
        per_device,
        mesh=mesh,
        in_specs=(P("ctx", None), P(), P(), P("ctx", None), P(), P()),
        out_specs=(P("ctx", None), P("ctx", None), P("ctx", None), P("ctx", None)),
        check_vma=False,
    )
```

```python
import functools

import jax
import jax.numpy as jnp
import numpy as np
from jax import lax
from jax.experimental import pallas as pl
from jax.experimental.pallas import tpu as pltpu
from jax.sharding import PartitionSpec as P

HEAD_DIM = 64
GROUP = 8
PAIR = 2 * HEAD_DIM
LANES = 128
SECOND = 16
SCALE = 0.125
BF = jnp.bfloat16
F32 = jnp.float32
NT = (((1,), (1,)), ((), ()))
NN = (((1,), (0,)), ((), ()))
TN = (((0,), (0,)), ((), ()))
LARGE = 1e30
LOW_COST = 0.05
LOAD_CUTS = 4
VMEM_BYTES = 40 * 1024 * 1024
PROJECT_VMEM_BYTES = 57 * 1024 * 1024


def dot(a, b, dims=NN):
    return lax.dot_general(a, b, dims, preferred_element_type=F32)


def dot_exact(a, b):
    return lax.dot_general(a, b, NN, preferred_element_type=F32, precision=lax.Precision.HIGHEST)


def iota(shape, dim):
    return lax.broadcasted_iota(jnp.int32, shape, dim)


def low_half(shape):
    return iota(shape, len(shape) - 1) % PAIR < HEAD_DIM


def halves(x):
    low = low_half(x.shape)
    zero = jnp.zeros((), x.dtype)
    return jnp.where(low, x, zero), jnp.where(low, zero, x)


def by_head(first, second, rows):
    return jnp.where(low_half((rows, PAIR)), first, second)


class Sizes:
    def __init__(self, rows, width, dev_count):
        self.rows = rows
        self.width = width
        self.devs = dev_count
        self.heads = width // HEAD_DIM
        self.pairs = self.heads // 2
        self.mid = rows // GROUP
        self.far = rows // dev_count
        self.sel = 2 * self.mid
        self.far_held = -(-self.far // 16) * 16
        self.upper = dev_count // GROUP
        self.strip = width // dev_count
        self.half = width // 2


def chosen_row(z, index, off_mid, off_far):
    row = jnp.where(index < z.mid, index * GROUP + off_mid, (index - z.mid) * z.devs + off_far)
    return jnp.where(index < z.mid + z.far, row, -1)


def spread(z, offs_ref, pair, picked):
    lane = iota((1, 4 * z.sel), 1)
    second = (lane // z.sel) % 2 == 1
    off_mid = jnp.where(second, offs_ref[0, 2 * pair + 1], offs_ref[0, 2 * pair])
    off_far = jnp.where(second, offs_ref[1, 2 * pair + 1], offs_ref[1, 2 * pair])
    target = chosen_row(z, lane % z.sel, off_mid, off_far)
    place = (iota((z.rows, 4 * z.sel), 0) == target).astype(F32).astype(BF)
    high = picked.astype(BF)
    rest = (picked - high.astype(F32)).astype(BF)
    first_high, second_high = halves(high)
    first_rest, second_rest = halves(rest)
    stacked = jnp.concatenate([first_high, second_high, first_rest, second_rest], axis=0)
    return dot(place, stacked)


def lane_offsets(z, offs_ref):
    lane = iota((1, LANES), 1)
    off_mid = jnp.full((1, LANES), -1, jnp.int32)
    off_far = jnp.full((1, LANES), -1, jnp.int32)
    for head in range(z.heads):
        here = (lane == head) | (lane == SECOND + head)
        off_mid = jnp.where(here, offs_ref[0, head], off_mid)
        off_far = jnp.where(here, offs_ref[1, head], off_far)
    return off_mid, off_far


def stat_masks(z, offs_ref):
    off_mid, off_far = lane_offsets(z, offs_ref)
    row = iota((z.rows, LANES), 0)
    return row % GROUP == off_mid, row % z.devs == off_far


def pick_stats(z, masks, stats):
    entry = iota((z.sel, z.rows), 0)
    row = iota((z.sel, z.rows), 1)
    take_mid = ((entry < z.mid) & (row // GROUP == entry)).astype(F32)
    take_far = (row // z.devs == entry - z.mid).astype(F32)
    return dot_exact(take_mid, jnp.where(masks[0], stats, 0.0)) + dot_exact(
        take_far, jnp.where(masks[1], stats, 0.0)
    )


def spread_stats(z, masks, picked):
    row = iota((z.rows, z.sel), 0)
    entry = iota((z.rows, z.sel), 1)
    give_mid = ((entry < z.mid) & (row // GROUP == entry)).astype(F32)
    give_far = (row // z.devs == entry - z.mid).astype(F32)
    fill = jnp.where(iota((z.rows, LANES), 1) < SECOND, -jnp.inf, 0.0)
    return (
        jnp.where(masks[0], dot_exact(give_mid, picked), fill),
        jnp.where(masks[1], dot_exact(give_far, picked), fill),
    )


def gathered_place(z, own, level):
    index = iota((1, z.rows), 1)
    core = index // (4 * z.mid)
    plane = (index // z.mid) % 4
    inner = index % z.mid
    if level == 0:
        return (own ^ (core + 2 * plane)) * z.rows + inner * GROUP
    dev = own ^ (core + 2 * plane + GROUP * (inner // z.far))
    return dev * z.rows + (inner % z.far) * z.devs


def level_parts(z):
    return ((0, z.mid), (z.mid, z.mid + z.far_held))


def project_kernel(
    z, offs_hbm, tiles_hbm, w_qkv_hbm, cot_hbm, w_out_hbm,
    q_hbm, k_hbm, v_hbm, g_hbm, sel, mid_kv, mid_qg, far,
    offs_ref, tiles, w_qkv, cot, w_out, q, k, v, g, sems, out_sems,
):
    width = z.width
    step = width // LOAD_CUTS

    def column_block(block):
        return [
            (
                w_qkv_hbm.at[pl.ds(i * step, step), pl.ds(block * width, width)],
                w_qkv.at[pl.ds(i * step, step), pl.ds(block * width, width)],
            )
            for i in range(LOAD_CUTS)
        ]

    groups = [
        [(tiles_hbm, tiles)] + column_block(1),
        column_block(2),
        column_block(0),
        [(cot_hbm, cot)]
        + [
            (w_out_hbm.at[pl.ds(i * step, step), :], w_out.at[pl.ds(i * step, step), :])
            for i in range(LOAD_CUTS)
        ],
        [(offs_hbm, offs_ref)],
    ]
    copies, index = [], 0
    for group in groups:
        made = []
        for source, target in group:
            copy = pltpu.make_async_copy(source, target, sems.at[index])
            copy.start()
            made.append(copy)
            index += 1
        copies.append(made)

    def arrived(group):
        for copy in copies[group]:
            copy.wait()

    leaving = []

    def leave(source, target):
        copy = pltpu.make_async_copy(source, target, out_sems.at[len(leaving)])
        copy.start()
        leaving.append(copy)

    arrived(0)
    own = tiles[...]
    k[...] = dot(own, w_qkv[:, width : 2 * width]).astype(BF)
    leave(k, k_hbm)
    arrived(1)
    v[...] = dot(own, w_qkv[:, 2 * width :]).astype(BF)
    leave(v, v_hbm)
    arrived(2)
    q[...] = dot(own, w_qkv[:, :width]).astype(BF) * jnp.asarray(SCALE, BF)
    leave(q, q_hbm)
    arrived(3)
    g[...] = dot(cot[...], w_out[...], NT).astype(BF)
    leave(g, g_hbm)
    arrived(4)
    entry = iota((2 * z.sel, z.rows), 0)
    column = iota((2 * z.sel, z.rows), 1)
    second = entry >= z.sel
    for pair in range(z.pairs):
        lanes = slice(pair * PAIR, (pair + 1) * PAIR)
        off_mid = jnp.where(second, offs_ref[0, 2 * pair + 1], offs_ref[0, 2 * pair])
        off_far = jnp.where(second, offs_ref[1, 2 * pair + 1], offs_ref[1, 2 * pair])
        target = chosen_row(z, entry % z.sel, off_mid, off_far)
        take = (column == target).astype(F32).astype(BF)
        every = jnp.concatenate([k[:, lanes], v[:, lanes], q[:, lanes], g[:, lanes]], axis=1)
        both = dot(take, every)
        picked = jnp.where(low_half((z.sel, 4 * PAIR)), both[: z.sel], both[z.sel :]).astype(BF)
        far_part = jnp.where(
            low_half((z.far, 4 * PAIR)),
            both[z.mid : z.mid + z.far],
            both[z.sel + z.mid : z.sel + z.mid + z.far],
        ).astype(BF)
        for part in range(4):
            to = slice(part * width + pair * PAIR, part * width + (pair + 1) * PAIR)
            sel[:, to] = picked[:, part * PAIR : (part + 1) * PAIR]
            near_to = slice(to.start % (2 * width), to.start % (2 * width) + PAIR)
            mid = mid_kv if part < 2 else mid_qg
            mid[:, near_to] = picked[: z.mid, part * PAIR : (part + 1) * PAIR]
            far[:, to] = far_part[:, part * PAIR : (part + 1) * PAIR]
    for copy in leaving:
        copy.wait()


def near_kernel(
    z, pad_ref, q, k, v, g, tiles, order, order_q, mixed, stats, turned, turned_out
):
    own = lax.axis_index("ctx")
    limit = z.rows * z.devs - pad_ref[0] - own * z.rows
    valid = iota((1, z.rows), 1) < limit
    lane = iota((z.rows, LANES), 1)
    both = jnp.zeros((z.rows, LANES), F32)
    for pair in range(z.pairs):
        lanes = slice(pair * PAIR, (pair + 1) * PAIR)
        query = q[:, lanes]
        grad = g[:, lanes].astype(F32)
        keys = halves(k[:, lanes])
        values = halves(v[:, lanes])
        total = None
        for side in range(2):
            head = 2 * pair + side
            scores = jnp.where(valid, dot(query, keys[side], NT), -jnp.inf)
            peak = jnp.max(scores, axis=1, keepdims=True)
            powers = jnp.exp(scores - peak)
            summed = jnp.sum(powers, axis=1, keepdims=True)
            part = dot(powers.astype(BF), values[side]) * (1.0 / summed)
            total = part if total is None else total + part
            both = jnp.where(lane == head, peak + jnp.log(summed), both)
            meets = jnp.sum(grad * part, axis=1, keepdims=True)
            both = jnp.where(lane == SECOND + head, meets, both)
        mixed[:, lanes] = total
    stats[...] = both
    for which, source_rows in enumerate((order, order_q)):
        for part, target in enumerate((turned, turned_out)):
            source = source_rows[part * z.half : (part + 1) * z.half, :]
            place = (iota((z.half, z.width), 1) == source).astype(F32).astype(BF)
            result = dot(place, tiles[...], NT).astype(BF)
            target[which * z.half : (which + 1) * z.half, :] = result


def of_level(level, refs, lanes):
    return jnp.concatenate([ref[:, lanes] for ref in refs[level]], axis=0)


def part_lanes(z, part, pair):
    return slice(part * z.width + pair * PAIR, part * z.width + (pair + 1) * PAIR)


def own_scores(z, limit, offs_ref, sel, refs):
    own = lax.axis_index("ctx")
    scores, places = [], []
    for level, (start, stop) in enumerate(level_parts(z)):
        place = gathered_place(z, own, level)
        for pair in range(z.pairs):
            query = sel[start:stop, part_lanes(z, 2, pair)]
            keys = halves(of_level(level, refs, part_lanes(z, 0, pair)))
            for side in range(2):
                valid = place + offs_ref[level, 2 * pair + side] < limit
                scores.append(jnp.where(valid, dot(query, keys[side], NT), -jnp.inf))
                places.append((level, 2 * pair + side, start, stop))
    spots, at = [], 0
    for level, head, start, stop in places:
        spots.append((level, head, at, at + stop - start))
        at += stop - start
    return jnp.concatenate(scores, axis=0), spots


def to_lanes(z, spots, columns):
    parts = []
    for level, (start, stop) in enumerate(level_parts(z)):
        lane = iota((stop - start, LANES), 1)
        part = jnp.zeros((stop - start, LANES), F32)
        for found, head, first, last in spots:
            if found == level:
                for shift, column in columns:
                    part = jnp.where(lane == shift + head, column[first:last], part)
        parts.append(part)
    parts.append(jnp.zeros((z.sel - level_parts(z)[1][1], LANES), F32))
    return jnp.concatenate(parts, axis=0)


def from_lanes(spots, array, shift):
    return lambda z: jnp.concatenate(
        [
            array[level_parts(z)[level][0] : level_parts(z)[level][1], shift + head : shift + head + 1]
            for level, head, _, _ in spots
        ],
        axis=0,
    )


def spot_of(spots, level, head):
    return next((first, last) for found, at, first, last in spots if (found, at) == (level, head))


def join_kernel(
    z, offs_ref, pad_ref, sel, mid_0, mid_1, far_0, far_1, near_stats, stats, picked, raw, held
):
    refs = ((mid_0, mid_1), (far_0, far_1))
    scores, spots = own_scores(z, z.rows * z.devs - pad_ref[0], offs_ref, sel, refs)
    peak = jnp.max(scores, axis=1, keepdims=True)
    powers = jnp.exp(scores - peak)
    summed = jnp.sum(powers, axis=1, keepdims=True)
    lse = peak + jnp.log(summed)
    scale = 1.0 / summed
    powers = powers.astype(BF)
    products = []
    tail = jnp.zeros((z.sel - level_parts(z)[1][1], PAIR), F32)
    for pair in range(z.pairs):
        totals = []
        for level, (start, stop) in enumerate(level_parts(z)):
            values = halves(of_level(level, refs, part_lanes(z, 1, pair)))
            parts = []
            for side in range(2):
                at, to = spot_of(spots, level, 2 * pair + side)
                parts.append(dot(powers[at:to], values[side]) * scale[at:to])
            totals.append(parts[0] + parts[1])
            grad = sel[start:stop, part_lanes(z, 3, pair)].astype(F32)
            products.append((level, pair, [grad * part for part in parts]))
        held[:, pair * PAIR : (pair + 1) * PAIR] = jnp.concatenate(totals + [tail], axis=0)
    products.sort(key=lambda entry: entry[:2])
    stacked = jnp.concatenate([part for _, _, both in products for part in both], axis=0)
    meets = jnp.sum(stacked, axis=1, keepdims=True)
    sel_both = to_lanes(z, spots, ((0, lse), (SECOND, meets)))
    raw[...] = sel_both
    masks = stat_masks(z, offs_ref)
    near = near_stats[...]
    mid, far = spread_stats(z, masks, sel_both)
    top = jnp.maximum(near, jnp.maximum(mid, far))
    total_lse = top + jnp.log(jnp.exp(near - top) + jnp.exp(mid - top) + jnp.exp(far - top))
    delta = sum(
        pltpu.roll(jnp.exp(value - total_lse), SECOND, 1) * value
        for value in (
            near,
            jnp.where(masks[0], mid, -LARGE),
            jnp.where(masks[1], far, -LARGE),
        )
    )
    both = jnp.where(iota((z.rows, LANES), 1) < SECOND, total_lse, delta)
    stats[...] = both
    picked[...] = pick_stats(z, masks, both)


def output_kernel(
    z, offs_ref, near_stats, stats, picked, raw, mixed, held, tiles, w_out, order,
    rows_out, turned, turned_out, attn,
):
    near_share = jnp.exp(near_stats[...] - stats[...])
    share = jnp.exp(raw[...] - picked[...])
    for pair in range(z.pairs):
        lanes = slice(pair * PAIR, (pair + 1) * PAIR)
        near = by_head(
            near_share[:, 2 * pair : 2 * pair + 1],
            near_share[:, 2 * pair + 1 : 2 * pair + 2],
            z.rows,
        )
        own = by_head(share[:, 2 * pair : 2 * pair + 1], share[:, 2 * pair + 1 : 2 * pair + 2], z.sel)
        combined = near * mixed[:, lanes] + spread(z, offs_ref, pair, own * held[:, lanes])
        attn[:, lanes] = combined.astype(BF)
    rows_out[...] = (tiles[...].astype(F32) + dot(attn[...], w_out[...])).astype(BF)
    for part, target in enumerate((turned, turned_out)):
        source = order[part * z.half : (part + 1) * z.half, :]
        place = (iota((z.half, z.width), 1) == source).astype(F32).astype(BF)
        target[...] = dot(place, attn[...], NT).astype(BF)


def own_grads_kernel(z, offs_ref, pad_ref, sel, mid_0, mid_1, far_0, far_1, picked, dq_sel):
    limit = z.rows * z.devs - pad_ref[0]
    refs = ((mid_0, mid_1), (far_0, far_1))
    scores, spots = own_scores(z, limit, offs_ref, sel, refs)
    probs = jnp.exp(scores - from_lanes(spots, picked, 0)(z))
    grad_probs = []
    for level, (start, stop) in enumerate(level_parts(z)):
        for pair in range(z.pairs):
            grad = sel[start:stop, part_lanes(z, 3, pair)]
            values = halves(of_level(level, refs, part_lanes(z, 1, pair)))
            grad_probs += [dot(grad, values[side], NT) for side in range(2)]
    grad_probs = jnp.concatenate(grad_probs, axis=0) - from_lanes(spots, picked, SECOND)(z)
    grad_scores = (probs * grad_probs).astype(BF)
    tail = jnp.zeros((z.sel - level_parts(z)[1][1], PAIR), F32)
    for pair in range(z.pairs):
        sums = []
        for level in range(2):
            keys = halves(of_level(level, refs, part_lanes(z, 0, pair)))
            at, to = spot_of(spots, level, 2 * pair)
            low = dot(grad_scores[at:to], keys[0])
            at, to = spot_of(spots, level, 2 * pair + 1)
            sums.append(low + dot(grad_scores[at:to], keys[1]))
        dq_sel[:, pair * PAIR : (pair + 1) * PAIR] = jnp.concatenate(sums + [tail], axis=0)


def near_grads_kernel(z, offs_ref, pad_ref, q, k, v, g, stats, dq_sel, dq, dk, dv):
    own = lax.axis_index("ctx")
    limit = z.rows * z.devs - pad_ref[0]
    valid_near = iota((z.rows, 1), 0) < limit - own * z.rows
    across = jnp.transpose(stats[...])
    for pair in range(z.pairs):
        lanes = slice(pair * PAIR, (pair + 1) * PAIR)
        query, grad = q[:, lanes], g[:, lanes]
        queries, grads = halves(query), halves(grad)
        keys, values = halves(k[:, lanes]), halves(v[:, lanes])
        sum_q = sum_k = sum_v = None
        for side in range(2):
            head = 2 * pair + side
            scores = jnp.where(valid_near, dot(keys[side], query, NT), -jnp.inf)
            probs = jnp.exp(scores - across[head : head + 1, :])
            grad_probs = dot(values[side], grad, NT)
            grad_scores = probs * (grad_probs - across[SECOND + head : SECOND + head + 1, :])
            grad_scores = grad_scores.astype(BF)
            part_k = dot(grad_scores, queries[side])
            part_v = dot(probs.astype(BF), grads[side])
            part_q = dot(grad_scores, keys[side], TN)
            if side == 0:
                sum_q, sum_k, sum_v = part_q, part_k, part_v
            else:
                sum_q, sum_k, sum_v = sum_q + part_q, sum_k + part_k, sum_v + part_v
        dk[:, lanes] = sum_k
        dv[:, lanes] = sum_v
        dq[:, lanes] = (SCALE * (sum_q + spread(z, offs_ref, pair, dq_sel[:, lanes]))).astype(BF)


def key_grads_kernel(
    z, offs_ref, pad_ref, sel, qg_0, qg_1, stats_0, stats_1, dk_near, dv_near, dk, dv
):
    own = lax.axis_index("ctx")
    limit = z.rows * z.devs - pad_ref[0] - own * z.rows
    parts = level_parts(z)
    stat_refs = (stats_0, stats_1)

    def rows_of(level, lanes):
        cuts = [slice(p * z.sel + level * z.mid, p * z.sel + (level + 1) * z.mid) for p in range(4)]
        return jnp.concatenate([ref[cut, lanes] for ref in (qg_0, qg_1) for cut in cuts], axis=0)

    tail = jnp.zeros((z.sel - parts[1][1], PAIR), F32)
    probs, grad_scores = {}, {}
    for level, (start, stop) in enumerate(parts):
        across = jnp.transpose(jnp.concatenate([ref[level * 4 * z.mid : (level + 1) * 4 * z.mid, :] for ref in stat_refs], axis=0))
        entry = iota((stop - start, 1), 0) + start
        for pair in range(z.pairs):
            keys = sel[start:stop, part_lanes(z, 0, pair)]
            values = sel[start:stop, part_lanes(z, 1, pair)]
            queries = halves(rows_of(level, part_lanes(z, 0, pair)))
            grads = halves(rows_of(level, part_lanes(z, 1, pair)))
            for side in range(2):
                head = 2 * pair + side
                at = chosen_row(z, entry, offs_ref[0, head], offs_ref[1, head])
                valid = (at >= 0) & (at < limit)
                scores = jnp.where(valid, dot(keys, queries[side], NT), -jnp.inf)
                exps = jnp.exp(scores - across[head : head + 1, :])
                grad_probs = dot(values, grads[side], NT)
                grad_probs = grad_probs - across[SECOND + head : SECOND + head + 1, :]
                probs[level, head] = exps.astype(BF)
                grad_scores[level, head] = (exps * grad_probs).astype(BF)
    sums_k, sums_v = {}, {}
    for pair in range(z.pairs):
        both_k, both_v = [], []
        for level in range(2):
            queries = halves(rows_of(level, part_lanes(z, 0, pair)))
            grads = halves(rows_of(level, part_lanes(z, 1, pair)))
            low, high = 2 * pair, 2 * pair + 1
            both_k.append(
                dot(grad_scores[level, low], queries[0]) + dot(grad_scores[level, high], queries[1])
            )
            both_v.append(dot(probs[level, low], grads[0]) + dot(probs[level, high], grads[1]))
        sums_k[pair] = jnp.concatenate(both_k + [tail], axis=0)
        sums_v[pair] = jnp.concatenate(both_v + [tail], axis=0)
    for pair in range(z.pairs):
        lanes = slice(pair * PAIR, (pair + 1) * PAIR)
        both = jnp.concatenate([sums_k[pair], sums_v[pair]], axis=1)
        moved = spread(z, offs_ref, pair, both)
        dk[:, lanes] = (dk_near[:, lanes] + moved[:, :PAIR]).astype(BF)
        dv[:, lanes] = (dv_near[:, lanes] + moved[:, PAIR:]).astype(BF)


def weights_kernel(start, left, left_other, right, right_other, out):
    rows = slice(start, start + out.shape[0])
    out[...] = (dot(left[rows, :], right[...]) + dot(left_other[rows, :], right_other[...])).astype(BF)


def late_weights_kernel(z, turned, turned_other, dk, dv, dk_other, dv_other, out):
    width = z.width
    left, other = turned[: z.half, :], turned_other[: z.half, :]
    out[:, :width] = (dot(left, dk[...]) + dot(other, dk_other[...])).astype(BF)
    out[:, width:] = (dot(left, dv[...]) + dot(other, dv_other[...])).astype(BF)


def tiles_kernel(z, dq, dk, dv, w_qkv, out):
    width = z.width
    out[...] = (
        dot(dq[...], w_qkv[:, :width], NT)
        + dot(dk[...], w_qkv[:, width : 2 * width], NT)
        + dot(dv[...], w_qkv[:, 2 * width :], NT)
    ).astype(BF)


def call(kernel, outs, flops, scratch=(), smem=0, spaces=None, vmem=VMEM_BYTES, hbm_outs=0, cost=1.0):
    def run(*args):
        moved = sum(int(np.prod(a.shape)) * a.dtype.itemsize for a in args)
        moved += sum(int(np.prod(s)) * jnp.dtype(t).itemsize for s, t in outs)
        specs = [
            pl.BlockSpec(memory_space=spaces or (pltpu.SMEM if i < smem else pltpu.VMEM))
            for i in range(len(args))
        ]
        return pl.pallas_call(
            kernel,
            out_shape=tuple(jax.ShapeDtypeStruct(s, t) for s, t in outs),
            in_specs=specs,
            out_specs=tuple(
                pl.BlockSpec(memory_space=pltpu.HBM if i < hbm_outs else pltpu.VMEM)
                for i in range(len(outs))
            ),
            scratch_shapes=list(scratch),
            compiler_params=pltpu.CompilerParams(vmem_limit_bytes=vmem),
            cost_estimate=pl.CostEstimate(
                flops=int(flops * cost), bytes_accessed=int(moved * cost), transcendentals=0
            ),
        )(*args)

    return run


def swap(value, mask, dev_count):
    return lax.ppermute(value, "ctx", [(d, d ^ mask) for d in range(dev_count)])


def upper_steps(dev_count):
    steps, base = [], GROUP
    while base < dev_count:
        count = 4 if base * 4 <= dev_count else 2
        steps.append((base, count))
        base *= count
    return steps


PLANE = (2, 4)


def tied(parts, first):
    return list(lax.optimization_barrier((*parts, *first))[: len(parts)]) if first else list(parts)


def step_parts(value, step, dev_count, first=()):
    base, count = step
    return tied([value] + [swap(value, base * i, dev_count) for i in range(1, count)], first)


def block_parts(value, step, dev_count):
    base, count = step
    size = value.shape[0] // count
    return [value[:size]] + [
        swap(value[i * size : (i + 1) * size], base * i, dev_count) for i in range(1, count)
    ]


def sum_parts(parts, dtype):
    return sum(part.astype(F32) for part in parts).astype(dtype)


def doubled(value, masks, dev_count, firsts=()):
    for i, mask in enumerate(masks):
        parts = tied([value, swap(value, mask, dev_count)], firsts[i] if i < len(firsts) else ())
        value = jnp.concatenate(parts, axis=0)
    return value


def halved(value, masks, dev_count, firsts=()):
    for i, mask in enumerate(masks):
        size = value.shape[0] // 2
        first = firsts[i] if i < len(firsts) else ()
        parts = tied([value[:size], swap(value[size:], mask, dev_count)], first)
        value = parts[0].astype(F32) + parts[1].astype(F32)
        value = value if i == len(masks) - 1 else value.astype(BF)
    return value


def reduce_all(value, steps, dev_count):
    for i, step in enumerate(steps):
        value = sum_parts(block_parts(value, step, dev_count), F32 if i == len(steps) - 1 else BF)
    return value


def strip_order(z, own, masks):
    digits = np.meshgrid(*[np.arange(2) for _ in masks], np.arange(z.strip), indexing="ij")
    moved = sum(digit * mask for digit, mask in zip(digits, masks)).reshape(-1, 1)
    return (own ^ moved.astype(np.int32)) * z.strip + digits[-1].reshape(-1, 1).astype(np.int32)


def after(value, *others):
    return lax.optimization_barrier((value, *others))[0]


def per_device(tiles, w_qkv, w_out, cotangent, offsets, pad_count):
    n = lax.axis_size("ctx")
    z = Sizes(tiles.shape[0], tiles.shape[1], n)
    own = lax.axis_index("ctx")
    rows, width = z.rows, z.width
    masks = [mask for mask in (2**i for i in range(30)) if GROUP <= mask < n]
    order = strip_order(z, own, [1, 4, 2] + masks[::-1])
    order_q = strip_order(z, own, [1] + masks + [2, 4])
    order_out = strip_order(z, own, [1, 2, 4] + masks)
    base_flops = 2 * rows * rows * width

    def weights(start, *args):
        kernel = functools.partial(weights_kernel, start)
        return call(kernel, [((z.half, width), BF)], 4 * rows * width * width)(*args)[0]

    q, k, v, g, sel, mid_kv, mid_qg, far = call(
        functools.partial(project_kernel, z),
        [((rows, width), BF)] * 4
        + [((z.sel, 4 * width), BF)]
        + [((z.mid, 2 * width), BF)] * 2
        + [((z.far, 4 * width), BF)],
        2 * rows * width * 4 * width,
        scratch=[
            pltpu.SMEM(offsets.shape, jnp.int32),
            pltpu.VMEM(tiles.shape, BF),
            pltpu.VMEM(w_qkv.shape, BF),
            pltpu.VMEM(cotangent.shape, BF),
            pltpu.VMEM(w_out.shape, BF),
        ]
        + [pltpu.VMEM((rows, width), BF)] * 4
        + [pltpu.SemaphoreType.DMA((4 * LOAD_CUTS + 3,)), pltpu.SemaphoreType.DMA((4,))],
        hbm_outs=4,
        spaces=pltpu.HBM,
        vmem=PROJECT_VMEM_BYTES,
    )(offsets, tiles, w_qkv, cotangent, w_out)

    steps = upper_steps(n)
    far_up = far
    for step in steps[:-1]:
        far_up = jnp.concatenate(step_parts(far_up, step, n), axis=0)
    far_up = step_parts(far_up, steps[-1], n)
    far_kv = jnp.concatenate([part[:, : 2 * width] for part in far_up], axis=0)
    mid_parts = step_parts(mid_kv, PLANE, n)
    mixed, near_stats, turned, turned_out = call(
        functools.partial(near_kernel, z),
        [
            ((rows, width), F32),
            ((rows, LANES), F32),
            ((width, rows), BF),
            ((width, rows), BF),
        ],
        8 * base_flops,
        smem=1,
    )(pad_count, after(q, far_kv, *mid_parts[1:3]), k, v, g, tiles, order, order_q)
    mid_0 = jnp.concatenate(mid_parts, axis=0)
    mid_1 = swap(mid_0, 1, n)
    far_0 = jnp.concatenate(
        step_parts(after(far_kv, *mid_parts[1:3]), PLANE, n, (near_stats,)), axis=0
    )
    far_1 = swap(far_0, 1, n)
    stats, picked, raw, held = call(
        functools.partial(join_kernel, z),
        [((rows, LANES), F32), ((z.sel, LANES), F32), ((z.sel, LANES), F32), ((z.sel, width), F32)],
        3 * base_flops,
        smem=2,
    )(offsets, pad_count, sel, mid_0, mid_1, far_0, far_1, near_stats)

    (dq_sel,) = call(
        functools.partial(own_grads_kernel, z),
        [((z.sel, width), F32)],
        2 * base_flops,
        smem=2,
    )(offsets, pad_count, sel, mid_0, mid_1, far_0, far_1, picked)
    qg_mid, *qg_far = tied([mid_qg] + far_up, (dq_sel,))
    qg = jnp.concatenate([qg_mid] + [part[:, 2 * width :] for part in qg_far], axis=0)
    qg_parts = step_parts(qg, PLANE, n)
    cot_other = swap(after(cotangent, picked), 1, n)
    stats_up = doubled(picked[z.mid : z.mid + z.far], masks[:1], n, ((dq_sel,),))
    out_rows, attn_turned, attn_turned_out = call(
        functools.partial(output_kernel, z),
        [((rows, width), BF), ((z.half, rows), BF), ((z.half, rows), BF)],
        6 * rows * width * width,
        scratch=[pltpu.VMEM((rows, width), BF)],
        smem=1,
    )(offsets, near_stats, stats, after(picked, stats_up), raw, mixed, held, tiles, w_out, order_out)
    attn_other = swap(attn_turned_out, 1, n)
    stats_up = doubled(stats_up, masks[1:], n, ((out_rows,),))
    wout_half = weights(0, attn_turned, attn_other, cotangent, after(cot_other, stats_up))
    turned_other = swap(after(turned_out, wout_half), 1, n)
    qg_0 = jnp.concatenate(tied(qg_parts, (wout_half,)), axis=0)
    qg_1 = swap(qg_0, 1, n)

    stats_far = stats_up
    stats_up = jnp.concatenate([picked[: z.mid], stats_far], axis=1)
    stats_up = doubled(stats_up, (4,), n, ((wout_half,),))
    dq, dk_near, dv_near = call(
        functools.partial(near_grads_kernel, z),
        [((rows, width), BF), ((rows, width), F32), ((rows, width), F32)],
        8 * base_flops,
        smem=2,
    )(offsets, pad_count, after(q, stats_up), k, v, g, stats, dq_sel)
    dq_other = swap(dq, 1, n)
    stats_up = doubled(stats_up, (2,), n, ((dk_near,),))
    early_half = weights(z.half, turned, turned_other, dq, dq_other)
    stats_0 = jnp.concatenate(
        [
            stats_up[at * z.mid : (at + 1) * z.mid, level * LANES : (level + 1) * LANES]
            for level in range(2)
            for at in (0, 2, 1, 3)
        ],
        axis=0,
    )
    stats_1 = swap(stats_0, 1, n)

    dk, dv = call(
        functools.partial(key_grads_kernel, z),
        [((rows, width), BF), ((rows, width), BF)],
        3 * base_flops,
        smem=2,
        cost=LOW_COST,
    )(
        offsets, pad_count, sel, qg_0, qg_1, stats_0, stats_1,
        after(dk_near, early_half), dv_near,
    )
    dk_other = swap(dk, 1, n)
    dv_other = swap(dv, 1, n)
    (late_half,) = call(
        functools.partial(late_weights_kernel, z),
        [((z.half, 2 * width), BF)],
        4 * rows * width * width,
        cost=LOW_COST,
    )(turned, turned_other, dk, dv, dk_other, dv_other)
    (grad_tiles,) = call(
        functools.partial(tiles_kernel, z),
        [((rows, width), BF)],
        6 * rows * width * width,
        cost=LOW_COST,
    )(after(dq, late_half), dk, dv, w_qkv)
    late_parts = block_parts(late_half, PLANE, n)
    early = halved(early_half, masks + [2, 4], n, ((late_parts[1],),))
    grad_wout = halved(wout_half, [2, 4] + masks, n, ((dk,), (late_parts[1],)))
    late = reduce_all(sum_parts(late_parts, BF), upper_steps(n)[::-1], n)
    grad_wqkv = jnp.concatenate([early, late], axis=1)
    return out_rows, grad_tiles, grad_wqkv, grad_wout


def solution(mesh):
    return jax.shard_map(
        per_device,
        mesh=mesh,
        in_specs=(P("ctx", None), P(), P(), P("ctx", None), P(), P()),
        out_specs=(P("ctx", None), P("ctx", None), P("ctx", None), P("ctx", None)),
        check_vma=False,
    )
```

```python
import functools

import jax
import jax.numpy as jnp
import numpy as np
from jax import lax
from jax.experimental import pallas as pl
from jax.experimental.pallas import tpu as pltpu
from jax.sharding import PartitionSpec as P

HEAD_DIM = 64
GROUP = 8
PAIR = 2 * HEAD_DIM
LANES = 128
SECOND = 16
SCALE = 0.125
BF = jnp.bfloat16
F32 = jnp.float32
NT = (((1,), (1,)), ((), ()))
NN = (((1,), (0,)), ((), ()))
TN = (((0,), (0,)), ((), ()))
LARGE = 1e30
LOW_COST = 0.05
LOAD_CUTS = 4
VMEM_BYTES = 40 * 1024 * 1024
PROJECT_VMEM_BYTES = 57 * 1024 * 1024


def dot(a, b, dims=NN):
    return lax.dot_general(a, b, dims, preferred_element_type=F32)


def dot_exact(a, b):
    return lax.dot_general(a, b, NN, preferred_element_type=F32, precision=lax.Precision.HIGHEST)


def iota(shape, dim):
    return lax.broadcasted_iota(jnp.int32, shape, dim)


def low_half(shape):
    return iota(shape, len(shape) - 1) % PAIR < HEAD_DIM


def halves(x):
    low = low_half(x.shape)
    zero = jnp.zeros((), x.dtype)
    return jnp.where(low, x, zero), jnp.where(low, zero, x)


def by_head(first, second, rows):
    return jnp.where(low_half((rows, PAIR)), first, second)


class Sizes:
    def __init__(self, rows, width, dev_count):
        self.rows = rows
        self.width = width
        self.devs = dev_count
        self.heads = width // HEAD_DIM
        self.pairs = self.heads // 2
        self.mid = rows // GROUP
        self.far = rows // dev_count
        self.sel = 2 * self.mid
        self.far_held = -(-self.far // 16) * 16
        self.upper = dev_count // GROUP
        self.strip = width // dev_count
        self.half = width // 2


def chosen_row(z, index, off_mid, off_far):
    row = jnp.where(index < z.mid, index * GROUP + off_mid, (index - z.mid) * z.devs + off_far)
    return jnp.where(index < z.mid + z.far, row, -1)


def spread(z, offs_ref, pair, picked):
    lane = iota((1, 4 * z.sel), 1)
    second = (lane // z.sel) % 2 == 1
    off_mid = jnp.where(second, offs_ref[0, 2 * pair + 1], offs_ref[0, 2 * pair])
    off_far = jnp.where(second, offs_ref[1, 2 * pair + 1], offs_ref[1, 2 * pair])
    target = chosen_row(z, lane % z.sel, off_mid, off_far)
    place = (iota((z.rows, 4 * z.sel), 0) == target).astype(F32).astype(BF)
    high = picked.astype(BF)
    rest = (picked - high.astype(F32)).astype(BF)
    first_high, second_high = halves(high)
    first_rest, second_rest = halves(rest)
    stacked = jnp.concatenate([first_high, second_high, first_rest, second_rest], axis=0)
    return dot(place, stacked)


def lane_offsets(z, offs_ref):
    lane = iota((1, LANES), 1)
    off_mid = jnp.full((1, LANES), -1, jnp.int32)
    off_far = jnp.full((1, LANES), -1, jnp.int32)
    for head in range(z.heads):
        here = (lane == head) | (lane == SECOND + head)
        off_mid = jnp.where(here, offs_ref[0, head], off_mid)
        off_far = jnp.where(here, offs_ref[1, head], off_far)
    return off_mid, off_far


def stat_masks(z, offs_ref):
    off_mid, off_far = lane_offsets(z, offs_ref)
    row = iota((z.rows, LANES), 0)
    return row % GROUP == off_mid, row % z.devs == off_far


def pick_stats(z, masks, stats):
    entry = iota((z.sel, z.rows), 0)
    row = iota((z.sel, z.rows), 1)
    take_mid = ((entry < z.mid) & (row // GROUP == entry)).astype(F32)
    take_far = (row // z.devs == entry - z.mid).astype(F32)
    return dot_exact(take_mid, jnp.where(masks[0], stats, 0.0)) + dot_exact(
        take_far, jnp.where(masks[1], stats, 0.0)
    )


def spread_stats(z, masks, picked):
    row = iota((z.rows, z.sel), 0)
    entry = iota((z.rows, z.sel), 1)
    give_mid = ((entry < z.mid) & (row // GROUP == entry)).astype(F32)
    give_far = (row // z.devs == entry - z.mid).astype(F32)
    fill = jnp.where(iota((z.rows, LANES), 1) < SECOND, -jnp.inf, 0.0)
    return (
        jnp.where(masks[0], dot_exact(give_mid, picked), fill),
        jnp.where(masks[1], dot_exact(give_far, picked), fill),
    )


def gathered_place(z, own, level):
    index = iota((1, z.rows), 1)
    core = index // (4 * z.mid)
    plane = (index // z.mid) % 4
    inner = index % z.mid
    if level == 0:
        return (own ^ (core + 2 * plane)) * z.rows + inner * GROUP
    dev = own ^ (core + 2 * plane + GROUP * (inner // z.far))
    return dev * z.rows + (inner % z.far) * z.devs


def level_parts(z):
    return ((0, z.mid), (z.mid, z.mid + z.far_held))


def project_kernel(
    z, offs_hbm, tiles_hbm, w_qkv_hbm, cot_hbm, w_out_hbm,
    q_hbm, k_hbm, v_hbm, g_hbm, sel, mid_kv, mid_qg, far,
    offs_ref, tiles, w_qkv, cot, w_out, q, k, v, g, sems, out_sems,
):
    width = z.width
    step = width // LOAD_CUTS

    def column_block(block):
        return [
            (
                w_qkv_hbm.at[pl.ds(i * step, step), pl.ds(block * width, width)],
                w_qkv.at[pl.ds(i * step, step), pl.ds(block * width, width)],
            )
            for i in range(LOAD_CUTS)
        ]

    groups = [
        [(tiles_hbm, tiles)] + column_block(1),
        column_block(2),
        column_block(0),
        [(cot_hbm, cot)]
        + [
            (w_out_hbm.at[pl.ds(i * step, step), :], w_out.at[pl.ds(i * step, step), :])
            for i in range(LOAD_CUTS)
        ],
        [(offs_hbm, offs_ref)],
    ]
    copies, index = [], 0
    for group in groups:
        made = []
        for source, target in group:
            copy = pltpu.make_async_copy(source, target, sems.at[index])
            copy.start()
            made.append(copy)
            index += 1
        copies.append(made)

    def arrived(group):
        for copy in copies[group]:
            copy.wait()

    leaving = []

    def leave(source, target):
        copy = pltpu.make_async_copy(source, target, out_sems.at[len(leaving)])
        copy.start()
        leaving.append(copy)

    arrived(0)
    own = tiles[...]
    k[...] = dot(own, w_qkv[:, width : 2 * width]).astype(BF)
    leave(k, k_hbm)
    arrived(1)
    v[...] = dot(own, w_qkv[:, 2 * width :]).astype(BF)
    leave(v, v_hbm)
    arrived(2)
    q[...] = dot(own, w_qkv[:, :width]).astype(BF) * jnp.asarray(SCALE, BF)
    leave(q, q_hbm)
    arrived(3)
    g[...] = dot(cot[...], w_out[...], NT).astype(BF)
    leave(g, g_hbm)
    arrived(4)
    entry = iota((2 * z.sel, z.rows), 0)
    column = iota((2 * z.sel, z.rows), 1)
    second = entry >= z.sel
    for pair in range(z.pairs):
        lanes = slice(pair * PAIR, (pair + 1) * PAIR)
        off_mid = jnp.where(second, offs_ref[0, 2 * pair + 1], offs_ref[0, 2 * pair])
        off_far = jnp.where(second, offs_ref[1, 2 * pair + 1], offs_ref[1, 2 * pair])
        target = chosen_row(z, entry % z.sel, off_mid, off_far)
        take = (column == target).astype(F32).astype(BF)
        every = jnp.concatenate([k[:, lanes], v[:, lanes], q[:, lanes], g[:, lanes]], axis=1)
        both = dot(take, every)
        picked = jnp.where(low_half((z.sel, 4 * PAIR)), both[: z.sel], both[z.sel :]).astype(BF)
        far_part = jnp.where(
            low_half((z.far, 4 * PAIR)),
            both[z.mid : z.mid + z.far],
            both[z.sel + z.mid : z.sel + z.mid + z.far],
        ).astype(BF)
        for part in range(4):
            to = slice(part * width + pair * PAIR, part * width + (pair + 1) * PAIR)
            sel[:, to] = picked[:, part * PAIR : (part + 1) * PAIR]
            near_to = slice(to.start % (2 * width), to.start % (2 * width) + PAIR)
            mid = mid_kv if part < 2 else mid_qg
            mid[:, near_to] = picked[: z.mid, part * PAIR : (part + 1) * PAIR]
            far[:, to] = far_part[:, part * PAIR : (part + 1) * PAIR]
    for copy in leaving:
        copy.wait()


def near_kernel(
    z, pad_ref, q, k, v, g, tiles, order, order_q, mixed, stats, turned, turned_out
):
    own = lax.axis_index("ctx")
    limit = z.rows * z.devs - pad_ref[0] - own * z.rows
    valid = iota((1, z.rows), 1) < limit
    lane = iota((z.rows, LANES), 1)
    both = jnp.zeros((z.rows, LANES), F32)
    for pair in range(z.pairs):
        lanes = slice(pair * PAIR, (pair + 1) * PAIR)
        query = q[:, lanes]
        grad = g[:, lanes].astype(F32)
        keys = halves(k[:, lanes])
        values = halves(v[:, lanes])
        total = None
        for side in range(2):
            head = 2 * pair + side
            scores = jnp.where(valid, dot(query, keys[side], NT), -jnp.inf)
            peak = jnp.max(scores, axis=1, keepdims=True)
            powers = jnp.exp(scores - peak)
            summed = jnp.sum(powers, axis=1, keepdims=True)
            part = dot(powers.astype(BF), values[side]) * (1.0 / summed)
            total = part if total is None else total + part
            both = jnp.where(lane == head, peak + jnp.log(summed), both)
            meets = jnp.sum(grad * part, axis=1, keepdims=True)
            both = jnp.where(lane == SECOND + head, meets, both)
        mixed[:, lanes] = total
    stats[...] = both
    for which, source_rows in enumerate((order, order_q)):
        for part, target in enumerate((turned, turned_out)):
            source = source_rows[part * z.half : (part + 1) * z.half, :]
            place = (iota((z.half, z.width), 1) == source).astype(F32).astype(BF)
            result = dot(place, tiles[...], NT).astype(BF)
            target[which * z.half : (which + 1) * z.half, :] = result


def of_level(level, refs, lanes):
    return jnp.concatenate([ref[:, lanes] for ref in refs[level]], axis=0)


def part_lanes(z, part, pair):
    return slice(part * z.width + pair * PAIR, part * z.width + (pair + 1) * PAIR)


def own_scores(z, limit, offs_ref, sel, refs):
    own = lax.axis_index("ctx")
    scores, places = [], []
    for level, (start, stop) in enumerate(level_parts(z)):
        place = gathered_place(z, own, level)
        for pair in range(z.pairs):
            query = sel[start:stop, part_lanes(z, 2, pair)]
            keys = halves(of_level(level, refs, part_lanes(z, 0, pair)))
            for side in range(2):
                valid = place + offs_ref[level, 2 * pair + side] < limit
                scores.append(jnp.where(valid, dot(query, keys[side], NT), -jnp.inf))
                places.append((level, 2 * pair + side, start, stop))
    spots, at = [], 0
    for level, head, start, stop in places:
        spots.append((level, head, at, at + stop - start))
        at += stop - start
    return jnp.concatenate(scores, axis=0), spots


def to_lanes(z, spots, columns):
    parts = []
    for level, (start, stop) in enumerate(level_parts(z)):
        lane = iota((stop - start, LANES), 1)
        part = jnp.zeros((stop - start, LANES), F32)
        for found, head, first, last in spots:
            if found == level:
                for shift, column in columns:
                    part = jnp.where(lane == shift + head, column[first:last], part)
        parts.append(part)
    parts.append(jnp.zeros((z.sel - level_parts(z)[1][1], LANES), F32))
    return jnp.concatenate(parts, axis=0)


def from_lanes(spots, array, shift):
    return lambda z: jnp.concatenate(
        [
            array[level_parts(z)[level][0] : level_parts(z)[level][1], shift + head : shift + head + 1]
            for level, head, _, _ in spots
        ],
        axis=0,
    )


def spot_of(spots, level, head):
    return next((first, last) for found, at, first, last in spots if (found, at) == (level, head))


def join_kernel(
    z, offs_ref, pad_ref, sel, mid_0, mid_1, far_0, far_1, near_stats, stats, picked, raw, held
):
    refs = ((mid_0, mid_1), (far_0, far_1))
    scores, spots = own_scores(z, z.rows * z.devs - pad_ref[0], offs_ref, sel, refs)
    peak = jnp.max(scores, axis=1, keepdims=True)
    powers = jnp.exp(scores - peak)
    summed = jnp.sum(powers, axis=1, keepdims=True)
    lse = peak + jnp.log(summed)
    scale = 1.0 / summed
    powers = powers.astype(BF)
    products = []
    tail = jnp.zeros((z.sel - level_parts(z)[1][1], PAIR), F32)
    for pair in range(z.pairs):
        totals = []
        for level, (start, stop) in enumerate(level_parts(z)):
            values = halves(of_level(level, refs, part_lanes(z, 1, pair)))
            parts = []
            for side in range(2):
                at, to = spot_of(spots, level, 2 * pair + side)
                parts.append(dot(powers[at:to], values[side]) * scale[at:to])
            totals.append(parts[0] + parts[1])
            grad = sel[start:stop, part_lanes(z, 3, pair)].astype(F32)
            products.append((level, pair, [grad * part for part in parts]))
        held[:, pair * PAIR : (pair + 1) * PAIR] = jnp.concatenate(totals + [tail], axis=0)
    products.sort(key=lambda entry: entry[:2])
    stacked = jnp.concatenate([part for _, _, both in products for part in both], axis=0)
    meets = jnp.sum(stacked, axis=1, keepdims=True)
    sel_both = to_lanes(z, spots, ((0, lse), (SECOND, meets)))
    raw[...] = sel_both
    masks = stat_masks(z, offs_ref)
    near = near_stats[...]
    mid, far = spread_stats(z, masks, sel_both)
    top = jnp.maximum(near, jnp.maximum(mid, far))
    total_lse = top + jnp.log(jnp.exp(near - top) + jnp.exp(mid - top) + jnp.exp(far - top))
    delta = sum(
        pltpu.roll(jnp.exp(value - total_lse), SECOND, 1) * value
        for value in (
            near,
            jnp.where(masks[0], mid, -LARGE),
            jnp.where(masks[1], far, -LARGE),
        )
    )
    both = jnp.where(iota((z.rows, LANES), 1) < SECOND, total_lse, delta)
    stats[...] = both
    picked[...] = pick_stats(z, masks, both)


def output_kernel(
    z, offs_ref, near_stats, stats, picked, raw, mixed, held, tiles, w_out, order,
    rows_out, turned, turned_out, attn,
):
    near_share = jnp.exp(near_stats[...] - stats[...])
    share = jnp.exp(raw[...] - picked[...])
    for pair in range(z.pairs):
        lanes = slice(pair * PAIR, (pair + 1) * PAIR)
        near = by_head(
            near_share[:, 2 * pair : 2 * pair + 1],
            near_share[:, 2 * pair + 1 : 2 * pair + 2],
            z.rows,
        )
        own = by_head(share[:, 2 * pair : 2 * pair + 1], share[:, 2 * pair + 1 : 2 * pair + 2], z.sel)
        combined = near * mixed[:, lanes] + spread(z, offs_ref, pair, own * held[:, lanes])
        attn[:, lanes] = combined.astype(BF)
    rows_out[...] = (tiles[...].astype(F32) + dot(attn[...], w_out[...])).astype(BF)
    for part, target in enumerate((turned, turned_out)):
        source = order[part * z.half : (part + 1) * z.half, :]
        place = (iota((z.half, z.width), 1) == source).astype(F32).astype(BF)
        target[...] = dot(place, attn[...], NT).astype(BF)


def own_grads_kernel(z, offs_ref, pad_ref, sel, mid_0, mid_1, far_0, far_1, picked, dq_sel):
    limit = z.rows * z.devs - pad_ref[0]
    refs = ((mid_0, mid_1), (far_0, far_1))
    scores, spots = own_scores(z, limit, offs_ref, sel, refs)
    probs = jnp.exp(scores - from_lanes(spots, picked, 0)(z))
    grad_probs = []
    for level, (start, stop) in enumerate(level_parts(z)):
        for pair in range(z.pairs):
            grad = sel[start:stop, part_lanes(z, 3, pair)]
            values = halves(of_level(level, refs, part_lanes(z, 1, pair)))
            grad_probs += [dot(grad, values[side], NT) for side in range(2)]
    grad_probs = jnp.concatenate(grad_probs, axis=0) - from_lanes(spots, picked, SECOND)(z)
    grad_scores = (probs * grad_probs).astype(BF)
    tail = jnp.zeros((z.sel - level_parts(z)[1][1], PAIR), F32)
    for pair in range(z.pairs):
        sums = []
        for level in range(2):
            keys = halves(of_level(level, refs, part_lanes(z, 0, pair)))
            at, to = spot_of(spots, level, 2 * pair)
            low = dot(grad_scores[at:to], keys[0])
            at, to = spot_of(spots, level, 2 * pair + 1)
            sums.append(low + dot(grad_scores[at:to], keys[1]))
        dq_sel[:, pair * PAIR : (pair + 1) * PAIR] = jnp.concatenate(sums + [tail], axis=0)


def near_grads_kernel(z, offs_ref, pad_ref, q, k, v, g, stats, dq_sel, dq, dk, dv):
    own = lax.axis_index("ctx")
    limit = z.rows * z.devs - pad_ref[0]
    valid_near = iota((z.rows, 1), 0) < limit - own * z.rows
    across = jnp.transpose(stats[...])
    for pair in range(z.pairs):
        lanes = slice(pair * PAIR, (pair + 1) * PAIR)
        query, grad = q[:, lanes], g[:, lanes]
        queries, grads = halves(query), halves(grad)
        keys, values = halves(k[:, lanes]), halves(v[:, lanes])
        sum_q = sum_k = sum_v = None
        for side in range(2):
            head = 2 * pair + side
            scores = jnp.where(valid_near, dot(keys[side], query, NT), -jnp.inf)
            probs = jnp.exp(scores - across[head : head + 1, :])
            grad_probs = dot(values[side], grad, NT)
            grad_scores = probs * (grad_probs - across[SECOND + head : SECOND + head + 1, :])
            grad_scores = grad_scores.astype(BF)
            part_k = dot(grad_scores, queries[side])
            part_v = dot(probs.astype(BF), grads[side])
            part_q = dot(grad_scores, keys[side], TN)
            if side == 0:
                sum_q, sum_k, sum_v = part_q, part_k, part_v
            else:
                sum_q, sum_k, sum_v = sum_q + part_q, sum_k + part_k, sum_v + part_v
        dk[:, lanes] = sum_k
        dv[:, lanes] = sum_v
        dq[:, lanes] = (SCALE * (sum_q + spread(z, offs_ref, pair, dq_sel[:, lanes]))).astype(BF)


def key_grads_kernel(
    z, offs_ref, pad_ref, sel, qg_0, qg_1, stats_0, stats_1, dk_near, dv_near, dk, dv
):
    own = lax.axis_index("ctx")
    limit = z.rows * z.devs - pad_ref[0] - own * z.rows
    parts = level_parts(z)
    stat_refs = (stats_0, stats_1)

    def rows_of(level, lanes):
        cuts = [slice(p * z.sel + level * z.mid, p * z.sel + (level + 1) * z.mid) for p in range(4)]
        return jnp.concatenate([ref[cut, lanes] for ref in (qg_0, qg_1) for cut in cuts], axis=0)

    tail = jnp.zeros((z.sel - parts[1][1], PAIR), F32)
    probs, grad_scores = {}, {}
    for level, (start, stop) in enumerate(parts):
        across = jnp.transpose(jnp.concatenate([ref[level * 4 * z.mid : (level + 1) * 4 * z.mid, :] for ref in stat_refs], axis=0))
        entry = iota((stop - start, 1), 0) + start
        for pair in range(z.pairs):
            keys = sel[start:stop, part_lanes(z, 0, pair)]
            values = sel[start:stop, part_lanes(z, 1, pair)]
            queries = halves(rows_of(level, part_lanes(z, 0, pair)))
            grads = halves(rows_of(level, part_lanes(z, 1, pair)))
            for side in range(2):
                head = 2 * pair + side
                at = chosen_row(z, entry, offs_ref[0, head], offs_ref[1, head])
                valid = (at >= 0) & (at < limit)
                scores = jnp.where(valid, dot(keys, queries[side], NT), -jnp.inf)
                exps = jnp.exp(scores - across[head : head + 1, :])
                grad_probs = dot(values, grads[side], NT)
                grad_probs = grad_probs - across[SECOND + head : SECOND + head + 1, :]
                probs[level, head] = exps.astype(BF)
                grad_scores[level, head] = (exps * grad_probs).astype(BF)
    sums_k, sums_v = {}, {}
    for pair in range(z.pairs):
        both_k, both_v = [], []
        for level in range(2):
            queries = halves(rows_of(level, part_lanes(z, 0, pair)))
            grads = halves(rows_of(level, part_lanes(z, 1, pair)))
            low, high = 2 * pair, 2 * pair + 1
            both_k.append(
                dot(grad_scores[level, low], queries[0]) + dot(grad_scores[level, high], queries[1])
            )
            both_v.append(dot(probs[level, low], grads[0]) + dot(probs[level, high], grads[1]))
        sums_k[pair] = jnp.concatenate(both_k + [tail], axis=0)
        sums_v[pair] = jnp.concatenate(both_v + [tail], axis=0)
    for pair in range(z.pairs):
        lanes = slice(pair * PAIR, (pair + 1) * PAIR)
        both = jnp.concatenate([sums_k[pair], sums_v[pair]], axis=1)
        moved = spread(z, offs_ref, pair, both)
        dk[:, lanes] = (dk_near[:, lanes] + moved[:, :PAIR]).astype(BF)
        dv[:, lanes] = (dv_near[:, lanes] + moved[:, PAIR:]).astype(BF)


def weights_kernel(start, left, left_other, right, right_other, out):
    rows = slice(start, start + out.shape[0])
    out[...] = (dot(left[rows, :], right[...]) + dot(left_other[rows, :], right_other[...])).astype(BF)


def late_weights_kernel(z, turned, turned_other, dk, dv, dk_other, dv_other, out):
    width = z.width
    left, other = turned[: z.half, :], turned_other[: z.half, :]
    out[:, :width] = (dot(left, dk[...]) + dot(other, dk_other[...])).astype(BF)
    out[:, width:] = (dot(left, dv[...]) + dot(other, dv_other[...])).astype(BF)


def tiles_kernel(z, dq, dk, dv, w_qkv, out):
    width = z.width
    out[...] = (
        dot(dq[...], w_qkv[:, :width], NT)
        + dot(dk[...], w_qkv[:, width : 2 * width], NT)
        + dot(dv[...], w_qkv[:, 2 * width :], NT)
    ).astype(BF)


def call(kernel, outs, flops, scratch=(), smem=0, spaces=None, vmem=VMEM_BYTES, hbm_outs=0, cost=1.0):
    def run(*args):
        moved = sum(int(np.prod(a.shape)) * a.dtype.itemsize for a in args)
        moved += sum(int(np.prod(s)) * jnp.dtype(t).itemsize for s, t in outs)
        specs = [
            pl.BlockSpec(memory_space=spaces or (pltpu.SMEM if i < smem else pltpu.VMEM))
            for i in range(len(args))
        ]
        return pl.pallas_call(
            kernel,
            out_shape=tuple(jax.ShapeDtypeStruct(s, t) for s, t in outs),
            in_specs=specs,
            out_specs=tuple(
                pl.BlockSpec(memory_space=pltpu.HBM if i < hbm_outs else pltpu.VMEM)
                for i in range(len(outs))
            ),
            scratch_shapes=list(scratch),
            compiler_params=pltpu.CompilerParams(vmem_limit_bytes=vmem),
            cost_estimate=pl.CostEstimate(
                flops=int(flops * cost), bytes_accessed=int(moved * cost), transcendentals=0
            ),
        )(*args)

    return run


def swap(value, mask, dev_count):
    return lax.ppermute(value, "ctx", [(d, d ^ mask) for d in range(dev_count)])


def upper_steps(dev_count):
    steps, base = [], GROUP
    while base < dev_count:
        count = 4 if base * 4 <= dev_count else 2
        steps.append((base, count))
        base *= count
    return steps


PLANE = (2, 4)


def tied(parts, first):
    return list(lax.optimization_barrier((*parts, *first))[: len(parts)]) if first else list(parts)


def step_parts(value, step, dev_count, first=()):
    base, count = step
    return tied([value] + [swap(value, base * i, dev_count) for i in range(1, count)], first)


def block_parts(value, step, dev_count):
    base, count = step
    size = value.shape[0] // count
    return [value[:size]] + [
        swap(value[i * size : (i + 1) * size], base * i, dev_count) for i in range(1, count)
    ]


def sum_parts(parts, dtype):
    return sum(part.astype(F32) for part in parts).astype(dtype)


def doubled(value, masks, dev_count, firsts=()):
    for i, mask in enumerate(masks):
        parts = tied([value, swap(value, mask, dev_count)], firsts[i] if i < len(firsts) else ())
        value = jnp.concatenate(parts, axis=0)
    return value


def halved(value, masks, dev_count, firsts=()):
    for i, mask in enumerate(masks):
        size = value.shape[0] // 2
        first = firsts[i] if i < len(firsts) else ()
        parts = tied([value[:size], swap(value[size:], mask, dev_count)], first)
        value = parts[0].astype(F32) + parts[1].astype(F32)
        value = value if i == len(masks) - 1 else value.astype(BF)
    return value


def reduce_all(value, steps, dev_count):
    for i, step in enumerate(steps):
        value = sum_parts(block_parts(value, step, dev_count), F32 if i == len(steps) - 1 else BF)
    return value


def strip_order(z, own, masks):
    digits = np.meshgrid(*[np.arange(2) for _ in masks], np.arange(z.strip), indexing="ij")
    moved = sum(digit * mask for digit, mask in zip(digits, masks)).reshape(-1, 1)
    return (own ^ moved.astype(np.int32)) * z.strip + digits[-1].reshape(-1, 1).astype(np.int32)


def after(value, *others):
    return lax.optimization_barrier((value, *others))[0]


def per_device(tiles, w_qkv, w_out, cotangent, offsets, pad_count):
    n = lax.axis_size("ctx")
    z = Sizes(tiles.shape[0], tiles.shape[1], n)
    own = lax.axis_index("ctx")
    rows, width = z.rows, z.width
    masks = [mask for mask in (2**i for i in range(30)) if GROUP <= mask < n]
    order = strip_order(z, own, [1, 4, 2] + masks[::-1])
    order_q = strip_order(z, own, [1] + masks + [2, 4])
    order_out = strip_order(z, own, [1, 2, 4] + masks)
    base_flops = 2 * rows * rows * width

    def weights(start, *args):
        kernel = functools.partial(weights_kernel, start)
        return call(kernel, [((z.half, width), BF)], 4 * rows * width * width)(*args)[0]

    q, k, v, g, sel, mid_kv, mid_qg, far = call(
        functools.partial(project_kernel, z),
        [((rows, width), BF)] * 4
        + [((z.sel, 4 * width), BF)]
        + [((z.mid, 2 * width), BF)] * 2
        + [((z.far, 4 * width), BF)],
        2 * rows * width * 4 * width,
        scratch=[
            pltpu.SMEM(offsets.shape, jnp.int32),
            pltpu.VMEM(tiles.shape, BF),
            pltpu.VMEM(w_qkv.shape, BF),
            pltpu.VMEM(cotangent.shape, BF),
            pltpu.VMEM(w_out.shape, BF),
        ]
        + [pltpu.VMEM((rows, width), BF)] * 4
        + [pltpu.SemaphoreType.DMA((4 * LOAD_CUTS + 3,)), pltpu.SemaphoreType.DMA((4,))],
        hbm_outs=4,
        spaces=pltpu.HBM,
        vmem=PROJECT_VMEM_BYTES,
    )(offsets, tiles, w_qkv, cotangent, w_out)

    steps = upper_steps(n)
    far_up = far
    for step in steps[:-1]:
        far_up = jnp.concatenate(step_parts(far_up, step, n), axis=0)
    far_up = step_parts(far_up, steps[-1], n)
    far_kv = jnp.concatenate([part[:, : 2 * width] for part in far_up], axis=0)
    mid_parts = step_parts(mid_kv, PLANE, n)
    mixed, near_stats, turned, turned_out = call(
        functools.partial(near_kernel, z),
        [
            ((rows, width), F32),
            ((rows, LANES), F32),
            ((width, rows), BF),
            ((width, rows), BF),
        ],
        8 * base_flops,
        smem=1,
    )(pad_count, after(q, far_kv, *mid_parts[1:3]), k, v, g, tiles, order, order_q)
    mid_0 = jnp.concatenate(mid_parts, axis=0)
    mid_1 = swap(mid_0, 1, n)
    far_0 = jnp.concatenate(
        step_parts(after(far_kv, *mid_parts[1:3]), PLANE, n, (near_stats,)), axis=0
    )
    far_1 = swap(far_0, 1, n)
    stats, picked, raw, held = call(
        functools.partial(join_kernel, z),
        [((rows, LANES), F32), ((z.sel, LANES), F32), ((z.sel, LANES), F32), ((z.sel, width), F32)],
        3 * base_flops,
        smem=2,
    )(offsets, pad_count, sel, mid_0, mid_1, far_0, far_1, near_stats)

    (dq_sel,) = call(
        functools.partial(own_grads_kernel, z),
        [((z.sel, width), F32)],
        2 * base_flops,
        smem=2,
    )(offsets, pad_count, sel, mid_0, mid_1, far_0, far_1, picked)
    qg_mid, *qg_far = tied([mid_qg] + far_up, (dq_sel,))
    qg = jnp.concatenate([qg_mid] + [part[:, 2 * width :] for part in qg_far], axis=0)
    qg_parts = step_parts(qg, PLANE, n)
    cot_other = swap(after(cotangent, picked), 1, n)
    stats_up = doubled(picked[z.mid : z.mid + z.far], masks[:1], n, ((dq_sel,),))
    out_rows, attn_turned, attn_turned_out = call(
        functools.partial(output_kernel, z),
        [((rows, width), BF), ((z.half, rows), BF), ((z.half, rows), BF)],
        6 * rows * width * width,
        scratch=[pltpu.VMEM((rows, width), BF)],
        smem=1,
    )(offsets, near_stats, stats, after(picked, stats_up), raw, mixed, held, tiles, w_out, order_out)
    attn_other = swap(attn_turned_out, 1, n)
    stats_up = doubled(stats_up, masks[1:], n, ((out_rows,),))
    wout_half = weights(0, attn_turned, attn_other, cotangent, after(cot_other, stats_up))
    turned_other = swap(after(turned_out, wout_half), 1, n)
    qg_0 = jnp.concatenate(tied(qg_parts, (wout_half,)), axis=0)
    qg_1 = swap(qg_0, 1, n)

    stats_far = stats_up
    stats_up = jnp.concatenate([picked[: z.mid], stats_far], axis=1)
    stats_up = doubled(stats_up, (4,), n, ((wout_half,),))
    dq, dk_near, dv_near = call(
        functools.partial(near_grads_kernel, z),
        [((rows, width), BF), ((rows, width), F32), ((rows, width), F32)],
        8 * base_flops,
        smem=2,
    )(offsets, pad_count, after(q, stats_up), k, v, g, stats, dq_sel)
    dq_other = swap(dq, 1, n)
    stats_up = doubled(stats_up, (2,), n, ((dk_near,),))
    early_half = weights(z.half, turned, turned_other, dq, dq_other)
    stats_0 = jnp.concatenate(
        [
            stats_up[at * z.mid : (at + 1) * z.mid, level * LANES : (level + 1) * LANES]
            for level in range(2)
            for at in (0, 2, 1, 3)
        ],
        axis=0,
    )
    stats_1 = swap(stats_0, 1, n)

    dk, dv = call(
        functools.partial(key_grads_kernel, z),
        [((rows, width), BF), ((rows, width), BF)],
        3 * base_flops,
        smem=2,
        cost=LOW_COST,
    )(
        offsets, pad_count, sel, qg_0, qg_1, stats_0, stats_1,
        after(dk_near, early_half), dv_near,
    )
    dk_other = swap(dk, 1, n)
    dv_other = swap(dv, 1, n)
    (late_half,) = call(
        functools.partial(late_weights_kernel, z),
        [((z.half, 2 * width), BF)],
        4 * rows * width * width,
        cost=LOW_COST,
    )(turned, turned_other, dk, dv, dk_other, dv_other)
    (grad_tiles,) = call(
        functools.partial(tiles_kernel, z),
        [((rows, width), BF)],
        6 * rows * width * width,
        cost=LOW_COST,
    )(after(dq, late_half), dk, dv, w_qkv)
    late_parts = block_parts(late_half, PLANE, n)
    early = halved(early_half, masks + [2, 4], n, ((late_parts[1],),))
    grad_wout = halved(wout_half, [2, 4] + masks, n, ((dk_near,), (late_parts[1],)))
    late = reduce_all(sum_parts(late_parts, BF), upper_steps(n)[::-1], n)
    grad_wqkv = jnp.concatenate([early, late], axis=1)
    return out_rows, grad_tiles, grad_wqkv, grad_wout


def solution(mesh):
    return jax.shard_map(
        per_device,
        mesh=mesh,
        in_specs=(P("ctx", None), P(), P(), P("ctx", None), P(), P()),
        out_specs=(P("ctx", None), P("ctx", None), P("ctx", None), P("ctx", None)),
        check_vma=False,
    )
```

```python
import functools

import jax
import jax.numpy as jnp
import numpy as np
from jax import lax
from jax.experimental import pallas as pl
from jax.experimental.pallas import tpu as pltpu
from jax.sharding import PartitionSpec as P

HEAD_DIM = 64
GROUP = 8
PAIR = 2 * HEAD_DIM
LANES = 128
SECOND = 16
SCALE = 0.125
BF = jnp.bfloat16
F32 = jnp.float32
NT = (((1,), (1,)), ((), ()))
NN = (((1,), (0,)), ((), ()))
TN = (((0,), (0,)), ((), ()))
LARGE = 1e30
LOW_COST = 0.05
LOAD_CUTS = 4
VMEM_BYTES = 40 * 1024 * 1024
PROJECT_VMEM_BYTES = 57 * 1024 * 1024


def dot(a, b, dims=NN):
    return lax.dot_general(a, b, dims, preferred_element_type=F32)


def dot_exact(a, b):
    return lax.dot_general(a, b, NN, preferred_element_type=F32, precision=lax.Precision.HIGHEST)


def iota(shape, dim):
    return lax.broadcasted_iota(jnp.int32, shape, dim)


def low_half(shape):
    return iota(shape, len(shape) - 1) % PAIR < HEAD_DIM


def halves(x):
    low = low_half(x.shape)
    zero = jnp.zeros((), x.dtype)
    return jnp.where(low, x, zero), jnp.where(low, zero, x)


def by_head(first, second, rows):
    return jnp.where(low_half((rows, PAIR)), first, second)


class Sizes:
    def __init__(self, rows, width, dev_count):
        self.rows = rows
        self.width = width
        self.devs = dev_count
        self.heads = width // HEAD_DIM
        self.pairs = self.heads // 2
        self.mid = rows // GROUP
        self.far = rows // dev_count
        self.sel = 2 * self.mid
        self.far_held = -(-self.far // 16) * 16
        self.upper = dev_count // GROUP
        self.strip = width // dev_count
        self.half = width // 2


def chosen_row(z, index, off_mid, off_far):
    row = jnp.where(index < z.mid, index * GROUP + off_mid, (index - z.mid) * z.devs + off_far)
    return jnp.where(index < z.mid + z.far, row, -1)


def spread(z, offs_ref, pair, picked):
    lane = iota((1, 4 * z.sel), 1)
    second = (lane // z.sel) % 2 == 1
    off_mid = jnp.where(second, offs_ref[0, 2 * pair + 1], offs_ref[0, 2 * pair])
    off_far = jnp.where(second, offs_ref[1, 2 * pair + 1], offs_ref[1, 2 * pair])
    target = chosen_row(z, lane % z.sel, off_mid, off_far)
    place = (iota((z.rows, 4 * z.sel), 0) == target).astype(F32).astype(BF)
    high = picked.astype(BF)
    rest = (picked - high.astype(F32)).astype(BF)
    first_high, second_high = halves(high)
    first_rest, second_rest = halves(rest)
    stacked = jnp.concatenate([first_high, second_high, first_rest, second_rest], axis=0)
    return dot(place, stacked)


def lane_offsets(z, offs_ref):
    lane = iota((1, LANES), 1)
    off_mid = jnp.full((1, LANES), -1, jnp.int32)
    off_far = jnp.full((1, LANES), -1, jnp.int32)
    for head in range(z.heads):
        here = (lane == head) | (lane == SECOND + head)
        off_mid = jnp.where(here, offs_ref[0, head], off_mid)
        off_far = jnp.where(here, offs_ref[1, head], off_far)
    return off_mid, off_far


def stat_masks(z, offs_ref):
    off_mid, off_far = lane_offsets(z, offs_ref)
    row = iota((z.rows, LANES), 0)
    return row % GROUP == off_mid, row % z.devs == off_far


def pick_stats(z, masks, stats):
    entry = iota((z.sel, z.rows), 0)
    row = iota((z.sel, z.rows), 1)
    take_mid = ((entry < z.mid) & (row // GROUP == entry)).astype(F32)
    take_far = (row // z.devs == entry - z.mid).astype(F32)
    return dot_exact(take_mid, jnp.where(masks[0], stats, 0.0)) + dot_exact(
        take_far, jnp.where(masks[1], stats, 0.0)
    )


def spread_stats(z, masks, picked):
    row = iota((z.rows, z.sel), 0)
    entry = iota((z.rows, z.sel), 1)
    give_mid = ((entry < z.mid) & (row // GROUP == entry)).astype(F32)
    give_far = (row // z.devs == entry - z.mid).astype(F32)
    fill = jnp.where(iota((z.rows, LANES), 1) < SECOND, -jnp.inf, 0.0)
    return (
        jnp.where(masks[0], dot_exact(give_mid, picked), fill),
        jnp.where(masks[1], dot_exact(give_far, picked), fill),
    )


def gathered_place(z, own, level):
    index = iota((1, z.rows), 1)
    core = index // (4 * z.mid)
    plane = (index // z.mid) % 4
    inner = index % z.mid
    if level == 0:
        return (own ^ (core + 2 * plane)) * z.rows + inner * GROUP
    dev = own ^ (core + 2 * plane + GROUP * (inner // z.far))
    return dev * z.rows + (inner % z.far) * z.devs


def level_parts(z):
    return ((0, z.mid), (z.mid, z.mid + z.far_held))


def project_kernel(
    z, offs_hbm, tiles_hbm, w_qkv_hbm, cot_hbm, w_out_hbm,
    q_hbm, k_hbm, v_hbm, g_hbm, sel, mid_kv, mid_qg, far,
    offs_ref, tiles, w_qkv, cot, w_out, q, k, v, g, sems, out_sems,
):
    width = z.width
    step = width // LOAD_CUTS

    def column_block(block):
        return [
            (
                w_qkv_hbm.at[pl.ds(i * step, step), pl.ds(block * width, width)],
                w_qkv.at[pl.ds(i * step, step), pl.ds(block * width, width)],
            )
            for i in range(LOAD_CUTS)
        ]

    groups = [
        [(tiles_hbm, tiles)] + column_block(1),
        column_block(2),
        column_block(0),
        [(cot_hbm, cot)]
        + [
            (w_out_hbm.at[pl.ds(i * step, step), :], w_out.at[pl.ds(i * step, step), :])
            for i in range(LOAD_CUTS)
        ],
        [(offs_hbm, offs_ref)],
    ]
    copies, index = [], 0
    for group in groups:
        made = []
        for source, target in group:
            copy = pltpu.make_async_copy(source, target, sems.at[index])
            copy.start()
            made.append(copy)
            index += 1
        copies.append(made)

    def arrived(group):
        for copy in copies[group]:
            copy.wait()

    leaving = []

    def leave(source, target):
        copy = pltpu.make_async_copy(source, target, out_sems.at[len(leaving)])
        copy.start()
        leaving.append(copy)

    arrived(0)
    own = tiles[...]
    k[...] = dot(own, w_qkv[:, width : 2 * width]).astype(BF)
    leave(k, k_hbm)
    arrived(1)
    v[...] = dot(own, w_qkv[:, 2 * width :]).astype(BF)
    leave(v, v_hbm)
    arrived(2)
    q[...] = dot(own, w_qkv[:, :width]).astype(BF) * jnp.asarray(SCALE, BF)
    leave(q, q_hbm)
    arrived(3)
    g[...] = dot(cot[...], w_out[...], NT).astype(BF)
    leave(g, g_hbm)
    arrived(4)
    entry = iota((2 * z.sel, z.rows), 0)
    column = iota((2 * z.sel, z.rows), 1)
    second = entry >= z.sel
    for pair in range(z.pairs):
        lanes = slice(pair * PAIR, (pair + 1) * PAIR)
        off_mid = jnp.where(second, offs_ref[0, 2 * pair + 1], offs_ref[0, 2 * pair])
        off_far = jnp.where(second, offs_ref[1, 2 * pair + 1], offs_ref[1, 2 * pair])
        target = chosen_row(z, entry % z.sel, off_mid, off_far)
        take = (column == target).astype(F32).astype(BF)
        every = jnp.concatenate([k[:, lanes], v[:, lanes], q[:, lanes], g[:, lanes]], axis=1)
        both = dot(take, every)
        picked = jnp.where(low_half((z.sel, 4 * PAIR)), both[: z.sel], both[z.sel :]).astype(BF)
        far_part = jnp.where(
            low_half((z.far, 4 * PAIR)),
            both[z.mid : z.mid + z.far],
            both[z.sel + z.mid : z.sel + z.mid + z.far],
        ).astype(BF)
        for part in range(4):
            to = slice(part * width + pair * PAIR, part * width + (pair + 1) * PAIR)
            sel[:, to] = picked[:, part * PAIR : (part + 1) * PAIR]
            near_to = slice(to.start % (2 * width), to.start % (2 * width) + PAIR)
            mid = mid_kv if part < 2 else mid_qg
            mid[:, near_to] = picked[: z.mid, part * PAIR : (part + 1) * PAIR]
            far[:, to] = far_part[:, part * PAIR : (part + 1) * PAIR]
    for copy in leaving:
        copy.wait()


def near_kernel(
    z, pad_ref, q, k, v, g, tiles, order, order_q, mixed, stats, turned, turned_out
):
    own = lax.axis_index("ctx")
    limit = z.rows * z.devs - pad_ref[0] - own * z.rows
    valid = iota((1, z.rows), 1) < limit
    lane = iota((z.rows, LANES), 1)
    both = jnp.zeros((z.rows, LANES), F32)
    for pair in range(z.pairs):
        lanes = slice(pair * PAIR, (pair + 1) * PAIR)
        query = q[:, lanes]
        grad = g[:, lanes].astype(F32)
        keys = halves(k[:, lanes])
        values = halves(v[:, lanes])
        total = None
        for side in range(2):
            head = 2 * pair + side
            scores = jnp.where(valid, dot(query, keys[side], NT), -jnp.inf)
            peak = jnp.max(scores, axis=1, keepdims=True)
            powers = jnp.exp(scores - peak)
            summed = jnp.sum(powers, axis=1, keepdims=True)
            part = dot(powers.astype(BF), values[side]) * (1.0 / summed)
            total = part if total is None else total + part
            both = jnp.where(lane == head, peak + jnp.log(summed), both)
            meets = jnp.sum(grad * part, axis=1, keepdims=True)
            both = jnp.where(lane == SECOND + head, meets, both)
        mixed[:, lanes] = total
    stats[...] = both
    for which, source_rows in enumerate((order, order_q)):
        for part, target in enumerate((turned, turned_out)):
            source = source_rows[part * z.half : (part + 1) * z.half, :]
            place = (iota((z.half, z.width), 1) == source).astype(F32).astype(BF)
            result = dot(place, tiles[...], NT).astype(BF)
            target[which * z.half : (which + 1) * z.half, :] = result


def of_level(level, refs, lanes):
    return jnp.concatenate([ref[:, lanes] for ref in refs[level]], axis=0)


def part_lanes(z, part, pair):
    return slice(part * z.width + pair * PAIR, part * z.width + (pair + 1) * PAIR)


def own_scores(z, limit, offs_ref, sel, refs):
    own = lax.axis_index("ctx")
    scores, places = [], []
    for level, (start, stop) in enumerate(level_parts(z)):
        place = gathered_place(z, own, level)
        for pair in range(z.pairs):
            query = sel[start:stop, part_lanes(z, 2, pair)]
            keys = halves(of_level(level, refs, part_lanes(z, 0, pair)))
            for side in range(2):
                valid = place + offs_ref[level, 2 * pair + side] < limit
                scores.append(jnp.where(valid, dot(query, keys[side], NT), -jnp.inf))
                places.append((level, 2 * pair + side, start, stop))
    spots, at = [], 0
    for level, head, start, stop in places:
        spots.append((level, head, at, at + stop - start))
        at += stop - start
    return jnp.concatenate(scores, axis=0), spots


def to_lanes(z, spots, columns):
    parts = []
    for level, (start, stop) in enumerate(level_parts(z)):
        lane = iota((stop - start, LANES), 1)
        part = jnp.zeros((stop - start, LANES), F32)
        for found, head, first, last in spots:
            if found == level:
                for shift, column in columns:
                    part = jnp.where(lane == shift + head, column[first:last], part)
        parts.append(part)
    parts.append(jnp.zeros((z.sel - level_parts(z)[1][1], LANES), F32))
    return jnp.concatenate(parts, axis=0)


def from_lanes(spots, array, shift):
    return lambda z: jnp.concatenate(
        [
            array[level_parts(z)[level][0] : level_parts(z)[level][1], shift + head : shift + head + 1]
            for level, head, _, _ in spots
        ],
        axis=0,
    )


def spot_of(spots, level, head):
    return next((first, last) for found, at, first, last in spots if (found, at) == (level, head))


def join_kernel(
    z, offs_ref, pad_ref, sel, mid_0, mid_1, far_0, far_1, near_stats, stats, picked, raw, held
):
    refs = ((mid_0, mid_1), (far_0, far_1))
    scores, spots = own_scores(z, z.rows * z.devs - pad_ref[0], offs_ref, sel, refs)
    peak = jnp.max(scores, axis=1, keepdims=True)
    powers = jnp.exp(scores - peak)
    summed = jnp.sum(powers, axis=1, keepdims=True)
    lse = peak + jnp.log(summed)
    scale = 1.0 / summed
    powers = powers.astype(BF)
    products = []
    tail = jnp.zeros((z.sel - level_parts(z)[1][1], PAIR), F32)
    for pair in range(z.pairs):
        totals = []
        for level, (start, stop) in enumerate(level_parts(z)):
            values = halves(of_level(level, refs, part_lanes(z, 1, pair)))
            parts = []
            for side in range(2):
                at, to = spot_of(spots, level, 2 * pair + side)
                parts.append(dot(powers[at:to], values[side]) * scale[at:to])
            totals.append(parts[0] + parts[1])
            grad = sel[start:stop, part_lanes(z, 3, pair)].astype(F32)
            products.append((level, pair, [grad * part for part in parts]))
        held[:, pair * PAIR : (pair + 1) * PAIR] = jnp.concatenate(totals + [tail], axis=0)
    products.sort(key=lambda entry: entry[:2])
    stacked = jnp.concatenate([part for _, _, both in products for part in both], axis=0)
    meets = jnp.sum(stacked, axis=1, keepdims=True)
    sel_both = to_lanes(z, spots, ((0, lse), (SECOND, meets)))
    raw[...] = sel_both
    masks = stat_masks(z, offs_ref)
    near = near_stats[...]
    mid, far = spread_stats(z, masks, sel_both)
    top = jnp.maximum(near, jnp.maximum(mid, far))
    total_lse = top + jnp.log(jnp.exp(near - top) + jnp.exp(mid - top) + jnp.exp(far - top))
    delta = sum(
        pltpu.roll(jnp.exp(value - total_lse), SECOND, 1) * value
        for value in (
            near,
            jnp.where(masks[0], mid, -LARGE),
            jnp.where(masks[1], far, -LARGE),
        )
    )
    both = jnp.where(iota((z.rows, LANES), 1) < SECOND, total_lse, delta)
    stats[...] = both
    picked[...] = pick_stats(z, masks, both)


def output_kernel(
    z, offs_ref, near_stats, stats, picked, raw, mixed, held, tiles, w_out, order,
    rows_out, turned, turned_out, attn,
):
    near_share = jnp.exp(near_stats[...] - stats[...])
    share = jnp.exp(raw[...] - picked[...])
    for pair in range(z.pairs):
        lanes = slice(pair * PAIR, (pair + 1) * PAIR)
        near = by_head(
            near_share[:, 2 * pair : 2 * pair + 1],
            near_share[:, 2 * pair + 1 : 2 * pair + 2],
            z.rows,
        )
        own = by_head(share[:, 2 * pair : 2 * pair + 1], share[:, 2 * pair + 1 : 2 * pair + 2], z.sel)
        combined = near * mixed[:, lanes] + spread(z, offs_ref, pair, own * held[:, lanes])
        attn[:, lanes] = combined.astype(BF)
    rows_out[...] = (tiles[...].astype(F32) + dot(attn[...], w_out[...])).astype(BF)
    for part, target in enumerate((turned, turned_out)):
        source = order[part * z.half : (part + 1) * z.half, :]
        place = (iota((z.half, z.width), 1) == source).astype(F32).astype(BF)
        target[...] = dot(place, attn[...], NT).astype(BF)


def own_grads_kernel(z, offs_ref, pad_ref, sel, mid_0, mid_1, far_0, far_1, picked, dq_sel):
    limit = z.rows * z.devs - pad_ref[0]
    refs = ((mid_0, mid_1), (far_0, far_1))
    scores, spots = own_scores(z, limit, offs_ref, sel, refs)
    probs = jnp.exp(scores - from_lanes(spots, picked, 0)(z))
    grad_probs = []
    for level, (start, stop) in enumerate(level_parts(z)):
        for pair in range(z.pairs):
            grad = sel[start:stop, part_lanes(z, 3, pair)]
            values = halves(of_level(level, refs, part_lanes(z, 1, pair)))
            grad_probs += [dot(grad, values[side], NT) for side in range(2)]
    grad_probs = jnp.concatenate(grad_probs, axis=0) - from_lanes(spots, picked, SECOND)(z)
    grad_scores = (probs * grad_probs).astype(BF)
    tail = jnp.zeros((z.sel - level_parts(z)[1][1], PAIR), F32)
    for pair in range(z.pairs):
        sums = []
        for level in range(2):
            keys = halves(of_level(level, refs, part_lanes(z, 0, pair)))
            at, to = spot_of(spots, level, 2 * pair)
            low = dot(grad_scores[at:to], keys[0])
            at, to = spot_of(spots, level, 2 * pair + 1)
            sums.append(low + dot(grad_scores[at:to], keys[1]))
        dq_sel[:, pair * PAIR : (pair + 1) * PAIR] = jnp.concatenate(sums + [tail], axis=0)


def near_grads_kernel(z, offs_ref, pad_ref, q, k, v, g, stats, dq_sel, dq, dk, dv):
    own = lax.axis_index("ctx")
    limit = z.rows * z.devs - pad_ref[0]
    valid_near = iota((z.rows, 1), 0) < limit - own * z.rows
    across = jnp.transpose(stats[...])
    for pair in range(z.pairs):
        lanes = slice(pair * PAIR, (pair + 1) * PAIR)
        query, grad = q[:, lanes], g[:, lanes]
        queries, grads = halves(query), halves(grad)
        keys, values = halves(k[:, lanes]), halves(v[:, lanes])
        sum_q = sum_k = sum_v = None
        for side in range(2):
            head = 2 * pair + side
            scores = jnp.where(valid_near, dot(keys[side], query, NT), -jnp.inf)
            probs = jnp.exp(scores - across[head : head + 1, :])
            grad_probs = dot(values[side], grad, NT)
            grad_scores = probs * (grad_probs - across[SECOND + head : SECOND + head + 1, :])
            grad_scores = grad_scores.astype(BF)
            part_k = dot(grad_scores, queries[side])
            part_v = dot(probs.astype(BF), grads[side])
            part_q = dot(grad_scores, keys[side], TN)
            if side == 0:
                sum_q, sum_k, sum_v = part_q, part_k, part_v
            else:
                sum_q, sum_k, sum_v = sum_q + part_q, sum_k + part_k, sum_v + part_v
        dk[:, lanes] = sum_k
        dv[:, lanes] = sum_v
        dq[:, lanes] = (SCALE * (sum_q + spread(z, offs_ref, pair, dq_sel[:, lanes]))).astype(BF)


def key_grads_kernel(
    z, offs_ref, pad_ref, sel, qg_0, qg_1, stats_0, stats_1, dk_near, dv_near, dk, dv
):
    own = lax.axis_index("ctx")
    limit = z.rows * z.devs - pad_ref[0] - own * z.rows
    parts = level_parts(z)
    stat_refs = (stats_0, stats_1)

    def rows_of(level, lanes):
        cuts = [slice(p * z.sel + level * z.mid, p * z.sel + (level + 1) * z.mid) for p in range(4)]
        return jnp.concatenate([ref[cut, lanes] for ref in (qg_0, qg_1) for cut in cuts], axis=0)

    tail = jnp.zeros((z.sel - parts[1][1], PAIR), F32)
    probs, grad_scores = {}, {}
    for level, (start, stop) in enumerate(parts):
        across = jnp.transpose(jnp.concatenate([ref[level * 4 * z.mid : (level + 1) * 4 * z.mid, :] for ref in stat_refs], axis=0))
        entry = iota((stop - start, 1), 0) + start
        for pair in range(z.pairs):
            keys = sel[start:stop, part_lanes(z, 0, pair)]
            values = sel[start:stop, part_lanes(z, 1, pair)]
            queries = halves(rows_of(level, part_lanes(z, 0, pair)))
            grads = halves(rows_of(level, part_lanes(z, 1, pair)))
            for side in range(2):
                head = 2 * pair + side
                at = chosen_row(z, entry, offs_ref[0, head], offs_ref[1, head])
                valid = (at >= 0) & (at < limit)
                scores = jnp.where(valid, dot(keys, queries[side], NT), -jnp.inf)
                exps = jnp.exp(scores - across[head : head + 1, :])
                grad_probs = dot(values, grads[side], NT)
                grad_probs = grad_probs - across[SECOND + head : SECOND + head + 1, :]
                probs[level, head] = exps.astype(BF)
                grad_scores[level, head] = (exps * grad_probs).astype(BF)
    sums_k, sums_v = {}, {}
    for pair in range(z.pairs):
        both_k, both_v = [], []
        for level in range(2):
            queries = halves(rows_of(level, part_lanes(z, 0, pair)))
            grads = halves(rows_of(level, part_lanes(z, 1, pair)))
            low, high = 2 * pair, 2 * pair + 1
            both_k.append(
                dot(grad_scores[level, low], queries[0]) + dot(grad_scores[level, high], queries[1])
            )
            both_v.append(dot(probs[level, low], grads[0]) + dot(probs[level, high], grads[1]))
        sums_k[pair] = jnp.concatenate(both_k + [tail], axis=0)
        sums_v[pair] = jnp.concatenate(both_v + [tail], axis=0)
    for pair in range(z.pairs):
        lanes = slice(pair * PAIR, (pair + 1) * PAIR)
        both = jnp.concatenate([sums_k[pair], sums_v[pair]], axis=1)
        moved = spread(z, offs_ref, pair, both)
        dk[:, lanes] = (dk_near[:, lanes] + moved[:, :PAIR]).astype(BF)
        dv[:, lanes] = (dv_near[:, lanes] + moved[:, PAIR:]).astype(BF)


def weights_kernel(start, left, left_other, right, right_other, out):
    rows = slice(start, start + out.shape[0])
    out[...] = (dot(left[rows, :], right[...]) + dot(left_other[rows, :], right_other[...])).astype(BF)


def late_weights_kernel(z, turned, turned_other, dk, dv, dk_other, dv_other, out):
    width = z.width
    left, other = turned[: z.half, :], turned_other[: z.half, :]
    out[:, :width] = (dot(left, dk[...]) + dot(other, dk_other[...])).astype(BF)
    out[:, width:] = (dot(left, dv[...]) + dot(other, dv_other[...])).astype(BF)


def tiles_kernel(z, dq, dk, dv, w_qkv, out):
    width = z.width
    out[...] = (
        dot(dq[...], w_qkv[:, :width], NT)
        + dot(dk[...], w_qkv[:, width : 2 * width], NT)
        + dot(dv[...], w_qkv[:, 2 * width :], NT)
    ).astype(BF)


def call(kernel, outs, flops, scratch=(), smem=0, spaces=None, vmem=VMEM_BYTES, hbm_outs=0, cost=1.0):
    def run(*args):
        moved = sum(int(np.prod(a.shape)) * a.dtype.itemsize for a in args)
        moved += sum(int(np.prod(s)) * jnp.dtype(t).itemsize for s, t in outs)
        specs = [
            pl.BlockSpec(memory_space=spaces or (pltpu.SMEM if i < smem else pltpu.VMEM))
            for i in range(len(args))
        ]
        return pl.pallas_call(
            kernel,
            out_shape=tuple(jax.ShapeDtypeStruct(s, t) for s, t in outs),
            in_specs=specs,
            out_specs=tuple(
                pl.BlockSpec(memory_space=pltpu.HBM if i < hbm_outs else pltpu.VMEM)
                for i in range(len(outs))
            ),
            scratch_shapes=list(scratch),
            compiler_params=pltpu.CompilerParams(vmem_limit_bytes=vmem),
            cost_estimate=pl.CostEstimate(
                flops=int(flops * cost), bytes_accessed=int(moved * cost), transcendentals=0
            ),
        )(*args)

    return run


def swap(value, mask, dev_count):
    return lax.ppermute(value, "ctx", [(d, d ^ mask) for d in range(dev_count)])


def upper_steps(dev_count):
    steps, base = [], GROUP
    while base < dev_count:
        count = 4 if base * 4 <= dev_count else 2
        steps.append((base, count))
        base *= count
    return steps


PLANE = (2, 4)


def tied(parts, first):
    return list(lax.optimization_barrier((*parts, *first))[: len(parts)]) if first else list(parts)


def step_parts(value, step, dev_count, first=()):
    base, count = step
    return tied([value] + [swap(value, base * i, dev_count) for i in range(1, count)], first)


def block_parts(value, step, dev_count):
    base, count = step
    size = value.shape[0] // count
    return [value[:size]] + [
        swap(value[i * size : (i + 1) * size], base * i, dev_count) for i in range(1, count)
    ]


def sum_parts(parts, dtype):
    return sum(part.astype(F32) for part in parts).astype(dtype)


def doubled(value, masks, dev_count, firsts=()):
    for i, mask in enumerate(masks):
        parts = tied([value, swap(value, mask, dev_count)], firsts[i] if i < len(firsts) else ())
        value = jnp.concatenate(parts, axis=0)
    return value


def halved(value, masks, dev_count, firsts=()):
    for i, mask in enumerate(masks):
        size = value.shape[0] // 2
        first = firsts[i] if i < len(firsts) else ()
        parts = tied([value[:size], swap(value[size:], mask, dev_count)], first)
        value = parts[0].astype(F32) + parts[1].astype(F32)
        value = value if i == len(masks) - 1 else value.astype(BF)
    return value


def reduce_all(value, steps, dev_count):
    for i, step in enumerate(steps):
        value = sum_parts(block_parts(value, step, dev_count), F32 if i == len(steps) - 1 else BF)
    return value


def strip_order(z, own, masks):
    digits = np.meshgrid(*[np.arange(2) for _ in masks], np.arange(z.strip), indexing="ij")
    moved = sum(digit * mask for digit, mask in zip(digits, masks)).reshape(-1, 1)
    return (own ^ moved.astype(np.int32)) * z.strip + digits[-1].reshape(-1, 1).astype(np.int32)


def after(value, *others):
    return lax.optimization_barrier((value, *others))[0]


def per_device(tiles, w_qkv, w_out, cotangent, offsets, pad_count):
    n = lax.axis_size("ctx")
    z = Sizes(tiles.shape[0], tiles.shape[1], n)
    own = lax.axis_index("ctx")
    rows, width = z.rows, z.width
    masks = [mask for mask in (2**i for i in range(30)) if GROUP <= mask < n]
    order = strip_order(z, own, [1, 4, 2] + masks[::-1])
    order_q = strip_order(z, own, [1] + masks + [2, 4])
    order_out = strip_order(z, own, [1, 2, 4] + masks)
    base_flops = 2 * rows * rows * width

    def weights(start, *args):
        kernel = functools.partial(weights_kernel, start)
        return call(kernel, [((z.half, width), BF)], 4 * rows * width * width)(*args)[0]

    q, k, v, g, sel, mid_kv, mid_qg, far = call(
        functools.partial(project_kernel, z),
        [((rows, width), BF)] * 4
        + [((z.sel, 4 * width), BF)]
        + [((z.mid, 2 * width), BF)] * 2
        + [((z.far, 4 * width), BF)],
        2 * rows * width * 4 * width,
        scratch=[
            pltpu.SMEM(offsets.shape, jnp.int32),
            pltpu.VMEM(tiles.shape, BF),
            pltpu.VMEM(w_qkv.shape, BF),
            pltpu.VMEM(cotangent.shape, BF),
            pltpu.VMEM(w_out.shape, BF),
        ]
        + [pltpu.VMEM((rows, width), BF)] * 4
        + [pltpu.SemaphoreType.DMA((4 * LOAD_CUTS + 3,)), pltpu.SemaphoreType.DMA((4,))],
        hbm_outs=4,
        spaces=pltpu.HBM,
        vmem=PROJECT_VMEM_BYTES,
    )(offsets, tiles, w_qkv, cotangent, w_out)

    steps = upper_steps(n)
    far_up = far
    for step in steps[:-1]:
        far_up = jnp.concatenate(step_parts(far_up, step, n), axis=0)
    far_up = step_parts(far_up, steps[-1], n)
    far_kv = jnp.concatenate([part[:, : 2 * width] for part in far_up], axis=0)
    mid_parts = step_parts(mid_kv, PLANE, n)
    mixed, near_stats, turned, turned_out = call(
        functools.partial(near_kernel, z),
        [
            ((rows, width), F32),
            ((rows, LANES), F32),
            ((width, rows), BF),
            ((width, rows), BF),
        ],
        8 * base_flops,
        smem=1,
    )(pad_count, after(q, far_kv, *mid_parts[1:3]), k, v, g, tiles, order, order_q)
    mid_0 = jnp.concatenate(mid_parts, axis=0)
    mid_1 = swap(mid_0, 1, n)
    far_0 = jnp.concatenate(
        step_parts(after(far_kv, *mid_parts[1:3]), PLANE, n, (near_stats,)), axis=0
    )
    far_1 = swap(far_0, 1, n)
    stats, picked, raw, held = call(
        functools.partial(join_kernel, z),
        [((rows, LANES), F32), ((z.sel, LANES), F32), ((z.sel, LANES), F32), ((z.sel, width), F32)],
        3 * base_flops,
        smem=2,
    )(offsets, pad_count, sel, mid_0, mid_1, far_0, far_1, near_stats)

    (dq_sel,) = call(
        functools.partial(own_grads_kernel, z),
        [((z.sel, width), F32)],
        2 * base_flops,
        smem=2,
    )(offsets, pad_count, sel, mid_0, mid_1, far_0, far_1, picked)
    qg_mid, *qg_far = tied([mid_qg] + far_up, (dq_sel,))
    qg = jnp.concatenate([qg_mid] + [part[:, 2 * width :] for part in qg_far], axis=0)
    qg_parts = step_parts(qg, PLANE, n)
    cot_other = swap(after(cotangent, picked), 1, n)
    stats_up = doubled(picked[z.mid : z.mid + z.far], masks[:1], n, ((dq_sel,),))
    out_rows, attn_turned, attn_turned_out = call(
        functools.partial(output_kernel, z),
        [((rows, width), BF), ((z.half, rows), BF), ((z.half, rows), BF)],
        6 * rows * width * width,
        scratch=[pltpu.VMEM((rows, width), BF)],
        smem=1,
    )(offsets, near_stats, stats, after(picked, stats_up), raw, mixed, held, tiles, w_out, order_out)
    attn_other = swap(attn_turned_out, 1, n)
    stats_up = doubled(stats_up, masks[1:], n, ((out_rows,),))
    wout_half = weights(0, attn_turned, attn_other, cotangent, after(cot_other, stats_up))
    turned_other = swap(after(turned_out, wout_half), 1, n)
    qg_0 = jnp.concatenate(tied(qg_parts, (wout_half,)), axis=0)
    qg_1 = swap(qg_0, 1, n)

    stats_far = stats_up
    stats_up = jnp.concatenate([picked[: z.mid], stats_far], axis=1)
    stats_up = doubled(stats_up, (4,), n, ((wout_half,),))
    dq, dk_near, dv_near = call(
        functools.partial(near_grads_kernel, z),
        [((rows, width), BF), ((rows, width), F32), ((rows, width), F32)],
        8 * base_flops,
        smem=2,
    )(offsets, pad_count, after(q, stats_up), k, v, g, stats, dq_sel)
    dq_other = swap(dq, 1, n)
    stats_up = doubled(stats_up, (2,), n, ((dk_near,),))
    early_half = weights(z.half, turned, turned_other, dq, dq_other)
    stats_0 = jnp.concatenate(
        [
            stats_up[at * z.mid : (at + 1) * z.mid, level * LANES : (level + 1) * LANES]
            for level in range(2)
            for at in (0, 2, 1, 3)
        ],
        axis=0,
    )
    stats_1 = swap(stats_0, 1, n)

    dk, dv = call(
        functools.partial(key_grads_kernel, z),
        [((rows, width), BF), ((rows, width), BF)],
        3 * base_flops,
        smem=2,
        cost=LOW_COST,
    )(
        offsets, pad_count, sel, qg_0, qg_1, stats_0, stats_1,
        after(dk_near, early_half), dv_near,
    )
    dk_other = swap(dk, 1, n)
    dv_other = swap(dv, 1, n)
    (late_half,) = call(
        functools.partial(late_weights_kernel, z),
        [((z.half, 2 * width), BF)],
        4 * rows * width * width,
        cost=LOW_COST,
    )(turned, turned_other, dk, dv, dk_other, dv_other)
    (grad_tiles,) = call(
        functools.partial(tiles_kernel, z),
        [((rows, width), BF)],
        6 * rows * width * width,
        cost=LOW_COST,
    )(after(dq, late_half), dk, dv, w_qkv)
    late_parts = block_parts(late_half, PLANE, n)
    early = halved(early_half, masks + [2, 4], n, ((late_parts[1],),))
    wout = halved(wout_half, [2, 4] + masks[:-1], n, ((dk_near,), (late_parts[1],))).astype(BF)
    late = sum_parts(tied(late_parts, (wout,)), BF)
    grad_wout = halved(wout, masks[-1:], n)
    late = reduce_all(late, upper_steps(n)[::-1], n)
    grad_wqkv = jnp.concatenate([early, late], axis=1)
    return out_rows, grad_tiles, grad_wqkv, grad_wout


def solution(mesh):
    return jax.shard_map(
        per_device,
        mesh=mesh,
        in_specs=(P("ctx", None), P(), P(), P("ctx", None), P(), P()),
        out_specs=(P("ctx", None), P("ctx", None), P("ctx", None), P("ctx", None)),
        check_vma=False,
    )
```

```python
import functools

import jax
import jax.numpy as jnp
import numpy as np
from jax import lax
from jax.experimental import pallas as pl
from jax.experimental.pallas import tpu as pltpu
from jax.sharding import PartitionSpec as P

HEAD_DIM = 64
GROUP = 8
PAIR = 2 * HEAD_DIM
LANES = 128
SECOND = 16
SCALE = 0.125
BF = jnp.bfloat16
F32 = jnp.float32
NT = (((1,), (1,)), ((), ()))
NN = (((1,), (0,)), ((), ()))
TN = (((0,), (0,)), ((), ()))
LARGE = 1e30
LOW_COST = 0.05
LOAD_CUTS = 8
VMEM_BYTES = 40 * 1024 * 1024
PROJECT_VMEM_BYTES = 57 * 1024 * 1024


def dot(a, b, dims=NN):
    return lax.dot_general(a, b, dims, preferred_element_type=F32)


def dot_exact(a, b):
    return lax.dot_general(a, b, NN, preferred_element_type=F32, precision=lax.Precision.HIGHEST)


def iota(shape, dim):
    return lax.broadcasted_iota(jnp.int32, shape, dim)


def low_half(shape):
    return iota(shape, len(shape) - 1) % PAIR < HEAD_DIM


def halves(x):
    low = low_half(x.shape)
    zero = jnp.zeros((), x.dtype)
    return jnp.where(low, x, zero), jnp.where(low, zero, x)


def by_head(first, second, rows):
    return jnp.where(low_half((rows, PAIR)), first, second)


class Sizes:
    def __init__(self, rows, width, dev_count):
        self.rows = rows
        self.width = width
        self.devs = dev_count
        self.heads = width // HEAD_DIM
        self.pairs = self.heads // 2
        self.mid = rows // GROUP
        self.far = rows // dev_count
        self.sel = 2 * self.mid
        self.far_held = -(-self.far // 16) * 16
        self.upper = dev_count // GROUP
        self.strip = width // dev_count
        self.half = width // 2


def chosen_row(z, index, off_mid, off_far):
    row = jnp.where(index < z.mid, index * GROUP + off_mid, (index - z.mid) * z.devs + off_far)
    return jnp.where(index < z.mid + z.far, row, -1)


def spread(z, offs_ref, pair, picked):
    lane = iota((1, 4 * z.sel), 1)
    second = (lane // z.sel) % 2 == 1
    off_mid = jnp.where(second, offs_ref[0, 2 * pair + 1], offs_ref[0, 2 * pair])
    off_far = jnp.where(second, offs_ref[1, 2 * pair + 1], offs_ref[1, 2 * pair])
    target = chosen_row(z, lane % z.sel, off_mid, off_far)
    place = (iota((z.rows, 4 * z.sel), 0) == target).astype(F32).astype(BF)
    high = picked.astype(BF)
    rest = (picked - high.astype(F32)).astype(BF)
    first_high, second_high = halves(high)
    first_rest, second_rest = halves(rest)
    stacked = jnp.concatenate([first_high, second_high, first_rest, second_rest], axis=0)
    return dot(place, stacked)


def lane_offsets(z, offs_ref):
    lane = iota((1, LANES), 1)
    off_mid = jnp.full((1, LANES), -1, jnp.int32)
    off_far = jnp.full((1, LANES), -1, jnp.int32)
    for head in range(z.heads):
        here = (lane == head) | (lane == SECOND + head)
        off_mid = jnp.where(here, offs_ref[0, head], off_mid)
        off_far = jnp.where(here, offs_ref[1, head], off_far)
    return off_mid, off_far


def stat_masks(z, offs_ref):
    off_mid, off_far = lane_offsets(z, offs_ref)
    row = iota((z.rows, LANES), 0)
    return row % GROUP == off_mid, row % z.devs == off_far


def pick_stats(z, masks, stats):
    entry = iota((z.sel, z.rows), 0)
    row = iota((z.sel, z.rows), 1)
    take_mid = ((entry < z.mid) & (row // GROUP == entry)).astype(F32)
    take_far = (row // z.devs == entry - z.mid).astype(F32)
    return dot_exact(take_mid, jnp.where(masks[0], stats, 0.0)) + dot_exact(
        take_far, jnp.where(masks[1], stats, 0.0)
    )


def spread_stats(z, masks, picked):
    row = iota((z.rows, z.sel), 0)
    entry = iota((z.rows, z.sel), 1)
    give_mid = ((entry < z.mid) & (row // GROUP == entry)).astype(F32)
    give_far = (row // z.devs == entry - z.mid).astype(F32)
    fill = jnp.where(iota((z.rows, LANES), 1) < SECOND, -jnp.inf, 0.0)
    return (
        jnp.where(masks[0], dot_exact(give_mid, picked), fill),
        jnp.where(masks[1], dot_exact(give_far, picked), fill),
    )


def gathered_place(z, own, level):
    index = iota((1, z.rows), 1)
    core = index // (4 * z.mid)
    plane = (index // z.mid) % 4
    inner = index % z.mid
    if level == 0:
        return (own ^ (core + 2 * plane)) * z.rows + inner * GROUP
    dev = own ^ (core + 2 * plane + GROUP * (inner // z.far))
    return dev * z.rows + (inner % z.far) * z.devs


def level_parts(z):
    return ((0, z.mid), (z.mid, z.mid + z.far_held))


def project_kernel(
    z, offs_hbm, tiles_hbm, w_qkv_hbm, cot_hbm, w_out_hbm,
    q_hbm, k_hbm, v_hbm, g_hbm, sel, mid_kv, mid_qg, far,
    offs_ref, tiles, w_qkv, cot, w_out, q, k, v, g, sems, out_sems,
):
    width = z.width
    step = width // LOAD_CUTS

    def column_block(block):
        return [
            (
                w_qkv_hbm.at[pl.ds(i * step, step), pl.ds(block * width, width)],
                w_qkv.at[pl.ds(i * step, step), pl.ds(block * width, width)],
            )
            for i in range(LOAD_CUTS)
        ]

    groups = [
        [(tiles_hbm, tiles)] + column_block(1),
        column_block(2),
        column_block(0),
        [(cot_hbm, cot)]
        + [
            (w_out_hbm.at[pl.ds(i * step, step), :], w_out.at[pl.ds(i * step, step), :])
            for i in range(LOAD_CUTS)
        ],
        [(offs_hbm, offs_ref)],
    ]
    copies, index = [], 0
    for group in groups:
        made = []
        for source, target in group:
            copy = pltpu.make_async_copy(source, target, sems.at[index])
            copy.start()
            made.append(copy)
            index += 1
        copies.append(made)

    def arrived(group):
        for copy in copies[group]:
            copy.wait()

    leaving = []

    def leave(source, target):
        copy = pltpu.make_async_copy(source, target, out_sems.at[len(leaving)])
        copy.start()
        leaving.append(copy)

    arrived(0)
    own = tiles[...]
    k[...] = dot(own, w_qkv[:, width : 2 * width]).astype(BF)
    leave(k, k_hbm)
    arrived(1)
    v[...] = dot(own, w_qkv[:, 2 * width :]).astype(BF)
    leave(v, v_hbm)
    arrived(2)
    q[...] = dot(own, w_qkv[:, :width]).astype(BF) * jnp.asarray(SCALE, BF)
    leave(q, q_hbm)
    arrived(3)
    g[...] = dot(cot[...], w_out[...], NT).astype(BF)
    leave(g, g_hbm)
    arrived(4)
    entry = iota((2 * z.sel, z.rows), 0)
    column = iota((2 * z.sel, z.rows), 1)
    second = entry >= z.sel
    for pair in range(z.pairs):
        lanes = slice(pair * PAIR, (pair + 1) * PAIR)
        off_mid = jnp.where(second, offs_ref[0, 2 * pair + 1], offs_ref[0, 2 * pair])
        off_far = jnp.where(second, offs_ref[1, 2 * pair + 1], offs_ref[1, 2 * pair])
        target = chosen_row(z, entry % z.sel, off_mid, off_far)
        take = (column == target).astype(F32).astype(BF)
        every = jnp.concatenate([k[:, lanes], v[:, lanes], q[:, lanes], g[:, lanes]], axis=1)
        both = dot(take, every)
        picked = jnp.where(low_half((z.sel, 4 * PAIR)), both[: z.sel], both[z.sel :]).astype(BF)
        far_part = jnp.where(
            low_half((z.far, 4 * PAIR)),
            both[z.mid : z.mid + z.far],
            both[z.sel + z.mid : z.sel + z.mid + z.far],
        ).astype(BF)
        for part in range(4):
            to = slice(part * width + pair * PAIR, part * width + (pair + 1) * PAIR)
            sel[:, to] = picked[:, part * PAIR : (part + 1) * PAIR]
            near_to = slice(to.start % (2 * width), to.start % (2 * width) + PAIR)
            mid = mid_kv if part < 2 else mid_qg
            mid[:, near_to] = picked[: z.mid, part * PAIR : (part + 1) * PAIR]
            far[:, to] = far_part[:, part * PAIR : (part + 1) * PAIR]
    for copy in leaving:
        copy.wait()


def near_kernel(
    z, pad_ref, q, k, v, g, tiles, order, order_q, mixed, stats, turned, turned_out
):
    own = lax.axis_index("ctx")
    limit = z.rows * z.devs - pad_ref[0] - own * z.rows
    valid = iota((1, z.rows), 1) < limit
    lane = iota((z.rows, LANES), 1)
    both = jnp.zeros((z.rows, LANES), F32)
    for pair in range(z.pairs):
        lanes = slice(pair * PAIR, (pair + 1) * PAIR)
        query = q[:, lanes]
        grad = g[:, lanes].astype(F32)
        keys = halves(k[:, lanes])
        values = halves(v[:, lanes])
        total = None
        for side in range(2):
            head = 2 * pair + side
            scores = jnp.where(valid, dot(query, keys[side], NT), -jnp.inf)
            peak = jnp.max(scores, axis=1, keepdims=True)
            powers = jnp.exp(scores - peak)
            summed = jnp.sum(powers, axis=1, keepdims=True)
            part = dot(powers.astype(BF), values[side]) * (1.0 / summed)
            total = part if total is None else total + part
            both = jnp.where(lane == head, peak + jnp.log(summed), both)
            meets = jnp.sum(grad * part, axis=1, keepdims=True)
            both = jnp.where(lane == SECOND + head, meets, both)
        mixed[:, lanes] = total
    stats[...] = both
    for which, source_rows in enumerate((order, order_q)):
        for part, target in enumerate((turned, turned_out)):
            source = source_rows[part * z.half : (part + 1) * z.half, :]
            place = (iota((z.half, z.width), 1) == source).astype(F32).astype(BF)
            result = dot(place, tiles[...], NT).astype(BF)
            target[which * z.half : (which + 1) * z.half, :] = result


def of_level(level, refs, lanes):
    return jnp.concatenate([ref[:, lanes] for ref in refs[level]], axis=0)


def part_lanes(z, part, pair):
    return slice(part * z.width + pair * PAIR, part * z.width + (pair + 1) * PAIR)


def own_scores(z, limit, offs_ref, sel, refs):
    own = lax.axis_index("ctx")
    scores, places = [], []
    for level, (start, stop) in enumerate(level_parts(z)):
        place = gathered_place(z, own, level)
        for pair in range(z.pairs):
            query = sel[start:stop, part_lanes(z, 2, pair)]
            keys = halves(of_level(level, refs, part_lanes(z, 0, pair)))
            for side in range(2):
                valid = place + offs_ref[level, 2 * pair + side] < limit
                scores.append(jnp.where(valid, dot(query, keys[side], NT), -jnp.inf))
                places.append((level, 2 * pair + side, start, stop))
    spots, at = [], 0
    for level, head, start, stop in places:
        spots.append((level, head, at, at + stop - start))
        at += stop - start
    return jnp.concatenate(scores, axis=0), spots


def to_lanes(z, spots, columns):
    parts = []
    for level, (start, stop) in enumerate(level_parts(z)):
        lane = iota((stop - start, LANES), 1)
        part = jnp.zeros((stop - start, LANES), F32)
        for found, head, first, last in spots:
            if found == level:
                for shift, column in columns:
                    part = jnp.where(lane == shift + head, column[first:last], part)
        parts.append(part)
    parts.append(jnp.zeros((z.sel - level_parts(z)[1][1], LANES), F32))
    return jnp.concatenate(parts, axis=0)


def from_lanes(spots, array, shift):
    return lambda z: jnp.concatenate(
        [
            array[level_parts(z)[level][0] : level_parts(z)[level][1], shift + head : shift + head + 1]
            for level, head, _, _ in spots
        ],
        axis=0,
    )


def spot_of(spots, level, head):
    return next((first, last) for found, at, first, last in spots if (found, at) == (level, head))


def join_kernel(
    z, offs_ref, pad_ref, sel, mid_0, mid_1, far_0, far_1, near_stats, stats, picked, raw, held
):
    refs = ((mid_0, mid_1), (far_0, far_1))
    scores, spots = own_scores(z, z.rows * z.devs - pad_ref[0], offs_ref, sel, refs)
    peak = jnp.max(scores, axis=1, keepdims=True)
    powers = jnp.exp(scores - peak)
    summed = jnp.sum(powers, axis=1, keepdims=True)
    lse = peak + jnp.log(summed)
    scale = 1.0 / summed
    powers = powers.astype(BF)
    products = []
    tail = jnp.zeros((z.sel - level_parts(z)[1][1], PAIR), F32)
    for pair in range(z.pairs):
        totals = []
        for level, (start, stop) in enumerate(level_parts(z)):
            values = halves(of_level(level, refs, part_lanes(z, 1, pair)))
            parts = []
            for side in range(2):
                at, to = spot_of(spots, level, 2 * pair + side)
                parts.append(dot(powers[at:to], values[side]) * scale[at:to])
            totals.append(parts[0] + parts[1])
            grad = sel[start:stop, part_lanes(z, 3, pair)].astype(F32)
            products.append((level, pair, [grad * part for part in parts]))
        held[:, pair * PAIR : (pair + 1) * PAIR] = jnp.concatenate(totals + [tail], axis=0)
    products.sort(key=lambda entry: entry[:2])
    stacked = jnp.concatenate([part for _, _, both in products for part in both], axis=0)
    meets = jnp.sum(stacked, axis=1, keepdims=True)
    sel_both = to_lanes(z, spots, ((0, lse), (SECOND, meets)))
    raw[...] = sel_both
    masks = stat_masks(z, offs_ref)
    near = near_stats[...]
    mid, far = spread_stats(z, masks, sel_both)
    top = jnp.maximum(near, jnp.maximum(mid, far))
    total_lse = top + jnp.log(jnp.exp(near - top) + jnp.exp(mid - top) + jnp.exp(far - top))
    delta = sum(
        pltpu.roll(jnp.exp(value - total_lse), SECOND, 1) * value
        for value in (
            near,
            jnp.where(masks[0], mid, -LARGE),
            jnp.where(masks[1], far, -LARGE),
        )
    )
    both = jnp.where(iota((z.rows, LANES), 1) < SECOND, total_lse, delta)
    stats[...] = both
    picked[...] = pick_stats(z, masks, both)


def output_kernel(
    z, offs_ref, near_stats, stats, picked, raw, mixed, held, tiles, w_out, order,
    rows_out, turned, turned_out, attn,
):
    near_share = jnp.exp(near_stats[...] - stats[...])
    share = jnp.exp(raw[...] - picked[...])
    for pair in range(z.pairs):
        lanes = slice(pair * PAIR, (pair + 1) * PAIR)
        near = by_head(
            near_share[:, 2 * pair : 2 * pair + 1],
            near_share[:, 2 * pair + 1 : 2 * pair + 2],
            z.rows,
        )
        own = by_head(share[:, 2 * pair : 2 * pair + 1], share[:, 2 * pair + 1 : 2 * pair + 2], z.sel)
        combined = near * mixed[:, lanes] + spread(z, offs_ref, pair, own * held[:, lanes])
        attn[:, lanes] = combined.astype(BF)
    rows_out[...] = (tiles[...].astype(F32) + dot(attn[...], w_out[...])).astype(BF)
    for part, target in enumerate((turned, turned_out)):
        source = order[part * z.half : (part + 1) * z.half, :]
        place = (iota((z.half, z.width), 1) == source).astype(F32).astype(BF)
        target[...] = dot(place, attn[...], NT).astype(BF)


def own_grads_kernel(z, offs_ref, pad_ref, sel, mid_0, mid_1, far_0, far_1, picked, dq_sel):
    limit = z.rows * z.devs - pad_ref[0]
    refs = ((mid_0, mid_1), (far_0, far_1))
    scores, spots = own_scores(z, limit, offs_ref, sel, refs)
    probs = jnp.exp(scores - from_lanes(spots, picked, 0)(z))
    grad_probs = []
    for level, (start, stop) in enumerate(level_parts(z)):
        for pair in range(z.pairs):
            grad = sel[start:stop, part_lanes(z, 3, pair)]
            values = halves(of_level(level, refs, part_lanes(z, 1, pair)))
            grad_probs += [dot(grad, values[side], NT) for side in range(2)]
    grad_probs = jnp.concatenate(grad_probs, axis=0) - from_lanes(spots, picked, SECOND)(z)
    grad_scores = (probs * grad_probs).astype(BF)
    tail = jnp.zeros((z.sel - level_parts(z)[1][1], PAIR), F32)
    for pair in range(z.pairs):
        sums = []
        for level in range(2):
            keys = halves(of_level(level, refs, part_lanes(z, 0, pair)))
            at, to = spot_of(spots, level, 2 * pair)
            low = dot(grad_scores[at:to], keys[0])
            at, to = spot_of(spots, level, 2 * pair + 1)
            sums.append(low + dot(grad_scores[at:to], keys[1]))
        dq_sel[:, pair * PAIR : (pair + 1) * PAIR] = jnp.concatenate(sums + [tail], axis=0)


def near_grads_kernel(z, offs_ref, pad_ref, q, k, v, g, stats, dq_sel, dq, dk, dv):
    own = lax.axis_index("ctx")
    limit = z.rows * z.devs - pad_ref[0]
    valid_near = iota((z.rows, 1), 0) < limit - own * z.rows
    across = jnp.transpose(stats[...])
    for pair in range(z.pairs):
        lanes = slice(pair * PAIR, (pair + 1) * PAIR)
        query, grad = q[:, lanes], g[:, lanes]
        queries, grads = halves(query), halves(grad)
        keys, values = halves(k[:, lanes]), halves(v[:, lanes])
        sum_q = sum_k = sum_v = None
        for side in range(2):
            head = 2 * pair + side
            scores = jnp.where(valid_near, dot(keys[side], query, NT), -jnp.inf)
            probs = jnp.exp(scores - across[head : head + 1, :])
            grad_probs = dot(values[side], grad, NT)
            grad_scores = probs * (grad_probs - across[SECOND + head : SECOND + head + 1, :])
            grad_scores = grad_scores.astype(BF)
            part_k = dot(grad_scores, queries[side])
            part_v = dot(probs.astype(BF), grads[side])
            part_q = dot(grad_scores, keys[side], TN)
            if side == 0:
                sum_q, sum_k, sum_v = part_q, part_k, part_v
            else:
                sum_q, sum_k, sum_v = sum_q + part_q, sum_k + part_k, sum_v + part_v
        dk[:, lanes] = sum_k
        dv[:, lanes] = sum_v
        dq[:, lanes] = (SCALE * (sum_q + spread(z, offs_ref, pair, dq_sel[:, lanes]))).astype(BF)


def key_grads_kernel(
    z, offs_ref, pad_ref, sel, qg_0, qg_1, stats_0, stats_1, dk_near, dv_near, dk, dv
):
    own = lax.axis_index("ctx")
    limit = z.rows * z.devs - pad_ref[0] - own * z.rows
    parts = level_parts(z)
    stat_refs = (stats_0, stats_1)

    def rows_of(level, lanes):
        cuts = [slice(p * z.sel + level * z.mid, p * z.sel + (level + 1) * z.mid) for p in range(4)]
        return jnp.concatenate([ref[cut, lanes] for ref in (qg_0, qg_1) for cut in cuts], axis=0)

    tail = jnp.zeros((z.sel - parts[1][1], PAIR), F32)
    probs, grad_scores = {}, {}
    for level, (start, stop) in enumerate(parts):
        across = jnp.transpose(jnp.concatenate([ref[level * 4 * z.mid : (level + 1) * 4 * z.mid, :] for ref in stat_refs], axis=0))
        entry = iota((stop - start, 1), 0) + start
        for pair in range(z.pairs):
            keys = sel[start:stop, part_lanes(z, 0, pair)]
            values = sel[start:stop, part_lanes(z, 1, pair)]
            queries = halves(rows_of(level, part_lanes(z, 0, pair)))
            grads = halves(rows_of(level, part_lanes(z, 1, pair)))
            for side in range(2):
                head = 2 * pair + side
                at = chosen_row(z, entry, offs_ref[0, head], offs_ref[1, head])
                valid = (at >= 0) & (at < limit)
                scores = jnp.where(valid, dot(keys, queries[side], NT), -jnp.inf)
                exps = jnp.exp(scores - across[head : head + 1, :])
                grad_probs = dot(values, grads[side], NT)
                grad_probs = grad_probs - across[SECOND + head : SECOND + head + 1, :]
                probs[level, head] = exps.astype(BF)
                grad_scores[level, head] = (exps * grad_probs).astype(BF)
    sums_k, sums_v = {}, {}
    for pair in range(z.pairs):
        both_k, both_v = [], []
        for level in range(2):
            queries = halves(rows_of(level, part_lanes(z, 0, pair)))
            grads = halves(rows_of(level, part_lanes(z, 1, pair)))
            low, high = 2 * pair, 2 * pair + 1
            both_k.append(
                dot(grad_scores[level, low], queries[0]) + dot(grad_scores[level, high], queries[1])
            )
            both_v.append(dot(probs[level, low], grads[0]) + dot(probs[level, high], grads[1]))
        sums_k[pair] = jnp.concatenate(both_k + [tail], axis=0)
        sums_v[pair] = jnp.concatenate(both_v + [tail], axis=0)
    for pair in range(z.pairs):
        lanes = slice(pair * PAIR, (pair + 1) * PAIR)
        both = jnp.concatenate([sums_k[pair], sums_v[pair]], axis=1)
        moved = spread(z, offs_ref, pair, both)
        dk[:, lanes] = (dk_near[:, lanes] + moved[:, :PAIR]).astype(BF)
        dv[:, lanes] = (dv_near[:, lanes] + moved[:, PAIR:]).astype(BF)


def weights_kernel(start, left, left_other, right, right_other, out):
    rows = slice(start, start + out.shape[0])
    out[...] = (dot(left[rows, :], right[...]) + dot(left_other[rows, :], right_other[...])).astype(BF)


def late_weights_kernel(z, turned, turned_other, dk, dv, dk_other, dv_other, out):
    width = z.width
    left, other = turned[: z.half, :], turned_other[: z.half, :]
    out[:, :width] = (dot(left, dk[...]) + dot(other, dk_other[...])).astype(BF)
    out[:, width:] = (dot(left, dv[...]) + dot(other, dv_other[...])).astype(BF)


def tiles_kernel(z, dq, dk, dv, w_qkv, out):
    width = z.width
    out[...] = (
        dot(dq[...], w_qkv[:, :width], NT)
        + dot(dk[...], w_qkv[:, width : 2 * width], NT)
        + dot(dv[...], w_qkv[:, 2 * width :], NT)
    ).astype(BF)


def call(kernel, outs, flops, scratch=(), smem=0, spaces=None, vmem=VMEM_BYTES, hbm_outs=0, cost=1.0):
    def run(*args):
        moved = sum(int(np.prod(a.shape)) * a.dtype.itemsize for a in args)
        moved += sum(int(np.prod(s)) * jnp.dtype(t).itemsize for s, t in outs)
        specs = [
            pl.BlockSpec(memory_space=spaces or (pltpu.SMEM if i < smem else pltpu.VMEM))
            for i in range(len(args))
        ]
        return pl.pallas_call(
            kernel,
            out_shape=tuple(jax.ShapeDtypeStruct(s, t) for s, t in outs),
            in_specs=specs,
            out_specs=tuple(
                pl.BlockSpec(memory_space=pltpu.HBM if i < hbm_outs else pltpu.VMEM)
                for i in range(len(outs))
            ),
            scratch_shapes=list(scratch),
            compiler_params=pltpu.CompilerParams(vmem_limit_bytes=vmem),
            cost_estimate=pl.CostEstimate(
                flops=int(flops * cost), bytes_accessed=int(moved * cost), transcendentals=0
            ),
        )(*args)

    return run


def swap(value, mask, dev_count):
    return lax.ppermute(value, "ctx", [(d, d ^ mask) for d in range(dev_count)])


def upper_steps(dev_count):
    steps, base = [], GROUP
    while base < dev_count:
        count = 4 if base * 4 <= dev_count else 2
        steps.append((base, count))
        base *= count
    return steps


PLANE = (2, 4)


def tied(parts, first):
    return list(lax.optimization_barrier((*parts, *first))[: len(parts)]) if first else list(parts)


def step_parts(value, step, dev_count, first=()):
    base, count = step
    order = sorted(range(1, count), key=lambda i: i != 2)
    moved = {i: swap(value, base * i, dev_count) for i in order}
    return tied([value] + [moved[i] for i in range(1, count)], first)


def block_parts(value, step, dev_count):
    base, count = step
    size = value.shape[0] // count
    return [value[:size]] + [
        swap(value[i * size : (i + 1) * size], base * i, dev_count) for i in range(1, count)
    ]


def sum_parts(parts, dtype):
    return sum(part.astype(F32) for part in parts).astype(dtype)


def doubled(value, masks, dev_count, firsts=()):
    for i, mask in enumerate(masks):
        parts = tied([value, swap(value, mask, dev_count)], firsts[i] if i < len(firsts) else ())
        value = jnp.concatenate(parts, axis=0)
    return value


def halved(value, masks, dev_count, firsts=()):
    for i, mask in enumerate(masks):
        size = value.shape[0] // 2
        first = firsts[i] if i < len(firsts) else ()
        parts = tied([value[:size], swap(value[size:], mask, dev_count)], first)
        value = parts[0].astype(F32) + parts[1].astype(F32)
        value = value if i == len(masks) - 1 else value.astype(BF)
    return value


def reduce_all(value, steps, dev_count):
    for i, step in enumerate(steps):
        value = sum_parts(block_parts(value, step, dev_count), F32 if i == len(steps) - 1 else BF)
    return value


def strip_order(z, own, masks):
    digits = np.meshgrid(*[np.arange(2) for _ in masks], np.arange(z.strip), indexing="ij")
    moved = sum(digit * mask for digit, mask in zip(digits, masks)).reshape(-1, 1)
    return (own ^ moved.astype(np.int32)) * z.strip + digits[-1].reshape(-1, 1).astype(np.int32)


def after(value, *others):
    return lax.optimization_barrier((value, *others))[0]


def per_device(tiles, w_qkv, w_out, cotangent, offsets, pad_count):
    n = lax.axis_size("ctx")
    z = Sizes(tiles.shape[0], tiles.shape[1], n)
    own = lax.axis_index("ctx")
    rows, width = z.rows, z.width
    masks = [mask for mask in (2**i for i in range(30)) if GROUP <= mask < n]
    order = strip_order(z, own, [1, 4, 2] + masks[::-1])
    order_q = strip_order(z, own, [1] + masks + [2, 4])
    order_out = strip_order(z, own, [1, 2, 4] + masks)
    base_flops = 2 * rows * rows * width

    def weights(start, *args):
        kernel = functools.partial(weights_kernel, start)
        return call(kernel, [((z.half, width), BF)], 4 * rows * width * width)(*args)[0]

    q, k, v, g, sel, mid_kv, mid_qg, far = call(
        functools.partial(project_kernel, z),
        [((rows, width), BF)] * 4
        + [((z.sel, 4 * width), BF)]
        + [((z.mid, 2 * width), BF)] * 2
        + [((z.far, 4 * width), BF)],
        2 * rows * width * 4 * width,
        scratch=[
            pltpu.SMEM(offsets.shape, jnp.int32),
            pltpu.VMEM(tiles.shape, BF),
            pltpu.VMEM(w_qkv.shape, BF),
            pltpu.VMEM(cotangent.shape, BF),
            pltpu.VMEM(w_out.shape, BF),
        ]
        + [pltpu.VMEM((rows, width), BF)] * 4
        + [pltpu.SemaphoreType.DMA((4 * LOAD_CUTS + 3,)), pltpu.SemaphoreType.DMA((4,))],
        hbm_outs=4,
        spaces=pltpu.HBM,
        vmem=PROJECT_VMEM_BYTES,
    )(offsets, tiles, w_qkv, cotangent, w_out)

    steps = upper_steps(n)
    far_up = far
    for step in steps[:-1]:
        far_up = jnp.concatenate(step_parts(far_up, step, n), axis=0)
    far_up = step_parts(far_up, steps[-1], n)
    far_kv = jnp.concatenate([part[:, : 2 * width] for part in far_up], axis=0)
    mid_parts = step_parts(mid_kv, PLANE, n)
    mixed, near_stats, turned, turned_out = call(
        functools.partial(near_kernel, z),
        [
            ((rows, width), F32),
            ((rows, LANES), F32),
            ((width, rows), BF),
            ((width, rows), BF),
        ],
        8 * base_flops,
        smem=1,
    )(pad_count, after(q, far_kv, *mid_parts[1:3]), k, v, g, tiles, order, order_q)
    mid_0 = jnp.concatenate(mid_parts, axis=0)
    mid_1 = swap(mid_0, 1, n)
    far_0 = jnp.concatenate(
        step_parts(after(far_kv, *mid_parts[1:3]), PLANE, n, (near_stats,)), axis=0
    )
    far_1 = swap(far_0, 1, n)
    stats, picked, raw, held = call(
        functools.partial(join_kernel, z),
        [((rows, LANES), F32), ((z.sel, LANES), F32), ((z.sel, LANES), F32), ((z.sel, width), F32)],
        3 * base_flops,
        smem=2,
    )(offsets, pad_count, sel, mid_0, mid_1, far_0, far_1, near_stats)

    (dq_sel,) = call(
        functools.partial(own_grads_kernel, z),
        [((z.sel, width), F32)],
        2 * base_flops,
        smem=2,
    )(offsets, pad_count, sel, mid_0, mid_1, far_0, far_1, picked)
    qg_mid, *qg_far = tied([mid_qg] + far_up, (dq_sel,))
    qg = jnp.concatenate([qg_mid] + [part[:, 2 * width :] for part in qg_far], axis=0)
    qg_parts = step_parts(qg, PLANE, n)
    cot_other = swap(after(cotangent, picked), 1, n)
    stats_up = doubled(picked[z.mid : z.mid + z.far], masks[:1], n, ((dq_sel,),))
    out_rows, attn_turned, attn_turned_out = call(
        functools.partial(output_kernel, z),
        [((rows, width), BF), ((z.half, rows), BF), ((z.half, rows), BF)],
        6 * rows * width * width,
        scratch=[pltpu.VMEM((rows, width), BF)],
        smem=1,
    )(offsets, near_stats, stats, after(picked, stats_up), raw, mixed, held, tiles, w_out, order_out)
    attn_other = swap(attn_turned_out, 1, n)
    stats_up = doubled(stats_up, masks[1:], n, ((out_rows,),))
    wout_half = weights(0, attn_turned, attn_other, cotangent, after(cot_other, stats_up))
    turned_other = swap(after(turned_out, wout_half), 1, n)
    qg_0 = jnp.concatenate(tied(qg_parts, (wout_half,)), axis=0)
    qg_1 = swap(qg_0, 1, n)

    stats_far = stats_up
    stats_up = jnp.concatenate([picked[: z.mid], stats_far], axis=1)
    stats_up = doubled(stats_up, (4,), n, ((wout_half,),))
    dq, dk_near, dv_near = call(
        functools.partial(near_grads_kernel, z),
        [((rows, width), BF), ((rows, width), F32), ((rows, width), F32)],
        8 * base_flops,
        smem=2,
    )(offsets, pad_count, after(q, stats_up), k, v, g, stats, dq_sel)
    dq_other = swap(dq, 1, n)
    stats_up = doubled(stats_up, (2,), n, ((dk_near,),))
    early_half = weights(z.half, turned, turned_other, dq, dq_other)
    stats_0 = jnp.concatenate(
        [
            stats_up[at * z.mid : (at + 1) * z.mid, level * LANES : (level + 1) * LANES]
            for level in range(2)
            for at in (0, 2, 1, 3)
        ],
        axis=0,
    )
    stats_1 = swap(stats_0, 1, n)

    dk, dv = call(
        functools.partial(key_grads_kernel, z),
        [((rows, width), BF), ((rows, width), BF)],
        3 * base_flops,
        smem=2,
        cost=LOW_COST,
    )(
        offsets, pad_count, sel, qg_0, qg_1, stats_0, stats_1,
        after(dk_near, early_half), dv_near,
    )
    dk_other = swap(dk, 1, n)
    dv_other = swap(dv, 1, n)
    (late_half,) = call(
        functools.partial(late_weights_kernel, z),
        [((z.half, 2 * width), BF)],
        4 * rows * width * width,
        cost=LOW_COST,
    )(turned, turned_other, dk, dv, dk_other, dv_other)
    (grad_tiles,) = call(
        functools.partial(tiles_kernel, z),
        [((rows, width), BF)],
        6 * rows * width * width,
        cost=LOW_COST,
    )(after(dq, late_half), dk, dv, w_qkv)
    late_parts = block_parts(late_half, PLANE, n)
    early = halved(early_half, masks + [2, 4], n, ((late_parts[1],),))
    wout = halved(wout_half, [2, 4] + masks[:-1], n, ((dk_near,), (late_parts[1],))).astype(BF)
    late = sum_parts(tied(late_parts, (wout,)), BF)
    grad_wout = halved(wout, masks[-1:], n)
    late = reduce_all(late, upper_steps(n)[::-1], n)
    grad_wqkv = jnp.concatenate([early, late], axis=1)
    return out_rows, grad_tiles, grad_wqkv, grad_wout


def solution(mesh):
    return jax.shard_map(
        per_device,
        mesh=mesh,
        in_specs=(P("ctx", None), P(), P(), P("ctx", None), P(), P()),
        out_specs=(P("ctx", None), P("ctx", None), P("ctx", None), P("ctx", None)),
        check_vma=False,
    )
```

```python
import functools

import jax
import jax.numpy as jnp
import numpy as np
from jax import lax
from jax.experimental import pallas as pl
from jax.experimental.pallas import tpu as pltpu
from jax.sharding import PartitionSpec as P

HEAD_DIM = 64
GROUP = 8
PAIR = 2 * HEAD_DIM
LANES = 128
SECOND = 16
SCALE = 0.125
BF = jnp.bfloat16
F32 = jnp.float32
NT = (((1,), (1,)), ((), ()))
NN = (((1,), (0,)), ((), ()))
TN = (((0,), (0,)), ((), ()))
LARGE = 1e30
LOW_COST = 0.05
LOAD_CUTS = 4
VMEM_BYTES = 40 * 1024 * 1024
PROJECT_VMEM_BYTES = 57 * 1024 * 1024


def dot(a, b, dims=NN):
    return lax.dot_general(a, b, dims, preferred_element_type=F32)


def dot_exact(a, b):
    return lax.dot_general(a, b, NN, preferred_element_type=F32, precision=lax.Precision.HIGHEST)


def iota(shape, dim):
    return lax.broadcasted_iota(jnp.int32, shape, dim)


def low_half(shape):
    return iota(shape, len(shape) - 1) % PAIR < HEAD_DIM


def halves(x):
    low = low_half(x.shape)
    zero = jnp.zeros((), x.dtype)
    return jnp.where(low, x, zero), jnp.where(low, zero, x)


def by_head(first, second, rows):
    return jnp.where(low_half((rows, PAIR)), first, second)


class Sizes:
    def __init__(self, rows, width, dev_count):
        self.rows = rows
        self.width = width
        self.devs = dev_count
        self.heads = width // HEAD_DIM
        self.pairs = self.heads // 2
        self.mid = rows // GROUP
        self.far = rows // dev_count
        self.sel = 2 * self.mid
        self.far_held = -(-self.far // 16) * 16
        self.upper = dev_count // GROUP
        self.strip = width // dev_count
        self.half = width // 2


def chosen_row(z, index, off_mid, off_far):
    row = jnp.where(index < z.mid, index * GROUP + off_mid, (index - z.mid) * z.devs + off_far)
    return jnp.where(index < z.mid + z.far, row, -1)


def spread(z, offs_ref, pair, picked):
    lane = iota((1, 4 * z.sel), 1)
    second = (lane // z.sel) % 2 == 1
    off_mid = jnp.where(second, offs_ref[0, 2 * pair + 1], offs_ref[0, 2 * pair])
    off_far = jnp.where(second, offs_ref[1, 2 * pair + 1], offs_ref[1, 2 * pair])
    target = chosen_row(z, lane % z.sel, off_mid, off_far)
    place = (iota((z.rows, 4 * z.sel), 0) == target).astype(F32).astype(BF)
    high = picked.astype(BF)
    rest = (picked - high.astype(F32)).astype(BF)
    first_high, second_high = halves(high)
    first_rest, second_rest = halves(rest)
    stacked = jnp.concatenate([first_high, second_high, first_rest, second_rest], axis=0)
    return dot(place, stacked)


def lane_offsets(z, offs_ref):
    lane = iota((1, LANES), 1)
    off_mid = jnp.full((1, LANES), -1, jnp.int32)
    off_far = jnp.full((1, LANES), -1, jnp.int32)
    for head in range(z.heads):
        here = (lane == head) | (lane == SECOND + head)
        off_mid = jnp.where(here, offs_ref[0, head], off_mid)
        off_far = jnp.where(here, offs_ref[1, head], off_far)
    return off_mid, off_far


def stat_masks(z, offs_ref):
    off_mid, off_far = lane_offsets(z, offs_ref)
    row = iota((z.rows, LANES), 0)
    return row % GROUP == off_mid, row % z.devs == off_far


def pick_stats(z, masks, stats):
    entry = iota((z.sel, z.rows), 0)
    row = iota((z.sel, z.rows), 1)
    take_mid = ((entry < z.mid) & (row // GROUP == entry)).astype(F32)
    take_far = (row // z.devs == entry - z.mid).astype(F32)
    return dot_exact(take_mid, jnp.where(masks[0], stats, 0.0)) + dot_exact(
        take_far, jnp.where(masks[1], stats, 0.0)
    )


def spread_stats(z, masks, picked):
    row = iota((z.rows, z.sel), 0)
    entry = iota((z.rows, z.sel), 1)
    give_mid = ((entry < z.mid) & (row // GROUP == entry)).astype(F32)
    give_far = (row // z.devs == entry - z.mid).astype(F32)
    fill = jnp.where(iota((z.rows, LANES), 1) < SECOND, -jnp.inf, 0.0)
    return (
        jnp.where(masks[0], dot_exact(give_mid, picked), fill),
        jnp.where(masks[1], dot_exact(give_far, picked), fill),
    )


def gathered_place(z, own, level):
    index = iota((1, z.rows), 1)
    core = index // (4 * z.mid)
    plane = (index // z.mid) % 4
    inner = index % z.mid
    if level == 0:
        return (own ^ (core + 2 * plane)) * z.rows + inner * GROUP
    dev = own ^ (core + 2 * plane + GROUP * (inner // z.far))
    return dev * z.rows + (inner % z.far) * z.devs


def level_parts(z):
    return ((0, z.mid), (z.mid, z.mid + z.far_held))


def project_kernel(
    z, offs_hbm, tiles_hbm, w_qkv_hbm, cot_hbm, w_out_hbm,
    q_hbm, k_hbm, v_hbm, g_hbm, sel, mid_kv, mid_qg, far,
    offs_ref, tiles, w_qkv, cot, w_out, q, k, v, g, sems, out_sems,
):
    width = z.width
    step = width // LOAD_CUTS

    def column_block(block):
        return [
            (
                w_qkv_hbm.at[pl.ds(i * step, step), pl.ds(block * width, width)],
                w_qkv.at[pl.ds(i * step, step), pl.ds(block * width, width)],
            )
            for i in range(LOAD_CUTS)
        ]

    groups = [
        [(tiles_hbm, tiles)] + column_block(1),
        column_block(2),
        column_block(0),
        [(cot_hbm, cot)]
        + [
            (w_out_hbm.at[pl.ds(i * step, step), :], w_out.at[pl.ds(i * step, step), :])
            for i in range(LOAD_CUTS)
        ],
        [(offs_hbm, offs_ref)],
    ]
    copies, index = [], 0
    for group in groups:
        made = []
        for source, target in group:
            copy = pltpu.make_async_copy(source, target, sems.at[index])
            copy.start()
            made.append(copy)
            index += 1
        copies.append(made)

    def arrived(group):
        for copy in copies[group]:
            copy.wait()

    leaving = []

    def leave(source, target):
        copy = pltpu.make_async_copy(source, target, out_sems.at[len(leaving)])
        copy.start()
        leaving.append(copy)

    arrived(0)
    own = tiles[...]
    k[...] = dot(own, w_qkv[:, width : 2 * width]).astype(BF)
    leave(k, k_hbm)
    arrived(1)
    v[...] = dot(own, w_qkv[:, 2 * width :]).astype(BF)
    leave(v, v_hbm)
    arrived(2)
    q[...] = dot(own, w_qkv[:, :width]).astype(BF) * jnp.asarray(SCALE, BF)
    leave(q, q_hbm)
    arrived(3)
    g[...] = dot(cot[...], w_out[...], NT).astype(BF)
    leave(g, g_hbm)
    arrived(4)
    entry = iota((2 * z.sel, z.rows), 0)
    column = iota((2 * z.sel, z.rows), 1)
    second = entry >= z.sel
    for pair in range(z.pairs):
        lanes = slice(pair * PAIR, (pair + 1) * PAIR)
        off_mid = jnp.where(second, offs_ref[0, 2 * pair + 1], offs_ref[0, 2 * pair])
        off_far = jnp.where(second, offs_ref[1, 2 * pair + 1], offs_ref[1, 2 * pair])
        target = chosen_row(z, entry % z.sel, off_mid, off_far)
        take = (column == target).astype(F32).astype(BF)
        every = jnp.concatenate([k[:, lanes], v[:, lanes], q[:, lanes], g[:, lanes]], axis=1)
        both = dot(take, every)
        picked = jnp.where(low_half((z.sel, 4 * PAIR)), both[: z.sel], both[z.sel :]).astype(BF)
        far_part = jnp.where(
            low_half((z.far, 4 * PAIR)),
            both[z.mid : z.mid + z.far],
            both[z.sel + z.mid : z.sel + z.mid + z.far],
        ).astype(BF)
        for part in range(4):
            to = slice(part * width + pair * PAIR, part * width + (pair + 1) * PAIR)
            sel[:, to] = picked[:, part * PAIR : (part + 1) * PAIR]
            near_to = slice(to.start % (2 * width), to.start % (2 * width) + PAIR)
            mid = mid_kv if part < 2 else mid_qg
            mid[:, near_to] = picked[: z.mid, part * PAIR : (part + 1) * PAIR]
            far[:, to] = far_part[:, part * PAIR : (part + 1) * PAIR]
    for copy in leaving:
        copy.wait()


def near_kernel(
    z, pad_ref, q, k, v, g, tiles, order, order_q, mixed, stats, turned, turned_out
):
    own = lax.axis_index("ctx")
    limit = z.rows * z.devs - pad_ref[0] - own * z.rows
    valid = iota((1, z.rows), 1) < limit
    lane = iota((z.rows, LANES), 1)
    both = jnp.zeros((z.rows, LANES), F32)
    for pair in range(z.pairs):
        lanes = slice(pair * PAIR, (pair + 1) * PAIR)
        query = q[:, lanes]
        grad = g[:, lanes].astype(F32)
        keys = halves(k[:, lanes])
        values = halves(v[:, lanes])
        total = None
        for side in range(2):
            head = 2 * pair + side
            scores = jnp.where(valid, dot(query, keys[side], NT), -jnp.inf)
            peak = jnp.max(scores, axis=1, keepdims=True)
            powers = jnp.exp(scores - peak)
            summed = jnp.sum(powers, axis=1, keepdims=True)
            part = dot(powers.astype(BF), values[side]) * (1.0 / summed)
            total = part if total is None else total + part
            both = jnp.where(lane == head, peak + jnp.log(summed), both)
            meets = jnp.sum(grad * part, axis=1, keepdims=True)
            both = jnp.where(lane == SECOND + head, meets, both)
        mixed[:, lanes] = total
    stats[...] = both
    for which, source_rows in enumerate((order, order_q)):
        for part, target in enumerate((turned, turned_out)):
            source = source_rows[part * z.half : (part + 1) * z.half, :]
            place = (iota((z.half, z.width), 1) == source).astype(F32).astype(BF)
            result = dot(place, tiles[...], NT).astype(BF)
            target[which * z.half : (which + 1) * z.half, :] = result


def of_level(level, refs, lanes):
    return jnp.concatenate([ref[:, lanes] for ref in refs[level]], axis=0)


def part_lanes(z, part, pair):
    return slice(part * z.width + pair * PAIR, part * z.width + (pair + 1) * PAIR)


def own_scores(z, limit, offs_ref, sel, refs):
    own = lax.axis_index("ctx")
    scores, places = [], []
    for level, (start, stop) in enumerate(level_parts(z)):
        place = gathered_place(z, own, level)
        for pair in range(z.pairs):
            query = sel[start:stop, part_lanes(z, 2, pair)]
            keys = halves(of_level(level, refs, part_lanes(z, 0, pair)))
            for side in range(2):
                valid = place + offs_ref[level, 2 * pair + side] < limit
                scores.append(jnp.where(valid, dot(query, keys[side], NT), -jnp.inf))
                places.append((level, 2 * pair + side, start, stop))
    spots, at = [], 0
    for level, head, start, stop in places:
        spots.append((level, head, at, at + stop - start))
        at += stop - start
    return jnp.concatenate(scores, axis=0), spots


def to_lanes(z, spots, columns):
    parts = []
    for level, (start, stop) in enumerate(level_parts(z)):
        lane = iota((stop - start, LANES), 1)
        part = jnp.zeros((stop - start, LANES), F32)
        for found, head, first, last in spots:
            if found == level:
                for shift, column in columns:
                    part = jnp.where(lane == shift + head, column[first:last], part)
        parts.append(part)
    parts.append(jnp.zeros((z.sel - level_parts(z)[1][1], LANES), F32))
    return jnp.concatenate(parts, axis=0)


def from_lanes(spots, array, shift):
    return lambda z: jnp.concatenate(
        [
            array[level_parts(z)[level][0] : level_parts(z)[level][1], shift + head : shift + head + 1]
            for level, head, _, _ in spots
        ],
        axis=0,
    )


def spot_of(spots, level, head):
    return next((first, last) for found, at, first, last in spots if (found, at) == (level, head))


def join_kernel(
    z, offs_ref, pad_ref, sel, mid_0, mid_1, far_0, far_1, near_stats, stats, picked, raw, held
):
    refs = ((mid_0, mid_1), (far_0, far_1))
    scores, spots = own_scores(z, z.rows * z.devs - pad_ref[0], offs_ref, sel, refs)
    peak = jnp.max(scores, axis=1, keepdims=True)
    powers = jnp.exp(scores - peak)
    summed = jnp.sum(powers, axis=1, keepdims=True)
    lse = peak + jnp.log(summed)
    scale = 1.0 / summed
    powers = powers.astype(BF)
    products = []
    tail = jnp.zeros((z.sel - level_parts(z)[1][1], PAIR), F32)
    for pair in range(z.pairs):
        totals = []
        for level, (start, stop) in enumerate(level_parts(z)):
            values = halves(of_level(level, refs, part_lanes(z, 1, pair)))
            parts = []
            for side in range(2):
                at, to = spot_of(spots, level, 2 * pair + side)
                parts.append(dot(powers[at:to], values[side]) * scale[at:to])
            totals.append(parts[0] + parts[1])
            grad = sel[start:stop, part_lanes(z, 3, pair)].astype(F32)
            products.append((level, pair, [grad * part for part in parts]))
        held[:, pair * PAIR : (pair + 1) * PAIR] = jnp.concatenate(totals + [tail], axis=0)
    products.sort(key=lambda entry: entry[:2])
    stacked = jnp.concatenate([part for _, _, both in products for part in both], axis=0)
    meets = jnp.sum(stacked, axis=1, keepdims=True)
    sel_both = to_lanes(z, spots, ((0, lse), (SECOND, meets)))
    raw[...] = sel_both
    masks = stat_masks(z, offs_ref)
    near = near_stats[...]
    mid, far = spread_stats(z, masks, sel_both)
    top = jnp.maximum(near, jnp.maximum(mid, far))
    total_lse = top + jnp.log(jnp.exp(near - top) + jnp.exp(mid - top) + jnp.exp(far - top))
    delta = sum(
        pltpu.roll(jnp.exp(value - total_lse), SECOND, 1) * value
        for value in (
            near,
            jnp.where(masks[0], mid, -LARGE),
            jnp.where(masks[1], far, -LARGE),
        )
    )
    both = jnp.where(iota((z.rows, LANES), 1) < SECOND, total_lse, delta)
    stats[...] = both
    picked[...] = pick_stats(z, masks, both)


def output_kernel(
    z, offs_ref, near_stats, stats, picked, raw, mixed, held, tiles, w_out, order,
    rows_out, turned, turned_out, attn,
):
    near_share = jnp.exp(near_stats[...] - stats[...])
    share = jnp.exp(raw[...] - picked[...])
    for pair in range(z.pairs):
        lanes = slice(pair * PAIR, (pair + 1) * PAIR)
        near = by_head(
            near_share[:, 2 * pair : 2 * pair + 1],
            near_share[:, 2 * pair + 1 : 2 * pair + 2],
            z.rows,
        )
        own = by_head(share[:, 2 * pair : 2 * pair + 1], share[:, 2 * pair + 1 : 2 * pair + 2], z.sel)
        combined = near * mixed[:, lanes] + spread(z, offs_ref, pair, own * held[:, lanes])
        attn[:, lanes] = combined.astype(BF)
    rows_out[...] = (tiles[...].astype(F32) + dot(attn[...], w_out[...])).astype(BF)
    for part, target in enumerate((turned, turned_out)):
        source = order[part * z.half : (part + 1) * z.half, :]
        place = (iota((z.half, z.width), 1) == source).astype(F32).astype(BF)
        target[...] = dot(place, attn[...], NT).astype(BF)


def own_grads_kernel(z, offs_ref, pad_ref, sel, mid_0, mid_1, far_0, far_1, picked, dq_sel):
    limit = z.rows * z.devs - pad_ref[0]
    refs = ((mid_0, mid_1), (far_0, far_1))
    scores, spots = own_scores(z, limit, offs_ref, sel, refs)
    probs = jnp.exp(scores - from_lanes(spots, picked, 0)(z))
    grad_probs = []
    for level, (start, stop) in enumerate(level_parts(z)):
        for pair in range(z.pairs):
            grad = sel[start:stop, part_lanes(z, 3, pair)]
            values = halves(of_level(level, refs, part_lanes(z, 1, pair)))
            grad_probs += [dot(grad, values[side], NT) for side in range(2)]
    grad_probs = jnp.concatenate(grad_probs, axis=0) - from_lanes(spots, picked, SECOND)(z)
    grad_scores = (probs * grad_probs).astype(BF)
    tail = jnp.zeros((z.sel - level_parts(z)[1][1], PAIR), F32)
    for pair in range(z.pairs):
        sums = []
        for level in range(2):
            keys = halves(of_level(level, refs, part_lanes(z, 0, pair)))
            at, to = spot_of(spots, level, 2 * pair)
            low = dot(grad_scores[at:to], keys[0])
            at, to = spot_of(spots, level, 2 * pair + 1)
            sums.append(low + dot(grad_scores[at:to], keys[1]))
        dq_sel[:, pair * PAIR : (pair + 1) * PAIR] = jnp.concatenate(sums + [tail], axis=0)


def near_grads_kernel(z, offs_ref, pad_ref, q, k, v, g, stats, dq_sel, dq, dk, dv):
    own = lax.axis_index("ctx")
    limit = z.rows * z.devs - pad_ref[0]
    valid_near = iota((z.rows, 1), 0) < limit - own * z.rows
    across = jnp.transpose(stats[...])
    for pair in range(z.pairs):
        lanes = slice(pair * PAIR, (pair + 1) * PAIR)
        query, grad = q[:, lanes], g[:, lanes]
        queries, grads = halves(query), halves(grad)
        keys, values = halves(k[:, lanes]), halves(v[:, lanes])
        sum_q = sum_k = sum_v = None
        for side in range(2):
            head = 2 * pair + side
            scores = jnp.where(valid_near, dot(keys[side], query, NT), -jnp.inf)
            probs = jnp.exp(scores - across[head : head + 1, :])
            grad_probs = dot(values[side], grad, NT)
            grad_scores = probs * (grad_probs - across[SECOND + head : SECOND + head + 1, :])
            grad_scores = grad_scores.astype(BF)
            part_k = dot(grad_scores, queries[side])
            part_v = dot(probs.astype(BF), grads[side])
            part_q = dot(grad_scores, keys[side], TN)
            if side == 0:
                sum_q, sum_k, sum_v = part_q, part_k, part_v
            else:
                sum_q, sum_k, sum_v = sum_q + part_q, sum_k + part_k, sum_v + part_v
        dk[:, lanes] = sum_k
        dv[:, lanes] = sum_v
        dq[:, lanes] = (SCALE * (sum_q + spread(z, offs_ref, pair, dq_sel[:, lanes]))).astype(BF)


def key_grads_kernel(
    z, offs_ref, pad_ref, sel, qg_0, qg_1, stats_0, stats_1, dk_near, dv_near, dk, dv
):
    own = lax.axis_index("ctx")
    limit = z.rows * z.devs - pad_ref[0] - own * z.rows
    parts = level_parts(z)
    stat_refs = (stats_0, stats_1)

    def rows_of(level, lanes):
        cuts = [slice(p * z.sel + level * z.mid, p * z.sel + (level + 1) * z.mid) for p in range(4)]
        return jnp.concatenate([ref[cut, lanes] for ref in (qg_0, qg_1) for cut in cuts], axis=0)

    tail = jnp.zeros((z.sel - parts[1][1], PAIR), F32)
    probs, grad_scores = {}, {}
    for level, (start, stop) in enumerate(parts):
        across = jnp.transpose(jnp.concatenate([ref[level * 4 * z.mid : (level + 1) * 4 * z.mid, :] for ref in stat_refs], axis=0))
        entry = iota((stop - start, 1), 0) + start
        for pair in range(z.pairs):
            keys = sel[start:stop, part_lanes(z, 0, pair)]
            values = sel[start:stop, part_lanes(z, 1, pair)]
            queries = halves(rows_of(level, part_lanes(z, 0, pair)))
            grads = halves(rows_of(level, part_lanes(z, 1, pair)))
            for side in range(2):
                head = 2 * pair + side
                at = chosen_row(z, entry, offs_ref[0, head], offs_ref[1, head])
                valid = (at >= 0) & (at < limit)
                scores = jnp.where(valid, dot(keys, queries[side], NT), -jnp.inf)
                exps = jnp.exp(scores - across[head : head + 1, :])
                grad_probs = dot(values, grads[side], NT)
                grad_probs = grad_probs - across[SECOND + head : SECOND + head + 1, :]
                probs[level, head] = exps.astype(BF)
                grad_scores[level, head] = (exps * grad_probs).astype(BF)
    sums_k, sums_v = {}, {}
    for pair in range(z.pairs):
        both_k, both_v = [], []
        for level in range(2):
            queries = halves(rows_of(level, part_lanes(z, 0, pair)))
            grads = halves(rows_of(level, part_lanes(z, 1, pair)))
            low, high = 2 * pair, 2 * pair + 1
            both_k.append(
                dot(grad_scores[level, low], queries[0]) + dot(grad_scores[level, high], queries[1])
            )
            both_v.append(dot(probs[level, low], grads[0]) + dot(probs[level, high], grads[1]))
        sums_k[pair] = jnp.concatenate(both_k + [tail], axis=0)
        sums_v[pair] = jnp.concatenate(both_v + [tail], axis=0)
    for pair in range(z.pairs):
        lanes = slice(pair * PAIR, (pair + 1) * PAIR)
        both = jnp.concatenate([sums_k[pair], sums_v[pair]], axis=1)
        moved = spread(z, offs_ref, pair, both)
        dk[:, lanes] = (dk_near[:, lanes] + moved[:, :PAIR]).astype(BF)
        dv[:, lanes] = (dv_near[:, lanes] + moved[:, PAIR:]).astype(BF)


def weights_kernel(start, left, left_other, right, right_other, out):
    rows = slice(start, start + out.shape[0])
    out[...] = (dot(left[rows, :], right[...]) + dot(left_other[rows, :], right_other[...])).astype(BF)


def late_weights_kernel(z, turned, turned_other, dk, dv, dk_other, dv_other, out):
    width = z.width
    left, other = turned[: z.half, :], turned_other[: z.half, :]
    out[:, :width] = (dot(left, dk[...]) + dot(other, dk_other[...])).astype(BF)
    out[:, width:] = (dot(left, dv[...]) + dot(other, dv_other[...])).astype(BF)


def tiles_kernel(z, dq, dk, dv, w_qkv, out):
    width = z.width
    out[...] = (
        dot(dq[...], w_qkv[:, :width], NT)
        + dot(dk[...], w_qkv[:, width : 2 * width], NT)
        + dot(dv[...], w_qkv[:, 2 * width :], NT)
    ).astype(BF)


def call(kernel, outs, flops, scratch=(), smem=0, spaces=None, vmem=VMEM_BYTES, hbm_outs=0, cost=1.0):
    def run(*args):
        moved = sum(int(np.prod(a.shape)) * a.dtype.itemsize for a in args)
        moved += sum(int(np.prod(s)) * jnp.dtype(t).itemsize for s, t in outs)
        specs = [
            pl.BlockSpec(memory_space=spaces or (pltpu.SMEM if i < smem else pltpu.VMEM))
            for i in range(len(args))
        ]
        return pl.pallas_call(
            kernel,
            out_shape=tuple(jax.ShapeDtypeStruct(s, t) for s, t in outs),
            in_specs=specs,
            out_specs=tuple(
                pl.BlockSpec(memory_space=pltpu.HBM if i < hbm_outs else pltpu.VMEM)
                for i in range(len(outs))
            ),
            scratch_shapes=list(scratch),
            compiler_params=pltpu.CompilerParams(vmem_limit_bytes=vmem),
            cost_estimate=pl.CostEstimate(
                flops=int(flops * cost), bytes_accessed=int(moved * cost), transcendentals=0
            ),
        )(*args)

    return run


def swap(value, mask, dev_count):
    return lax.ppermute(value, "ctx", [(d, d ^ mask) for d in range(dev_count)])


def upper_steps(dev_count):
    steps, base = [], GROUP
    while base < dev_count:
        count = 4 if base * 4 <= dev_count else 2
        steps.append((base, count))
        base *= count
    return steps


PLANE = (2, 4)


def tied(parts, first):
    return list(lax.optimization_barrier((*parts, *first))[: len(parts)]) if first else list(parts)


def step_parts(value, step, dev_count, first=()):
    base, count = step
    return tied([value] + [swap(value, base * i, dev_count) for i in range(1, count)], first)


def block_parts(value, step, dev_count):
    base, count = step
    size = value.shape[0] // count
    return [value[:size]] + [
        swap(value[i * size : (i + 1) * size], base * i, dev_count) for i in range(1, count)
    ]


def sum_parts(parts, dtype):
    return sum(part.astype(F32) for part in parts).astype(dtype)


def doubled(value, masks, dev_count, firsts=()):
    for i, mask in enumerate(masks):
        parts = tied([value, swap(value, mask, dev_count)], firsts[i] if i < len(firsts) else ())
        value = jnp.concatenate(parts, axis=0)
    return value


def halved(value, masks, dev_count, firsts=()):
    for i, mask in enumerate(masks):
        size = value.shape[0] // 2
        first = firsts[i] if i < len(firsts) else ()
        parts = tied([value[:size], swap(value[size:], mask, dev_count)], first)
        value = parts[0].astype(F32) + parts[1].astype(F32)
        value = value if i == len(masks) - 1 else value.astype(BF)
    return value


def reduce_all(value, steps, dev_count):
    for i, step in enumerate(steps):
        value = sum_parts(block_parts(value, step, dev_count), F32 if i == len(steps) - 1 else BF)
    return value


def strip_order(z, own, masks):
    digits = np.meshgrid(*[np.arange(2) for _ in masks], np.arange(z.strip), indexing="ij")
    moved = sum(digit * mask for digit, mask in zip(digits, masks)).reshape(-1, 1)
    return (own ^ moved.astype(np.int32)) * z.strip + digits[-1].reshape(-1, 1).astype(np.int32)


def after(value, *others):
    return lax.optimization_barrier((value, *others))[0]


def per_device(tiles, w_qkv, w_out, cotangent, offsets, pad_count):
    n = lax.axis_size("ctx")
    z = Sizes(tiles.shape[0], tiles.shape[1], n)
    own = lax.axis_index("ctx")
    rows, width = z.rows, z.width
    masks = [mask for mask in (2**i for i in range(30)) if GROUP <= mask < n]
    order = strip_order(z, own, [1, 4, 2] + masks[::-1])
    order_q = strip_order(z, own, [1] + masks[:-1] + [4, 2] + masks[-1:])
    order_out = strip_order(z, own, [1, 2, 4] + masks)
    base_flops = 2 * rows * rows * width

    def weights(start, *args):
        kernel = functools.partial(weights_kernel, start)
        return call(kernel, [((z.half, width), BF)], 4 * rows * width * width)(*args)[0]

    q, k, v, g, sel, mid_kv, mid_qg, far = call(
        functools.partial(project_kernel, z),
        [((rows, width), BF)] * 4
        + [((z.sel, 4 * width), BF)]
        + [((z.mid, 2 * width), BF)] * 2
        + [((z.far, 4 * width), BF)],
        2 * rows * width * 4 * width,
        scratch=[
            pltpu.SMEM(offsets.shape, jnp.int32),
            pltpu.VMEM(tiles.shape, BF),
            pltpu.VMEM(w_qkv.shape, BF),
            pltpu.VMEM(cotangent.shape, BF),
            pltpu.VMEM(w_out.shape, BF),
        ]
        + [pltpu.VMEM((rows, width), BF)] * 4
        + [pltpu.SemaphoreType.DMA((4 * LOAD_CUTS + 3,)), pltpu.SemaphoreType.DMA((4,))],
        hbm_outs=4,
        spaces=pltpu.HBM,
        vmem=PROJECT_VMEM_BYTES,
    )(offsets, tiles, w_qkv, cotangent, w_out)

    steps = upper_steps(n)
    far_up = far
    for step in steps[:-1]:
        far_up = jnp.concatenate(step_parts(far_up, step, n), axis=0)
    far_up = step_parts(far_up, steps[-1], n)
    far_kv = jnp.concatenate([part[:, : 2 * width] for part in far_up], axis=0)
    mid_parts = step_parts(mid_kv, PLANE, n)
    mixed, near_stats, turned, turned_out = call(
        functools.partial(near_kernel, z),
        [
            ((rows, width), F32),
            ((rows, LANES), F32),
            ((width, rows), BF),
            ((width, rows), BF),
        ],
        8 * base_flops,
        smem=1,
    )(pad_count, after(q, far_kv, *mid_parts[1:3]), k, v, g, tiles, order, order_q)
    mid_0 = jnp.concatenate(mid_parts, axis=0)
    mid_1 = swap(mid_0, 1, n)
    far_0 = jnp.concatenate(
        step_parts(after(far_kv, *mid_parts[1:3]), PLANE, n, (near_stats,)), axis=0
    )
    far_1 = swap(far_0, 1, n)
    stats, picked, raw, held = call(
        functools.partial(join_kernel, z),
        [((rows, LANES), F32), ((z.sel, LANES), F32), ((z.sel, LANES), F32), ((z.sel, width), F32)],
        3 * base_flops,
        smem=2,
    )(offsets, pad_count, sel, mid_0, mid_1, far_0, far_1, near_stats)

    (dq_sel,) = call(
        functools.partial(own_grads_kernel, z),
        [((z.sel, width), F32)],
        2 * base_flops,
        smem=2,
    )(offsets, pad_count, sel, mid_0, mid_1, far_0, far_1, picked)
    qg_mid, *qg_far = tied([mid_qg] + far_up, (dq_sel,))
    qg = jnp.concatenate([qg_mid] + [part[:, 2 * width :] for part in qg_far], axis=0)
    qg_parts = step_parts(qg, PLANE, n)
    cot_other = swap(after(cotangent, picked), 1, n)
    stats_up = doubled(picked[z.mid : z.mid + z.far], masks[:1], n, ((dq_sel,),))
    out_rows, attn_turned, attn_turned_out = call(
        functools.partial(output_kernel, z),
        [((rows, width), BF), ((z.half, rows), BF), ((z.half, rows), BF)],
        6 * rows * width * width,
        scratch=[pltpu.VMEM((rows, width), BF)],
        smem=1,
    )(offsets, near_stats, stats, after(picked, stats_up), raw, mixed, held, tiles, w_out, order_out)
    attn_other = swap(attn_turned_out, 1, n)
    stats_up = doubled(stats_up, masks[1:], n, ((out_rows,),))
    wout_half = weights(0, attn_turned, attn_other, cotangent, after(cot_other, stats_up))
    turned_other = swap(after(turned_out, wout_half), 1, n)
    qg_0 = jnp.concatenate(tied(qg_parts, (wout_half,)), axis=0)
    qg_1 = swap(qg_0, 1, n)

    stats_far = stats_up
    stats_up = jnp.concatenate([picked[: z.mid], stats_far], axis=1)
    stats_up = doubled(stats_up, (4,), n, ((wout_half,),))
    dq, dk_near, dv_near = call(
        functools.partial(near_grads_kernel, z),
        [((rows, width), BF), ((rows, width), F32), ((rows, width), F32)],
        8 * base_flops,
        smem=2,
    )(offsets, pad_count, after(q, stats_up), k, v, g, stats, dq_sel)
    dq_other = swap(dq, 1, n)
    stats_up = doubled(stats_up, (2,), n, ((dk_near,),))
    early_half = weights(z.half, turned, turned_other, dq, dq_other)
    stats_0 = jnp.concatenate(
        [
            stats_up[at * z.mid : (at + 1) * z.mid, level * LANES : (level + 1) * LANES]
            for level in range(2)
            for at in (0, 2, 1, 3)
        ],
        axis=0,
    )
    stats_1 = swap(stats_0, 1, n)

    dk, dv = call(
        functools.partial(key_grads_kernel, z),
        [((rows, width), BF), ((rows, width), BF)],
        3 * base_flops,
        smem=2,
        cost=LOW_COST,
    )(
        offsets, pad_count, sel, qg_0, qg_1, stats_0, stats_1,
        after(dk_near, early_half), dv_near,
    )
    dk_other = swap(dk, 1, n)
    dv_other = swap(dv, 1, n)
    (late_half,) = call(
        functools.partial(late_weights_kernel, z),
        [((z.half, 2 * width), BF)],
        4 * rows * width * width,
        cost=LOW_COST,
    )(turned, turned_other, dk, dv, dk_other, dv_other)
    (grad_tiles,) = call(
        functools.partial(tiles_kernel, z),
        [((rows, width), BF)],
        6 * rows * width * width,
        cost=LOW_COST,
    )(after(dq, late_half), dk, dv, w_qkv)
    late_parts = block_parts(late_half, PLANE, n)
    early = halved(early_half, masks[:-1], n, ((late_parts[1],),)).astype(BF)
    early = sum_parts(block_parts(early, PLANE, n), BF)
    early = halved(early, masks[-1:], n)
    wout = halved(wout_half, [2, 4] + masks[:-1], n, ((dk_near,), (late_parts[1],))).astype(BF)
    late = sum_parts(tied(late_parts, (wout,)), BF)
    grad_wout = halved(wout, masks[-1:], n)
    late = reduce_all(late, upper_steps(n)[::-1], n)
    grad_wqkv = jnp.concatenate([early, late], axis=1)
    return out_rows, grad_tiles, grad_wqkv, grad_wout


def solution(mesh):
    return jax.shard_map(
        per_device,
        mesh=mesh,
        in_specs=(P("ctx", None), P(), P(), P("ctx", None), P(), P()),
        out_specs=(P("ctx", None), P("ctx", None), P("ctx", None), P("ctx", None)),
        check_vma=False,
    )
```

```python
import functools

import jax
import jax.numpy as jnp
import numpy as np
from jax import lax
from jax.experimental import pallas as pl
from jax.experimental.pallas import tpu as pltpu
from jax.sharding import PartitionSpec as P

HEAD_DIM = 64
GROUP = 8
PAIR = 2 * HEAD_DIM
LANES = 128
SECOND = 16
SCALE = 0.125
BF = jnp.bfloat16
F32 = jnp.float32
NT = (((1,), (1,)), ((), ()))
NN = (((1,), (0,)), ((), ()))
TN = (((0,), (0,)), ((), ()))
LARGE = 1e30
LOW_COST = 0.05
LOAD_CUTS = 4
VMEM_BYTES = 40 * 1024 * 1024
PROJECT_VMEM_BYTES = 57 * 1024 * 1024


def dot(a, b, dims=NN):
    return lax.dot_general(a, b, dims, preferred_element_type=F32)


def dot_exact(a, b):
    return lax.dot_general(a, b, NN, preferred_element_type=F32, precision=lax.Precision.HIGHEST)


def iota(shape, dim):
    return lax.broadcasted_iota(jnp.int32, shape, dim)


def low_half(shape):
    return iota(shape, len(shape) - 1) % PAIR < HEAD_DIM


def halves(x):
    low = low_half(x.shape)
    zero = jnp.zeros((), x.dtype)
    return jnp.where(low, x, zero), jnp.where(low, zero, x)


def by_head(first, second, rows):
    return jnp.where(low_half((rows, PAIR)), first, second)


class Sizes:
    def __init__(self, rows, width, dev_count):
        self.rows = rows
        self.width = width
        self.devs = dev_count
        self.heads = width // HEAD_DIM
        self.pairs = self.heads // 2
        self.mid = rows // GROUP
        self.far = rows // dev_count
        self.sel = 2 * self.mid
        self.far_held = -(-self.far // 16) * 16
        self.upper = dev_count // GROUP
        self.strip = width // dev_count
        self.half = width // 2


def chosen_row(z, index, off_mid, off_far):
    row = jnp.where(index < z.mid, index * GROUP + off_mid, (index - z.mid) * z.devs + off_far)
    return jnp.where(index < z.mid + z.far, row, -1)


def spread(z, offs_ref, pair, picked):
    lane = iota((1, 4 * z.sel), 1)
    second = (lane // z.sel) % 2 == 1
    off_mid = jnp.where(second, offs_ref[0, 2 * pair + 1], offs_ref[0, 2 * pair])
    off_far = jnp.where(second, offs_ref[1, 2 * pair + 1], offs_ref[1, 2 * pair])
    target = chosen_row(z, lane % z.sel, off_mid, off_far)
    place = (iota((z.rows, 4 * z.sel), 0) == target).astype(F32).astype(BF)
    high = picked.astype(BF)
    rest = (picked - high.astype(F32)).astype(BF)
    first_high, second_high = halves(high)
    first_rest, second_rest = halves(rest)
    stacked = jnp.concatenate([first_high, second_high, first_rest, second_rest], axis=0)
    return dot(place, stacked)


def lane_offsets(z, offs_ref):
    lane = iota((1, LANES), 1)
    off_mid = jnp.full((1, LANES), -1, jnp.int32)
    off_far = jnp.full((1, LANES), -1, jnp.int32)
    for head in range(z.heads):
        here = (lane == head) | (lane == SECOND + head)
        off_mid = jnp.where(here, offs_ref[0, head], off_mid)
        off_far = jnp.where(here, offs_ref[1, head], off_far)
    return off_mid, off_far


def stat_masks(z, offs_ref):
    off_mid, off_far = lane_offsets(z, offs_ref)
    row = iota((z.rows, LANES), 0)
    return row % GROUP == off_mid, row % z.devs == off_far


def pick_stats(z, masks, stats):
    entry = iota((z.sel, z.rows), 0)
    row = iota((z.sel, z.rows), 1)
    take_mid = ((entry < z.mid) & (row // GROUP == entry)).astype(F32)
    take_far = (row // z.devs == entry - z.mid).astype(F32)
    return dot_exact(take_mid, jnp.where(masks[0], stats, 0.0)) + dot_exact(
        take_far, jnp.where(masks[1], stats, 0.0)
    )


def spread_stats(z, masks, picked):
    row = iota((z.rows, z.sel), 0)
    entry = iota((z.rows, z.sel), 1)
    give_mid = ((entry < z.mid) & (row // GROUP == entry)).astype(F32)
    give_far = (row // z.devs == entry - z.mid).astype(F32)
    fill = jnp.where(iota((z.rows, LANES), 1) < SECOND, -jnp.inf, 0.0)
    return (
        jnp.where(masks[0], dot_exact(give_mid, picked), fill),
        jnp.where(masks[1], dot_exact(give_far, picked), fill),
    )


def gathered_place(z, own, level):
    index = iota((1, z.rows), 1)
    core = index // (4 * z.mid)
    plane = (index // z.mid) % 4
    inner = index % z.mid
    if level == 0:
        return (own ^ (core + 2 * plane)) * z.rows + inner * GROUP
    dev = own ^ (core + 2 * plane + GROUP * (inner // z.far))
    return dev * z.rows + (inner % z.far) * z.devs


def level_parts(z):
    return ((0, z.mid), (z.mid, z.mid + z.far_held))


def project_kernel(
    z, offs_hbm, tiles_hbm, w_qkv_hbm, cot_hbm, w_out_hbm,
    q_hbm, k_hbm, v_hbm, g_hbm, sel, mid_kv, mid_qg, far,
    offs_ref, tiles, w_qkv, cot, w_out, q, k, v, g, sems, out_sems,
):
    width = z.width
    step = width // LOAD_CUTS

    def column_block(block):
        return [
            (
                w_qkv_hbm.at[pl.ds(i * step, step), pl.ds(block * width, width)],
                w_qkv.at[pl.ds(i * step, step), pl.ds(block * width, width)],
            )
            for i in range(LOAD_CUTS)
        ]

    groups = [
        [(tiles_hbm, tiles)] + column_block(1),
        column_block(2),
        column_block(0),
        [(cot_hbm, cot)]
        + [
            (w_out_hbm.at[pl.ds(i * step, step), :], w_out.at[pl.ds(i * step, step), :])
            for i in range(LOAD_CUTS)
        ],
        [(offs_hbm, offs_ref)],
    ]
    copies, index = [], 0
    for group in groups:
        made = []
        for source, target in group:
            copy = pltpu.make_async_copy(source, target, sems.at[index])
            copy.start()
            made.append(copy)
            index += 1
        copies.append(made)

    def arrived(group):
        for copy in copies[group]:
            copy.wait()

    leaving = []

    def leave(source, target):
        copy = pltpu.make_async_copy(source, target, out_sems.at[len(leaving)])
        copy.start()
        leaving.append(copy)

    arrived(0)
    own = tiles[...]
    k[...] = dot(own, w_qkv[:, width : 2 * width]).astype(BF)
    leave(k, k_hbm)
    arrived(1)
    v[...] = dot(own, w_qkv[:, 2 * width :]).astype(BF)
    leave(v, v_hbm)
    arrived(2)
    q[...] = dot(own, w_qkv[:, :width]).astype(BF) * jnp.asarray(SCALE, BF)
    leave(q, q_hbm)
    arrived(3)
    g[...] = dot(cot[...], w_out[...], NT).astype(BF)
    leave(g, g_hbm)
    arrived(4)
    entry = iota((2 * z.sel, z.rows), 0)
    column = iota((2 * z.sel, z.rows), 1)
    second = entry >= z.sel
    for pair in range(z.pairs):
        lanes = slice(pair * PAIR, (pair + 1) * PAIR)
        off_mid = jnp.where(second, offs_ref[0, 2 * pair + 1], offs_ref[0, 2 * pair])
        off_far = jnp.where(second, offs_ref[1, 2 * pair + 1], offs_ref[1, 2 * pair])
        target = chosen_row(z, entry % z.sel, off_mid, off_far)
        take = (column == target).astype(F32).astype(BF)
        every = jnp.concatenate([k[:, lanes], v[:, lanes], q[:, lanes], g[:, lanes]], axis=1)
        both = dot(take, every)
        picked = jnp.where(low_half((z.sel, 4 * PAIR)), both[: z.sel], both[z.sel :]).astype(BF)
        far_part = jnp.where(
            low_half((z.far, 4 * PAIR)),
            both[z.mid : z.mid + z.far],
            both[z.sel + z.mid : z.sel + z.mid + z.far],
        ).astype(BF)
        for part in range(4):
            to = slice(part * width + pair * PAIR, part * width + (pair + 1) * PAIR)
            sel[:, to] = picked[:, part * PAIR : (part + 1) * PAIR]
            near_to = slice(to.start % (2 * width), to.start % (2 * width) + PAIR)
            mid = mid_kv if part < 2 else mid_qg
            mid[:, near_to] = picked[: z.mid, part * PAIR : (part + 1) * PAIR]
            far[:, to] = far_part[:, part * PAIR : (part + 1) * PAIR]
    for copy in leaving:
        copy.wait()


def near_kernel(
    z, pad_ref, q, k, v, g, tiles, order, order_q, mixed, stats, turned, turned_out
):
    own = lax.axis_index("ctx")
    limit = z.rows * z.devs - pad_ref[0] - own * z.rows
    valid = iota((1, z.rows), 1) < limit
    lane = iota((z.rows, LANES), 1)
    both = jnp.zeros((z.rows, LANES), F32)
    for pair in range(z.pairs):
        lanes = slice(pair * PAIR, (pair + 1) * PAIR)
        query = q[:, lanes]
        grad = g[:, lanes].astype(F32)
        keys = halves(k[:, lanes])
        values = halves(v[:, lanes])
        total = None
        for side in range(2):
            head = 2 * pair + side
            scores = jnp.where(valid, dot(query, keys[side], NT), -jnp.inf)
            peak = jnp.max(scores, axis=1, keepdims=True)
            powers = jnp.exp(scores - peak)
            summed = jnp.sum(powers, axis=1, keepdims=True)
            part = dot(powers.astype(BF), values[side]) * (1.0 / summed)
            total = part if total is None else total + part
            both = jnp.where(lane == head, peak + jnp.log(summed), both)
            meets = jnp.sum(grad * part, axis=1, keepdims=True)
            both = jnp.where(lane == SECOND + head, meets, both)
        mixed[:, lanes] = total
    stats[...] = both
    for which, source_rows in enumerate((order, order_q)):
        for part, target in enumerate((turned, turned_out)):
            source = source_rows[part * z.half : (part + 1) * z.half, :]
            place = (iota((z.half, z.width), 1) == source).astype(F32).astype(BF)
            result = dot(place, tiles[...], NT).astype(BF)
            target[which * z.half : (which + 1) * z.half, :] = result


def of_level(level, refs, lanes):
    return jnp.concatenate([ref[:, lanes] for ref in refs[level]], axis=0)


def part_lanes(z, part, pair):
    return slice(part * z.width + pair * PAIR, part * z.width + (pair + 1) * PAIR)


def own_scores(z, limit, offs_ref, sel, refs):
    own = lax.axis_index("ctx")
    scores, places = [], []
    for level, (start, stop) in enumerate(level_parts(z)):
        place = gathered_place(z, own, level)
        for pair in range(z.pairs):
            query = sel[start:stop, part_lanes(z, 2, pair)]
            keys = halves(of_level(level, refs, part_lanes(z, 0, pair)))
            for side in range(2):
                valid = place + offs_ref[level, 2 * pair + side] < limit
                scores.append(jnp.where(valid, dot(query, keys[side], NT), -jnp.inf))
                places.append((level, 2 * pair + side, start, stop))
    spots, at = [], 0
    for level, head, start, stop in places:
        spots.append((level, head, at, at + stop - start))
        at += stop - start
    return jnp.concatenate(scores, axis=0), spots


def to_lanes(z, spots, columns):
    parts = []
    for level, (start, stop) in enumerate(level_parts(z)):
        lane = iota((stop - start, LANES), 1)
        part = jnp.zeros((stop - start, LANES), F32)
        for found, head, first, last in spots:
            if found == level:
                for shift, column in columns:
                    part = jnp.where(lane == shift + head, column[first:last], part)
        parts.append(part)
    parts.append(jnp.zeros((z.sel - level_parts(z)[1][1], LANES), F32))
    return jnp.concatenate(parts, axis=0)


def from_lanes(spots, array, shift):
    return lambda z: jnp.concatenate(
        [
            array[level_parts(z)[level][0] : level_parts(z)[level][1], shift + head : shift + head + 1]
            for level, head, _, _ in spots
        ],
        axis=0,
    )


def spot_of(spots, level, head):
    return next((first, last) for found, at, first, last in spots if (found, at) == (level, head))


def join_kernel(
    z, offs_ref, pad_ref, sel, mid_0, mid_1, far_0, far_1, near_stats, stats, picked, raw, held
):
    refs = ((mid_0, mid_1), (far_0, far_1))
    scores, spots = own_scores(z, z.rows * z.devs - pad_ref[0], offs_ref, sel, refs)
    peak = jnp.max(scores, axis=1, keepdims=True)
    powers = jnp.exp(scores - peak)
    summed = jnp.sum(powers, axis=1, keepdims=True)
    lse = peak + jnp.log(summed)
    scale = 1.0 / summed
    powers = powers.astype(BF)
    products = []
    tail = jnp.zeros((z.sel - level_parts(z)[1][1], PAIR), F32)
    for pair in range(z.pairs):
        totals = []
        for level, (start, stop) in enumerate(level_parts(z)):
            values = halves(of_level(level, refs, part_lanes(z, 1, pair)))
            parts = []
            for side in range(2):
                at, to = spot_of(spots, level, 2 * pair + side)
                parts.append(dot(powers[at:to], values[side]) * scale[at:to])
            totals.append(parts[0] + parts[1])
            grad = sel[start:stop, part_lanes(z, 3, pair)].astype(F32)
            products.append((level, pair, [grad * part for part in parts]))
        held[:, pair * PAIR : (pair + 1) * PAIR] = jnp.concatenate(totals + [tail], axis=0)
    products.sort(key=lambda entry: entry[:2])
    stacked = jnp.concatenate([part for _, _, both in products for part in both], axis=0)
    meets = jnp.sum(stacked, axis=1, keepdims=True)
    sel_both = to_lanes(z, spots, ((0, lse), (SECOND, meets)))
    raw[...] = sel_both
    masks = stat_masks(z, offs_ref)
    near = near_stats[...]
    mid, far = spread_stats(z, masks, sel_both)
    top = jnp.maximum(near, jnp.maximum(mid, far))
    total_lse = top + jnp.log(jnp.exp(near - top) + jnp.exp(mid - top) + jnp.exp(far - top))
    delta = sum(
        pltpu.roll(jnp.exp(value - total_lse), SECOND, 1) * value
        for value in (
            near,
            jnp.where(masks[0], mid, -LARGE),
            jnp.where(masks[1], far, -LARGE),
        )
    )
    both = jnp.where(iota((z.rows, LANES), 1) < SECOND, total_lse, delta)
    stats[...] = both
    picked[...] = pick_stats(z, masks, both)


def output_kernel(
    z, offs_ref, near_stats, stats, picked, raw, mixed, held, tiles, w_out, order,
    rows_out, turned, turned_out, attn,
):
    near_share = jnp.exp(near_stats[...] - stats[...])
    share = jnp.exp(raw[...] - picked[...])
    for pair in range(z.pairs):
        lanes = slice(pair * PAIR, (pair + 1) * PAIR)
        near = by_head(
            near_share[:, 2 * pair : 2 * pair + 1],
            near_share[:, 2 * pair + 1 : 2 * pair + 2],
            z.rows,
        )
        own = by_head(share[:, 2 * pair : 2 * pair + 1], share[:, 2 * pair + 1 : 2 * pair + 2], z.sel)
        combined = near * mixed[:, lanes] + spread(z, offs_ref, pair, own * held[:, lanes])
        attn[:, lanes] = combined.astype(BF)
    rows_out[...] = (tiles[...].astype(F32) + dot(attn[...], w_out[...])).astype(BF)
    for part, target in enumerate((turned, turned_out)):
        source = order[part * z.half : (part + 1) * z.half, :]
        place = (iota((z.half, z.width), 1) == source).astype(F32).astype(BF)
        target[...] = dot(place, attn[...], NT).astype(BF)


def own_grads_kernel(z, offs_ref, pad_ref, sel, mid_0, mid_1, far_0, far_1, picked, dq_sel):
    limit = z.rows * z.devs - pad_ref[0]
    refs = ((mid_0, mid_1), (far_0, far_1))
    scores, spots = own_scores(z, limit, offs_ref, sel, refs)
    probs = jnp.exp(scores - from_lanes(spots, picked, 0)(z))
    grad_probs = []
    for level, (start, stop) in enumerate(level_parts(z)):
        for pair in range(z.pairs):
            grad = sel[start:stop, part_lanes(z, 3, pair)]
            values = halves(of_level(level, refs, part_lanes(z, 1, pair)))
            grad_probs += [dot(grad, values[side], NT) for side in range(2)]
    grad_probs = jnp.concatenate(grad_probs, axis=0) - from_lanes(spots, picked, SECOND)(z)
    grad_scores = (probs * grad_probs).astype(BF)
    tail = jnp.zeros((z.sel - level_parts(z)[1][1], PAIR), F32)
    for pair in range(z.pairs):
        sums = []
        for level in range(2):
            keys = halves(of_level(level, refs, part_lanes(z, 0, pair)))
            at, to = spot_of(spots, level, 2 * pair)
            low = dot(grad_scores[at:to], keys[0])
            at, to = spot_of(spots, level, 2 * pair + 1)
            sums.append(low + dot(grad_scores[at:to], keys[1]))
        dq_sel[:, pair * PAIR : (pair + 1) * PAIR] = jnp.concatenate(sums + [tail], axis=0)


def near_grads_kernel(z, offs_ref, pad_ref, q, k, v, g, stats, dq_sel, dq, dk, dv):
    own = lax.axis_index("ctx")
    limit = z.rows * z.devs - pad_ref[0]
    valid_near = iota((z.rows, 1), 0) < limit - own * z.rows
    across = jnp.transpose(stats[...])
    for pair in range(z.pairs):
        lanes = slice(pair * PAIR, (pair + 1) * PAIR)
        query, grad = q[:, lanes], g[:, lanes]
        queries, grads = halves(query), halves(grad)
        keys, values = halves(k[:, lanes]), halves(v[:, lanes])
        sum_q = sum_k = sum_v = None
        for side in range(2):
            head = 2 * pair + side
            scores = jnp.where(valid_near, dot(keys[side], query, NT), -jnp.inf)
            probs = jnp.exp(scores - across[head : head + 1, :])
            grad_probs = dot(values[side], grad, NT)
            grad_scores = probs * (grad_probs - across[SECOND + head : SECOND + head + 1, :])
            grad_scores = grad_scores.astype(BF)
            part_k = dot(grad_scores, queries[side])
            part_v = dot(probs.astype(BF), grads[side])
            part_q = dot(grad_scores, keys[side], TN)
            if side == 0:
                sum_q, sum_k, sum_v = part_q, part_k, part_v
            else:
                sum_q, sum_k, sum_v = sum_q + part_q, sum_k + part_k, sum_v + part_v
        dk[:, lanes] = sum_k
        dv[:, lanes] = sum_v
        dq[:, lanes] = (SCALE * (sum_q + spread(z, offs_ref, pair, dq_sel[:, lanes]))).astype(BF)


def key_grads_kernel(
    z, offs_ref, pad_ref, sel, qg_0, qg_1, stats_0, stats_1, dk_near, dv_near, dk, dv
):
    own = lax.axis_index("ctx")
    limit = z.rows * z.devs - pad_ref[0] - own * z.rows
    parts = level_parts(z)
    stat_refs = (stats_0, stats_1)

    def rows_of(level, lanes):
        cuts = [slice(p * z.sel + level * z.mid, p * z.sel + (level + 1) * z.mid) for p in range(4)]
        return jnp.concatenate([ref[cut, lanes] for ref in (qg_0, qg_1) for cut in cuts], axis=0)

    tail = jnp.zeros((z.sel - parts[1][1], PAIR), F32)
    probs, grad_scores = {}, {}
    for level, (start, stop) in enumerate(parts):
        across = jnp.transpose(jnp.concatenate([ref[level * 4 * z.mid : (level + 1) * 4 * z.mid, :] for ref in stat_refs], axis=0))
        entry = iota((stop - start, 1), 0) + start
        for pair in range(z.pairs):
            keys = sel[start:stop, part_lanes(z, 0, pair)]
            values = sel[start:stop, part_lanes(z, 1, pair)]
            queries = halves(rows_of(level, part_lanes(z, 0, pair)))
            grads = halves(rows_of(level, part_lanes(z, 1, pair)))
            for side in range(2):
                head = 2 * pair + side
                at = chosen_row(z, entry, offs_ref[0, head], offs_ref[1, head])
                valid = (at >= 0) & (at < limit)
                scores = jnp.where(valid, dot(keys, queries[side], NT), -jnp.inf)
                exps = jnp.exp(scores - across[head : head + 1, :])
                grad_probs = dot(values, grads[side], NT)
                grad_probs = grad_probs - across[SECOND + head : SECOND + head + 1, :]
                probs[level, head] = exps.astype(BF)
                grad_scores[level, head] = (exps * grad_probs).astype(BF)
    sums_k, sums_v = {}, {}
    for pair in range(z.pairs):
        both_k, both_v = [], []
        for level in range(2):
            queries = halves(rows_of(level, part_lanes(z, 0, pair)))
            grads = halves(rows_of(level, part_lanes(z, 1, pair)))
            low, high = 2 * pair, 2 * pair + 1
            both_k.append(
                dot(grad_scores[level, low], queries[0]) + dot(grad_scores[level, high], queries[1])
            )
            both_v.append(dot(probs[level, low], grads[0]) + dot(probs[level, high], grads[1]))
        sums_k[pair] = jnp.concatenate(both_k + [tail], axis=0)
        sums_v[pair] = jnp.concatenate(both_v + [tail], axis=0)
    for pair in range(z.pairs):
        lanes = slice(pair * PAIR, (pair + 1) * PAIR)
        both = jnp.concatenate([sums_k[pair], sums_v[pair]], axis=1)
        moved = spread(z, offs_ref, pair, both)
        dk[:, lanes] = (dk_near[:, lanes] + moved[:, :PAIR]).astype(BF)
        dv[:, lanes] = (dv_near[:, lanes] + moved[:, PAIR:]).astype(BF)


def weights_kernel(start, left, left_other, right, right_other, out):
    rows = slice(start, start + out.shape[0])
    out[...] = (dot(left[rows, :], right[...]) + dot(left_other[rows, :], right_other[...])).astype(BF)


def late_weights_kernel(z, turned, turned_other, dk, dv, dk_other, dv_other, out):
    width = z.width
    left, other = turned[: z.half, :], turned_other[: z.half, :]
    out[:, :width] = (dot(left, dk[...]) + dot(other, dk_other[...])).astype(BF)
    out[:, width:] = (dot(left, dv[...]) + dot(other, dv_other[...])).astype(BF)


def tiles_kernel(z, dq, dk, dv, w_qkv, out):
    width = z.width
    out[...] = (
        dot(dq[...], w_qkv[:, :width], NT)
        + dot(dk[...], w_qkv[:, width : 2 * width], NT)
        + dot(dv[...], w_qkv[:, 2 * width :], NT)
    ).astype(BF)


def call(kernel, outs, flops, scratch=(), smem=0, spaces=None, vmem=VMEM_BYTES, hbm_outs=0, cost=1.0):
    def run(*args):
        moved = sum(int(np.prod(a.shape)) * a.dtype.itemsize for a in args)
        moved += sum(int(np.prod(s)) * jnp.dtype(t).itemsize for s, t in outs)
        specs = [
            pl.BlockSpec(memory_space=spaces or (pltpu.SMEM if i < smem else pltpu.VMEM))
            for i in range(len(args))
        ]
        return pl.pallas_call(
            kernel,
            out_shape=tuple(jax.ShapeDtypeStruct(s, t) for s, t in outs),
            in_specs=specs,
            out_specs=tuple(
                pl.BlockSpec(memory_space=pltpu.HBM if i < hbm_outs else pltpu.VMEM)
                for i in range(len(outs))
            ),
            scratch_shapes=list(scratch),
            compiler_params=pltpu.CompilerParams(vmem_limit_bytes=vmem),
            cost_estimate=pl.CostEstimate(
                flops=int(flops * cost), bytes_accessed=int(moved * cost), transcendentals=0
            ),
        )(*args)

    return run


def swap(value, mask, dev_count):
    return lax.ppermute(value, "ctx", [(d, d ^ mask) for d in range(dev_count)])


def upper_steps(dev_count):
    steps, base = [], GROUP
    while base < dev_count:
        count = 4 if base * 4 <= dev_count else 2
        steps.append((base, count))
        base *= count
    return steps


PLANE = (2, 4)


def tied(parts, first):
    return list(lax.optimization_barrier((*parts, *first))[: len(parts)]) if first else list(parts)


def step_parts(value, step, dev_count, first=()):
    base, count = step
    return tied([value] + [swap(value, base * i, dev_count) for i in range(1, count)], first)


def block_parts(value, step, dev_count):
    base, count = step
    size = value.shape[0] // count
    return [value[:size]] + [
        swap(value[i * size : (i + 1) * size], base * i, dev_count) for i in range(1, count)
    ]


def sum_parts(parts, dtype):
    return sum(part.astype(F32) for part in parts).astype(dtype)


def doubled(value, masks, dev_count, firsts=()):
    for i, mask in enumerate(masks):
        parts = tied([value, swap(value, mask, dev_count)], firsts[i] if i < len(firsts) else ())
        value = jnp.concatenate(parts, axis=0)
    return value


def halved(value, masks, dev_count, firsts=()):
    for i, mask in enumerate(masks):
        size = value.shape[0] // 2
        first = firsts[i] if i < len(firsts) else ()
        parts = tied([value[:size], swap(value[size:], mask, dev_count)], first)
        value = parts[0].astype(F32) + parts[1].astype(F32)
        value = value if i == len(masks) - 1 else value.astype(BF)
    return value


def reduce_all(value, steps, dev_count):
    for i, step in enumerate(steps):
        value = sum_parts(block_parts(value, step, dev_count), F32 if i == len(steps) - 1 else BF)
    return value


def strip_order(z, own, masks):
    digits = np.meshgrid(*[np.arange(2) for _ in masks], np.arange(z.strip), indexing="ij")
    moved = sum(digit * mask for digit, mask in zip(digits, masks)).reshape(-1, 1)
    return (own ^ moved.astype(np.int32)) * z.strip + digits[-1].reshape(-1, 1).astype(np.int32)


def after(value, *others):
    return lax.optimization_barrier((value, *others))[0]


def per_device(tiles, w_qkv, w_out, cotangent, offsets, pad_count):
    n = lax.axis_size("ctx")
    z = Sizes(tiles.shape[0], tiles.shape[1], n)
    own = lax.axis_index("ctx")
    rows, width = z.rows, z.width
    masks = [mask for mask in (2**i for i in range(30)) if GROUP <= mask < n]
    order = strip_order(z, own, [1, 4, 2] + masks[::-1])
    order_q = strip_order(z, own, [1] + masks[:-1] + [4, 2] + masks[-1:])
    order_out = strip_order(z, own, [1, 2, 4] + masks)
    base_flops = 2 * rows * rows * width

    def weights(start, *args):
        kernel = functools.partial(weights_kernel, start)
        return call(kernel, [((z.half, width), BF)], 4 * rows * width * width)(*args)[0]

    q, k, v, g, sel, mid_kv, mid_qg, far = call(
        functools.partial(project_kernel, z),
        [((rows, width), BF)] * 4
        + [((z.sel, 4 * width), BF)]
        + [((z.mid, 2 * width), BF)] * 2
        + [((z.far, 4 * width), BF)],
        2 * rows * width * 4 * width,
        scratch=[
            pltpu.SMEM(offsets.shape, jnp.int32),
            pltpu.VMEM(tiles.shape, BF),
            pltpu.VMEM(w_qkv.shape, BF),
            pltpu.VMEM(cotangent.shape, BF),
            pltpu.VMEM(w_out.shape, BF),
        ]
        + [pltpu.VMEM((rows, width), BF)] * 4
        + [pltpu.SemaphoreType.DMA((4 * LOAD_CUTS + 3,)), pltpu.SemaphoreType.DMA((4,))],
        hbm_outs=4,
        spaces=pltpu.HBM,
        vmem=PROJECT_VMEM_BYTES,
    )(offsets, tiles, w_qkv, cotangent, w_out)

    steps = upper_steps(n)
    far_up = far
    for step in steps[:-1]:
        far_up = jnp.concatenate(step_parts(far_up, step, n), axis=0)
    far_up = step_parts(far_up, steps[-1], n)
    far_kv = jnp.concatenate([part[:, : 2 * width] for part in far_up], axis=0)
    mid_parts = step_parts(mid_kv, PLANE, n)
    mixed, near_stats, turned, turned_out = call(
        functools.partial(near_kernel, z),
        [
            ((rows, width), F32),
            ((rows, LANES), F32),
            ((width, rows), BF),
            ((width, rows), BF),
        ],
        8 * base_flops,
        smem=1,
    )(pad_count, after(q, far_kv, *mid_parts[1:3]), k, v, g, tiles, order, order_q)
    mid_0 = jnp.concatenate(mid_parts, axis=0)
    mid_1 = swap(mid_0, 1, n)
    far_0 = jnp.concatenate(
        step_parts(after(far_kv, *mid_parts[1:3]), PLANE, n, (near_stats,)), axis=0
    )
    far_1 = swap(far_0, 1, n)
    stats, picked, raw, held = call(
        functools.partial(join_kernel, z),
        [((rows, LANES), F32), ((z.sel, LANES), F32), ((z.sel, LANES), F32), ((z.sel, width), F32)],
        3 * base_flops,
        smem=2,
    )(offsets, pad_count, sel, mid_0, mid_1, far_0, far_1, near_stats)

    (dq_sel,) = call(
        functools.partial(own_grads_kernel, z),
        [((z.sel, width), F32)],
        2 * base_flops,
        smem=2,
    )(offsets, pad_count, sel, mid_0, mid_1, far_0, far_1, picked)
    qg_mid, *qg_far = tied([mid_qg] + far_up, (dq_sel,))
    qg = jnp.concatenate([qg_mid] + [part[:, 2 * width :] for part in qg_far], axis=0)
    qg_parts = step_parts(qg, PLANE, n)
    cot_other = swap(after(cotangent, picked), 1, n)
    stats_up = doubled(picked[z.mid : z.mid + z.far], masks[:1], n, ((dq_sel,),))
    out_rows, attn_turned, attn_turned_out = call(
        functools.partial(output_kernel, z),
        [((rows, width), BF), ((z.half, rows), BF), ((z.half, rows), BF)],
        6 * rows * width * width,
        scratch=[pltpu.VMEM((rows, width), BF)],
        smem=1,
    )(offsets, near_stats, stats, after(picked, stats_up), raw, mixed, held, tiles, w_out, order_out)
    attn_other = swap(attn_turned_out, 1, n)
    stats_up = doubled(stats_up, masks[1:], n, ((out_rows,),))
    wout_half = weights(0, attn_turned, attn_other, cotangent, after(cot_other, stats_up))
    turned_other = swap(after(turned_out, wout_half), 1, n)
    qg_0 = jnp.concatenate(tied(qg_parts, (wout_half,)), axis=0)
    qg_1 = swap(qg_0, 1, n)

    stats_far = stats_up
    stats_up = jnp.concatenate([picked[: z.mid], stats_far], axis=1)
    stats_up = doubled(stats_up, (4,), n, ((wout_half,),))
    dq, dk_near, dv_near = call(
        functools.partial(near_grads_kernel, z),
        [((rows, width), BF), ((rows, width), F32), ((rows, width), F32)],
        8 * base_flops,
        smem=2,
    )(offsets, pad_count, after(q, stats_up), k, v, g, stats, dq_sel)
    dq_other = swap(dq, 1, n)
    stats_up = doubled(stats_up, (2,), n, ((dk_near,),))
    early_half = weights(z.half, turned, turned_other, dq, dq_other)
    stats_0 = jnp.concatenate(
        [
            stats_up[at * z.mid : (at + 1) * z.mid, level * LANES : (level + 1) * LANES]
            for level in range(2)
            for at in (0, 2, 1, 3)
        ],
        axis=0,
    )
    stats_1 = swap(stats_0, 1, n)

    dk, dv = call(
        functools.partial(key_grads_kernel, z),
        [((rows, width), BF), ((rows, width), BF)],
        3 * base_flops,
        smem=2,
        cost=LOW_COST,
    )(
        offsets, pad_count, sel, qg_0, qg_1, stats_0, stats_1,
        after(dk_near, early_half), dv_near,
    )
    dk_other = swap(dk, 1, n)
    dv_other = swap(dv, 1, n)
    (late_half,) = call(
        functools.partial(late_weights_kernel, z),
        [((z.half, 2 * width), BF)],
        4 * rows * width * width,
        cost=LOW_COST,
    )(turned, turned_other, dk, dv, dk_other, dv_other)
    (grad_tiles,) = call(
        functools.partial(tiles_kernel, z),
        [((rows, width), BF)],
        6 * rows * width * width,
        cost=LOW_COST,
    )(after(dq, late_half), dk, dv, w_qkv)
    late_parts = block_parts(late_half, PLANE, n)
    early = halved(early_half, masks[:-1], n, ((late_parts[1],),)).astype(BF)
    early = sum_parts(block_parts(early, PLANE, n), BF)
    wout = halved(wout_half, [2, 4] + masks[:-1], n, ((dk_near,), (late_parts[1],))).astype(BF)
    late = sum_parts(late_parts, BF)
    early = halved(after(early, late), masks[-1:], n)
    grad_wout = halved(after(wout, late), masks[-1:], n)
    late = reduce_all(late, upper_steps(n)[::-1], n)
    grad_wqkv = jnp.concatenate([early, late], axis=1)
    return out_rows, grad_tiles, grad_wqkv, grad_wout


def solution(mesh):
    return jax.shard_map(
        per_device,
        mesh=mesh,
        in_specs=(P("ctx", None), P(), P(), P("ctx", None), P(), P()),
        out_specs=(P("ctx", None), P("ctx", None), P("ctx", None), P("ctx", None)),
        check_vma=False,
    )
```
